32 devices in a mesh: ctx: 4 (over z), wt: 8 (over y, x, core).
Axes of the slice: x: 2, y: 2, z: 4, core: 2. Of those that a mesh axis runs over, the one named last changes fastest.
Arguments:
- inputs: bfloat16 [8, 2, 2048, 960], P('wt', None, 'ctx'), may hold values from -6 to 6
- cotangent: bfloat16 [8, 2, 2048, 960], P('wt', None, 'ctx'), may hold values from -6 to 6
- lengths: int32 [8, 2], P('wt'), may hold values from 512 to 2048, as said below
- order: int32 [8], replicated, may hold values from 0 to 7, as said below
- owner_slots: int32 [2400], replicated, may hold values from 0 to 2783, as said below
- master: float32 [2784, 64, 64], P(('ctx', 'wt'))
- stat_left: float32 [2784, 64, 64], P(('ctx', 'wt'))
- stat_right: float32 [2784, 64, 64], P(('ctx', 'wt'))
- root_left: float32 [2784, 64, 64], P(('ctx', 'wt'))
- root_right: float32 [2784, 64, 64], P(('ctx', 'wt'))
- gains: float32 [2, 960], replicated, may hold values from 0.5 to 1.5
- gain_stats: float32 [2, 960], replicated
Outputs:
- mixed: bfloat16 [8, 2, 2048, 960], P('wt', None, 'ctx')
- input_grad: float32 [8, 2, 2048, 960], P('wt', None, 'ctx')
- tile_grads: float32 [2784, 64, 64], P(('ctx', 'wt'))
- new_left: float32 [2784, 64, 64], P(('ctx', 'wt'))
- new_right: float32 [2784, 64, 64], P(('ctx', 'wt'))
- new_master: float32 [2784, 64, 64], P(('ctx', 'wt'))
- gain_grads: float32 [2, 960], replicated
- new_gain_stats: float32 [2, 960], replicated
- new_gains: float32 [2, 960], replicated
The draws below stay inside these ranges and needn't reach their ends.
Inputs may be any that keep to these rules, and one draw needn't show every extreme that they name: `lengths`: in every row one micro-batch's sequence has length 2048. `order`: A permutation of the 8 blocks. `owner_slots`: entries are distinct; a tile's owner is its entry // 87 and its slot there the entry % 87. The first 600 tiles take slots below 22, the others slots from 22 on; in each of these two ranges some owner has every slot filled.
All inputs are finite; a program needn't handle non-finite values.
Results may differ from the reference program's by a relative error of at most 0.014.
Values may be sent and summed in bfloat16 or wider, within the bound.
A program may use at most 640 MiB of HBM per device.

```python
import math
import jax
import jax.numpy as jnp
import numpy as np
from jax import lax

D = 960
FF = 2560
QH = 15
KVH = 5
HD = 64
TL = 64
MB = 2
LEN = 2048
ROWS = 512
BLK = 256
NBLK = 8
NSEQ = 8
QW = 960
KVW = 320
GRP = 3
NTA = 600
NT = 2400
CAP_A = 22
CAP_F = 65
CAP = 87
SLOTS = 2784
NTOK = 32768
DEVICES = 32


def matrix_ids():
    shapes_list = [(D, QW), (D, KVW), (D, KVW), (QW, D), (D, FF), (D, FF), (FF, D)]
    counts_list = [height // TL * (across // TL) for height, across in shapes_list]
    return np.repeat(np.arange(7), counts_list).astype(np.int32)


def place_group(group_key, amount, group_cap, shift_by):
    full_owner = jax.random.randint(jax.random.fold_in(group_key, 1), (), 0, DEVICES)
    ranking = jax.random.permutation(jax.random.fold_in(group_key, 2), DEVICES * group_cap).astype(jnp.int32)
    owners = jnp.arange(DEVICES * group_cap, dtype=jnp.int32) // group_cap
    ranking = jnp.where(owners == full_owner, ranking - DEVICES * group_cap, ranking)
    chosen = jnp.argsort(ranking, stable=True)[:amount].astype(jnp.int32)
    return chosen // group_cap * CAP + chosen % group_cap + shift_by


def owner_entries(key):
    group_base = jax.random.fold_in(key, 77)
    first_part = place_group(jax.random.fold_in(group_base, 1), NTA, CAP_A, 0)
    second_part = place_group(jax.random.fold_in(group_base, 2), NT - NTA, CAP_F, CAP_A)
    return jnp.concatenate([first_part, second_part]).astype(jnp.int32)


def slot_matrix(key):
    entries = owner_entries(key)
    return jnp.zeros((SLOTS,), jnp.int32).at[entries].set(jnp.asarray(matrix_ids()))


def grad_guess():
    return np.array([0.05, 0.05, 0.1, 0.1, 0.3, 0.3, 0.5])


def symmetric_draw(noise_key, level, diag_low, diag_high, spread):
    diag_key = jax.random.fold_in(noise_key, 1)
    off_key = jax.random.fold_in(noise_key, 2)
    diagonal = jnp.exp(jax.random.uniform(diag_key, (SLOTS, TL), jnp.float32, math.log(diag_low), math.log(diag_high)))
    noise = jax.random.normal(off_key, (SLOTS, TL, TL), jnp.float32)
    offdiag = 0.5 * spread * (noise + jnp.swapaxes(noise, 1, 2))
    identity = jnp.eye(TL, dtype=jnp.float32)
    return level[:, None, None] * (offdiag * (1.0 - identity) + identity * diagonal[:, :, None])


def stat_level(matrix_of):
    table = 0.6 * NTOK * TL * grad_guess() ** 2 * (0.05 / 0.95)
    return jnp.asarray(table, jnp.float32)[matrix_of]


def root_level(matrix_of):
    table = (0.1 * 0.6 * NTOK * TL * grad_guess() ** 2) ** (-0.25)
    return jnp.asarray(table, jnp.float32)[matrix_of]


def draw_lengths(key, part):
    key = jax.random.fold_in(key, 5)
    base_lengths = jax.random.randint(jax.random.fold_in(key, 1), (NSEQ, MB), LEN // 4, LEN + 1)
    full_pick = jax.random.randint(jax.random.fold_in(key, 2), (NSEQ,), 0, MB)
    is_full = jnp.arange(MB, dtype=jnp.int32)[None, :] == full_pick[:, None]
    return jnp.where(is_full, LEN, base_lengths).astype(jnp.int32)


def draw_order(key, part):
    key = jax.random.fold_in(key, 7)
    return jax.random.permutation(key, NBLK).astype(jnp.int32)


def draw_owner_slots(key, part):
    return owner_entries(key)


def draw_master(key, part):
    matrix_of = slot_matrix(key)
    key = jax.random.fold_in(key, 9)
    spread_table = np.array([D ** (-0.5), D ** (-0.5), D ** (-0.5), (LEN / (8.0 * QW)) ** 0.5, D ** (-0.5), D ** (-0.5), FF ** (-0.5)])
    scale_rows = jnp.asarray(spread_table, jnp.float32)[matrix_of]
    return jax.random.normal(key, (SLOTS, TL, TL), jnp.float32) * scale_rows[:, None, None]


def draw_stat_left(key, part):
    matrix_of = slot_matrix(key)
    key = jax.random.fold_in(key, 11)
    return symmetric_draw(key, stat_level(matrix_of), 1.0, 4.0, 0.03)


def draw_stat_right(key, part):
    matrix_of = slot_matrix(key)
    key = jax.random.fold_in(key, 13)
    return symmetric_draw(key, stat_level(matrix_of), 1.0, 4.0, 0.03)


def draw_root_left(key, part):
    matrix_of = slot_matrix(key)
    key = jax.random.fold_in(key, 17)
    return symmetric_draw(key, root_level(matrix_of), 1.0, 2.0, 0.03)


def draw_root_right(key, part):
    matrix_of = slot_matrix(key)
    key = jax.random.fold_in(key, 19)
    return symmetric_draw(key, root_level(matrix_of), 1.0, 2.0, 0.03)


def draw_gain_stats(key, part):
    key = jax.random.fold_in(key, 23)
    row_guess = jnp.asarray(np.array([0.3, 1.0]), jnp.float32)
    level = 0.05 / 0.95 * 0.6 * NTOK * row_guess ** 2
    factor = jnp.exp(jax.random.uniform(key, (2, D), jnp.float32, 0.0, math.log(4.0)))
    return level[:, None] * factor


def block_levels(key, dims, shards, smallest, high):
    def one(dim, blocks):
        heights = jax.random.uniform(jax.random.fold_in(jax.random.fold_in(key, 6), dim), (blocks,), jnp.float32, smallest / len(shards), high / len(shards))
        return jnp.repeat(jnp.exp(heights), dims[dim] // blocks).reshape((-1,) + (1,) * (len(dims) - dim - 1))

    level = one(*shards[0])
    for cut in shards[1:]:
        level = level * one(*cut)
    return level


def bell_draw(own_key, extent, width, most, pieces=(), kind=jnp.bfloat16):
    values = width * jax.random.normal(own_key, extent, jnp.float32)
    if pieces:
        values = values * block_levels(own_key, extent, pieces, -0.22, 0.18)
    return jnp.clip(values, -most, most).astype(kind)


def setup_inputs(seed: int = 0) -> dict:
    arg_keys = jax.random.split(jax.random.key(seed), 13)
    return {
        "inputs": bell_draw(arg_keys[0], (NSEQ, MB, LEN, D), 1.0, 6.0, ((0, 8), (2, 4))),
        "cotangent": bell_draw(arg_keys[1], (NSEQ, MB, LEN, D), 1.0, 6.0, ((0, 8), (2, 4))),
        "lengths": draw_lengths(jax.random.fold_in(arg_keys[12], 71), 0),
        "order": draw_order(jax.random.fold_in(arg_keys[12], 71), 0),
        "owner_slots": draw_owner_slots(jax.random.fold_in(arg_keys[12], 71), 0),
        "master": draw_master(jax.random.fold_in(arg_keys[12], 71), 0),
        "stat_left": draw_stat_left(jax.random.fold_in(arg_keys[12], 71), 0),
        "stat_right": draw_stat_right(jax.random.fold_in(arg_keys[12], 71), 0),
        "root_left": draw_root_left(jax.random.fold_in(arg_keys[12], 71), 0),
        "root_right": draw_root_right(jax.random.fold_in(arg_keys[12], 71), 0),
        "gains": jnp.clip(1.0 + 0.1 * jax.random.normal(arg_keys[10], (2, D), jnp.float32), 0.5, 1.5),
        "gain_stats": draw_gain_stats(jax.random.fold_in(arg_keys[12], 71), 0),
    }


@jax.custom_vjp
def low(v):
    return lax.optimization_barrier(v.astype(jnp.bfloat16)).astype(jnp.float32)

@jax.custom_vjp
def low_back(v):
    return v

def low_keep(v):
    return (low(v), None)

def low_pass(kept, grad):
    return (grad,)

def back_keep(v):
    return (v, None)

def back_low(kept, grad):
    return (low(grad),)
low.defvjp(low_keep, low_pass)
low_back.defvjp(back_keep, back_low)
epsilon = 1e-05
decay_rate = 0.95
step_rate = 0.05
gain_rate = 0.05
rope_base = 10000.0
blocked_score = -1e+30

def matrix_shapes():
    return [(D, QW), (D, KVW), (D, KVW), (QW, D), (D, FF), (D, FF), (FF, D)]

def slot_positions(order, slot_index, block_rows, per_device):
    device = slot_index // per_device
    block_pick = 2 * device + slot_index % per_device // block_rows
    choices_row = jnp.arange(order.shape[0], dtype=jnp.int32)
    block_id = lax.optimization_barrier(jnp.sum(jnp.where(choices_row[None, :] == block_pick[:, None], order[None, :], 0), axis=1))
    return (block_id * block_rows + slot_index % block_rows).astype(jnp.int32)

def rotate(values, position, direction):
    half_dim = values.shape[-1] // 2
    frequency = rope_base ** (-jnp.arange(half_dim, dtype=jnp.float32) * 2.0 / values.shape[-1])
    angle = position.astype(jnp.float32)[:, None] * frequency[None, :]
    cosine = jnp.cos(angle)[:, None, :]
    sine = direction * jnp.sin(angle)[:, None, :]
    first_half = values[..., :half_dim]
    second_half = values[..., half_dim:]
    return jnp.concatenate([first_half * cosine - second_half * sine, second_half * cosine + first_half * sine], axis=-1)

def assemble_all(tile_pool):
    matrices = []
    first_tile = 0
    for height, across in matrix_shapes():
        amount = height // TL * (across // TL)
        tile_block = tile_pool[first_tile:first_tile + amount].reshape(height // TL, across // TL, TL, TL)
        matrices.append(tile_block.transpose(0, 2, 1, 3).reshape(height, across))
        first_tile += amount
    return matrices

def normalize(vector_rows, gain):
    inverse_rms = lax.rsqrt(lax.optimization_barrier(jnp.mean(vector_rows * vector_rows, axis=-1, keepdims=True)) + epsilon)
    return low(vector_rows * inverse_rms * gain)

def sequence_layer(values, live_row, position, causal, matrices, gain_pair):
    highest = lax.Precision.HIGHEST
    w_query, w_key, w_value, w_out, w_gate, w_up, w_down = matrices
    normed_attn = normalize(values, gain_pair[0])
    query_pre = low_back(jnp.dot(normed_attn, w_query, precision=highest))
    key_pre = low_back(jnp.dot(normed_attn, w_key, precision=highest))
    values_rows = low(low_back(jnp.dot(normed_attn, w_value, precision=highest)))
    queries = low(rotate(query_pre.reshape(LEN, QH, HD), position, 1.0)).reshape(LEN, KVH, GRP, HD)
    keys_rot = low(rotate(key_pre.reshape(LEN, KVH, HD), position, 1.0))
    value_heads = values_rows.reshape(LEN, KVH, HD)
    scores = low_back(jnp.einsum('qhgd,khd->hgqk', queries, keys_rot, precision=highest) * HD ** (-0.5))
    allowed = jnp.logical_and(causal, live_row[None, :])
    scores = jnp.where(allowed[None, None], scores, blocked_score)
    row_peak = lax.optimization_barrier(jnp.max(scores, axis=-1, keepdims=True))
    exp_scores = jnp.exp(scores - row_peak)
    probs = low(exp_scores / lax.optimization_barrier(jnp.sum(exp_scores, axis=-1, keepdims=True)))
    attn_heads = jnp.einsum('hgqk,khd->qhgd', probs, value_heads, precision=highest)
    attn_out = low(low_back(attn_heads.reshape(LEN, QW)))
    residual = values + low_back(jnp.dot(attn_out, w_out, precision=highest))
    normed_ffn = normalize(residual, gain_pair[1])
    gate_pre = low_back(jnp.dot(normed_ffn, w_gate, precision=highest))
    up_pre = low_back(jnp.dot(normed_ffn, w_up, precision=highest))
    hidden = low(jax.nn.silu(gate_pre) * up_pre)
    return residual + jnp.dot(hidden, w_down, precision=highest)

def reference(inputs, cotangent, lengths, order, owner_slots, master, stat_left, stat_right, root_left, root_right, gains, gain_stats):
    highest = lax.Precision.HIGHEST
    position = slot_positions(order, jnp.arange(LEN, dtype=jnp.int32), BLK, ROWS)
    live_mask = (position[None, None, :] < lengths[:, :, None]).reshape(NSEQ * MB, LEN)
    causal = position[None, :] <= position[:, None]
    inputs_flat = inputs.astype(jnp.float32).reshape(NSEQ * MB, LEN, D)
    grad_seed = jnp.where(live_mask[:, :, None], cotangent.astype(jnp.float32).reshape(NSEQ * MB, LEN, D), jnp.zeros((), jnp.float32))

    def forward(master_pool, gain_pair, activations):
        tile_pool = low(master_pool[owner_slots])
        matrices = assemble_all(tile_pool)

        def one_sequence(pair_in):
            return sequence_layer(pair_in[0], pair_in[1], position, causal, matrices, gain_pair)
        return lax.map(jax.checkpoint(one_sequence), (activations, live_mask))
    result, pullback = jax.vjp(forward, master, gains, inputs_flat)
    tile_grads, gain_grads, input_grad = pullback(grad_seed)
    gram_left = jnp.einsum('sij,skj->sik', tile_grads, tile_grads, precision=highest)
    gram_right = jnp.einsum('sji,sjk->sik', tile_grads, tile_grads, precision=highest)
    new_left = decay_rate * stat_left + (1.0 - decay_rate) * gram_left
    new_right = decay_rate * stat_right + (1.0 - decay_rate) * gram_right
    step_left = jnp.einsum('sij,sjk->sik', root_left, tile_grads, precision=highest)
    step_full = jnp.einsum('sij,sjk->sik', step_left, root_right, precision=highest)
    new_master = master - step_rate * step_full
    new_gain_stats = decay_rate * gain_stats + (1.0 - decay_rate) * gain_grads * gain_grads
    new_gains = gains - gain_rate * gain_grads * lax.rsqrt(new_gain_stats)
    mixed = result.astype(jnp.bfloat16).reshape(NSEQ, MB, LEN, D)
    input_grad = input_grad.reshape(NSEQ, MB, LEN, D)
    return (mixed, input_grad, tile_grads, new_left, new_right, new_master, gain_grads, new_gain_stats, new_gains)
```

```python
import functools

import jax
import jax.numpy as jnp
import numpy as np
from jax import lax
from jax.experimental import pallas as pl
from jax.experimental.pallas import tpu as pltpu
from jax.sharding import PartitionSpec as P

D = 960
FF = 2560
QH = 15
KVH = 5
HD = 64
TL = 64
QW = 960
KVW = 320
GRP = 3
NTA = 600
NT = 2400
QP = 1024
CW = 1664
BLK = 256
AXES = ("ctx", "wt")

epsilon = 1e-05
decay_rate = 0.95
step_rate = 0.05
gain_rate = 0.05
rope_base = 10000.0
blocked_score = -1e30
bf16 = jnp.bfloat16
f32 = jnp.float32
VM = pl.BlockSpec(memory_space=pltpu.VMEM)
SM = pl.BlockSpec(memory_space=pltpu.SMEM)
ANY = pl.BlockSpec(memory_space=pl.ANY)


def params(megabytes, **kwargs):
    return pltpu.CompilerParams(vmem_limit_bytes=megabytes << 20, **kwargs)


def cost(flops, nbytes, trans=0):
    return pl.CostEstimate(flops=int(flops), bytes_accessed=int(nbytes), transcendentals=int(trans))


def is_line(n_ctx, n_wt):
    return n_ctx == 4 and n_wt == 8


def flip(x, bit):
    return lax.ppermute(x, "wt", [(i, i ^ bit) for i in range(8)])


def go_up(x, sources=(0, 1, 2)):
    return lax.ppermute(x, "ctx", [(i, i + 1) for i in sources])


def go_down(x, sources=(1, 2, 3)):
    return lax.ppermute(x, "ctx", [(i, i - 1) for i in sources])


def line_parts(x):
    ups, downs = [], []
    low, high = x, x
    for _ in range(3):
        low = go_up(low)
        high = go_down(high)
        ups.append(low)
        downs.append(high)
    return [x] + ups + downs


def line_cyclic(x, c):
    _, u1, u2, u3, d1, d2, d3 = line_parts(x)
    return [x, jnp.where(c >= 1, u1, d3), jnp.where(c >= 2, u2, d2), jnp.where(c >= 3, u3, d1)]


def tile_halves(n):
    return (n + 1) // 2


def gather_tiles(own, c, n_ctx, n_wt):
    if not is_line(n_ctx, n_wt):
        return [lax.all_gather(own, AXES, axis=0, tiled=True)]
    n1 = tile_halves(own.shape[0])
    here = jnp.stack(line_cyclic(own, c))
    over_x = flip(here, 2)
    over_y = flip(here, 4)
    diag_a = flip(over_y[:, :n1], 2)
    diag_b = flip(over_x[:, n1:], 4)
    near = [here, over_x, over_y, diag_a, diag_b]
    far = [flip(a, 1) for a in near]
    return [a.reshape((-1,) + a.shape[2:]) for a in near + far]


def part_index(owner, slot, n, c, w, n_ctx, n_wt):
    if not is_line(n_ctx, n_wt):
        return owner * n + slot
    n1 = tile_halves(n)
    n2 = n - n1
    d = (c - owner // n_wt) & 3
    xw = (owner % n_wt) ^ w
    core, quad = xw & 1, xw >> 1
    plain = quad * (4 * n) + d * n + slot
    diag = 12 * n + jnp.where(slot < n1, d * n1 + slot, 4 * n1 + d * n2 + slot - n1)
    return core * (16 * n) + jnp.where(quad == 3, diag, plain)


def reduce_tiles(mine, other, n, c, n_ctx, n_wt):
    n1 = tile_halves(n)
    n2 = n - n1

    def add(a, b):
        return (a.astype(f32) + b.astype(f32)).astype(bf16)

    total = add(mine, flip(other, 1))
    tail = total.shape[1:]
    s0 = total[: 4 * n].reshape((4, n) + tail)
    s1 = total[4 * n : 8 * n].reshape((4, n) + tail)
    s2 = total[8 * n : 12 * n].reshape((4, n) + tail)
    s3a = total[12 * n : 12 * n + 4 * n1].reshape((4, n1) + tail)
    s3b = total[12 * n + 4 * n1 : 16 * n].reshape((4, n2) + tail)
    ra = flip(s3a, 2)
    rb = flip(s3b, 4)
    t1 = jnp.concatenate([s1[:, :n1], add(s1[:, n1:], rb)], axis=1)
    t2 = jnp.concatenate([add(s2[:, :n1], ra), s2[:, n1:]], axis=1)
    rx = flip(t1, 2)
    ry = flip(t2, 4)
    own = s0.astype(f32) + rx.astype(f32) + ry.astype(f32)
    return line_reduce([own[0], own[1], own[2], own[3]])


def line_reduce(parts):
    low = [p.astype(bf16) for p in parts]
    wide = [p.astype(f32) for p in parts]
    up = go_up(low[1], (0,))
    up = go_up((wide[2] + up.astype(f32)).astype(bf16), (0, 1))
    up = go_up((wide[3] + up.astype(f32)).astype(bf16), (0, 1, 2))
    down = go_down(low[3], (3,))
    down = go_down((wide[2] + down.astype(f32)).astype(bf16), (2, 3))
    down = go_down((wide[1] + down.astype(f32)).astype(bf16), (1, 2, 3))
    return wide[0] + up.astype(f32) + down.astype(f32)


def load_parts(parts, pool, sems):
    at = 0
    copies = []
    for i, part in enumerate(parts):
        rows = part.shape[0]
        copies.append(pltpu.make_async_copy(part, pool.at[pl.ds(at, rows)], sems.at[i]))
        at += rows
    for copy in copies:
        copy.start()
    for copy in copies:
        copy.wait()


def place_pair(pool, table, ref, row, lane, a, b):
    first = pool[table[a]]
    second = pool[table[b]]
    ref[pl.ds(row, 32), lane : lane + 128] = jnp.concatenate([first[:, :64], second[:, :64]], axis=1)
    ref[pl.ds(row + 32, 32), lane : lane + 128] = jnp.concatenate([first[:, 64:], second[:, 64:]], axis=1)


def place_single(pool, table, ref, row, lane, a):
    first = pool[table[a]]
    ref[pl.ds(row, 32), lane : lane + 64] = first[:, :64]
    ref[pl.ds(row + 32, 32), lane : lane + 64] = first[:, 64:]


def assemble_attn_kernel(count, table, *refs):
    parts, (wqkv, wo, pool, sems) = refs[:count], refs[count:]
    load_parts(parts, pool, sems)

    def qkv_row(r, _):
        row = pl.multiple_of(r * 64, 64)
        for p in range(7):
            place_pair(pool, table, wqkv, row, 128 * p, r * 15 + 2 * p, r * 15 + 2 * p + 1)
        place_single(pool, table, wqkv, row, 896, r * 15 + 14)
        wqkv[pl.ds(row, 64), 960:1024] = jnp.zeros((64, 64), bf16)
        for g in range(KVH):
            place_pair(pool, table, wqkv, row, QP + 128 * g, 225 + r * 5 + g, 300 + r * 5 + g)
        for p in range(7):
            place_pair(pool, table, wo, row, 128 * p, 375 + r * 15 + 2 * p, 375 + r * 15 + 2 * p + 1)
        place_single(pool, table, wo, row, 896, 375 + r * 15 + 14)
        return 0

    lax.fori_loop(0, 15, qkv_row, 0)
    wo[pl.ds(960, 64), :] = jnp.zeros((64, D), bf16)


def assemble_ffn_kernel(count, table, *refs):
    parts, (wgu, wd, pool, sems) = refs[:count], refs[count:]
    load_parts(parts, pool, sems)

    def gu_row(r, _):
        row = pl.multiple_of(r * 64, 64)
        for m in range(2):
            for p in range(20):
                base = 600 * m + r * 40 + 2 * p
                place_pair(pool, table, wgu, row, FF * m + 128 * p, base, base + 1)
        return 0

    lax.fori_loop(0, 15, gu_row, 0)

    def d_row(r, _):
        row = pl.multiple_of(r * 64, 64)
        for p in range(7):
            place_pair(pool, table, wd, row, 128 * p, 1200 + r * 15 + 2 * p, 1200 + r * 15 + 2 * p + 1)
        place_single(pool, table, wd, row, 896, 1200 + r * 15 + 14)
        return 0

    lax.fori_loop(0, 40, d_row, 0)


def assemble(kernel, parts, table, shapes):
    total = sum(p.shape[0] for p in parts)
    out_bytes = sum(2 * a * b for a, b in shapes)
    return pl.pallas_call(
        functools.partial(kernel, len(parts)),
        out_shape=[jax.ShapeDtypeStruct(s, bf16) for s in shapes],
        in_specs=[SM] + [ANY] * len(parts),
        out_specs=[VM] * len(shapes),
        scratch_shapes=[pltpu.VMEM((total, 32, 128), bf16), pltpu.SemaphoreType.DMA((len(parts),))],
        compiler_params=params(52),
        cost_estimate=cost(0, 4 * out_bytes),
    )(table, *parts)


def pick_pair(pool, table, ref, row, lane, a, b):
    block = ref[pl.ds(row, 64), lane : lane + 128]
    pool[table[a]] = jnp.concatenate([block[:32, :64], block[32:, :64]], axis=1)
    pool[table[b]] = jnp.concatenate([block[:32, 64:], block[32:, 64:]], axis=1)


def pick_single(pool, table, ref, row, lane, a):
    block = ref[pl.ds(row, 64), lane : lane + 64]
    pool[table[a]] = jnp.concatenate([block[:32], block[32:]], axis=1)


def clear_pool(pool):
    step = 8
    whole = pool.shape[0] // step

    def clear(i, _):
        pool[pl.ds(i * step, step)] = jnp.zeros((step, 32, 128), bf16)
        return 0

    lax.fori_loop(0, whole, clear, 0)
    rest = pool.shape[0] - whole * step
    if rest:
        pool[whole * step :] = jnp.zeros((rest, 32, 128), bf16)


def flush_pool(pool, outs, sems):
    at = 0
    copies = []
    for i, out in enumerate(outs):
        rows = out.shape[0]
        copies.append(pltpu.make_async_copy(pool.at[pl.ds(at, rows)], out, sems.at[i]))
        at += rows
    for copy in copies:
        copy.start()
    for copy in copies:
        copy.wait()


def pack_attn_kernel(table, dqkv, dwo, *refs):
    outs, (pool, sems) = refs[:-2], refs[-2:]
    clear_pool(pool)

    def qkv_row(r, _):
        row = pl.multiple_of(r * 64, 64)
        for p in range(7):
            pick_pair(pool, table, dqkv, row, 128 * p, r * 15 + 2 * p, r * 15 + 2 * p + 1)
        pick_single(pool, table, dqkv, row, 896, r * 15 + 14)
        for g in range(KVH):
            pick_pair(pool, table, dqkv, row, QP + 128 * g, 225 + r * 5 + g, 300 + r * 5 + g)
        for p in range(7):
            pick_pair(pool, table, dwo, row, 128 * p, 375 + r * 15 + 2 * p, 375 + r * 15 + 2 * p + 1)
        pick_single(pool, table, dwo, row, 896, 375 + r * 15 + 14)
        return 0

    lax.fori_loop(0, 15, qkv_row, 0)
    flush_pool(pool, outs, sems)


def pack_ffn_kernel(table, dgu, dwd, *refs):
    outs, (pool, sems) = refs[:-2], refs[-2:]
    clear_pool(pool)

    def gu_row(r, _):
        row = pl.multiple_of(r * 64, 64)
        for m in range(2):
            for p in range(20):
                base = 600 * m + r * 40 + 2 * p
                pick_pair(pool, table, dgu, row, FF * m + 128 * p, base, base + 1)
        return 0

    lax.fori_loop(0, 15, gu_row, 0)

    def d_row(r, _):
        row = pl.multiple_of(r * 64, 64)
        for p in range(7):
            pick_pair(pool, table, dwd, row, 128 * p, 1200 + r * 15 + 2 * p, 1200 + r * 15 + 2 * p + 1)
        pick_single(pool, table, dwd, row, 896, 1200 + r * 15 + 14)
        return 0

    lax.fori_loop(0, 40, d_row, 0)
    flush_pool(pool, outs, sems)


def pack(kernel, table, first, second, total, pieces):
    return pl.pallas_call(
        kernel,
        out_shape=[jax.ShapeDtypeStruct((total // pieces, 32, 128), bf16)] * pieces,
        in_specs=[SM, VM, VM],
        out_specs=[ANY] * pieces,
        scratch_shapes=[pltpu.VMEM((total, 32, 128), bf16), pltpu.SemaphoreType.DMA((pieces,))],
        compiler_params=params(52),
        cost_estimate=cost(0, 8 * (first.size + second.size)),
    )(table, first, second)


def swap_halves(x):
    lane = lax.broadcasted_iota(jnp.int32, x.shape, 1)
    return jnp.where(lane % 64 < 32, pltpu.roll(x, 96, 1), pltpu.roll(x, 32, 1))


def qkv_kernel(x_ref, gain_ref, w_ref, cos_ref, sin_ref, q_ref, kv_ref, normed_ref):
    x = x_ref[...].astype(f32)
    inverse = lax.rsqrt(jnp.mean(x * x, axis=1, keepdims=True) + epsilon)
    normed = (x * inverse * gain_ref[...]).astype(bf16)
    normed_ref[...] = normed
    cosine, sine = cos_ref[...], sin_ref[...]
    lane = lax.broadcasted_iota(jnp.int32, cosine.shape, 1)
    left = lane < 64
    for p in range(8):
        rows = jnp.dot(normed, w_ref[:, 128 * p : 128 * p + 128], preferred_element_type=f32)
        rows = (rows * cosine + swap_halves(rows) * sine).astype(bf16).astype(f32) * 0.125
        q_ref[2 * p] = jnp.where(left, rows, 0.0).astype(bf16)
        if 2 * p + 1 < QH:
            q_ref[2 * p + 1] = jnp.where(left, pltpu.roll(rows, 64, 1), 0.0).astype(bf16)
    cosine = jnp.where(left, cosine, 1.0)
    sine = jnp.where(left, sine, 0.0)
    for g in range(KVH):
        at = QP + 128 * g
        rows = jnp.dot(normed, w_ref[:, at : at + 128], preferred_element_type=f32)
        kv_ref[0, g] = (rows * cosine + swap_halves(rows) * sine).astype(bf16)


def qkv_rows(x, gain, wqkv, cosine, sine, micro):
    tokens = x.shape[0]
    rows = tokens // micro
    blk = min(BLK, rows)
    steps = tokens // blk
    per = steps // micro
    return pl.pallas_call(
        qkv_kernel,
        grid=(steps,),
        out_shape=[
            jax.ShapeDtypeStruct((QH, tokens, 128), bf16),
            jax.ShapeDtypeStruct((micro, KVH, rows, 128), bf16),
            jax.ShapeDtypeStruct((tokens, D), bf16),
        ],
        in_specs=[
            pl.BlockSpec((blk, D), lambda i: (i, 0)),
            pl.BlockSpec((1, D), lambda i: (0, 0)),
            pl.BlockSpec((D, CW), lambda i: (0, 0)),
            pl.BlockSpec((blk, 128), lambda i: (i % per, 0)),
            pl.BlockSpec((blk, 128), lambda i: (i % per, 0)),
        ],
        out_specs=[
            pl.BlockSpec((QH, blk, 128), lambda i: (0, i, 0)),
            pl.BlockSpec((1, KVH, blk, 128), lambda i: (i // per, 0, i % per, 0)),
            pl.BlockSpec((blk, D), lambda i: (i, 0)),
        ],
        compiler_params=params(40),
        cost_estimate=cost(2 * tokens * D * CW, 14 << 20),
    )(x, gain, wqkv, cosine, sine)


META = 4


def load_chunks(meta, parts, pool, sems, line):
    c = meta[3]

    def moves(act):
        if not line:
            act(pltpu.make_async_copy(parts[0], pool, sems.at[0]))
            return
        act(pltpu.make_async_copy(parts[0], pool.at[0], sems.at[0]))
        for d in range(1, 4):

            @pl.when(c >= d)
            def _(d=d):
                act(pltpu.make_async_copy(parts[d], pool.at[d], sems.at[d]))

            @pl.when(c < d)
            def _(d=d):
                act(pltpu.make_async_copy(parts[3 + 4 - d], pool.at[d], sems.at[d]))

    moves(lambda copy: copy.start())
    moves(lambda copy: copy.wait())


def masked(scores, block, q_block, length):
    blk = scores.shape[0]
    key = block * blk + lax.broadcasted_iota(jnp.int32, scores.shape, 0)
    query = q_block * blk + lax.broadcasted_iota(jnp.int32, scores.shape, 1)
    return jnp.where(jnp.logical_and(key <= query, key < length), scores, blocked_score)


def nt_dot(a, b):
    return lax.dot_general(a, b, (((1,), (1,)), ((), ())), preferred_element_type=f32)


def tn_dot(a, b):
    return lax.dot_general(a, b, (((0,), (0,)), ((), ())), preferred_element_type=f32)


def key_block(pool, meta, block, g):
    spot = meta[META + block]
    blk = pool.shape[2] // 2
    return pool[spot // 2, g, pl.ds(pl.multiple_of((spot % 2) * blk, blk), blk), :]


def flash_forward_kernel(line, count, meta, q_ref, *refs):
    parts, (out_ref, lse_ref, pool, peak, acc, turned, sems) = refs[:count], refs[count:]
    load_chunks(meta, parts, pool, sems, line)
    length = meta[2]
    blk = q_ref.shape[1] // 2
    live_blocks = (length + blk - 1) // blk
    turned[960:, :] = jnp.zeros((64, blk), f32)
    for qi in range(2):
        q_block = meta[qi]
        blocks = jnp.minimum(q_block + 1, live_blocks)

        def group(g, _):
            queries = [q_ref[GRP * g + h, blk * qi : blk * qi + blk, :] for h in range(GRP)]
            for h in range(GRP):
                peak[h] = jnp.full((1, blk), blocked_score, f32)
                acc[h] = jnp.zeros((128, blk), f32)

            def step(block, with_mask):
                kv = key_block(pool, meta, block, g)
                lane = lax.broadcasted_iota(jnp.int32, kv.shape, 1)
                summed = jnp.where(lane < 64, jnp.ones((), bf16), kv)
                for h in range(GRP):
                    scores = nt_dot(kv, queries[h])
                    if with_mask:
                        scores = masked(scores, block, q_block, length)
                    before = peak[h]
                    now = jnp.maximum(before, jnp.max(scores, axis=0, keepdims=True))
                    weights = jnp.exp(scores - now).astype(bf16)
                    peak[h] = now
                    acc[h] = acc[h] * jnp.exp(before - now) + tn_dot(summed, weights)

            def plain(block, _):
                step(block, False)
                return 0

            lax.fori_loop(0, blocks - 1, plain, 0)
            step(blocks - 1, True)
            for h in range(GRP):
                total = acc[h][0:1, :]
                turned[pl.ds(pl.multiple_of((GRP * g + h) * HD, HD), HD), :] = acc[h][64:, :] / total
                lse_ref[GRP * g + h, :, blk * qi : blk * qi + blk] = peak[h] + jnp.log(total)
            return 0

        lax.fori_loop(0, KVH, group, 0)
        out_ref[blk * qi : blk * qi + blk, :] = turned[...].T.astype(bf16)


def flash_forward(m, meta, q, parts, line, n_ctx):
    rows = parts[0].shape[-2]
    blk = rows // 2
    return pl.pallas_call(
        functools.partial(flash_forward_kernel, line, len(parts)),
        grid=(1,),
        out_shape=[jax.ShapeDtypeStruct((rows, QP), bf16), jax.ShapeDtypeStruct((16, 1, rows), f32)],
        in_specs=[SM, pl.BlockSpec((QH, rows, 128), lambda i: (0, m, 0))] + [ANY] * len(parts),
        out_specs=[
            pl.BlockSpec((rows, QP), lambda i: (0, 0)),
            pl.BlockSpec((16, 1, rows), lambda i: (0, 0, 0)),
        ],
        scratch_shapes=[
            pltpu.VMEM((n_ctx, KVH, rows, 128), bf16),
            pltpu.VMEM((GRP, 1, blk), f32),
            pltpu.VMEM((GRP, 128, blk), f32),
            pltpu.VMEM((QP, blk), f32),
            pltpu.SemaphoreType.DMA((4,)),
        ],
        compiler_params=params(48),
        cost_estimate=cost(2 * 4 * rows * rows * n_ctx * QP, 8 << 20, rows * rows * n_ctx * QH // 2),
    )(meta, q, *parts)


def flash_backward_kernel(line, count, meta, q_ref, out_ref, grad_ref, lse_ref, cos_ref, sin_ref, *refs):
    parts, rest = refs[:count], refs[count:]
    gq_ref, gkv_ref, pool, wide, delta, total, acc, turned, sems = rest
    load_chunks(meta, parts, pool, sems, line)
    length = meta[2]
    blk = q_ref.shape[1] // 2
    live_blocks = (length + blk - 1) // blk
    total[...] = jnp.zeros_like(total)
    rows = q_ref.shape[1]
    lane = lax.broadcasted_iota(jnp.int32, (rows, 128), 1)
    pick = lax.broadcasted_iota(jnp.int32, (16, 128), 0) == lax.broadcasted_iota(jnp.int32, (16, 128), 1) // 64
    pick = jnp.where(pick, 1.0, 0.0).astype(bf16)
    for p in range(8):
        slab = grad_ref[:, 128 * p : 128 * p + 128].astype(f32)
        wide[2 * p] = jnp.where(lane >= 64, pltpu.roll(slab, 64, 1), 0.0).astype(bf16)
        if 2 * p + 1 < QH:
            wide[2 * p + 1] = jnp.where(lane >= 64, slab, 0.0).astype(bf16)
        product = slab * out_ref[:, 128 * p : 128 * p + 128].astype(f32)
        high = product.astype(bf16)
        low = (product - high.astype(f32)).astype(bf16)
        both = nt_dot(pick, high) + nt_dot(pick, low)
        delta[2 * p] = both[0:1, :]
        delta[2 * p + 1] = both[1:2, :]
    turned[960:, :] = jnp.zeros((64, blk), f32)
    for qi in range(2):
        q_block = meta[qi]
        blocks = jnp.where(q_block < live_blocks, q_block + 1, 0)
        span = slice(blk * qi, blk * qi + blk)

        def group(g, _):
            for h in range(GRP):
                acc[h] = jnp.zeros((64, blk), f32)

            def step(block, with_mask):
                kv = key_block(pool, meta, block, g)
                spot = meta[META + block]
                at = pl.ds(pl.multiple_of((spot % 2) * blk, blk), blk)
                terms = []
                for h in range(GRP):
                    head = GRP * g + h
                    query = q_ref[head, span, :]
                    grad = wide[head, span, :]
                    scores = nt_dot(kv, query)
                    if with_mask:
                        scores = masked(scores, block, q_block, length)
                    probs = jnp.exp(scores - lse_ref[head, :, span])
                    change = (probs * (nt_dot(kv, grad) - delta[head, :, span])).astype(bf16)
                    terms.append(
                        jnp.dot(change, query, preferred_element_type=f32)
                        + jnp.dot(probs.astype(bf16), grad, preferred_element_type=f32)
                    )
                    acc[h] = acc[h] + tn_dot(kv[:, :64], change)
                total[spot // 2, g, at, :] += terms[0] + terms[1] + terms[2]

            def plain(block, _):
                step(block, False)
                return 0

            lax.fori_loop(0, blocks - 1, plain, 0)

            @pl.when(blocks > 0)
            def _():
                step(blocks - 1, True)

            for h in range(GRP):
                turned[pl.ds(pl.multiple_of((GRP * g + h) * HD, HD), HD), :] = acc[h] * 0.125
            return 0

        lax.fori_loop(0, KVH, group, 0)
        grads = turned[...].T
        cosine, sine = cos_ref[span, :], sin_ref[span, :]
        for p in range(8):
            slab = grads[:, 128 * p : 128 * p + 128]
            gq_ref[span, 128 * p : 128 * p + 128] = (slab * cosine - swap_halves(slab) * sine).astype(bf16)
    gkv_ref[...] = total[...].astype(bf16)


def flash_backward(m, meta, q, out, grad, lse, cosine, sine, parts, line, n_ctx):
    rows = parts[0].shape[-2]
    blk = rows // 2
    return pl.pallas_call(
        functools.partial(flash_backward_kernel, line, len(parts)),
        grid=(1,),
        out_shape=[
            jax.ShapeDtypeStruct((rows, QP), bf16),
            jax.ShapeDtypeStruct((n_ctx, KVH, rows, 128), bf16),
        ],
        in_specs=[
            SM,
            pl.BlockSpec((QH, rows, 128), lambda i: (0, m, 0)),
            pl.BlockSpec((rows, QP), lambda i: (0, 0)),
            pl.BlockSpec((rows, QP), lambda i: (m, 0)),
            pl.BlockSpec((16, 1, rows), lambda i: (0, 0, 0)),
            pl.BlockSpec((rows, 128), lambda i: (0, 0)),
            pl.BlockSpec((rows, 128), lambda i: (0, 0)),
        ]
        + [ANY] * len(parts),
        out_specs=[
            pl.BlockSpec((rows, QP), lambda i: (0, 0)),
            pl.BlockSpec((n_ctx, KVH, rows, 128), lambda i: (0, 0, 0, 0)),
        ],
        scratch_shapes=[
            pltpu.VMEM((n_ctx, KVH, rows, 128), bf16),
            pltpu.VMEM((QH, rows, 128), bf16),
            pltpu.VMEM((16, 1, rows), f32),
            pltpu.VMEM((n_ctx, KVH, rows, 128), f32),
            pltpu.VMEM((GRP, 64, blk), f32),
            pltpu.VMEM((QP, blk), f32),
            pltpu.SemaphoreType.DMA((4,)),
        ],
        compiler_params=params(56),
        cost_estimate=cost(5 * 4 * rows * rows * n_ctx * QP, 16 << 20, rows * rows * n_ctx * QH // 2),
    )(meta, q, out, grad, lse, cosine, sine, *parts)


def normalize(values, gain):
    inverse_rms = lax.rsqrt(jnp.mean(values * values, axis=-1, keepdims=True) + epsilon)
    return (inverse_rms, (values * inverse_rms * gain).astype(bf16))


def norm_back(values, inverse_rms, gain, grad_normed):
    unit_rows = values * inverse_rms
    gain_part = jnp.sum(grad_normed * unit_rows, axis=0)
    scaled = grad_normed * gain
    grad_values = inverse_rms * (
        scaled - unit_rows * jnp.mean(scaled * unit_rows, axis=-1, keepdims=True)
    )
    return (grad_values, gain_part)


def fold(tiles):
    return jnp.concatenate([tiles[:, :32, :], tiles[:, 32:, :]], axis=2)


def unfold(tiles):
    return jnp.concatenate([tiles[:, :, :64], tiles[:, :, 64:]], axis=1)


def mm(a, b):
    return jnp.dot(a, b, preferred_element_type=f32)


def shards(
    inputs,
    cotangent,
    lengths,
    order,
    owner_slots,
    master,
    stat_left,
    stat_right,
    root_left,
    root_right,
    gains,
    gain_stats,
):
    highest = lax.Precision.HIGHEST
    micro, rows = inputs.shape[1], inputs.shape[2]
    n_ctx, n_wt = lax.axis_size("ctx"), lax.axis_size("wt")
    devices = n_ctx * n_wt
    line = is_line(n_ctx, n_wt)
    tokens = micro * rows
    cap = master.shape[0]
    cap_a = NTA // devices + NTA // (8 * devices) + 2
    cap_f = cap - cap_a
    c = lax.axis_index("ctx")
    w = lax.axis_index("wt")

    low_master = fold(master.astype(bf16))
    parts_a = gather_tiles(low_master[:cap_a], c, n_ctx, n_wt)
    parts_f = gather_tiles(low_master[cap_a:], c, n_ctx, n_wt)
    owner, within = owner_slots // cap, owner_slots % cap
    table_a = part_index(owner[:NTA], within[:NTA], cap_a, c, w, n_ctx, n_wt)
    table_f = part_index(owner[NTA:], within[NTA:] - cap_a, cap_f, c, w, n_ctx, n_wt)

    blocks = order.shape[0]
    ids = jnp.arange(blocks, dtype=jnp.int32)
    dealt = jnp.sum(jnp.where(order[None, :] == ids[:, None], ids[None, :], 0), axis=1)
    chunk = (c - dealt // 2) % n_ctx if line else dealt // 2
    spots = 2 * chunk + dealt % 2
    my_blocks = jnp.sum(jnp.where(ids[None, :] == 2 * c + jnp.arange(2)[:, None], order[None, :], 0), axis=1)
    position = (my_blocks[:, None] * (rows // 2) + jnp.arange(rows // 2, dtype=jnp.int32)[None, :]).reshape(rows)
    lane = np.arange(128)
    frequency = jnp.asarray(rope_base, f32) ** (-(jnp.asarray(lane % 32, f32)) * 2.0 / HD)
    angle = position.astype(f32)[:, None] * frequency[None, :]
    cosine = jnp.cos(angle)
    sine = jnp.sin(angle) * jnp.where(lane % 64 < 32, -1.0, 1.0).astype(f32)[None, :]
    live = position[None, :] < lengths[0][:, None]
    metas = [
        jnp.concatenate([my_blocks, lengths[0, m][None], c[None], spots]).astype(jnp.int32)
        for m in range(micro)
    ]

    wqkv, wo = assemble(assemble_attn_kernel, parts_a, table_a, [(D, CW), (QP, D)])
    x_low = inputs.reshape(tokens, D)
    q, kv, normed_attn = qkv_rows(x_low, gains[0:1], wqkv, cosine, sine, micro)
    chunks = []
    for m in range(micro):
        if line:
            chunks.append(line_parts(kv[m]))
        else:
            chunks.append([lax.all_gather(kv[m], "ctx", axis=0)])
    forward = [flash_forward(m, metas[m], q, chunks[m], line, n_ctx) for m in range(micro)]
    attn_out = jnp.concatenate([f[0] for f in forward], axis=0)

    wgu, wd = assemble(assemble_ffn_kernel, parts_f, table_f, [(D, 2 * FF), (FF, D)])
    x = x_low.astype(f32)
    residual = x + mm(attn_out, wo)
    rms_ffn, normed_ffn = normalize(residual, gains[1])
    gate_pre = mm(normed_ffn, wgu[:, :FF])
    up_pre = mm(normed_ffn, wgu[:, FF:])
    sigma = jax.nn.sigmoid(gate_pre)
    hidden = (gate_pre * sigma * up_pre).astype(bf16)
    mixed = (residual + mm(hidden, wd)).astype(bf16)
    grad_out = jnp.where(live.reshape(tokens, 1), cotangent.reshape(tokens, D), jnp.zeros((), bf16))
    grad_hidden = mm(grad_out, wd.T)
    grad_gate = (grad_hidden * up_pre * sigma * (1.0 + gate_pre * (1.0 - sigma))).astype(bf16)
    grad_up = (grad_hidden * gate_pre * sigma).astype(bf16)
    grad_gu = jnp.concatenate([grad_gate, grad_up], axis=1)
    grad_normed_ffn = mm(grad_gu, wgu.T)
    grad_ffn_in, gain_ffn = norm_back(residual, rms_ffn, gains[1], grad_normed_ffn)
    grad_residual = grad_out.astype(f32) + grad_ffn_in
    grad_branch = grad_residual.astype(bf16)
    grad_attn = mm(grad_branch, wo.T).astype(bf16)

    def reduce_pool(kernel, table, first, second, n):
        total = devices * n
        if line:
            mine, other = pack(kernel, table, first, second, total, 2)
            return reduce_tiles(mine, other, n, c, n_ctx, n_wt)
        (whole,) = pack(kernel, table, first, second, total, 1)
        return lax.psum_scatter(whole.astype(f32), AXES, scatter_dimension=0, tiled=True)

    dgu = mm(normed_ffn.T, grad_gu).astype(bf16)
    dwd = mm(hidden.T, grad_out).astype(bf16)
    tiles_f = unfold(reduce_pool(pack_ffn_kernel, table_f, dgu, dwd, cap_f))

    grad_q, grad_kv = [], []
    for m in range(micro):
        gq, gkv = flash_backward(
            m, metas[m], q, forward[m][0], grad_attn, forward[m][1], cosine, sine, chunks[m], line, n_ctx
        )
        if line:
            own = line_reduce([gkv[d] for d in range(4)])
        else:
            own = lax.psum_scatter(gkv.astype(f32), "ctx", scatter_dimension=0, tiled=False)
        grad_q.append(gq)
        grad_kv.append(own)
    left = jnp.asarray(lane < 64)
    rows_kv = jnp.stack(grad_kv)
    swapped = jnp.concatenate(
        [rows_kv[..., 32:64], rows_kv[..., :32], rows_kv[..., 64:]], axis=-1
    )
    rows_kv = rows_kv * jnp.where(left, cosine, 1.0) - swapped * jnp.where(left, sine, 0.0)
    rows_kv = rows_kv.astype(bf16).transpose(0, 2, 1, 3).reshape(tokens, KVH * 128)
    grad_cat = jnp.concatenate([jnp.concatenate(grad_q, axis=0), rows_kv], axis=1)
    grad_normed_attn = mm(grad_cat, wqkv.T)
    rms_attn = lax.rsqrt(jnp.mean(x * x, axis=-1, keepdims=True) + epsilon)
    grad_input_norm, gain_attn = norm_back(x, rms_attn, gains[0], grad_normed_attn)
    input_grad = grad_residual + grad_input_norm

    dqkv = mm(normed_attn.T, grad_cat).astype(bf16)
    dwo = mm(attn_out.T, grad_branch).astype(bf16)
    tiles_a = unfold(reduce_pool(pack_attn_kernel, table_a, dqkv, dwo, cap_a))

    tile_grads = jnp.concatenate([tiles_a, tiles_f], axis=0)
    gain_grads = lax.psum(jnp.stack([gain_attn, gain_ffn]), AXES)
    gram_left = jnp.einsum("sij,skj->sik", tile_grads, tile_grads, precision=highest)
    gram_right = jnp.einsum("sji,sjk->sik", tile_grads, tile_grads, precision=highest)
    new_left = decay_rate * stat_left + (1.0 - decay_rate) * gram_left
    new_right = decay_rate * stat_right + (1.0 - decay_rate) * gram_right
    step_left = jnp.einsum("sij,sjk->sik", root_left, tile_grads, precision=highest)
    step_full = jnp.einsum("sij,sjk->sik", step_left, root_right, precision=highest)
    new_master = master - step_rate * step_full
    new_gain_stats = decay_rate * gain_stats + (1.0 - decay_rate) * gain_grads * gain_grads
    new_gains = gains - gain_rate * gain_grads * lax.rsqrt(new_gain_stats)
    return (
        mixed.reshape(1, micro, rows, D),
        input_grad.reshape(1, micro, rows, D),
        tile_grads,
        new_left,
        new_right,
        new_master,
        gain_grads,
        new_gain_stats,
        new_gains,
    )


def solution(mesh):
    in_specs = (
        P("wt", None, "ctx", None),
        P("wt", None, "ctx", None),
        P("wt", None),
        P(),
        P(),
        P(AXES, None, None),
        P(AXES, None, None),
        P(AXES, None, None),
        P(AXES, None, None),
        P(AXES, None, None),
        P(),
        P(),
    )
    out_specs = (
        P("wt", None, "ctx", None),
        P("wt", None, "ctx", None),
        P(AXES, None, None),
        P(AXES, None, None),
        P(AXES, None, None),
        P(AXES, None, None),
        P(),
        P(),
        P(),
    )
    return jax.shard_map(shards, mesh=mesh, in_specs=in_specs, out_specs=out_specs, check_vma=False)
```

```python
import functools

import jax
import jax.numpy as jnp
import numpy as np
from jax import lax
from jax.experimental import pallas as pl
from jax.experimental.pallas import tpu as pltpu
from jax.sharding import PartitionSpec as P

D = 960
FF = 2560
QH = 15
KVH = 5
HD = 64
TL = 64
QW = 960
KVW = 320
GRP = 3
NTA = 600
NT = 2400
QP = 1024
CW = 1664
BLK = 256
AXES = ("ctx", "wt")

epsilon = 1e-05
decay_rate = 0.95
step_rate = 0.05
gain_rate = 0.05
rope_base = 10000.0
blocked_score = -1e30
bf16 = jnp.bfloat16
f32 = jnp.float32
VM = pl.BlockSpec(memory_space=pltpu.VMEM)
SM = pl.BlockSpec(memory_space=pltpu.SMEM)
ANY = pl.BlockSpec(memory_space=pl.ANY)


def params(megabytes, **kwargs):
    return pltpu.CompilerParams(vmem_limit_bytes=megabytes << 20, **kwargs)


def cost(flops, nbytes, trans=0):
    return pl.CostEstimate(flops=int(flops), bytes_accessed=int(nbytes), transcendentals=int(trans))


def after(x, *others):
    return lax.optimization_barrier((x, others))[0]


def is_line(n_ctx, n_wt):
    return n_ctx == 4 and n_wt == 8


def flip(x, bit):
    return lax.ppermute(x, "wt", [(i, i ^ bit) for i in range(8)])


def go_up(x, sources=(0, 1, 2)):
    return lax.ppermute(x, "ctx", [(i, i + 1) for i in sources])


def go_down(x, sources=(1, 2, 3)):
    return lax.ppermute(x, "ctx", [(i, i - 1) for i in sources])


def cyclic(x, d):
    return lax.ppermute(x, "ctx", [(i, (i + d) % 4) for i in range(4)])


def tile_halves(n):
    return (n + 1) // 2


def gather_line(own):
    return jnp.stack([own, cyclic(own, 1), cyclic(own, 2), cyclic(own, 3)])


def gather_near(here):
    return flip(here, 2), flip(here, 4)


def gather_diag(over_x, over_y):
    n1 = tile_halves(over_x.shape[1])
    return flip(over_y[:, :n1], 2), flip(over_x[:, n1:], 4)


def gather_core(near):
    far = [flip(a, 1) for a in near]
    return [a.reshape((-1,) + a.shape[2:]) for a in near + far]


def part_index(owner, slot, n, c, w, n_ctx, n_wt):
    if not is_line(n_ctx, n_wt):
        return owner * n + slot
    n1 = tile_halves(n)
    n2 = n - n1
    d = (c - owner // n_wt) & 3
    xw = (owner % n_wt) ^ w
    core, quad = xw & 1, xw >> 1
    plain = quad * (4 * n) + d * n + slot
    diag = 12 * n + jnp.where(slot < n1, d * n1 + slot, 4 * n1 + d * n2 + slot - n1)
    return core * (16 * n) + jnp.where(quad == 3, diag, plain)


def add(a, b):
    return (a.astype(f32) + b.astype(f32)).astype(bf16)


def reduce_core(mine, other, n):
    n1 = tile_halves(n)
    total = add(mine, flip(other, 1))
    quads = [total[4 * n * i : 4 * n * i + 4 * n].reshape((4, n, 32, 128)) for i in range(3)]
    cut = 12 * n + 4 * n1
    return quads + [total[12 * n : cut].reshape((4, n1, 32, 128)), total[cut:].reshape((4, n - n1, 32, 128))]


def reduce_diag(quads):
    return flip(quads[3], 2), flip(quads[4], 4)


def reduce_near(quads, diag):
    n1 = quads[3].shape[1]
    s1, s2 = quads[1], quads[2]
    t1 = jnp.concatenate([s1[:, :n1], add(s1[:, n1:], diag[1])], axis=1)
    t2 = jnp.concatenate([add(s2[:, :n1], diag[0]), s2[:, n1:]], axis=1)
    return flip(t1, 2), flip(t2, 4)


def reduce_line(quads, near):
    own = quads[0].astype(f32) + near[0].astype(f32) + near[1].astype(f32)
    return line_reduce([own[0], own[1], own[2], own[3]])


def line_reduce(parts):
    low = [p.astype(bf16) for p in parts]
    wide = [p.astype(f32) for p in parts]
    up = go_up(low[1], (0,))
    up = go_up((wide[2] + up.astype(f32)).astype(bf16), (0, 1))
    up = go_up((wide[3] + up.astype(f32)).astype(bf16), (0, 1, 2))
    down = go_down(low[3], (3,))
    down = go_down((wide[2] + down.astype(f32)).astype(bf16), (2, 3))
    down = go_down((wide[1] + down.astype(f32)).astype(bf16), (1, 2, 3))
    return wide[0] + up.astype(f32) + down.astype(f32)


def load_parts(parts, pool, sems):
    at = 0
    copies = []
    for i, part in enumerate(parts):
        rows = part.shape[0]
        copies.append(pltpu.make_async_copy(part, pool.at[pl.ds(at, rows)], sems.at[i]))
        at += rows
    for copy in copies:
        copy.start()
    for copy in copies:
        copy.wait()


def place_pair(pool, table, ref, row, lane, a, b):
    first = pool[table[a]]
    second = pool[table[b]]
    ref[pl.ds(row, 32), lane : lane + 128] = jnp.concatenate([first[:, :64], second[:, :64]], axis=1)
    ref[pl.ds(row + 32, 32), lane : lane + 128] = jnp.concatenate([first[:, 64:], second[:, 64:]], axis=1)


def place_single(pool, table, ref, row, lane, a):
    first = pool[table[a]]
    ref[pl.ds(row, 32), lane : lane + 64] = first[:, :64]
    ref[pl.ds(row + 32, 32), lane : lane + 64] = first[:, 64:]


def assemble_attn_kernel(count, table, *refs):
    parts, (wqkv, wo, pool, sems) = refs[:count], refs[count:]
    load_parts(parts, pool, sems)
    attn_rows(pool, table, wqkv, wo)


def attn_rows(pool, table, wqkv, wo):
    def qkv_row(r, _):
        row = pl.multiple_of(r * 64, 64)
        for p in range(7):
            place_pair(pool, table, wqkv, row, 128 * p, r * 15 + 2 * p, r * 15 + 2 * p + 1)
        place_single(pool, table, wqkv, row, 896, r * 15 + 14)
        wqkv[pl.ds(row, 64), 960:1024] = jnp.zeros((64, 64), bf16)
        for g in range(KVH):
            place_pair(pool, table, wqkv, row, QP + 128 * g, 225 + r * 5 + g, 300 + r * 5 + g)
        for p in range(7):
            place_pair(pool, table, wo, row, 128 * p, 375 + r * 15 + 2 * p, 375 + r * 15 + 2 * p + 1)
        place_single(pool, table, wo, row, 896, 375 + r * 15 + 14)
        return 0

    lax.fori_loop(0, 15, qkv_row, 0)
    wo[pl.ds(960, 64), :] = jnp.zeros((64, D), bf16)


def ffn_rows(pool, table, wgu, wd):
    def gu_row(r, _):
        row = pl.multiple_of(r * 64, 64)
        for m in range(2):
            for p in range(20):
                base = 600 * m + r * 40 + 2 * p
                place_pair(pool, table, wgu, row, FF * m + 128 * p, base, base + 1)
        return 0

    lax.fori_loop(0, 15, gu_row, 0)

    def d_row(r, _):
        row = pl.multiple_of(r * 64, 64)
        for p in range(7):
            place_pair(pool, table, wd, row, 128 * p, 1200 + r * 15 + 2 * p, 1200 + r * 15 + 2 * p + 1)
        place_single(pool, table, wd, row, 896, 1200 + r * 15 + 14)
        return 0

    lax.fori_loop(0, 40, d_row, 0)


def assemble(kernel, parts, table, shapes):
    total = sum(p.shape[0] for p in parts)
    out_bytes = sum(2 * a * b for a, b in shapes)
    return pl.pallas_call(
        functools.partial(kernel, len(parts)),
        out_shape=[jax.ShapeDtypeStruct(s, bf16) for s in shapes],
        in_specs=[SM] + [ANY] * len(parts),
        out_specs=[VM] * len(shapes),
        scratch_shapes=[pltpu.VMEM((total, 32, 128), bf16), pltpu.SemaphoreType.DMA((len(parts),))],
        compiler_params=params(52),
        cost_estimate=cost(0, 4 * out_bytes),
    )(table, *parts)


def pick_pair(pool, table, ref, row, lane, a, b):
    block = ref[pl.ds(row, 64), lane : lane + 128]
    pool[table[a]] = jnp.concatenate([block[:32, :64], block[32:, :64]], axis=1)
    pool[table[b]] = jnp.concatenate([block[:32, 64:], block[32:, 64:]], axis=1)


def pick_single(pool, table, ref, row, lane, a):
    block = ref[pl.ds(row, 64), lane : lane + 64]
    pool[table[a]] = jnp.concatenate([block[:32], block[32:]], axis=1)


def clear_pool(pool):
    step = 8
    whole = pool.shape[0] // step

    def clear(i, _):
        pool[pl.ds(i * step, step)] = jnp.zeros((step, 32, 128), bf16)
        return 0

    lax.fori_loop(0, whole, clear, 0)
    rest = pool.shape[0] - whole * step
    if rest:
        pool[whole * step :] = jnp.zeros((rest, 32, 128), bf16)


def flush_pool(pool, outs, sems):
    at = 0
    copies = []
    for i, out in enumerate(outs):
        rows = out.shape[0]
        copies.append(pltpu.make_async_copy(pool.at[pl.ds(at, rows)], out, sems.at[i]))
        at += rows
    for copy in copies:
        copy.start()
    for copy in copies:
        copy.wait()


def pack_attn_kernel(table, dqkv, dwo, *refs):
    outs, (pool, sems) = refs[:-2], refs[-2:]
    clear_pool(pool)

    def qkv_row(r, _):
        row = pl.multiple_of(r * 64, 64)
        for p in range(7):
            pick_pair(pool, table, dqkv, row, 128 * p, r * 15 + 2 * p, r * 15 + 2 * p + 1)
        pick_single(pool, table, dqkv, row, 896, r * 15 + 14)
        for g in range(KVH):
            pick_pair(pool, table, dqkv, row, QP + 128 * g, 225 + r * 5 + g, 300 + r * 5 + g)
        for p in range(7):
            pick_pair(pool, table, dwo, row, 128 * p, 375 + r * 15 + 2 * p, 375 + r * 15 + 2 * p + 1)
        pick_single(pool, table, dwo, row, 896, 375 + r * 15 + 14)
        return 0

    lax.fori_loop(0, 15, qkv_row, 0)
    flush_pool(pool, outs, sems)


def pack(kernel, table, first, second, total, pieces):
    return pl.pallas_call(
        kernel,
        out_shape=[jax.ShapeDtypeStruct((total // pieces, 32, 128), bf16)] * pieces,
        in_specs=[SM, VM, VM],
        out_specs=[ANY] * pieces,
        scratch_shapes=[pltpu.VMEM((total, 32, 128), bf16), pltpu.SemaphoreType.DMA((pieces,))],
        compiler_params=params(52),
        cost_estimate=cost(0, 8 * (first.size + second.size)),
    )(table, first, second)


def swap_halves(x):
    lane = lax.broadcasted_iota(jnp.int32, x.shape, 1)
    return jnp.where(lane % 64 < 32, pltpu.roll(x, 96, 1), pltpu.roll(x, 32, 1))


def qkv_kernel(x_ref, gain_ref, w_ref, cos_ref, sin_ref, q_ref, kv_ref, normed_ref):
    x = x_ref[...].astype(f32)
    inverse = lax.rsqrt(jnp.mean(x * x, axis=1, keepdims=True) + epsilon)
    normed = (x * inverse * gain_ref[...]).astype(bf16)
    normed_ref[...] = normed
    cosine, sine = cos_ref[...], sin_ref[...]
    lane = lax.broadcasted_iota(jnp.int32, cosine.shape, 1)
    left = lane < 64
    for p in range(8):
        rows = jnp.dot(normed, w_ref[:, 128 * p : 128 * p + 128], preferred_element_type=f32)
        rows = (rows * cosine + swap_halves(rows) * sine).astype(bf16).astype(f32) * 0.125
        q_ref[2 * p] = jnp.where(left, rows, 0.0).astype(bf16)
        if 2 * p + 1 < QH:
            q_ref[2 * p + 1] = jnp.where(left, pltpu.roll(rows, 64, 1), 0.0).astype(bf16)
    cosine = jnp.where(left, cosine, 1.0)
    sine = jnp.where(left, sine, 0.0)
    for g in range(KVH):
        at = QP + 128 * g
        rows = jnp.dot(normed, w_ref[:, at : at + 128], preferred_element_type=f32)
        kv_ref[0, g] = (rows * cosine + swap_halves(rows) * sine).astype(bf16)


def qkv_rows(x, gain, wqkv, cosine, sine, micro):
    tokens = x.shape[0]
    rows = tokens // micro
    blk = min(BLK, rows)
    steps = tokens // blk
    per = steps // micro
    return pl.pallas_call(
        qkv_kernel,
        grid=(steps,),
        out_shape=[
            jax.ShapeDtypeStruct((QH, tokens, 128), bf16),
            jax.ShapeDtypeStruct((micro, KVH, rows, 128), bf16),
            jax.ShapeDtypeStruct((tokens, D), bf16),
        ],
        in_specs=[
            pl.BlockSpec((blk, D), lambda i: (i, 0)),
            pl.BlockSpec((1, D), lambda i: (0, 0)),
            pl.BlockSpec((D, CW), lambda i: (0, 0)),
            pl.BlockSpec((blk, 128), lambda i: (i % per, 0)),
            pl.BlockSpec((blk, 128), lambda i: (i % per, 0)),
        ],
        out_specs=[
            pl.BlockSpec((QH, blk, 128), lambda i: (0, i, 0)),
            pl.BlockSpec((1, KVH, blk, 128), lambda i: (i // per, 0, i % per, 0)),
            pl.BlockSpec((blk, D), lambda i: (i, 0)),
        ],
        compiler_params=params(40),
        cost_estimate=cost(2 * tokens * D * CW, 14 << 20),
    )(x, gain, wqkv, cosine, sine)


def remote(src, dst, send, recv, device):
    return pltpu.make_async_remote_copy(
        src_ref=src,
        dst_ref=dst,
        send_sem=send,
        recv_sem=recv,
        device_id=device,
        device_id_type=pl.DeviceIdType.MESH,
    )


def greet(c, w, far):
    barrier = pltpu.get_barrier_semaphore()

    def hail(device):
        pl.semaphore_signal(barrier, inc=1, device_id=device, device_id_type=pl.DeviceIdType.MESH)

    for bit in (1, 2, 4):
        hail({"wt": w ^ bit})
    if far:
        hail({"ctx": c ^ 2})

    @pl.when(c < 3)
    def _():
        hail({"ctx": c + 1})

    @pl.when(c > 0)
    def _():
        hail({"ctx": c - 1})

    inner = jnp.logical_and(c > 0, c < 3)

    @pl.when(inner)
    def _():
        pl.semaphore_wait(barrier, 5 + far)

    @pl.when(jnp.logical_not(inner))
    def _():
        pl.semaphore_wait(barrier, 4 + far)


class Gather:
    def __init__(self, pool, sems, c, w):
        self.pool, self.sems, self.c, self.w = pool, sems, c, w
        self.n = pool.shape[2]
        self.n1 = tile_halves(self.n)
        self.x, self.y, self.core = {"wt": w ^ 2}, {"wt": w ^ 4}, {"wt": w ^ 1}

    def copy(self, k, owner, lane, device, part=None):
        ref = self.pool.at[k, owner]
        if part is not None:
            ref = ref.at[pl.ds(part[0], part[1])]
        return remote(ref, ref, self.sems.at[k, lane], self.sems.at[k, lane + 1], device)

    def up(self, k):
        return self.copy(k, self.w, 0, {"ctx": self.c + 1})

    def down(self, k):
        return self.copy(k, self.w, 2, {"ctx": self.c - 1})

    def over_x(self, k, back=0):
        return self.copy(k, self.w ^ back, 4, self.x)

    def over_y(self, k, back=0):
        return self.copy(k, self.w ^ back, 6, self.y)

    def diag_x(self, k, owner):
        return self.copy(k, owner, 8, self.x, (0, self.n1))

    def diag_y(self, k, owner):
        return self.copy(k, owner, 10, self.y, (self.n1, self.n - self.n1))

    def over_core(self, k, quad, back=0):
        return self.copy(k, self.w ^ (2 * quad) ^ back, 12 + 2 * quad, self.core)

    def send_line(self, k, low, high):
        if low:

            @pl.when(self.c < 3)
            def _():
                self.up(k).start()

        if high:

            @pl.when(self.c > 0)
            def _():
                self.down(k).start()

    def send_near(self, k):
        self.over_x(k).start()
        self.over_y(k).start()
        self.over_core(k, 0).start()

    def first(self):
        self.send_line(self.c, True, True)

    def sides(self, s):
        return [(self.c >= s, self.c - s, True), (self.c + s <= 3, self.c + s, False)]

    def line_step(self, s, near=True):
        for valid, k, below in self.sides(s):

            @pl.when(valid)
            def _(k=k, below=below):
                if below:
                    self.up(k).wait_recv()
                else:
                    self.down(k).wait_recv()
                if s < 3:
                    self.send_line(k, below, not below)
                if near:
                    self.send_near(k)

    def each(self, s, act):
        if s == 0:
            act(self.c)
            return
        for valid, k, _ in self.sides(s):

            @pl.when(valid)
            def _(k=k):
                act(k)

    def near_step(self, s):
        def act(k):
            self.over_x(k, 2).wait_recv()
            self.diag_y(k, self.w ^ 2).start()
            self.over_core(k, 1).start()
            self.over_y(k, 4).wait_recv()
            self.diag_x(k, self.w ^ 4).start()
            self.over_core(k, 2).start()

        self.each(s, act)

    def diag_step(self, s):
        def act(k):
            self.diag_x(k, self.w ^ 6).wait_recv()
            self.diag_y(k, self.w ^ 6).wait_recv()
            self.over_core(k, 3).start()

        self.each(s, act)

    def finish(self):
        for k in range(4):
            for quad in range(4):
                self.over_core(k, quad, 1).wait_recv()

    def drain(self):
        for k in range(4):

            @pl.when(jnp.logical_and(k <= self.c, self.c < 3))
            def _(k=k):
                self.up(k).wait_send()

            @pl.when(jnp.logical_and(k >= self.c, self.c > 0))
            def _(k=k):
                self.down(k).wait_send()

            self.over_x(k).wait_send()
            self.over_y(k).wait_send()
            self.diag_x(k, self.w ^ 4).wait_send()
            self.diag_y(k, self.w ^ 2).wait_send()
            for quad in range(4):
                self.over_core(k, quad).wait_send()


def front_kernel(
    table, own_a, own_f, x_ref, gain_ref, cos_ref, sin_ref,
    q_ref, normed_ref, rows_ref, kv_ref, late_ref, wqkv, wo, pool_f,
    pool_a, kv_own, sems_a, sems_f, sems_kv, sems,
):
    c, w = lax.axis_index("ctx"), lax.axis_index("wt")
    take_a = pltpu.make_async_copy(own_a, pool_a.at[c, w], sems.at[0])
    take_f = pltpu.make_async_copy(own_f, pool_f.at[c, w], sems.at[1])
    take_a.start()
    take_f.start()
    greet(c, w, 0)
    take_a.wait()
    a = Gather(pool_a, sems_a, c, w)
    f = Gather(pool_f, sems_f, c, w)
    a.first()
    a.send_near(c)

    rows = x_ref.shape[2]
    blk = BLK
    for m in range(2):
        for half in range(rows // blk):
            part = x_ref[m, :, blk * half : blk * half + blk].T
            span = slice(m * rows + blk * half, m * rows + blk * half + blk)
            rows_ref[span, :] = part
            wide = part.astype(f32)
            inverse = lax.rsqrt(jnp.mean(wide * wide, axis=1, keepdims=True) + epsilon)
            normed_ref[span, :] = (wide * inverse * gain_ref[...]).astype(bf16)

    a.line_step(1)
    a.near_step(0)
    a.line_step(2)
    take_f.wait()
    f.first()
    a.near_step(1)
    a.diag_step(0)
    a.line_step(3)
    a.near_step(2)
    a.diag_step(1)
    a.near_step(3)
    f.send_near(c)
    a.diag_step(2)
    a.diag_step(3)
    f.line_step(1)
    a.finish()

    flat = pool_a.reshape(pool_a.shape[0] * pool_a.shape[1] * pool_a.shape[2], 32, 128)
    attn_rows(flat, table, wqkv, wo)
    f.line_step(2)
    f.near_step(0)

    lane = lax.broadcasted_iota(jnp.int32, (blk, 128), 1)
    left = lane < 64

    def qkv_block(i, _):
        at = pl.multiple_of(i * blk, blk)
        normed = normed_ref[pl.ds(at, blk), :]
        within = pl.multiple_of((i % (rows // blk)) * blk, blk)
        cosine, sine = cos_ref[pl.ds(within, blk), :], sin_ref[pl.ds(within, blk), :]
        key_cosine = jnp.where(left, cosine, 1.0)
        key_sine = jnp.where(left, sine, 0.0)
        for g in range(KVH):
            spot = QP + 128 * g
            part = jnp.dot(normed, wqkv[:, spot : spot + 128], preferred_element_type=f32)
            part = (part * key_cosine + swap_halves(part) * key_sine).astype(bf16)
            kv_own[i // (rows // blk), g, pl.ds(within, blk), :] = part
        for p in range(8):
            part = jnp.dot(normed, wqkv[:, 128 * p : 128 * p + 128], preferred_element_type=f32)
            part = (part * cosine + swap_halves(part) * sine).astype(bf16).astype(f32) * 0.125
            q_ref[2 * p, pl.ds(at, blk), :] = jnp.where(left, part, 0.0).astype(bf16)
            if 2 * p + 1 < QH:
                other = jnp.where(left, pltpu.roll(part, 64, 1), 0.0).astype(bf16)
                q_ref[2 * p + 1, pl.ds(at, blk), :] = other
        return 0

    def kv_move(src, k, lane, step):
        return remote(src, kv_ref.at[k], sems_kv.at[k, lane], sems_kv.at[k, lane + 1], {"ctx": c + step})

    lax.fori_loop(0, rows // blk, qkv_block, 0)
    keep = pltpu.make_async_copy(kv_own.at[0], kv_ref.at[c], sems.at[2])
    keep.start()

    @pl.when(c < 3)
    def _():
        kv_move(kv_own.at[0], c, 0, 1).start()

    @pl.when(c > 0)
    def _():
        kv_move(kv_own.at[0], c, 2, -1).start()

    lax.fori_loop(rows // blk, 2 * rows // blk, qkv_block, 0)
    late = pltpu.make_async_copy(kv_own.at[1], late_ref, sems.at[3])
    late.start()

    def kv_step(s):
        @pl.when(c >= s)
        def _():
            kv_move(kv_ref.at[c - s], c - s, 0, 1).wait_recv()
            if s < 3:

                @pl.when(c < 3)
                def _():
                    kv_move(kv_ref.at[c - s], c - s, 0, 1).start()

        @pl.when(c + s <= 3)
        def _():
            kv_move(kv_ref.at[c + s], c + s, 2, -1).wait_recv()
            if s < 3:

                @pl.when(c > 0)
                def _():
                    kv_move(kv_ref.at[c + s], c + s, 2, -1).start()

    f.line_step(3)
    f.near_step(1)
    f.diag_step(0)
    kv_step(1)
    f.near_step(2)
    f.diag_step(1)
    f.near_step(3)
    kv_step(2)
    f.diag_step(2)
    f.diag_step(3)
    f.finish()
    kv_step(3)
    keep.wait()
    late.wait()
    for k in range(4):

        @pl.when(jnp.logical_and(k <= c, c < 3))
        def _(k=k):
            kv_move(kv_ref.at[k], k, 0, 1).wait_send()

        @pl.when(jnp.logical_and(k >= c, c > 0))
        def _(k=k):
            kv_move(kv_ref.at[k], k, 2, -1).wait_send()

    a.drain()
    f.drain()


def front(table, own_a, own_f, x_t, gain, cosine, sine):
    micro, _, rows = x_t.shape
    tokens = micro * rows
    n_a, n_f = own_a.shape[0], own_f.shape[0]
    return pl.pallas_call(
        front_kernel,
        out_shape=[
            jax.ShapeDtypeStruct((QH, tokens, 128), bf16),
            jax.ShapeDtypeStruct((tokens, D), bf16),
            jax.ShapeDtypeStruct((tokens, D), bf16),
            jax.ShapeDtypeStruct((4, KVH, rows, 128), bf16),
            jax.ShapeDtypeStruct((KVH, rows, 128), bf16),
            jax.ShapeDtypeStruct((D, CW), bf16),
            jax.ShapeDtypeStruct((QP, D), bf16),
            jax.ShapeDtypeStruct((4, 8, n_f, 32, 128), bf16),
        ],
        in_specs=[SM, ANY, ANY, VM, VM, VM, VM],
        out_specs=[VM, VM, VM, ANY, ANY, VM, VM, ANY],
        scratch_shapes=[
            pltpu.VMEM((4, 8, n_a, 32, 128), bf16),
            pltpu.VMEM((micro, KVH, rows, 128), bf16),
            pltpu.SemaphoreType.DMA((4, 20)),
            pltpu.SemaphoreType.DMA((4, 20)),
            pltpu.SemaphoreType.DMA((4, 4)),
            pltpu.SemaphoreType.DMA((4,)),
        ],
        compiler_params=params(48, collective_id=0, has_side_effects=True),
        cost_estimate=cost(40e9, 40 << 20),
    )(table, own_a, own_f, x_t, gain, cosine, sine)


def tail_kernel(
    pool, gain_ref, sum_ref, gain_out,
    mine, theirs, diag_send, diag_recv, near_send, near_recv, own, line_send, line_recv,
    gain_send, gain_recv, sems_load, sems_core, sems_diag, sems_near, sems_line, sems_gain,
):
    c, w = lax.axis_index("ctx"), lax.axis_index("wt")
    yx, core = w // 2, w % 2
    n = pool.shape[3]
    n1 = tile_halves(n)
    over_x, over_y, over_core = {"wt": w ^ 2}, {"wt": w ^ 4}, {"wt": w ^ 1}
    order = (3, 1, 2, 0)
    loads = [pltpu.make_async_copy(pool.at[:, yx ^ q, core], mine.at[q], sems_load.at[q]) for q in range(4)]
    for q in order:
        loads[q].start()
    greet(c, w, 1)
    cores = [
        remote(pool.at[:, yx ^ q, 1 - core], theirs.at[q], sems_core.at[q, 0], sems_core.at[q, 1], over_core)
        for q in range(4)
    ]
    for q in order:
        cores[q].start()

    gain_stage = [over_core, over_x, over_y, {"ctx": c ^ 1}, {"ctx": c ^ 2}]
    gain_copies = [
        remote(gain_send.at[i], gain_recv.at[i], sems_gain.at[i, 0], sems_gain.at[i, 1], gain_stage[i])
        for i in range(5)
    ]
    gain_send[0] = gain_ref[...]
    gain_copies[0].start()

    def gain_step(i):
        gain_copies[i].wait()
        total = gain_send[i] + gain_recv[i]
        if i < 4:
            gain_send[i + 1] = total
            gain_copies[i + 1].start()
        else:
            gain_out[...] = total

    def both(q, k):
        return mine[q, k].astype(f32) + theirs[q, k].astype(f32)

    def ready(q):
        loads[q].wait()
        cores[q].wait()

    diag_x = remote(
        diag_send.at[:, :n1], diag_recv.at[:, :n1], sems_diag.at[0, 0], sems_diag.at[0, 1], over_x
    )
    diag_y = remote(
        diag_send.at[:, n1:], diag_recv.at[:, n1:], sems_diag.at[1, 0], sems_diag.at[1, 1], over_y
    )
    ready(3)

    def diag_sum(k, _):
        diag_send[k] = both(3, k).astype(bf16)
        return 0

    lax.fori_loop(0, 4, diag_sum, 0)
    diag_x.start()
    diag_y.start()
    gain_step(0)

    def near(q, part, device):
        cut = slice(0, n1) if part == 0 else slice(n1, n)
        ref = near_send.at[q - 1, :, cut], near_recv.at[q - 1, :, cut]
        at = 2 * (q - 1) + part
        return remote(ref[0], ref[1], sems_near.at[at, 0], sems_near.at[at, 1], device)

    nears = {(q, part): near(q, part, over_x if q == 1 else over_y) for q in (1, 2) for part in (0, 1)}
    for q in (1, 2):
        ready(q)

        def near_sum(k, _, q=q):
            near_send[q - 1, k] = both(q, k).astype(bf16)
            return 0

        lax.fori_loop(0, 4, near_sum, 0)
        nears[q, q - 1].start()
    gain_step(1)
    diag_y.wait_recv()

    def join_x(k, _):
        near_send[0, k, n1:] = (near_send[0, k, n1:].astype(f32) + diag_recv[k, n1:].astype(f32)).astype(bf16)
        return 0

    lax.fori_loop(0, 4, join_x, 0)
    nears[1, 1].start()
    diag_x.wait_recv()

    def join_y(k, _):
        near_send[1, k, :n1] = (near_send[1, k, :n1].astype(f32) + diag_recv[k, :n1].astype(f32)).astype(bf16)
        return 0

    lax.fori_loop(0, 4, join_y, 0)
    nears[2, 0].start()
    gain_step(2)
    ready(0)

    def own_core(k, _):
        own[k] = both(0, k)
        return 0

    lax.fori_loop(0, 4, own_core, 0)
    for part in (0, 1):
        for q in (1, 2):
            nears[q, part].wait_recv()

    def own_sum(k, _):
        own[k] = own[k] + near_recv[0, k].astype(f32) + near_recv[1, k].astype(f32)
        return 0

    lax.fori_loop(0, 4, own_sum, 0)

    def line(way, k):
        step = 1 - 2 * way
        return remote(
            line_send.at[way, k], line_recv.at[way, k], sems_line.at[way, k, 0], sems_line.at[way, k, 1],
            {"ctx": c + step},
        )

    def pass_on(way, k):
        first = c == (0 if way == 0 else 3)

        @pl.when(first)
        def _():
            line_send[way, k] = own[k].astype(bf16)

        @pl.when(jnp.logical_not(first))
        def _():
            line(way, k).wait_recv()
            line_send[way, k] = (own[k] + line_recv[way, k].astype(f32)).astype(bf16)

        line(way, k).start()

    for far in (3, 2, 1):
        for way, k in ((0, far), (1, 3 - far)):

            @pl.when(c < k if way == 0 else c > k)
            def _(way=way, k=k):
                pass_on(way, k)

    gain_step(3)
    sum_ref[...] = own[c]

    @pl.when(c > 0)
    def _():
        line(0, c).wait_recv()
        sum_ref[...] += line_recv[0, c].astype(f32)

    @pl.when(c < 3)
    def _():
        line(1, c).wait_recv()
        sum_ref[...] += line_recv[1, c].astype(f32)

    gain_step(4)
    diag_x.wait_send()
    diag_y.wait_send()
    for copy in nears.values():
        copy.wait_send()
    for far in (3, 2, 1):
        for way, k in ((0, far), (1, 3 - far)):

            @pl.when(c < k if way == 0 else c > k)
            def _(way=way, k=k):
                line(way, k).wait_send()


def tail(pool, gains):
    n = pool.shape[3]
    tile = (32, 128)
    return pl.pallas_call(
        tail_kernel,
        out_shape=[jax.ShapeDtypeStruct((n,) + tile, f32), jax.ShapeDtypeStruct(gains.shape, f32)],
        in_specs=[ANY, VM],
        out_specs=[VM, VM],
        scratch_shapes=[
            pltpu.VMEM((4, 4, n) + tile, bf16),
            pltpu.VMEM((4, 4, n) + tile, bf16),
            pltpu.VMEM((4, n) + tile, bf16),
            pltpu.VMEM((4, n) + tile, bf16),
            pltpu.VMEM((2, 4, n) + tile, bf16),
            pltpu.VMEM((2, 4, n) + tile, bf16),
            pltpu.VMEM((4, n) + tile, f32),
            pltpu.VMEM((2, 4, n) + tile, bf16),
            pltpu.VMEM((2, 4, n) + tile, bf16),
            pltpu.VMEM((5,) + gains.shape, f32),
            pltpu.VMEM((5,) + gains.shape, f32),
            pltpu.SemaphoreType.DMA((4,)),
            pltpu.SemaphoreType.DMA((4, 2)),
            pltpu.SemaphoreType.DMA((2, 2)),
            pltpu.SemaphoreType.DMA((4, 2)),
            pltpu.SemaphoreType.DMA((2, 4, 2)),
            pltpu.SemaphoreType.DMA((5, 2)),
        ],
        compiler_params=params(48, collective_id=1, has_side_effects=True),
        cost_estimate=cost(30e9, 16 << 20),
    )(pool, gains)


META = 4


def load_blocks(meta, part, pool, sems):
    blk = part.shape[2] // 2
    copies = []
    for k in range(2 * part.shape[0]):
        at = pl.multiple_of(meta[META + k] * blk, blk)
        source = part.at[k // 2, :, pl.ds(k % 2 * blk, blk), :]
        copies.append(pltpu.make_async_copy(source, pool.at[:, pl.ds(at, blk), :], sems.at[k]))
    for copy in copies:
        copy.start()
    for copy in copies:
        copy.wait()


def masked(scores, block, q_block, length):
    blk = scores.shape[1]
    key = block + lax.broadcasted_iota(jnp.int32, scores.shape, 0)
    query = q_block * blk + lax.broadcasted_iota(jnp.int32, scores.shape, 1)
    return jnp.where(jnp.logical_and(key <= query, key < length), scores, blocked_score)


def nt_dot(a, b):
    return lax.dot_general(a, b, (((1,), (1,)), ((), ())), preferred_element_type=f32)


def tn_dot(a, b):
    return lax.dot_general(a, b, (((0,), (0,)), ((), ())), preferred_element_type=f32)


def key_block(pool, meta, block, g):
    spot = meta[META + block]
    blk = pool.shape[2] // 2
    return pool[spot // 2, g, pl.ds(pl.multiple_of((spot % 2) * blk, blk), blk), :]


def flash_forward_kernel(meta, q_ref, part, out_ref, lse_ref, pool, vt, peak, acc, turned, sems):
    load_blocks(meta, part, pool, sems)
    length = meta[2]
    blk = q_ref.shape[1] // 2
    live_blocks = (length + blk - 1) // blk
    turned[960:, :] = jnp.zeros((64, blk), f32)
    for g in range(KVH):
        vt[g, :64, :] = jnp.ones((64, vt.shape[2]), bf16)
        for k in range(pool.shape[1] // 256):
            vt[g, 64:, 256 * k : 256 * k + 256] = pool[g, 256 * k : 256 * k + 256, :].T[64:]
    for qi in range(2):
        q_block = meta[qi]
        blocks = jnp.minimum(q_block + 1, live_blocks)

        def group(g, _):
            queries = [q_ref[GRP * g + h, blk * qi : blk * qi + blk, :] for h in range(GRP)]
            for h in range(GRP):
                peak[h] = jnp.full((1, blk), blocked_score, f32)
                acc[h] = jnp.zeros((128, blk), f32)

            def step(block, wide, with_mask):
                start = pl.multiple_of(block * blk, blk)
                span = pl.ds(start, wide * blk)
                kv = pool[g, span, :]
                vals = vt[g, :, span]
                scores = [nt_dot(kv, queries[h]) for h in range(GRP)]
                if with_mask:
                    scores = [masked(t, start, q_block, length) for t in scores]
                before = [peak[h] for h in range(GRP)]
                now = [jnp.maximum(before[h], jnp.max(scores[h], axis=0, keepdims=True)) for h in range(GRP)]
                weights = [jnp.exp(scores[h] - now[h]).astype(bf16) for h in range(GRP)]
                for h in range(GRP):
                    peak[h] = now[h]
                    acc[h] = acc[h] * jnp.exp(before[h] - now[h]) + jnp.dot(
                        vals, weights[h], preferred_element_type=f32
                    )

            def plain(pair, _):
                step(2 * pair, 2, False)
                return 0

            lax.fori_loop(0, (blocks - 1) // 2, plain, 0)

            @pl.when(blocks % 2 == 1)
            def _():
                step(blocks - 1, 1, True)

            @pl.when(blocks % 2 == 0)
            def _():
                step(blocks - 2, 2, True)

            for h in range(GRP):
                total = acc[h][0:1, :]
                turned[pl.ds(pl.multiple_of((GRP * g + h) * HD, HD), HD), :] = acc[h][64:, :] / total
                lse_ref[GRP * g + h, :, blk * qi : blk * qi + blk] = peak[h] + jnp.log(total)
            return 0

        lax.fori_loop(0, KVH, group, 0)
        out_ref[blk * qi : blk * qi + blk, :] = turned[...].T.astype(bf16)


def flash_forward(m, meta, q, part):
    n_ctx, _, rows, _ = part.shape
    blk = rows // 2
    return pl.pallas_call(
        flash_forward_kernel,
        grid=(1,),
        out_shape=[jax.ShapeDtypeStruct((rows, QP), bf16), jax.ShapeDtypeStruct((16, 1, rows), f32)],
        in_specs=[SM, pl.BlockSpec((QH, rows, 128), lambda i: (0, m, 0)), ANY],
        out_specs=[
            pl.BlockSpec((rows, QP), lambda i: (0, 0)),
            pl.BlockSpec((16, 1, rows), lambda i: (0, 0, 0)),
        ],
        scratch_shapes=[
            pltpu.VMEM((KVH, n_ctx * rows, 128), bf16),
            pltpu.VMEM((KVH, 128, n_ctx * rows), bf16),
            pltpu.VMEM((GRP, 1, blk), f32),
            pltpu.VMEM((GRP, 128, blk), f32),
            pltpu.VMEM((QP, blk), f32),
            pltpu.SemaphoreType.DMA((2 * n_ctx,)),
        ],
        compiler_params=params(48),
        cost_estimate=cost(40e9, 8 << 20),
    )(meta, q, part)


def flash_backward_kernel(
    meta, q_ref, out_ref, grad_ref, lse_ref, cos_ref, sin_ref, part, gq_ref, gkv_ref,
    pool, kt, wide, delta, total, acc, turned, sides, sems,
):
    load_blocks(meta, part, pool, sems)
    length = meta[2]
    rows = q_ref.shape[1]
    blk = rows // 2
    live_blocks = (length + blk - 1) // blk
    total[...] = jnp.zeros_like(total)
    lane = lax.broadcasted_iota(jnp.int32, (rows, 128), 1)
    pick = lax.broadcasted_iota(jnp.int32, (16, 128), 0) == lax.broadcasted_iota(jnp.int32, (16, 128), 1) // 64
    pick = jnp.where(pick, 1.0, 0.0).astype(bf16)
    for g in range(KVH):
        for k in range(pool.shape[1] // 256):
            kt[g, :, 256 * k : 256 * k + 256] = pool[g, 256 * k : 256 * k + 256, :].T[:64]
    for p in range(8):
        slab = grad_ref[:, 128 * p : 128 * p + 128].astype(f32)
        wide[2 * p] = jnp.where(lane >= 64, pltpu.roll(slab, 64, 1), 0.0).astype(bf16)
        if 2 * p + 1 < QH:
            wide[2 * p + 1] = jnp.where(lane >= 64, slab, 0.0).astype(bf16)
        product = slab * out_ref[:, 128 * p : 128 * p + 128].astype(f32)
        high = product.astype(bf16)
        low = (product - high.astype(f32)).astype(bf16)
        both = nt_dot(pick, high) + nt_dot(pick, low)
        delta[2 * p] = both[0:1, :]
        delta[2 * p + 1] = both[1:2, :]
    turned[960:, :] = jnp.zeros((64, blk), f32)
    for qi in range(2):
        q_block = meta[qi]
        blocks = jnp.where(q_block < live_blocks, q_block + 1, 0)
        span = slice(blk * qi, blk * qi + blk)

        def group(g, _):
            for h in range(GRP):
                acc[h] = jnp.zeros((64, blk), f32)
                sides[2 * blk * h : 2 * blk * h + blk] = q_ref[GRP * g + h, span, :]
                sides[2 * blk * h + blk : 2 * blk * h + 2 * blk] = wide[GRP * g + h, span, :]

            def step(block, count, with_mask):
                start = pl.multiple_of(block * blk, blk)
                keys = pl.ds(start, count * blk)
                kv = pool[g, keys, :]
                keys_t = kt[g, :, keys]
                heads = [GRP * g + h for h in range(GRP)]
                scores = [nt_dot(kv, sides[2 * blk * h : 2 * blk * h + blk]) for h in range(GRP)]
                inner = [nt_dot(kv, sides[2 * blk * h + blk : 2 * blk * h + 2 * blk]) for h in range(GRP)]
                if with_mask:
                    scores = [masked(t, start, q_block, length) for t in scores]
                probs = [jnp.exp(scores[h] - lse_ref[heads[h], :, span]) for h in range(GRP)]
                change = [(probs[h] * (inner[h] - delta[heads[h], :, span])).astype(bf16) for h in range(GRP)]
                terms = []
                for h in range(GRP):
                    terms += [change[h], probs[h].astype(bf16)]
                total[g, keys, :] += jnp.dot(
                    jnp.concatenate(terms, axis=1), sides[...], preferred_element_type=f32
                )
                for h in range(GRP):
                    acc[h] = acc[h] + jnp.dot(keys_t, change[h], preferred_element_type=f32)

            def plain(pair, _):
                step(2 * pair, 2, False)
                return 0

            lax.fori_loop(0, (blocks - 1) // 2, plain, 0)

            @pl.when(jnp.logical_and(blocks > 0, blocks % 2 == 1))
            def _():
                step(blocks - 1, 1, True)

            @pl.when(jnp.logical_and(blocks > 0, blocks % 2 == 0))
            def _():
                step(blocks - 2, 2, True)

            for h in range(GRP):
                turned[pl.ds(pl.multiple_of((GRP * g + h) * HD, HD), HD), :] = acc[h] * 0.125
            return 0

        lax.fori_loop(0, KVH, group, 0)
        grads = turned[...].T
        cosine, sine = cos_ref[span, :], sin_ref[span, :]
        for p in range(8):
            slab = grads[:, 128 * p : 128 * p + 128]
            gq_ref[span, 128 * p : 128 * p + 128] = (slab * cosine - swap_halves(slab) * sine).astype(bf16)
    for k in range(2 * gkv_ref.shape[0]):
        at = pl.multiple_of(meta[META + k] * blk, blk)
        gkv_ref[k // 2, :, k % 2 * blk : k % 2 * blk + blk, :] = total[:, pl.ds(at, blk), :].astype(bf16)


def flash_backward(m, meta, q, out, grad, lse, cosine, sine, part):
    n_ctx, _, rows, _ = part.shape
    blk = rows // 2
    return pl.pallas_call(
        flash_backward_kernel,
        grid=(1,),
        out_shape=[
            jax.ShapeDtypeStruct((rows, QP), bf16),
            jax.ShapeDtypeStruct((n_ctx, KVH, rows, 128), bf16),
        ],
        in_specs=[
            SM,
            pl.BlockSpec((QH, rows, 128), lambda i: (0, m, 0)),
            pl.BlockSpec((rows, QP), lambda i: (0, 0)),
            pl.BlockSpec((rows, QP), lambda i: (m, 0)),
            pl.BlockSpec((16, 1, rows), lambda i: (0, 0, 0)),
            pl.BlockSpec((rows, 128), lambda i: (0, 0)),
            pl.BlockSpec((rows, 128), lambda i: (0, 0)),
            ANY,
        ],
        out_specs=[
            pl.BlockSpec((rows, QP), lambda i: (0, 0)),
            pl.BlockSpec((n_ctx, KVH, rows, 128), lambda i: (0, 0, 0, 0)),
        ],
        scratch_shapes=[
            pltpu.VMEM((KVH, n_ctx * rows, 128), bf16),
            pltpu.VMEM((KVH, 64, n_ctx * rows), bf16),
            pltpu.VMEM((QH, rows, 128), bf16),
            pltpu.VMEM((16, 1, rows), f32),
            pltpu.VMEM((KVH, n_ctx * rows, 128), f32),
            pltpu.VMEM((GRP, 64, blk), f32),
            pltpu.VMEM((QP, blk), f32),
            pltpu.VMEM((2 * GRP * blk, 128), bf16),
            pltpu.SemaphoreType.DMA((2 * n_ctx,)),
        ],
        compiler_params=params(56),
        cost_estimate=cost(50e9, 16 << 20),
    )(meta, q, out, grad, lse, cosine, sine, part)


CHUNK = 512


def middle_kernel(
    table, scalars, pool_ref, out_0, out_1, wo, x_ref, cot_ref, gain_ref,
    mixed_ref, normed_t, hidden_t, ggu_ref, go_ref, branch_ref, residual_ref, attn_ref, gain_out,
    pool, wgu, wd, sems,
):
    i = pl.program_id(0)
    blk = x_ref.shape[0]
    load = pltpu.make_async_copy(pool_ref, pool, sems.at[0])

    @pl.when(i == 0)
    def _():
        load.start()

    attn = jnp.where(i < 2, out_0[...], out_1[...])
    residual = x_ref[...].astype(f32) + jnp.dot(attn, wo[...], preferred_element_type=f32)
    inverse = lax.rsqrt(jnp.mean(residual * residual, axis=1, keepdims=True) + epsilon)
    gain = gain_ref[...]
    normed = (residual * inverse * gain).astype(bf16)
    normed_t[...] = normed.T
    row = scalars[i % 2] * blk + lax.broadcasted_iota(jnp.int32, (blk, D), 0)
    grad_out = cot_ref[0].T
    grad_out = jnp.where(row < scalars[2 + i // 2], grad_out, jnp.zeros((), bf16))
    go_ref[...] = grad_out

    @pl.when(i == 0)
    def _():
        load.wait()
        ffn_rows(pool, table, wgu, wd)

    def first(j):
        at = CHUNK * j
        return (
            jnp.dot(normed, wgu[:, at : at + CHUNK], preferred_element_type=f32),
            jnp.dot(normed, wgu[:, FF + at : FF + at + CHUNK], preferred_element_type=f32),
            nt_dot(grad_out, wd[at : at + CHUNK, :]),
        )

    mixed = residual
    grad_normed = jnp.zeros((blk, D), f32)
    ahead = first(0)
    for j in range(FF // CHUNK):
        at = CHUNK * j
        gate, up, grad_hidden = ahead
        if j + 1 < FF // CHUNK:
            ahead = first(j + 1)
        sigma = jax.nn.sigmoid(gate)
        silu = gate * sigma
        hidden = (silu * up).astype(bf16)
        grad_up = (grad_hidden * silu).astype(bf16)
        grad_gate = (grad_hidden * up * (sigma + silu * (1.0 - sigma))).astype(bf16)
        hidden_t[at : at + CHUNK, :] = hidden.T
        ggu_ref[:, at : at + CHUNK] = grad_gate
        ggu_ref[:, FF + at : FF + at + CHUNK] = grad_up
        mixed = mixed + jnp.dot(hidden, wd[at : at + CHUNK, :], preferred_element_type=f32)
        grad_normed = grad_normed + nt_dot(grad_gate, wgu[:, at : at + CHUNK])
        grad_normed = grad_normed + nt_dot(grad_up, wgu[:, FF + at : FF + at + CHUNK])

    mixed_ref[0] = mixed.astype(bf16).T
    unit = residual * inverse
    scaled = grad_normed * gain
    back = inverse * (scaled - unit * jnp.mean(scaled * unit, axis=1, keepdims=True))
    grad_residual = grad_out.astype(f32) + back
    residual_ref[...] = grad_residual
    branch = grad_residual.astype(bf16)
    branch_ref[...] = branch
    attn_ref[...] = nt_dot(branch, wo[...]).astype(bf16)
    term = jnp.sum(grad_normed * unit, axis=0, keepdims=True)

    @pl.when(i == 0)
    def _():
        gain_out[...] = term

    @pl.when(i > 0)
    def _():
        gain_out[...] += term


def middle(table, scalars, pool, outs, wo, x_rows, cot_t, gain):
    micro, _, rows = cot_t.shape
    tokens = micro * rows
    blk = rows // 2

    def rows_of(width, kind):
        return jax.ShapeDtypeStruct((tokens, width), kind), pl.BlockSpec((blk, width), lambda i: (i, 0))

    def columns_of(height):
        return jax.ShapeDtypeStruct((height, tokens), bf16), pl.BlockSpec((height, blk), lambda i: (0, i))

    native = pl.BlockSpec((1, D, blk), lambda i: (i // 2, 0, i % 2))
    whole = pl.BlockSpec((1, D), lambda i: (0, 0))
    results = [
        (jax.ShapeDtypeStruct((micro, D, rows), bf16), native),
        columns_of(D),
        columns_of(FF),
        rows_of(2 * FF, bf16),
        rows_of(D, bf16),
        rows_of(D, bf16),
        rows_of(D, f32),
        rows_of(QP, bf16),
        (jax.ShapeDtypeStruct((1, D), f32), whole),
    ]
    return pl.pallas_call(
        middle_kernel,
        grid=(2 * micro,),
        out_shape=[r[0] for r in results],
        in_specs=[
            SM,
            SM,
            ANY,
            pl.BlockSpec((blk, QP), lambda i: (jnp.minimum(i, 1), 0)),
            pl.BlockSpec((blk, QP), lambda i: (jnp.maximum(i - 2, 0), 0)),
            pl.BlockSpec((QP, D), lambda i: (0, 0)),
            pl.BlockSpec((blk, D), lambda i: (i, 0)),
            native,
            whole,
        ],
        out_specs=[r[1] for r in results],
        scratch_shapes=[
            pltpu.VMEM(pool.shape, bf16),
            pltpu.VMEM((D, 2 * FF), bf16),
            pltpu.VMEM((FF, D), bf16),
            pltpu.SemaphoreType.DMA((1,)),
        ],
        compiler_params=params(62),
        cost_estimate=cost(40e9, 40 << 20),
    )(table, scalars, pool, outs[0], outs[1], wo, x_rows, cot_t, gain)


def ffn_grads_kernel(pieces, table, normed_t, ggu_ref, hidden_t, go_ref, *refs):
    outs, (pool, first, second, sems) = refs[:pieces], refs[pieces:]
    j = pl.program_id(0)

    @pl.when(j == 0)
    def _():
        clear_pool(pool)

    first[...] = jnp.dot(normed_t[...], ggu_ref[...], preferred_element_type=f32).astype(bf16)
    second[...] = jnp.dot(hidden_t[...], go_ref[...], preferred_element_type=f32).astype(bf16)
    base = 600 * (j // 5) + 8 * (j % 5)

    def gu_row(r, _):
        row = pl.multiple_of(r * 64, 64)
        for p in range(4):
            at = base + r * 40 + 2 * p
            pick_pair(pool, table, first, row, 128 * p, at, at + 1)
        return 0

    lax.fori_loop(0, 15, gu_row, 0)

    def d_row(r, _):
        row = pl.multiple_of(r * 64, 64)
        at = 1200 + (4 * j + r) * 15
        for p in range(7):
            pick_pair(pool, table, second, row, 128 * p, at + 2 * p, at + 2 * p + 1)
        pick_single(pool, table, second, row, 896, at + 14)
        return 0

    lax.fori_loop(0, 4, d_row, 0)

    @pl.when(j == 9)
    def _():
        flush_pool(pool, outs, sems)


def ffn_grads(table, normed_t, ggu, hidden_t, go, total, pieces):
    tokens = go.shape[0]
    return pl.pallas_call(
        functools.partial(ffn_grads_kernel, pieces),
        grid=(10,),
        out_shape=[jax.ShapeDtypeStruct((total // pieces, 32, 128), bf16)] * pieces,
        in_specs=[
            SM,
            pl.BlockSpec((D, tokens), lambda j: (0, 0)),
            pl.BlockSpec((tokens, 512), lambda j: (0, j)),
            pl.BlockSpec((256, tokens), lambda j: (j, 0)),
            pl.BlockSpec((tokens, D), lambda j: (0, 0)),
        ],
        out_specs=[ANY] * pieces,
        scratch_shapes=[
            pltpu.VMEM((total, 32, 128), bf16),
            pltpu.VMEM((D, 512), bf16),
            pltpu.VMEM((256, D), bf16),
            pltpu.SemaphoreType.DMA((pieces,)),
        ],
        compiler_params=params(52),
        cost_estimate=cost(15e9, 60 << 20),
    )(table, normed_t, ggu, hidden_t, go)


def normalize(values, gain):
    inverse_rms = lax.rsqrt(jnp.mean(values * values, axis=-1, keepdims=True) + epsilon)
    return (inverse_rms, (values * inverse_rms * gain).astype(bf16))


def norm_back(values, inverse_rms, gain, grad_normed):
    unit_rows = values * inverse_rms
    gain_part = jnp.sum(grad_normed * unit_rows, axis=0)
    scaled = grad_normed * gain
    grad_values = inverse_rms * (
        scaled - unit_rows * jnp.mean(scaled * unit_rows, axis=-1, keepdims=True)
    )
    return (grad_values, gain_part)


def fold(tiles):
    return jnp.concatenate([tiles[:, :32, :], tiles[:, 32:, :]], axis=2)


def unfold(tiles):
    return jnp.concatenate([tiles[:, :, :64], tiles[:, :, 64:]], axis=1)


def mm(a, b):
    return jnp.dot(a, b, preferred_element_type=f32)


def shards(
    inputs,
    cotangent,
    lengths,
    order,
    owner_slots,
    master,
    stat_left,
    stat_right,
    root_left,
    root_right,
    gains,
    gain_stats,
):
    highest = lax.Precision.HIGHEST
    micro, rows = inputs.shape[1], inputs.shape[2]
    n_ctx, n_wt = lax.axis_size("ctx"), lax.axis_size("wt")
    devices = n_ctx * n_wt
    line = is_line(n_ctx, n_wt)
    tokens = micro * rows
    cap = master.shape[0]
    cap_a = NTA // devices + NTA // (8 * devices) + 2
    cap_f = cap - cap_a
    c = lax.axis_index("ctx")
    w = lax.axis_index("wt")

    x_t = inputs[0].transpose(0, 2, 1)
    low_master = fold(master.astype(bf16))
    own_a, own_f = low_master[:cap_a], low_master[cap_a:]
    own_a, own_f = low_master[:cap_a], low_master[cap_a:]
    owner, within = owner_slots // cap, owner_slots % cap
    whole_a = owner[:NTA] * cap_a + within[:NTA]
    whole_f = owner[NTA:] * cap_f + within[NTA:] - cap_a
    table_a = part_index(owner[:NTA], within[:NTA], cap_a, c, w, n_ctx, n_wt)
    table_f = part_index(owner[NTA:], within[NTA:] - cap_a, cap_f, c, w, n_ctx, n_wt)

    blocks = order.shape[0]
    ids = jnp.arange(blocks, dtype=jnp.int32)
    my_blocks = jnp.sum(jnp.where(ids[None, :] == 2 * c + jnp.arange(2)[:, None], order[None, :], 0), axis=1)
    position = (my_blocks[:, None] * (rows // 2) + jnp.arange(rows // 2, dtype=jnp.int32)[None, :]).reshape(rows)
    lane = np.arange(128)
    frequency = jnp.asarray(rope_base, f32) ** (-(jnp.asarray(lane % 32, f32)) * 2.0 / HD)
    angle = position.astype(f32)[:, None] * frequency[None, :]
    cosine = jnp.cos(angle)
    sine = jnp.sin(angle) * jnp.where(lane % 64 < 32, -1.0, 1.0).astype(f32)[None, :]
    metas = [
        jnp.concatenate([my_blocks, lengths[0, m][None], c[None], order]).astype(jnp.int32)
        for m in range(micro)
    ]

    if line:
        q, normed_attn, x_low, kv_first, kv_late, wqkv, wo, pool_f = front(
            whole_a, own_a, own_f, x_t, gains[0:1], cosine, sine
        )
        pool_f = pool_f.reshape(devices * cap_f, 32, 128)
        chunks = [kv_first, lax.all_gather(kv_late, "ctx", axis=0)]
    else:
        parts_a = [lax.all_gather(own_a, AXES, axis=0, tiled=True)]
        pool_f = lax.all_gather(own_f, AXES, axis=0, tiled=True)
        wqkv, wo = assemble(assemble_attn_kernel, parts_a, whole_a, [(D, CW), (QP, D)])
        x_low = inputs.reshape(tokens, D)
        q, kv, normed_attn = qkv_rows(x_low, gains[0:1], wqkv, cosine, sine, micro)
        chunks = [lax.all_gather(kv[m], "ctx", axis=0) for m in range(micro)]
    forward = [flash_forward(m, metas[m], q, chunks[m]) for m in range(micro)]
    scalars = jnp.concatenate([my_blocks, lengths[0]]).astype(jnp.int32)
    cot_t = cotangent[0].transpose(0, 2, 1)
    outs = [f[0] for f in forward]
    (mixed_t, normed_ffn_t, hidden_t, grad_gu, grad_out, grad_branch, grad_residual, grad_attn, gain_ffn) = middle(
        whole_f, scalars, pool_f, outs, wo, x_low, cot_t, gains[1:2]
    )
    if line:
        mine_f, other_f = ffn_grads(table_f, normed_ffn_t, grad_gu, hidden_t, grad_out, devices * cap_f, 2)
        grad_attn = after(grad_attn, mine_f)
        quads_f = reduce_core(mine_f, other_f, cap_f)
        diag_f = reduce_diag(quads_f)
        near_f = reduce_near(quads_f, diag_f)
        sum_f = reduce_line(quads_f, near_f)
    else:
        (whole_terms,) = ffn_grads(whole_f, normed_ffn_t, grad_gu, hidden_t, grad_out, devices * cap_f, 1)
        sum_f = lax.psum_scatter(whole_terms.astype(f32), AXES, scatter_dimension=0, tiled=True)
    attn_out = jnp.concatenate(outs, axis=0)
    x = x_low.astype(f32)

    grad_q, grad_kv = [], []
    for m in range(micro):
        waits = [] if not line else [quads_f, diag_f][m]
        gq, gkv = flash_backward(
            m, metas[m], q, forward[m][0], after(grad_attn, *waits), forward[m][1], cosine, sine, chunks[m]
        )
        own = lax.psum_scatter(gkv, "ctx", scatter_dimension=0, tiled=False).astype(f32)
        grad_q.append(gq)
        grad_kv.append(own)
    left = jnp.asarray(lane < 64)
    rows_kv = jnp.stack(grad_kv)
    swapped = jnp.concatenate(
        [rows_kv[..., 32:64], rows_kv[..., :32], rows_kv[..., 64:]], axis=-1
    )
    rows_kv = rows_kv * jnp.where(left, cosine, 1.0) - swapped * jnp.where(left, sine, 0.0)
    rows_kv = rows_kv.astype(bf16).transpose(0, 2, 1, 3).reshape(tokens, KVH * 128)
    grad_cat = jnp.concatenate([jnp.concatenate(grad_q, axis=0), rows_kv], axis=1)
    if line:
        grad_cat = after(grad_cat, *near_f)
    grad_normed_attn = mm(grad_cat, wqkv.T)
    rms_attn = lax.rsqrt(jnp.mean(x * x, axis=-1, keepdims=True) + epsilon)
    grad_input_norm, gain_attn = norm_back(x, rms_attn, gains[0], grad_normed_attn)
    input_grad = grad_residual + grad_input_norm

    dqkv = mm(normed_attn.T, grad_cat).astype(bf16)
    dwo = mm(attn_out.T, grad_branch).astype(bf16)
    (whole_terms,) = pack(pack_attn_kernel, whole_a, dqkv, dwo, devices * cap_a, 1)
    gain_terms = jnp.stack([gain_attn, gain_ffn[0]])
    if line:
        gain_rows = jnp.pad(gain_terms.reshape(15, 128), ((0, 1), (0, 0)))
        sum_a, gain_rows = tail(whole_terms.reshape(4, 4, 2, cap_a, 32, 128), gain_rows)
        gain_grads = gain_rows[:15].reshape(2, D)
    else:
        sum_a = lax.psum_scatter(whole_terms.astype(f32), AXES, scatter_dimension=0, tiled=True)
        gain_grads = lax.psum(gain_terms, AXES)

    tile_grads = unfold(jnp.concatenate([sum_a, sum_f], axis=0))
    gram_left = jnp.einsum("sij,skj->sik", tile_grads, tile_grads, precision=highest)
    gram_right = jnp.einsum("sji,sjk->sik", tile_grads, tile_grads, precision=highest)
    new_left = decay_rate * stat_left + (1.0 - decay_rate) * gram_left
    new_right = decay_rate * stat_right + (1.0 - decay_rate) * gram_right
    step_left = jnp.einsum("sij,sjk->sik", root_left, tile_grads, precision=highest)
    step_full = jnp.einsum("sij,sjk->sik", step_left, root_right, precision=highest)
    new_master = master - step_rate * step_full
    new_gain_stats = decay_rate * gain_stats + (1.0 - decay_rate) * gain_grads * gain_grads
    new_gains = gains - gain_rate * gain_grads * lax.rsqrt(new_gain_stats)
    return (
        mixed_t.transpose(0, 2, 1)[None],
        input_grad.reshape(1, micro, rows, D),
        tile_grads,
        new_left,
        new_right,
        new_master,
        gain_grads,
        new_gain_stats,
        new_gains,
    )


def solution(mesh):
    in_specs = (
        P("wt", None, "ctx", None),
        P("wt", None, "ctx", None),
        P("wt", None),
        P(),
        P(),
        P(AXES, None, None),
        P(AXES, None, None),
        P(AXES, None, None),
        P(AXES, None, None),
        P(AXES, None, None),
        P(),
        P(),
    )
    out_specs = (
        P("wt", None, "ctx", None),
        P("wt", None, "ctx", None),
        P(AXES, None, None),
        P(AXES, None, None),
        P(AXES, None, None),
        P(AXES, None, None),
        P(),
        P(),
        P(),
    )
    return jax.shard_map(shards, mesh=mesh, in_specs=in_specs, out_specs=out_specs, check_vma=False)
```

```python
import functools

import jax
import jax.numpy as jnp
import numpy as np
from jax import lax
from jax.experimental import pallas as pl
from jax.experimental.pallas import tpu as pltpu
from jax.sharding import PartitionSpec as P

D = 960
FF = 2560
QH = 15
KVH = 5
HD = 64
TL = 64
QW = 960
KVW = 320
GRP = 3
NTA = 600
NT = 2400
QP = 1024
CW = 1664
BLK = 256
AXES = ("ctx", "wt")

epsilon = 1e-05
decay_rate = 0.95
step_rate = 0.05
gain_rate = 0.05
rope_base = 10000.0
blocked_score = -1e30
bf16 = jnp.bfloat16
f32 = jnp.float32
VM = pl.BlockSpec(memory_space=pltpu.VMEM)
SM = pl.BlockSpec(memory_space=pltpu.SMEM)
ANY = pl.BlockSpec(memory_space=pl.ANY)


def params(megabytes, **kwargs):
    return pltpu.CompilerParams(vmem_limit_bytes=megabytes << 20, **kwargs)


def cost(flops, nbytes, trans=0):
    return pl.CostEstimate(flops=int(flops), bytes_accessed=int(nbytes), transcendentals=int(trans))


def after(x, *others):
    return lax.optimization_barrier((x, others))[0]


def is_line(n_ctx, n_wt):
    return n_ctx == 4 and n_wt == 8


def tile_halves(n):
    return (n + 1) // 2


def load_parts(parts, pool, sems):
    at = 0
    copies = []
    for i, part in enumerate(parts):
        rows = part.shape[0]
        copies.append(pltpu.make_async_copy(part, pool.at[pl.ds(at, rows)], sems.at[i]))
        at += rows
    for copy in copies:
        copy.start()
    for copy in copies:
        copy.wait()


def place_pair(pool, table, ref, row, lane, a, b):
    first = pool[table[a]]
    second = pool[table[b]]
    ref[pl.ds(row, 32), lane : lane + 128] = jnp.concatenate([first[:, :64], second[:, :64]], axis=1)
    ref[pl.ds(row + 32, 32), lane : lane + 128] = jnp.concatenate([first[:, 64:], second[:, 64:]], axis=1)


def place_single(pool, table, ref, row, lane, a):
    first = pool[table[a]]
    ref[pl.ds(row, 32), lane : lane + 64] = first[:, :64]
    ref[pl.ds(row + 32, 32), lane : lane + 64] = first[:, 64:]


def assemble_attn_kernel(count, table, *refs):
    parts, (wqkv, wo, pool, sems) = refs[:count], refs[count:]
    load_parts(parts, pool, sems)
    attn_rows(pool, table, wqkv, wo)


def attn_rows(pool, table, wqkv, wo):
    def qkv_row(r, _):
        row = pl.multiple_of(r * 64, 64)
        for p in range(7):
            place_pair(pool, table, wqkv, row, 128 * p, r * 15 + 2 * p, r * 15 + 2 * p + 1)
        place_single(pool, table, wqkv, row, 896, r * 15 + 14)
        wqkv[pl.ds(row, 64), 960:1024] = jnp.zeros((64, 64), bf16)
        for g in range(KVH):
            place_pair(pool, table, wqkv, row, QP + 128 * g, 225 + r * 5 + g, 300 + r * 5 + g)
        for p in range(7):
            place_pair(pool, table, wo, row, 128 * p, 375 + r * 15 + 2 * p, 375 + r * 15 + 2 * p + 1)
        place_single(pool, table, wo, row, 896, 375 + r * 15 + 14)
        return 0

    lax.fori_loop(0, 15, qkv_row, 0)
    wo[pl.ds(960, 64), :] = jnp.zeros((64, D), bf16)


def ffn_rows(pool, table, wgu, wd):
    def gu_row(r, _):
        row = pl.multiple_of(r * 64, 64)
        for m in range(2):
            for p in range(20):
                base = 600 * m + r * 40 + 2 * p
                place_pair(pool, table, wgu, row, FF * m + 128 * p, base, base + 1)
        return 0

    lax.fori_loop(0, 15, gu_row, 0)

    def d_row(r, _):
        row = pl.multiple_of(r * 64, 64)
        for p in range(7):
            place_pair(pool, table, wd, row, 128 * p, 1200 + r * 15 + 2 * p, 1200 + r * 15 + 2 * p + 1)
        place_single(pool, table, wd, row, 896, 1200 + r * 15 + 14)
        return 0

    lax.fori_loop(0, 40, d_row, 0)


def assemble(kernel, parts, table, shapes):
    total = sum(p.shape[0] for p in parts)
    out_bytes = sum(2 * a * b for a, b in shapes)
    return pl.pallas_call(
        functools.partial(kernel, len(parts)),
        out_shape=[jax.ShapeDtypeStruct(s, bf16) for s in shapes],
        in_specs=[SM] + [ANY] * len(parts),
        out_specs=[VM] * len(shapes),
        scratch_shapes=[pltpu.VMEM((total, 32, 128), bf16), pltpu.SemaphoreType.DMA((len(parts),))],
        compiler_params=params(52),
        cost_estimate=cost(0, 4 * out_bytes),
    )(table, *parts)


def pick_pair(pool, table, ref, row, lane, a, b):
    block = ref[pl.ds(row, 64), lane : lane + 128]
    pool[table[a]] = jnp.concatenate([block[:32, :64], block[32:, :64]], axis=1)
    pool[table[b]] = jnp.concatenate([block[:32, 64:], block[32:, 64:]], axis=1)


def pick_single(pool, table, ref, row, lane, a):
    block = ref[pl.ds(row, 64), lane : lane + 64]
    pool[table[a]] = jnp.concatenate([block[:32], block[32:]], axis=1)


def clear_pool(pool):
    step = 8
    whole = pool.shape[0] // step

    def clear(i, _):
        pool[pl.ds(i * step, step)] = jnp.zeros((step, 32, 128), bf16)
        return 0

    lax.fori_loop(0, whole, clear, 0)
    rest = pool.shape[0] - whole * step
    if rest:
        pool[whole * step :] = jnp.zeros((rest, 32, 128), bf16)


def flush_pool(pool, outs, sems):
    at = 0
    copies = []
    for i, out in enumerate(outs):
        rows = out.shape[0]
        copies.append(pltpu.make_async_copy(pool.at[pl.ds(at, rows)], out, sems.at[i]))
        at += rows
    for copy in copies:
        copy.start()
    for copy in copies:
        copy.wait()


def attn_tiles(pool, table, dqkv, dwo):
    def qkv_row(r, _):
        row = pl.multiple_of(r * 64, 64)
        for p in range(7):
            pick_pair(pool, table, dqkv, row, 128 * p, r * 15 + 2 * p, r * 15 + 2 * p + 1)
        pick_single(pool, table, dqkv, row, 896, r * 15 + 14)
        for g in range(KVH):
            pick_pair(pool, table, dqkv, row, QP + 128 * g, 225 + r * 5 + g, 300 + r * 5 + g)
        for p in range(7):
            pick_pair(pool, table, dwo, row, 128 * p, 375 + r * 15 + 2 * p, 375 + r * 15 + 2 * p + 1)
        pick_single(pool, table, dwo, row, 896, 375 + r * 15 + 14)
        return 0

    lax.fori_loop(0, 15, qkv_row, 0)


def swap_halves(x):
    lane = lax.broadcasted_iota(jnp.int32, x.shape, 1)
    return jnp.where(lane % 64 < 32, pltpu.roll(x, 96, 1), pltpu.roll(x, 32, 1))


def qkv_kernel(x_ref, gain_ref, w_ref, cos_ref, sin_ref, q_ref, kv_ref, normed_ref):
    x = x_ref[...].astype(f32)
    inverse = lax.rsqrt(jnp.mean(x * x, axis=1, keepdims=True) + epsilon)
    normed = (x * inverse * gain_ref[...]).astype(bf16)
    normed_ref[...] = normed
    cosine, sine = cos_ref[...], sin_ref[...]
    lane = lax.broadcasted_iota(jnp.int32, cosine.shape, 1)
    left = lane < 64
    for p in range(8):
        rows = jnp.dot(normed, w_ref[:, 128 * p : 128 * p + 128], preferred_element_type=f32)
        rows = (rows * cosine + swap_halves(rows) * sine).astype(bf16).astype(f32) * 0.125
        q_ref[2 * p] = jnp.where(left, rows, 0.0).astype(bf16)
        if 2 * p + 1 < QH:
            q_ref[2 * p + 1] = jnp.where(left, pltpu.roll(rows, 64, 1), 0.0).astype(bf16)
    cosine = jnp.where(left, cosine, 1.0)
    sine = jnp.where(left, sine, 0.0)
    for g in range(KVH):
        at = QP + 128 * g
        rows = jnp.dot(normed, w_ref[:, at : at + 128], preferred_element_type=f32)
        kv_ref[0, g] = (rows * cosine + swap_halves(rows) * sine).astype(bf16)


def qkv_rows(x, gain, wqkv, cosine, sine, micro):
    tokens = x.shape[0]
    rows = tokens // micro
    blk = min(BLK, rows)
    steps = tokens // blk
    per = steps // micro
    return pl.pallas_call(
        qkv_kernel,
        grid=(steps,),
        out_shape=[
            jax.ShapeDtypeStruct((QH, tokens, 128), bf16),
            jax.ShapeDtypeStruct((micro, KVH, rows, 128), bf16),
            jax.ShapeDtypeStruct((tokens, D), bf16),
        ],
        in_specs=[
            pl.BlockSpec((blk, D), lambda i: (i, 0)),
            pl.BlockSpec((1, D), lambda i: (0, 0)),
            pl.BlockSpec((D, CW), lambda i: (0, 0)),
            pl.BlockSpec((blk, 128), lambda i: (i % per, 0)),
            pl.BlockSpec((blk, 128), lambda i: (i % per, 0)),
        ],
        out_specs=[
            pl.BlockSpec((QH, blk, 128), lambda i: (0, i, 0)),
            pl.BlockSpec((1, KVH, blk, 128), lambda i: (i // per, 0, i % per, 0)),
            pl.BlockSpec((blk, D), lambda i: (i, 0)),
        ],
        compiler_params=params(40),
        cost_estimate=cost(2 * tokens * D * CW, 14 << 20),
    )(x, gain, wqkv, cosine, sine)


def remote(src, dst, send, recv, device):
    return pltpu.make_async_remote_copy(
        src_ref=src,
        dst_ref=dst,
        send_sem=send,
        recv_sem=recv,
        device_id=device,
        device_id_type=pl.DeviceIdType.MESH,
    )


def greet(c, w, far):
    barrier = pltpu.get_barrier_semaphore()

    def hail(device):
        pl.semaphore_signal(barrier, inc=1, device_id=device, device_id_type=pl.DeviceIdType.MESH)

    for bit in (1, 2, 4):
        hail({"wt": w ^ bit})
    if far:
        hail({"ctx": c ^ 2})

    @pl.when(c < 3)
    def _():
        hail({"ctx": c + 1})

    @pl.when(c > 0)
    def _():
        hail({"ctx": c - 1})

    inner = jnp.logical_and(c > 0, c < 3)

    @pl.when(inner)
    def _():
        pl.semaphore_wait(barrier, 5 + far)

    @pl.when(jnp.logical_not(inner))
    def _():
        pl.semaphore_wait(barrier, 4 + far)


class Gather:
    def __init__(self, pool, sems, c, w):
        self.pool, self.sems, self.c, self.w = pool, sems, c, w
        self.n = pool.shape[2]
        self.n1 = tile_halves(self.n)
        self.x, self.y, self.core = {"wt": w ^ 2}, {"wt": w ^ 4}, {"wt": w ^ 1}

    def copy(self, k, owner, lane, device, part=None):
        ref = self.pool.at[k, owner]
        if part is not None:
            ref = ref.at[pl.ds(part[0], part[1])]
        return remote(ref, ref, self.sems.at[k, lane], self.sems.at[k, lane + 1], device)

    def up(self, k):
        return self.copy(k, self.w, 0, {"ctx": self.c + 1})

    def down(self, k):
        return self.copy(k, self.w, 2, {"ctx": self.c - 1})

    def over_x(self, k, back=0):
        return self.copy(k, self.w ^ back, 4, self.x)

    def over_y(self, k, back=0):
        return self.copy(k, self.w ^ back, 6, self.y)

    def diag_x(self, k, owner):
        return self.copy(k, owner, 8, self.x, (0, self.n1))

    def diag_y(self, k, owner):
        return self.copy(k, owner, 10, self.y, (self.n1, self.n - self.n1))

    def over_core(self, k, quad, back=0):
        return self.copy(k, self.w ^ (2 * quad) ^ back, 12 + 2 * quad, self.core)

    def send_line(self, k, low, high):
        if low:

            @pl.when(self.c < 3)
            def _():
                self.up(k).start()

        if high:

            @pl.when(self.c > 0)
            def _():
                self.down(k).start()

    def send_near(self, k):
        self.over_x(k).start()
        self.over_y(k).start()
        self.over_core(k, 0).start()

    def first(self):
        self.send_line(self.c, True, True)

    def sides(self, s):
        return [(self.c >= s, self.c - s, True), (self.c + s <= 3, self.c + s, False)]

    def line_step(self, s, near=True):
        for valid, k, below in self.sides(s):

            @pl.when(valid)
            def _(k=k, below=below):
                if below:
                    self.up(k).wait_recv()
                else:
                    self.down(k).wait_recv()
                if s < 3:
                    self.send_line(k, below, not below)
                if near:
                    self.send_near(k)

    def each(self, s, act):
        if s == 0:
            act(self.c)
            return
        for valid, k, _ in self.sides(s):

            @pl.when(valid)
            def _(k=k):
                act(k)

    def near_step(self, s):
        def act(k):
            self.over_x(k, 2).wait_recv()
            self.diag_y(k, self.w ^ 2).start()
            self.over_core(k, 1).start()
            self.over_y(k, 4).wait_recv()
            self.diag_x(k, self.w ^ 4).start()
            self.over_core(k, 2).start()

        self.each(s, act)

    def diag_step(self, s):
        def act(k):
            self.diag_x(k, self.w ^ 6).wait_recv()
            self.diag_y(k, self.w ^ 6).wait_recv()
            self.over_core(k, 3).start()

        self.each(s, act)

    def finish(self):
        for k in range(4):
            for quad in range(4):
                self.over_core(k, quad, 1).wait_recv()

    def drain(self):
        for k in range(4):

            @pl.when(jnp.logical_and(k <= self.c, self.c < 3))
            def _(k=k):
                self.up(k).wait_send()

            @pl.when(jnp.logical_and(k >= self.c, self.c > 0))
            def _(k=k):
                self.down(k).wait_send()

            self.over_x(k).wait_send()
            self.over_y(k).wait_send()
            self.diag_x(k, self.w ^ 4).wait_send()
            self.diag_y(k, self.w ^ 2).wait_send()
            for quad in range(4):
                self.over_core(k, quad).wait_send()


def front_kernel(
    table, own_a, own_f, x_ref, gain_ref, cos_ref, sin_ref,
    q_ref, normed_ref, rows_ref, kv_ref, late_ref, wqkv, wo, pool_f,
    pool_a, kv_own, sems_a, sems_f, sems_kv, sems,
):
    c, w = lax.axis_index("ctx"), lax.axis_index("wt")
    take_a = pltpu.make_async_copy(own_a, pool_a.at[c, w], sems.at[0])
    take_f = pltpu.make_async_copy(own_f, pool_f.at[c, w], sems.at[1])
    take_a.start()
    take_f.start()
    greet(c, w, 0)
    take_a.wait()
    a = Gather(pool_a, sems_a, c, w)
    f = Gather(pool_f, sems_f, c, w)
    a.first()
    a.send_near(c)

    rows = x_ref.shape[2]
    blk = BLK
    for m in range(2):
        for half in range(rows // blk):
            part = x_ref[m, :, blk * half : blk * half + blk].T
            span = slice(m * rows + blk * half, m * rows + blk * half + blk)
            rows_ref[span, :] = part
            wide = part.astype(f32)
            inverse = lax.rsqrt(jnp.mean(wide * wide, axis=1, keepdims=True) + epsilon)
            normed_ref[span, :] = (wide * inverse * gain_ref[...]).astype(bf16)

    a.line_step(1)
    a.near_step(0)
    a.line_step(2)
    take_f.wait()
    f.first()
    a.near_step(1)
    a.diag_step(0)
    a.line_step(3)
    a.near_step(2)
    a.diag_step(1)
    a.near_step(3)
    f.send_near(c)
    a.diag_step(2)
    a.diag_step(3)
    f.line_step(1)
    a.finish()

    flat = pool_a.reshape(pool_a.shape[0] * pool_a.shape[1] * pool_a.shape[2], 32, 128)
    attn_rows(flat, table, wqkv, wo)
    f.line_step(2)
    f.near_step(0)

    lane = lax.broadcasted_iota(jnp.int32, (blk, 128), 1)
    left = lane < 64

    def qkv_block(i, _):
        at = pl.multiple_of(i * blk, blk)
        normed = normed_ref[pl.ds(at, blk), :]
        within = pl.multiple_of((i % (rows // blk)) * blk, blk)
        cosine, sine = cos_ref[pl.ds(within, blk), :], sin_ref[pl.ds(within, blk), :]
        key_cosine = jnp.where(left, cosine, 1.0)
        key_sine = jnp.where(left, sine, 0.0)
        for g in range(KVH):
            spot = QP + 128 * g
            part = jnp.dot(normed, wqkv[:, spot : spot + 128], preferred_element_type=f32)
            part = (part * key_cosine + swap_halves(part) * key_sine).astype(bf16)
            kv_own[i // (rows // blk), g, pl.ds(within, blk), :] = part
        for p in range(8):
            part = jnp.dot(normed, wqkv[:, 128 * p : 128 * p + 128], preferred_element_type=f32)
            part = (part * cosine + swap_halves(part) * sine).astype(bf16).astype(f32) * 0.125
            q_ref[2 * p, pl.ds(at, blk), :] = jnp.where(left, part, 0.0).astype(bf16)
            if 2 * p + 1 < QH:
                other = jnp.where(left, pltpu.roll(part, 64, 1), 0.0).astype(bf16)
                q_ref[2 * p + 1, pl.ds(at, blk), :] = other
        return 0

    def kv_move(src, k, lane, step):
        return remote(src, kv_ref.at[k], sems_kv.at[k, lane], sems_kv.at[k, lane + 1], {"ctx": c + step})

    lax.fori_loop(0, rows // blk, qkv_block, 0)
    keep = pltpu.make_async_copy(kv_own.at[0], kv_ref.at[c], sems.at[2])
    keep.start()

    @pl.when(c < 3)
    def _():
        kv_move(kv_own.at[0], c, 0, 1).start()

    @pl.when(c > 0)
    def _():
        kv_move(kv_own.at[0], c, 2, -1).start()

    lax.fori_loop(rows // blk, 2 * rows // blk, qkv_block, 0)
    late = pltpu.make_async_copy(kv_own.at[1], late_ref, sems.at[3])
    late.start()

    def kv_step(s):
        @pl.when(c >= s)
        def _():
            kv_move(kv_ref.at[c - s], c - s, 0, 1).wait_recv()
            if s < 3:

                @pl.when(c < 3)
                def _():
                    kv_move(kv_ref.at[c - s], c - s, 0, 1).start()

        @pl.when(c + s <= 3)
        def _():
            kv_move(kv_ref.at[c + s], c + s, 2, -1).wait_recv()
            if s < 3:

                @pl.when(c > 0)
                def _():
                    kv_move(kv_ref.at[c + s], c + s, 2, -1).start()

    f.line_step(3)
    f.near_step(1)
    f.diag_step(0)
    kv_step(1)
    f.near_step(2)
    f.diag_step(1)
    f.near_step(3)
    kv_step(2)
    f.diag_step(2)
    f.diag_step(3)
    f.finish()
    kv_step(3)
    keep.wait()
    late.wait()
    for k in range(4):

        @pl.when(jnp.logical_and(k <= c, c < 3))
        def _(k=k):
            kv_move(kv_ref.at[k], k, 0, 1).wait_send()

        @pl.when(jnp.logical_and(k >= c, c > 0))
        def _(k=k):
            kv_move(kv_ref.at[k], k, 2, -1).wait_send()

    a.drain()
    f.drain()


def front(table, own_a, own_f, x_t, gain, cosine, sine):
    micro, _, rows = x_t.shape
    tokens = micro * rows
    n_a, n_f = own_a.shape[0], own_f.shape[0]
    return pl.pallas_call(
        front_kernel,
        out_shape=[
            jax.ShapeDtypeStruct((QH, tokens, 128), bf16),
            jax.ShapeDtypeStruct((tokens, D), bf16),
            jax.ShapeDtypeStruct((tokens, D), bf16),
            jax.ShapeDtypeStruct((4, KVH, rows, 128), bf16),
            jax.ShapeDtypeStruct((KVH, rows, 128), bf16),
            jax.ShapeDtypeStruct((D, CW), bf16),
            jax.ShapeDtypeStruct((QP, D), bf16),
            jax.ShapeDtypeStruct((4, 8, n_f, 32, 128), bf16),
        ],
        in_specs=[SM, ANY, ANY, VM, VM, VM, VM],
        out_specs=[VM, VM, VM, ANY, ANY, VM, VM, ANY],
        scratch_shapes=[
            pltpu.VMEM((4, 8, n_a, 32, 128), bf16),
            pltpu.VMEM((micro, KVH, rows, 128), bf16),
            pltpu.SemaphoreType.DMA((4, 20)),
            pltpu.SemaphoreType.DMA((4, 20)),
            pltpu.SemaphoreType.DMA((4, 4)),
            pltpu.SemaphoreType.DMA((4,)),
        ],
        compiler_params=params(48, collective_id=0, has_side_effects=True),
        cost_estimate=cost(40e9, 40 << 20),
    )(table, own_a, own_f, x_t, gain, cosine, sine)


class Line:
    def __init__(self, terms, send, recv, sems, c):
        self.terms, self.send, self.recv, self.sems, self.c = terms, send, recv, sems, c
        self.count = recv.shape[2]

    def copy(self, way, k):
        sems = self.sems
        return remote(
            self.send.at[k], self.recv.at[way, k], sems.at[way, k, 0], sems.at[way, k, 1],
            {"ctx": self.c + 1 - 2 * way},
        )

    def loop(self, act):
        def body(j, _):
            act(j)
            return 0

        lax.fori_loop(0, self.count, body, 0)

    def start(self):
        for way in (0, 1):

            @pl.when(self.c == 3 * way)
            def _(way=way):
                for far in (3, 2, 1):
                    k = far if way == 0 else 3 - far

                    def take(j, k=k):
                        self.send[k, j] = self.terms(k, j).astype(bf16)

                    self.loop(take)
                    self.copy(way, k).start()

    def join(self, way, k):
        self.copy(way, k).wait_recv()

        def act(j):
            self.send[k, j] = (self.terms(k, j) + self.recv[way, k, j].astype(f32)).astype(bf16)

        self.loop(act)
        self.copy(way, k).start()

    def step(self, number):
        lists = {1: ((0, 3), (0, 2), (1, 0)), 2: ((1, 0), (1, 1), (0, 3))}
        for inner, order in lists.items():

            @pl.when(self.c == inner)
            def _(order=order):
                self.join(*order[number])

    def finish(self, out):
        c, recv = self.c, self.recv

        @pl.when(c > 0)
        def _():
            self.copy(0, c).wait_recv()

        @pl.when(c < 3)
        def _():
            self.copy(1, c).wait_recv()

        def total(j):
            low = jnp.where(c > 0, recv[0, c, j].astype(f32), 0.0)
            high = jnp.where(c < 3, recv[1, c, j].astype(f32), 0.0)
            out[j] = self.terms(c, j) + low + high

        self.loop(total)

    def drain(self):
        for far in (3, 2, 1):
            for way, k in ((0, far), (1, 3 - far)):

                @pl.when(self.c < k if way == 0 else self.c > k)
                def _(way=way, k=k):
                    self.copy(way, k).wait_send()


class Plane:
    def __init__(self, pool, bufs, sems, c, w):
        self.pool, self.sems, self.c, self.w = pool, sems, c, w
        self.mine, self.theirs, self.diag_send, self.diag_recv, self.near_send, self.near_recv = bufs
        self.n = pool.shape[3]
        n1 = self.n1 = tile_halves(self.n)
        yx, core = w // 2, w % 2
        over_x, over_y, over_core = {"wt": w ^ 2}, {"wt": w ^ 4}, {"wt": w ^ 1}
        self.loads = [
            pltpu.make_async_copy(pool.at[:, yx ^ q, core], self.mine.at[q], sems.at[10 + q, 0]) for q in range(4)
        ]
        self.cores = [
            remote(pool.at[:, yx ^ q, 1 - core], self.theirs.at[q], sems.at[q, 0], sems.at[q, 1], over_core)
            for q in range(4)
        ]
        low, high = slice(0, n1), slice(n1, self.n)
        self.diag_x = self.move(self.diag_send.at[:, low], self.diag_recv.at[:, low], 4, over_x)
        self.diag_y = self.move(self.diag_send.at[:, high], self.diag_recv.at[:, high], 5, over_y)
        self.nears = {}
        for q in (1, 2):
            for part, cut in enumerate((low, high)):
                self.nears[q, part] = self.move(
                    self.near_send.at[q - 1, :, cut],
                    self.near_recv.at[q - 1, :, cut],
                    4 + 2 * q + part,
                    over_x if q == 1 else over_y,
                )

    def move(self, src, dst, lane, device):
        return remote(src, dst, self.sems.at[lane, 0], self.sems.at[lane, 1], device)

    def begin_loads(self):
        for q in (3, 1, 2, 0):
            self.loads[q].start()

    def begin(self):
        for q in (3, 1, 2, 0):
            self.cores[q].start()

    def each(self, act):
        def body(k, _):
            act(k)
            return 0

        lax.fori_loop(0, 4, body, 0)

    def both(self, q, k):
        return self.mine[q, k].astype(f32) + self.theirs[q, k].astype(f32)

    def ready(self, q):
        self.loads[q].wait()
        self.cores[q].wait()

    def diag(self):
        self.ready(3)

        def act(k):
            self.diag_send[k] = self.both(3, k).astype(bf16)

        self.each(act)
        self.diag_x.start()
        self.diag_y.start()

    def near(self, q):
        self.ready(q)

        def act(k):
            self.near_send[q - 1, k] = self.both(q, k).astype(bf16)

        self.each(act)
        self.nears[q, q - 1].start()

    def join(self, q):
        cut = slice(self.n1, self.n) if q == 1 else slice(0, self.n1)
        (self.diag_y if q == 1 else self.diag_x).wait_recv()

        def act(k):
            ours = self.near_send[q - 1, k, cut].astype(f32)
            self.near_send[q - 1, k, cut] = (ours + self.diag_recv[k, cut].astype(f32)).astype(bf16)

        self.each(act)
        self.nears[q, 2 - q].start()

    def arrive(self):
        self.ready(0)
        for part in (0, 1):
            for q in (1, 2):
                self.nears[q, part].wait_recv()

    def own(self, k):
        return self.both(0, k) + self.near_recv[0, k].astype(f32) + self.near_recv[1, k].astype(f32)

    def drain(self):
        self.diag_x.wait_send()
        self.diag_y.wait_send()
        for copy in self.nears.values():
            copy.wait_send()


def plane_scratch(n):
    tile = (32, 128)
    return [
        pltpu.VMEM((4, 4, n) + tile, bf16),
        pltpu.VMEM((4, 4, n) + tile, bf16),
        pltpu.VMEM((4, n) + tile, bf16),
        pltpu.VMEM((4, n) + tile, bf16),
        pltpu.VMEM((2, 4, n) + tile, bf16),
        pltpu.VMEM((2, 4, n) + tile, bf16),
        pltpu.SemaphoreType.DMA((14, 2)),
    ]


def line_scratch(shape):
    return [
        pltpu.VMEM((4,) + shape, bf16),
        pltpu.VMEM((2, 4) + shape, bf16),
        pltpu.SemaphoreType.DMA((2, 4, 2)),
    ]


def return_kernel(pool, kv_ref, sum_ref, kv_out, *scratch):
    c, w = lax.axis_index("ctx"), lax.axis_index("wt")
    plane = Plane(pool, scratch[:6], scratch[6], c, w)
    line = Line(lambda k, j: kv_ref[k, j].astype(f32), *scratch[7:], c)
    plane.begin_loads()
    greet(c, w, 0)
    plane.begin()

    line.start()
    plane.diag()
    plane.near(1)
    plane.near(2)
    line.step(0)
    plane.join(1)
    line.step(1)
    plane.join(2)
    line.step(2)
    plane.arrive()

    def own(k):
        sum_ref[k] = plane.own(k).astype(bf16)

    plane.each(own)
    line.finish(kv_out)
    plane.drain()
    line.drain()


def back_home(pool, kv_terms):
    n = pool.shape[3]
    return pl.pallas_call(
        return_kernel,
        out_shape=[
            jax.ShapeDtypeStruct((4, n, 32, 128), bf16),
            jax.ShapeDtypeStruct(kv_terms.shape[1:], f32),
        ],
        in_specs=[ANY, VM],
        out_specs=[VM, VM],
        scratch_shapes=plane_scratch(n) + line_scratch(kv_terms.shape[1:]),
        compiler_params=params(60, collective_id=2, has_side_effects=True),
        cost_estimate=cost(30e9, 16 << 20),
    )(pool, kv_terms)


def tail_kernel(pool, ffn_ref, gain_ref, sum_ref, ffn_out, gain_out, own, gain_send, gain_recv, sems_gain, *scratch):
    c, w = lax.axis_index("ctx"), lax.axis_index("wt")
    plane = Plane(pool, scratch[:6], scratch[6], c, w)
    line = Line(lambda k, j: own[k, j], *scratch[7:10], c)
    ffn_line = Line(lambda k, j: ffn_ref[k, j].astype(f32), *scratch[10:13], c)
    plane.begin_loads()
    greet(c, w, 1)
    plane.begin()

    stages = [{"wt": w ^ 1}, {"wt": w ^ 2}, {"wt": w ^ 4}, {"ctx": c ^ 1}, {"ctx": c ^ 2}]
    copies = [
        remote(gain_send.at[i], gain_recv.at[i], sems_gain.at[i, 0], sems_gain.at[i, 1], stages[i]) for i in range(5)
    ]
    gain_send[0] = gain_ref[...]
    copies[0].start()

    def gain_step(i):
        copies[i].wait()
        total = gain_send[i] + gain_recv[i]
        if i < 4:
            gain_send[i + 1] = total
            copies[i + 1].start()
        else:
            gain_out[...] = total

    ffn_line.start()
    plane.diag()
    gain_step(0)
    plane.near(1)
    plane.near(2)
    ffn_line.step(0)
    gain_step(1)
    plane.join(1)
    plane.join(2)
    ffn_line.step(1)
    gain_step(2)
    plane.arrive()

    def own_sum(k):
        own[k] = plane.own(k)

    plane.each(own_sum)
    line.start()
    ffn_line.step(2)
    gain_step(3)
    for number in range(3):
        line.step(number)
    ffn_line.finish(ffn_out)
    gain_step(4)
    line.finish(sum_ref)
    plane.drain()
    line.drain()
    ffn_line.drain()


def tail(pool, ffn_terms, gains):
    n, n_f = pool.shape[3], ffn_terms.shape[1]
    tile = (32, 128)
    return pl.pallas_call(
        tail_kernel,
        out_shape=[
            jax.ShapeDtypeStruct((n,) + tile, f32),
            jax.ShapeDtypeStruct((n_f,) + tile, f32),
            jax.ShapeDtypeStruct(gains.shape, f32),
        ],
        in_specs=[ANY, VM, VM],
        out_specs=[VM, VM, VM],
        scratch_shapes=[
            pltpu.VMEM((4, n) + tile, f32),
            pltpu.VMEM((5,) + gains.shape, f32),
            pltpu.VMEM((5,) + gains.shape, f32),
            pltpu.SemaphoreType.DMA((5, 2)),
        ]
        + plane_scratch(n)
        + line_scratch((n,) + tile)
        + line_scratch((n_f,) + tile),
        compiler_params=params(48, collective_id=1, has_side_effects=True),
        cost_estimate=cost(30e9, 16 << 20),
    )(pool, ffn_terms, gains)


META = 4


def load_blocks(meta, part, pool, sems):
    blk = part.shape[2] // 2
    copies = []
    for k in range(2 * part.shape[0]):
        at = pl.multiple_of(meta[META + k] * blk, blk)
        source = part.at[k // 2, :, pl.ds(k % 2 * blk, blk), :]
        copies.append(pltpu.make_async_copy(source, pool.at[:, pl.ds(at, blk), :], sems.at[k]))
    for copy in copies:
        copy.start()
    for copy in copies:
        copy.wait()


def masked(scores, block, q_block, length):
    blk = scores.shape[1]
    key = block + lax.broadcasted_iota(jnp.int32, scores.shape, 0)
    query = q_block * blk + lax.broadcasted_iota(jnp.int32, scores.shape, 1)
    return jnp.where(jnp.logical_and(key <= query, key < length), scores, blocked_score)


def nt_dot(a, b):
    return lax.dot_general(a, b, (((1,), (1,)), ((), ())), preferred_element_type=f32)


def tn_dot(a, b):
    return lax.dot_general(a, b, (((0,), (0,)), ((), ())), preferred_element_type=f32)


def flash_forward_kernel(meta, q_ref, part, out_ref, lse_ref, pool, vt, peak, acc, turned, sems):
    load_blocks(meta, part, pool, sems)
    length = meta[2]
    blk = q_ref.shape[1] // 2
    live_blocks = (length + blk - 1) // blk
    turned[960:, :] = jnp.zeros((64, blk), f32)
    for g in range(KVH):
        vt[g, :64, :] = jnp.ones((64, vt.shape[2]), bf16)
        for k in range(pool.shape[1] // 256):
            vt[g, 64:, 256 * k : 256 * k + 256] = pool[g, 256 * k : 256 * k + 256, :].T[64:]
    for qi in range(2):
        q_block = meta[qi]
        blocks = jnp.minimum(q_block + 1, live_blocks)

        def group(g, _):
            queries = [q_ref[GRP * g + h, blk * qi : blk * qi + blk, :] for h in range(GRP)]
            for h in range(GRP):
                peak[h] = jnp.full((1, blk), blocked_score, f32)
                acc[h] = jnp.zeros((128, blk), f32)

            def step(block, wide, with_mask):
                start = pl.multiple_of(block * blk, blk)
                span = pl.ds(start, wide * blk)
                kv = pool[g, span, :]
                vals = vt[g, :, span]
                scores = [nt_dot(kv, queries[h]) for h in range(GRP)]
                if with_mask:
                    scores = [masked(t, start, q_block, length) for t in scores]
                before = [peak[h] for h in range(GRP)]
                now = [jnp.maximum(before[h], jnp.max(scores[h], axis=0, keepdims=True)) for h in range(GRP)]
                weights = [jnp.exp(scores[h] - now[h]).astype(bf16) for h in range(GRP)]
                for h in range(GRP):
                    peak[h] = now[h]
                    acc[h] = acc[h] * jnp.exp(before[h] - now[h]) + jnp.dot(
                        vals, weights[h], preferred_element_type=f32
                    )

            def plain(pair, _):
                step(2 * pair, 2, False)
                return 0

            lax.fori_loop(0, (blocks - 1) // 2, plain, 0)

            @pl.when(blocks % 2 == 1)
            def _():
                step(blocks - 1, 1, True)

            @pl.when(blocks % 2 == 0)
            def _():
                step(blocks - 2, 2, True)

            for h in range(GRP):
                total = acc[h][0:1, :]
                turned[pl.ds(pl.multiple_of((GRP * g + h) * HD, HD), HD), :] = acc[h][64:, :] / total
                lse_ref[GRP * g + h, :, blk * qi : blk * qi + blk] = peak[h] + jnp.log(total)
            return 0

        lax.fori_loop(0, KVH, group, 0)
        out_ref[blk * qi : blk * qi + blk, :] = turned[...].T.astype(bf16)


def flash_forward(m, meta, q, part):
    n_ctx, _, rows, _ = part.shape
    blk = rows // 2
    return pl.pallas_call(
        flash_forward_kernel,
        grid=(1,),
        out_shape=[jax.ShapeDtypeStruct((rows, QP), bf16), jax.ShapeDtypeStruct((16, 1, rows), f32)],
        in_specs=[SM, pl.BlockSpec((QH, rows, 128), lambda i: (0, m, 0)), ANY],
        out_specs=[
            pl.BlockSpec((rows, QP), lambda i: (0, 0)),
            pl.BlockSpec((16, 1, rows), lambda i: (0, 0, 0)),
        ],
        scratch_shapes=[
            pltpu.VMEM((KVH, n_ctx * rows, 128), bf16),
            pltpu.VMEM((KVH, 128, n_ctx * rows), bf16),
            pltpu.VMEM((GRP, 1, blk), f32),
            pltpu.VMEM((GRP, 128, blk), f32),
            pltpu.VMEM((QP, blk), f32),
            pltpu.SemaphoreType.DMA((2 * n_ctx,)),
        ],
        compiler_params=params(48),
        cost_estimate=cost(40e9, 8 << 20),
    )(meta, q, part)


def flash_backward_kernel(
    meta, q_ref, out_ref, grad_ref, lse_ref, cos_ref, sin_ref, part, gq_ref, gkv_ref,
    pool, kt, wide, delta, total, acc, turned, sides, sems,
):
    load_blocks(meta, part, pool, sems)
    length = meta[2]
    rows = q_ref.shape[1]
    blk = rows // 2
    live_blocks = (length + blk - 1) // blk
    total[...] = jnp.zeros_like(total)
    lane = lax.broadcasted_iota(jnp.int32, (rows, 128), 1)
    pick = lax.broadcasted_iota(jnp.int32, (16, 128), 0) == lax.broadcasted_iota(jnp.int32, (16, 128), 1) // 64
    pick = jnp.where(pick, 1.0, 0.0).astype(bf16)
    for g in range(KVH):
        for k in range(pool.shape[1] // 256):
            kt[g, :, 256 * k : 256 * k + 256] = pool[g, 256 * k : 256 * k + 256, :].T[:64]
    for p in range(8):
        slab = grad_ref[:, 128 * p : 128 * p + 128].astype(f32)
        wide[2 * p] = jnp.where(lane >= 64, pltpu.roll(slab, 64, 1), 0.0).astype(bf16)
        if 2 * p + 1 < QH:
            wide[2 * p + 1] = jnp.where(lane >= 64, slab, 0.0).astype(bf16)
        product = slab * out_ref[:, 128 * p : 128 * p + 128].astype(f32)
        high = product.astype(bf16)
        low = (product - high.astype(f32)).astype(bf16)
        both = nt_dot(pick, high) + nt_dot(pick, low)
        delta[2 * p] = both[0:1, :]
        delta[2 * p + 1] = both[1:2, :]
    turned[960:, :] = jnp.zeros((64, blk), f32)
    for qi in range(2):
        q_block = meta[qi]
        blocks = jnp.where(q_block < live_blocks, q_block + 1, 0)
        span = slice(blk * qi, blk * qi + blk)

        def group(g, _):
            for h in range(GRP):
                acc[h] = jnp.zeros((64, blk), f32)
                sides[2 * blk * h : 2 * blk * h + blk] = q_ref[GRP * g + h, span, :]
                sides[2 * blk * h + blk : 2 * blk * h + 2 * blk] = wide[GRP * g + h, span, :]

            def step(block, count, with_mask):
                start = pl.multiple_of(block * blk, blk)
                keys = pl.ds(start, count * blk)
                kv = pool[g, keys, :]
                keys_t = kt[g, :, keys]
                heads = [GRP * g + h for h in range(GRP)]
                scores = [nt_dot(kv, sides[2 * blk * h : 2 * blk * h + blk]) for h in range(GRP)]
                inner = [nt_dot(kv, sides[2 * blk * h + blk : 2 * blk * h + 2 * blk]) for h in range(GRP)]
                if with_mask:
                    scores = [masked(t, start, q_block, length) for t in scores]
                probs = [jnp.exp(scores[h] - lse_ref[heads[h], :, span]) for h in range(GRP)]
                change = [(probs[h] * (inner[h] - delta[heads[h], :, span])).astype(bf16) for h in range(GRP)]
                terms = []
                for h in range(GRP):
                    terms += [change[h], probs[h].astype(bf16)]
                total[g, keys, :] += jnp.dot(
                    jnp.concatenate(terms, axis=1), sides[...], preferred_element_type=f32
                )
                for h in range(GRP):
                    acc[h] = acc[h] + jnp.dot(keys_t, change[h], preferred_element_type=f32)

            def plain(pair, _):
                step(2 * pair, 2, False)
                return 0

            lax.fori_loop(0, (blocks - 1) // 2, plain, 0)

            @pl.when(jnp.logical_and(blocks > 0, blocks % 2 == 1))
            def _():
                step(blocks - 1, 1, True)

            @pl.when(jnp.logical_and(blocks > 0, blocks % 2 == 0))
            def _():
                step(blocks - 2, 2, True)

            for h in range(GRP):
                turned[pl.ds(pl.multiple_of((GRP * g + h) * HD, HD), HD), :] = acc[h] * 0.125
            return 0

        lax.fori_loop(0, KVH, group, 0)
        grads = turned[...].T
        cosine, sine = cos_ref[span, :], sin_ref[span, :]
        for p in range(8):
            slab = grads[:, 128 * p : 128 * p + 128]
            gq_ref[span, 128 * p : 128 * p + 128] = (slab * cosine - swap_halves(slab) * sine).astype(bf16)
    for k in range(2 * gkv_ref.shape[0]):
        at = pl.multiple_of(meta[META + k] * blk, blk)
        gkv_ref[k // 2, :, k % 2 * blk : k % 2 * blk + blk, :] = total[:, pl.ds(at, blk), :].astype(bf16)


def flash_backward(m, meta, q, out, grad, lse, cosine, sine, part):
    n_ctx, _, rows, _ = part.shape
    blk = rows // 2
    return pl.pallas_call(
        flash_backward_kernel,
        grid=(1,),
        out_shape=[
            jax.ShapeDtypeStruct((rows, QP), bf16),
            jax.ShapeDtypeStruct((n_ctx, KVH, rows, 128), bf16),
        ],
        in_specs=[
            SM,
            pl.BlockSpec((QH, rows, 128), lambda i: (0, m, 0)),
            pl.BlockSpec((rows, QP), lambda i: (0, 0)),
            pl.BlockSpec((rows, QP), lambda i: (m, 0)),
            pl.BlockSpec((16, 1, rows), lambda i: (0, 0, 0)),
            pl.BlockSpec((rows, 128), lambda i: (0, 0)),
            pl.BlockSpec((rows, 128), lambda i: (0, 0)),
            ANY,
        ],
        out_specs=[
            pl.BlockSpec((rows, QP), lambda i: (0, 0)),
            pl.BlockSpec((n_ctx, KVH, rows, 128), lambda i: (0, 0, 0, 0)),
        ],
        scratch_shapes=[
            pltpu.VMEM((KVH, n_ctx * rows, 128), bf16),
            pltpu.VMEM((KVH, 64, n_ctx * rows), bf16),
            pltpu.VMEM((QH, rows, 128), bf16),
            pltpu.VMEM((16, 1, rows), f32),
            pltpu.VMEM((KVH, n_ctx * rows, 128), f32),
            pltpu.VMEM((GRP, 64, blk), f32),
            pltpu.VMEM((QP, blk), f32),
            pltpu.VMEM((2 * GRP * blk, 128), bf16),
            pltpu.SemaphoreType.DMA((2 * n_ctx,)),
        ],
        compiler_params=params(56),
        cost_estimate=cost(50e9, 16 << 20),
    )(meta, q, out, grad, lse, cosine, sine, part)


def assemble_ffn_kernel(table, pool_ref, gu_out, d_out, pool, wgu, wd, sems):
    load = pltpu.make_async_copy(pool_ref, pool, sems.at[0])
    load.start()
    load.wait()
    ffn_rows(pool, table, wgu, wd)
    stores = [pltpu.make_async_copy(wgu, gu_out, sems.at[1]), pltpu.make_async_copy(wd, d_out, sems.at[2])]
    for copy in stores:
        copy.start()
    for copy in stores:
        copy.wait()


def assemble_ffn(table, pool):
    shapes = [(D, 2 * FF), (FF, D)]
    return pl.pallas_call(
        assemble_ffn_kernel,
        out_shape=[jax.ShapeDtypeStruct(s, bf16) for s in shapes],
        in_specs=[SM, ANY],
        out_specs=[ANY, ANY],
        scratch_shapes=[pltpu.VMEM(s, bf16) for s in [pool.shape] + shapes] + [pltpu.SemaphoreType.DMA((3,))],
        compiler_params=params(52),
        cost_estimate=cost(0, 64 << 20),
    )(table, pool)


CHUNK = 512


def middle_kernel(
    scalars, gu_ref, d_ref, out_0, out_1, wo, x_ref, cot_ref, gain_ref,
    mixed_ref, normed_t, hidden_t, ggu_ref, go_ref, branch_ref, residual_ref, attn_ref, gain_out,
    wgu, wd, sems,
):
    i = pl.program_id(0)
    blk = x_ref.shape[0]
    loads = [pltpu.make_async_copy(gu_ref, wgu, sems.at[0]), pltpu.make_async_copy(d_ref, wd, sems.at[1])]

    @pl.when(i == 0)
    def _():
        for load in loads:
            load.start()

    attn = jnp.where(i < 2, out_0[...], out_1[...])
    residual = x_ref[...].astype(f32) + jnp.dot(attn, wo[...], preferred_element_type=f32)
    inverse = lax.rsqrt(jnp.mean(residual * residual, axis=1, keepdims=True) + epsilon)
    gain = gain_ref[...]
    normed = (residual * inverse * gain).astype(bf16)
    normed_t[...] = normed.T
    row = scalars[i % 2] * blk + lax.broadcasted_iota(jnp.int32, (blk, D), 0)
    grad_out = cot_ref[0].T
    grad_out = jnp.where(row < scalars[2 + i // 2], grad_out, jnp.zeros((), bf16))
    go_ref[...] = grad_out

    @pl.when(i == 0)
    def _():
        for load in loads:
            load.wait()

    def first(j):
        at = CHUNK * j
        return (
            jnp.dot(normed, wgu[:, at : at + CHUNK], preferred_element_type=f32),
            jnp.dot(normed, wgu[:, FF + at : FF + at + CHUNK], preferred_element_type=f32),
            nt_dot(grad_out, wd[at : at + CHUNK, :]),
        )

    mixed = residual
    grad_normed = jnp.zeros((blk, D), f32)
    ahead = first(0)
    for j in range(FF // CHUNK):
        at = CHUNK * j
        gate, up, grad_hidden = ahead
        if j + 1 < FF // CHUNK:
            ahead = first(j + 1)
        sigma = jax.nn.sigmoid(gate)
        silu = gate * sigma
        hidden = (silu * up).astype(bf16)
        grad_up = (grad_hidden * silu).astype(bf16)
        grad_gate = (grad_hidden * up * (sigma + silu * (1.0 - sigma))).astype(bf16)
        hidden_t[at : at + CHUNK, :] = hidden.T
        ggu_ref[:, at : at + CHUNK] = grad_gate
        ggu_ref[:, FF + at : FF + at + CHUNK] = grad_up
        mixed = mixed + jnp.dot(hidden, wd[at : at + CHUNK, :], preferred_element_type=f32)
        grad_normed = grad_normed + nt_dot(grad_gate, wgu[:, at : at + CHUNK])
        grad_normed = grad_normed + nt_dot(grad_up, wgu[:, FF + at : FF + at + CHUNK])

    mixed_ref[0] = mixed.astype(bf16).T
    unit = residual * inverse
    scaled = grad_normed * gain
    back = inverse * (scaled - unit * jnp.mean(scaled * unit, axis=1, keepdims=True))
    grad_residual = grad_out.astype(f32) + back
    residual_ref[...] = grad_residual
    branch = grad_residual.astype(bf16)
    branch_ref[...] = branch
    attn_ref[...] = nt_dot(branch, wo[...]).astype(bf16)
    term = jnp.sum(grad_normed * unit, axis=0, keepdims=True)

    @pl.when(i == 0)
    def _():
        gain_out[...] = term

    @pl.when(i > 0)
    def _():
        gain_out[...] += term


def middle(scalars, wgu, wd, outs, wo, x_rows, cot_t, gain):
    micro, _, rows = cot_t.shape
    tokens = micro * rows
    blk = rows // 2

    def rows_of(width, kind):
        return jax.ShapeDtypeStruct((tokens, width), kind), pl.BlockSpec((blk, width), lambda i: (i, 0))

    def columns_of(height):
        return jax.ShapeDtypeStruct((height, tokens), bf16), pl.BlockSpec((height, blk), lambda i: (0, i))

    native = pl.BlockSpec((1, D, blk), lambda i: (i // 2, 0, i % 2))
    whole = pl.BlockSpec((1, D), lambda i: (0, 0))
    results = [
        (jax.ShapeDtypeStruct((micro, D, rows), bf16), native),
        columns_of(D),
        columns_of(FF),
        rows_of(2 * FF, bf16),
        rows_of(D, bf16),
        rows_of(D, bf16),
        rows_of(D, f32),
        rows_of(QP, bf16),
        (jax.ShapeDtypeStruct((1, D), f32), whole),
    ]
    return pl.pallas_call(
        middle_kernel,
        grid=(2 * micro,),
        out_shape=[r[0] for r in results],
        in_specs=[
            SM,
            ANY,
            ANY,
            pl.BlockSpec((blk, QP), lambda i: (jnp.minimum(i, 1), 0)),
            pl.BlockSpec((blk, QP), lambda i: (jnp.maximum(i - 2, 0), 0)),
            pl.BlockSpec((QP, D), lambda i: (0, 0)),
            pl.BlockSpec((blk, D), lambda i: (i, 0)),
            native,
            whole,
        ],
        out_specs=[r[1] for r in results],
        scratch_shapes=[
            pltpu.VMEM((D, 2 * FF), bf16),
            pltpu.VMEM((FF, D), bf16),
            pltpu.SemaphoreType.DMA((2,)),
        ],
        compiler_params=params(62),
        cost_estimate=cost(40e9, 40 << 20),
    )(scalars, wgu, wd, outs[0], outs[1], wo, x_rows, cot_t, gain)


def ffn_grads_kernel(table, normed_t, ggu_ref, hidden_t, go_ref, pool_out, pool, first, second, sems):
    j = pl.program_id(0)

    @pl.when(j == 0)
    def _():
        clear_pool(pool)

    first[...] = jnp.dot(normed_t[...], ggu_ref[...], preferred_element_type=f32).astype(bf16)
    second[...] = jnp.dot(hidden_t[...], go_ref[...], preferred_element_type=f32).astype(bf16)
    base = 600 * (j // 5) + 8 * (j % 5)

    def gu_row(r, _):
        row = pl.multiple_of(r * 64, 64)
        for p in range(4):
            at = base + r * 40 + 2 * p
            pick_pair(pool, table, first, row, 128 * p, at, at + 1)
        return 0

    lax.fori_loop(0, 15, gu_row, 0)

    def d_row(r, _):
        row = pl.multiple_of(r * 64, 64)
        at = 1200 + (4 * j + r) * 15
        for p in range(7):
            pick_pair(pool, table, second, row, 128 * p, at + 2 * p, at + 2 * p + 1)
        pick_single(pool, table, second, row, 896, at + 14)
        return 0

    lax.fori_loop(0, 4, d_row, 0)

    @pl.when(j == 9)
    def _():
        flush_pool(pool, [pool_out], sems)


def ffn_grads(table, normed_t, ggu, hidden_t, go, total):
    tokens = go.shape[0]
    return pl.pallas_call(
        ffn_grads_kernel,
        grid=(10,),
        out_shape=jax.ShapeDtypeStruct((total, 32, 128), bf16),
        in_specs=[
            SM,
            pl.BlockSpec((D, tokens), lambda j: (0, 0)),
            pl.BlockSpec((tokens, 512), lambda j: (0, j)),
            pl.BlockSpec((256, tokens), lambda j: (j, 0)),
            pl.BlockSpec((tokens, D), lambda j: (0, 0)),
        ],
        out_specs=ANY,
        scratch_shapes=[
            pltpu.VMEM((total, 32, 128), bf16),
            pltpu.VMEM((D, 512), bf16),
            pltpu.VMEM((256, D), bf16),
            pltpu.SemaphoreType.DMA((1,)),
        ],
        compiler_params=params(52),
        cost_estimate=cost(15e9, 60 << 20),
    )(table, normed_t, ggu, hidden_t, go)


def inward_kernel(
    table, gq_0, gq_1, gkv_0, gkv_1, cos_ref, sin_ref, w_ref, normed_ref, out_0, out_1,
    branch_ref, x_ref, residual_ref, gain_ref, grad_ref, gain_out, pool_out,
    cat, dqkv, dwo, low_qkv, low_wo, pool, sems,
):
    i = pl.program_id(0)
    blk = x_ref.shape[0]
    early = i < 2
    cosine, sine = cos_ref[...], sin_ref[...]
    left = lax.broadcasted_iota(jnp.int32, (blk, 128), 1) < 64
    key_cosine = jnp.where(left, cosine, 1.0)
    key_sine = jnp.where(left, sine, 0.0)
    cat[:, :QP] = jnp.where(early, gq_0[...], gq_1[...])
    for g in range(KVH):
        slab = jnp.where(early, gkv_0[g].astype(f32), gkv_1[g])
        slab = (slab * key_cosine - swap_halves(slab) * key_sine).astype(bf16)
        cat[:, QP + 128 * g : QP + 128 * g + 128] = slab
    terms = cat[...]
    grad_normed = nt_dot(terms, w_ref[...])
    x = x_ref[...].astype(f32)
    inverse = lax.rsqrt(jnp.mean(x * x, axis=1, keepdims=True) + epsilon)
    unit = x * inverse
    scaled = grad_normed * gain_ref[...]
    back = inverse * (scaled - unit * jnp.mean(scaled * unit, axis=1, keepdims=True))
    grad_ref[0] = (residual_ref[...] + back).T
    term = jnp.sum(grad_normed * unit, axis=0, keepdims=True)
    attn = jnp.where(early, out_0[...], out_1[...])
    new_qkv = tn_dot(normed_ref[...], terms)
    new_wo = tn_dot(attn, branch_ref[...])

    @pl.when(i == 0)
    def _():
        gain_out[...] = term
        dqkv[...] = new_qkv
        dwo[...] = new_wo
        clear_pool(pool)

    @pl.when(i > 0)
    def _():
        gain_out[...] += term
        dqkv[...] += new_qkv
        dwo[...] += new_wo

    @pl.when(i == pl.num_programs(0) - 1)
    def _():
        low_qkv[...] = dqkv[...].astype(bf16)
        low_wo[...] = dwo[...].astype(bf16)
        attn_tiles(pool, table, low_qkv, low_wo)
        flush_pool(pool, [pool_out], sems)


def inward(table, gq, gkv, cosine, sine, wqkv, normed, outs, branch, x_rows, residual, gain, total):
    rows = cosine.shape[0]
    tokens = x_rows.shape[0]
    blk = rows // 2

    def early(i):
        return jnp.minimum(i, 1)

    def late(i):
        return jnp.maximum(i - 2, 0)

    def rows_of(width, at=lambda i: i):
        return pl.BlockSpec((blk, width), lambda i: (at(i), 0))

    def slabs(at):
        return pl.BlockSpec((KVH, blk, 128), lambda i: (0, at(i), 0))

    whole = pl.BlockSpec((1, D), lambda i: (0, 0))
    return pl.pallas_call(
        inward_kernel,
        grid=(tokens // blk,),
        out_shape=[
            jax.ShapeDtypeStruct((tokens // rows, D, rows), f32),
            jax.ShapeDtypeStruct((1, D), f32),
            jax.ShapeDtypeStruct((total, 32, 128), bf16),
        ],
        in_specs=[
            SM, rows_of(QP, early), rows_of(QP, late), slabs(early), slabs(late),
            rows_of(128, lambda i: i % 2), rows_of(128, lambda i: i % 2),
            pl.BlockSpec((D, CW), lambda i: (0, 0)), rows_of(D), rows_of(QP, early), rows_of(QP, late),
            rows_of(D), rows_of(D), rows_of(D), whole,
        ],
        out_specs=[pl.BlockSpec((1, D, blk), lambda i: (i // 2, 0, i % 2)), whole, ANY],
        scratch_shapes=[
            pltpu.VMEM((blk, CW), bf16),
            pltpu.VMEM((D, CW), f32),
            pltpu.VMEM((QP, D), f32),
            pltpu.VMEM((D, CW), bf16),
            pltpu.VMEM((QP, D), bf16),
            pltpu.VMEM((total, 32, 128), bf16),
            pltpu.SemaphoreType.DMA((1,)),
        ],
        compiler_params=params(60),
        cost_estimate=cost(12e9, 30 << 20),
    )(table, *gq, *gkv, cosine, sine, wqkv, normed, *outs, branch, x_rows, residual, gain)


def shampoo_kernel(
    sum_a, sum_f, master, stat_left, stat_right, root_left, root_right,
    grads_out, left_out, right_out, master_out, lefts, rights, gram_left, gram_right, step,
):
    slots = master.shape[1]
    n_a = sum_a.shape[0] // 32
    for source, target in ((root_left, lefts), (root_right, rights)):
        for r in range(32):
            both = jnp.concatenate(
                [source[64 * r : 64 * r + 64, :], source[64 * (r + 32) : 64 * (r + 32) + 64, :]], axis=0
            )
            target[pl.ds(r, slots, stride=32), :] = both.T

    def square(rows):
        return jnp.concatenate([rows[:, :64], rows[:, 64:]], axis=0)

    def folded(rows):
        return jnp.concatenate([rows[:32], rows[32:]], axis=1)

    def tile(grad, at):
        span = pl.ds(pl.multiple_of(at * 32, 32), 32)
        grad = square(grad).astype(bf16)
        left = square(lefts[span, :]).astype(bf16)
        right = square(rights[span, :]).astype(bf16)
        gram_left[span, :] = folded(nt_dot(grad, grad))
        gram_right[span, :] = folded(tn_dot(grad, grad))
        half = jnp.dot(left, grad, preferred_element_type=f32).astype(bf16)
        step[span, :] = folded(jnp.dot(half, right, preferred_element_type=f32))

    def some(source, count, shift):
        def one(s, _):
            tile(source[pl.ds(pl.multiple_of(s * 32, 32), 32), :], s + shift)
            return 0

        lax.fori_loop(0, count, one, 0, unroll=4)

    some(sum_a, n_a, 0)
    some(sum_f, slots - n_a, n_a)

    for r in range(32):
        first = slice(64 * r, 64 * r + 64)
        second = slice(64 * (r + 32), 64 * (r + 32) + 64)
        rows = pl.ds(r, slots, stride=32)
        grads = jnp.concatenate(
            [sum_a[pl.ds(r, n_a, stride=32), :], sum_f[pl.ds(r, slots - n_a, stride=32), :]], axis=0
        ).T
        grads_out[first, :] = grads[:64]
        grads_out[second, :] = grads[64:]
        for source, stat, out in ((gram_left, stat_left, left_out), (gram_right, stat_right, right_out)):
            flipped = source[rows, :].T
            out[first, :] = decay_rate * stat[first, :] + (1.0 - decay_rate) * flipped[:64]
            out[second, :] = decay_rate * stat[second, :] + (1.0 - decay_rate) * flipped[64:]
        flipped = step[rows, :].T
        master_out[first, :] = master[first, :] - step_rate * flipped[:64]
        master_out[second, :] = master[second, :] - step_rate * flipped[64:]


def shampoo(sum_a, sum_f, *arrays):
    slots = arrays[0].shape[0]
    native = [a.transpose(1, 2, 0).reshape(TL * TL, slots) for a in arrays]
    scratch = pltpu.VMEM((slots * 32, 128), f32)
    results = pl.pallas_call(
        shampoo_kernel,
        out_shape=[jax.ShapeDtypeStruct((TL * TL, slots), f32)] * 4,
        in_specs=[VM] * 7,
        out_specs=[VM] * 4,
        scratch_shapes=[scratch] * 5,
        compiler_params=params(48),
        cost_estimate=cost(1e9, 24 << 20),
    )(sum_a.reshape(-1, 128), sum_f.reshape(-1, 128), *native)
    return [r.reshape(TL, TL, slots).transpose(2, 0, 1) for r in results]


def fold(tiles):
    return jnp.concatenate([tiles[:, :32, :], tiles[:, 32:, :]], axis=2)


def shards(
    inputs,
    cotangent,
    lengths,
    order,
    owner_slots,
    master,
    stat_left,
    stat_right,
    root_left,
    root_right,
    gains,
    gain_stats,
):
    micro, rows = inputs.shape[1], inputs.shape[2]
    n_ctx, n_wt = lax.axis_size("ctx"), lax.axis_size("wt")
    devices = n_ctx * n_wt
    line = is_line(n_ctx, n_wt)
    tokens = micro * rows
    cap = master.shape[0]
    cap_a = NTA // devices + NTA // (8 * devices) + 2
    cap_f = cap - cap_a
    c = lax.axis_index("ctx")
    w = lax.axis_index("wt")

    x_t = inputs[0].transpose(0, 2, 1)
    low_master = fold(master.astype(bf16))
    own_a, own_f = low_master[:cap_a], low_master[cap_a:]
    own_a, own_f = low_master[:cap_a], low_master[cap_a:]
    owner, within = owner_slots // cap, owner_slots % cap
    whole_a = owner[:NTA] * cap_a + within[:NTA]
    whole_f = owner[NTA:] * cap_f + within[NTA:] - cap_a

    blocks = order.shape[0]
    ids = jnp.arange(blocks, dtype=jnp.int32)
    my_blocks = jnp.sum(jnp.where(ids[None, :] == 2 * c + jnp.arange(2)[:, None], order[None, :], 0), axis=1)
    position = (my_blocks[:, None] * (rows // 2) + jnp.arange(rows // 2, dtype=jnp.int32)[None, :]).reshape(rows)
    lane = np.arange(128)
    frequency = jnp.asarray(rope_base, f32) ** (-(jnp.asarray(lane % 32, f32)) * 2.0 / HD)
    angle = position.astype(f32)[:, None] * frequency[None, :]
    cosine = jnp.cos(angle)
    sine = jnp.sin(angle) * jnp.where(lane % 64 < 32, -1.0, 1.0).astype(f32)[None, :]
    metas = [
        jnp.concatenate([my_blocks, lengths[0, m][None], c[None], order]).astype(jnp.int32)
        for m in range(micro)
    ]

    if line:
        q, normed_attn, x_low, kv_first, kv_late, wqkv, wo, pool_f = front(
            whole_a, own_a, own_f, x_t, gains[0:1], cosine, sine
        )
        pool_f = pool_f.reshape(devices * cap_f, 32, 128)
        chunks = [kv_first, lax.all_gather(kv_late, "ctx", axis=0)]
    else:
        parts_a = [lax.all_gather(own_a, AXES, axis=0, tiled=True)]
        pool_f = lax.all_gather(own_f, AXES, axis=0, tiled=True)
        wqkv, wo = assemble(assemble_attn_kernel, parts_a, whole_a, [(D, CW), (QP, D)])
        x_low = inputs.reshape(tokens, D)
        q, kv, normed_attn = qkv_rows(x_low, gains[0:1], wqkv, cosine, sine, micro)
        chunks = [lax.all_gather(kv[m], "ctx", axis=0) for m in range(micro)]
    forward = [flash_forward(0, metas[0], q, chunks[0])]
    wgu, wd = assemble_ffn(after(whole_f, forward[0][0]), pool_f)
    forward.append(flash_forward(1, metas[1], q, after(chunks[1], wgu)))
    scalars = jnp.concatenate([my_blocks, lengths[0]]).astype(jnp.int32)
    cot_t = cotangent[0].transpose(0, 2, 1)
    outs = [f[0] for f in forward]
    (mixed_t, normed_ffn_t, hidden_t, grad_gu, grad_out, grad_branch, grad_residual, grad_attn, gain_ffn) = middle(
        scalars, wgu, wd, outs, wo, x_low, cot_t, gains[1:2]
    )
    def flash_back(m):
        out, lse = forward[m]
        return flash_backward(m, metas[m], q, out, grad_attn, lse, cosine, sine, chunks[m])

    gq_0, gkv_0 = flash_back(0)
    gkv_0 = lax.psum_scatter(gkv_0, "ctx", scatter_dimension=0, tiled=False)
    grad_out = after(grad_out, gq_0)
    pool_f = ffn_grads(whole_f, normed_ffn_t, grad_gu, hidden_t, grad_out, devices * cap_f)
    grad_attn = after(grad_attn, pool_f)
    gq_1, gkv_1 = flash_back(1)
    if line:
        near_f, gkv_1 = back_home(pool_f.reshape(4, 4, 2, cap_f, 32, 128), gkv_1)
    else:
        sum_f = lax.psum_scatter(pool_f.astype(f32), AXES, scatter_dimension=0, tiled=True)
        gkv_1 = lax.psum_scatter(gkv_1, "ctx", scatter_dimension=0, tiled=False).astype(f32)
    input_grad_t, gain_attn, pool_a = inward(
        whole_a, (gq_0, gq_1), (gkv_0, gkv_1), cosine, sine, wqkv, normed_attn, outs, grad_branch, x_low,
        grad_residual, gains[0:1], devices * cap_a,
    )
    gain_terms = jnp.concatenate([gain_attn, gain_ffn])
    if line:
        gain_rows = jnp.pad(gain_terms.reshape(15, 128), ((0, 1), (0, 0)))
        sum_a, sum_f, gain_rows = tail(pool_a.reshape(4, 4, 2, cap_a, 32, 128), near_f, gain_rows)
        gain_grads = gain_rows[:15].reshape(2, D)
    else:
        sum_a = lax.psum_scatter(pool_a.astype(f32), AXES, scatter_dimension=0, tiled=True)
        gain_grads = lax.psum(gain_terms, AXES)

    tile_grads, new_left, new_right, new_master = shampoo(
        sum_a, sum_f, master, stat_left, stat_right, root_left, root_right
    )
    new_gain_stats = decay_rate * gain_stats + (1.0 - decay_rate) * gain_grads * gain_grads
    new_gains = gains - gain_rate * gain_grads * lax.rsqrt(new_gain_stats)
    return (
        mixed_t.transpose(0, 2, 1)[None],
        input_grad_t.transpose(0, 2, 1)[None],
        tile_grads,
        new_left,
        new_right,
        new_master,
        gain_grads,
        new_gain_stats,
        new_gains,
    )


def solution(mesh):
    in_specs = (
        P("wt", None, "ctx", None),
        P("wt", None, "ctx", None),
        P("wt", None),
        P(),
        P(),
        P(AXES, None, None),
        P(AXES, None, None),
        P(AXES, None, None),
        P(AXES, None, None),
        P(AXES, None, None),
        P(),
        P(),
    )
    out_specs = (
        P("wt", None, "ctx", None),
        P("wt", None, "ctx", None),
        P(AXES, None, None),
        P(AXES, None, None),
        P(AXES, None, None),
        P(AXES, None, None),
        P(),
        P(),
        P(),
    )
    return jax.shard_map(shards, mesh=mesh, in_specs=in_specs, out_specs=out_specs, check_vma=False)
```

```python
import functools

import jax
import jax.numpy as jnp
import numpy as np
from jax import lax
from jax.experimental import pallas as pl
from jax.experimental.pallas import tpu as pltpu
from jax.sharding import PartitionSpec as P

D = 960
FF = 2560
QH = 15
KVH = 5
HD = 64
TL = 64
QW = 960
KVW = 320
GRP = 3
NTA = 600
NT = 2400
QP = 1024
CW = 1664
BLK = 256
AXES = ("ctx", "wt")

epsilon = 1e-05
decay_rate = 0.95
step_rate = 0.05
gain_rate = 0.05
rope_base = 10000.0
blocked_score = -1e30
bf16 = jnp.bfloat16
f32 = jnp.float32
VM = pl.BlockSpec(memory_space=pltpu.VMEM)
SM = pl.BlockSpec(memory_space=pltpu.SMEM)
ANY = pl.BlockSpec(memory_space=pl.ANY)


def params(megabytes, **kwargs):
    return pltpu.CompilerParams(vmem_limit_bytes=megabytes << 20, **kwargs)


def cost(flops, nbytes, trans=0):
    return pl.CostEstimate(flops=int(flops), bytes_accessed=int(nbytes), transcendentals=int(trans))


def after(x, *others):
    return lax.optimization_barrier((x, others))[0]


def is_line(n_ctx, n_wt):
    return n_ctx == 4 and n_wt == 8


def tile_halves(n):
    return (n + 1) // 2


def load_parts(parts, pool, sems):
    at = 0
    copies = []
    for i, part in enumerate(parts):
        rows = part.shape[0]
        copies.append(pltpu.make_async_copy(part, pool.at[pl.ds(at, rows)], sems.at[i]))
        at += rows
    for copy in copies:
        copy.start()
    for copy in copies:
        copy.wait()


def place_pair(pool, table, ref, row, lane, a, b):
    first = pool[table[a]]
    second = pool[table[b]]
    ref[pl.ds(row, 32), lane : lane + 128] = jnp.concatenate([first[:, :64], second[:, :64]], axis=1)
    ref[pl.ds(row + 32, 32), lane : lane + 128] = jnp.concatenate([first[:, 64:], second[:, 64:]], axis=1)


def place_single(pool, table, ref, row, lane, a):
    first = pool[table[a]]
    ref[pl.ds(row, 32), lane : lane + 64] = first[:, :64]
    ref[pl.ds(row + 32, 32), lane : lane + 64] = first[:, 64:]


def assemble_attn_kernel(count, table, *refs):
    parts, (wqkv, wo, pool, sems) = refs[:count], refs[count:]
    load_parts(parts, pool, sems)
    attn_rows(pool, table, wqkv, wo)


def attn_rows(pool, table, wqkv, wo):
    def qkv_row(r, _):
        row = pl.multiple_of(r * 64, 64)
        for p in range(7):
            place_pair(pool, table, wqkv, row, 128 * p, r * 15 + 2 * p, r * 15 + 2 * p + 1)
        place_single(pool, table, wqkv, row, 896, r * 15 + 14)
        wqkv[pl.ds(row, 64), 960:1024] = jnp.zeros((64, 64), bf16)
        for g in range(KVH):
            place_pair(pool, table, wqkv, row, QP + 128 * g, 225 + r * 5 + g, 300 + r * 5 + g)
        for p in range(7):
            place_pair(pool, table, wo, row, 128 * p, 375 + r * 15 + 2 * p, 375 + r * 15 + 2 * p + 1)
        place_single(pool, table, wo, row, 896, 375 + r * 15 + 14)
        return 0

    lax.fori_loop(0, 15, qkv_row, 0)
    wo[pl.ds(960, 64), :] = jnp.zeros((64, D), bf16)


def ffn_rows(pool, table, wgu, wd):
    def gu_row(r, _):
        row = pl.multiple_of(r * 64, 64)
        for m in range(2):
            for p in range(20):
                base = 600 * m + r * 40 + 2 * p
                place_pair(pool, table, wgu, row, FF * m + 128 * p, base, base + 1)
        return 0

    lax.fori_loop(0, 15, gu_row, 0)

    def d_row(r, _):
        row = pl.multiple_of(r * 64, 64)
        for p in range(7):
            place_pair(pool, table, wd, row, 128 * p, 1200 + r * 15 + 2 * p, 1200 + r * 15 + 2 * p + 1)
        place_single(pool, table, wd, row, 896, 1200 + r * 15 + 14)
        return 0

    lax.fori_loop(0, 40, d_row, 0)


def assemble(kernel, parts, table, shapes):
    total = sum(p.shape[0] for p in parts)
    out_bytes = sum(2 * a * b for a, b in shapes)
    return pl.pallas_call(
        functools.partial(kernel, len(parts)),
        out_shape=[jax.ShapeDtypeStruct(s, bf16) for s in shapes],
        in_specs=[SM] + [ANY] * len(parts),
        out_specs=[VM] * len(shapes),
        scratch_shapes=[pltpu.VMEM((total, 32, 128), bf16), pltpu.SemaphoreType.DMA((len(parts),))],
        compiler_params=params(52),
        cost_estimate=cost(0, 4 * out_bytes),
    )(table, *parts)


def pick_pair(pool, table, ref, row, lane, a, b):
    block = ref[pl.ds(row, 64), lane : lane + 128]
    pool[table[a]] = jnp.concatenate([block[:32, :64], block[32:, :64]], axis=1)
    pool[table[b]] = jnp.concatenate([block[:32, 64:], block[32:, 64:]], axis=1)


def pick_single(pool, table, ref, row, lane, a):
    block = ref[pl.ds(row, 64), lane : lane + 64]
    pool[table[a]] = jnp.concatenate([block[:32], block[32:]], axis=1)


def flush_pool(pool, outs, sems):
    at = 0
    copies = []
    for i, out in enumerate(outs):
        rows = out.shape[0]
        copies.append(pltpu.make_async_copy(pool.at[pl.ds(at, rows)], out, sems.at[i]))
        at += rows
    for copy in copies:
        copy.start()
    for copy in copies:
        copy.wait()


def swap_halves(x):
    lane = lax.broadcasted_iota(jnp.int32, x.shape, 1)
    return jnp.where(lane % 64 < 32, pltpu.roll(x, 96, 1), pltpu.roll(x, 32, 1))


def qkv_kernel(x_ref, gain_ref, w_ref, cos_ref, sin_ref, q_ref, kv_ref, normed_ref):
    x = x_ref[...].astype(f32)
    inverse = lax.rsqrt(jnp.mean(x * x, axis=1, keepdims=True) + epsilon)
    normed = (x * inverse * gain_ref[...]).astype(bf16)
    normed_ref[...] = normed
    cosine, sine = cos_ref[...], sin_ref[...]
    lane = lax.broadcasted_iota(jnp.int32, cosine.shape, 1)
    left = lane < 64
    for p in range(8):
        rows = jnp.dot(normed, w_ref[:, 128 * p : 128 * p + 128], preferred_element_type=f32)
        rows = (rows * cosine + swap_halves(rows) * sine).astype(bf16).astype(f32) * 0.125
        q_ref[2 * p] = jnp.where(left, rows, 0.0).astype(bf16)
        if 2 * p + 1 < QH:
            q_ref[2 * p + 1] = jnp.where(left, pltpu.roll(rows, 64, 1), 0.0).astype(bf16)
    cosine = jnp.where(left, cosine, 1.0)
    sine = jnp.where(left, sine, 0.0)
    for g in range(KVH):
        at = QP + 128 * g
        rows = jnp.dot(normed, w_ref[:, at : at + 128], preferred_element_type=f32)
        kv_ref[0, g] = (rows * cosine + swap_halves(rows) * sine).astype(bf16)


def qkv_rows(x, gain, wqkv, cosine, sine, micro):
    tokens = x.shape[0]
    rows = tokens // micro
    blk = min(BLK, rows)
    steps = tokens // blk
    per = steps // micro
    return pl.pallas_call(
        qkv_kernel,
        grid=(steps,),
        out_shape=[
            jax.ShapeDtypeStruct((QH, tokens, 128), bf16),
            jax.ShapeDtypeStruct((micro, KVH, rows, 128), bf16),
            jax.ShapeDtypeStruct((tokens, D), bf16),
        ],
        in_specs=[
            pl.BlockSpec((blk, D), lambda i: (i, 0)),
            pl.BlockSpec((1, D), lambda i: (0, 0)),
            pl.BlockSpec((D, CW), lambda i: (0, 0)),
            pl.BlockSpec((blk, 128), lambda i: (i % per, 0)),
            pl.BlockSpec((blk, 128), lambda i: (i % per, 0)),
        ],
        out_specs=[
            pl.BlockSpec((QH, blk, 128), lambda i: (0, i, 0)),
            pl.BlockSpec((1, KVH, blk, 128), lambda i: (i // per, 0, i % per, 0)),
            pl.BlockSpec((blk, D), lambda i: (i, 0)),
        ],
        compiler_params=params(40),
        cost_estimate=cost(2 * tokens * D * CW, 14 << 20),
    )(x, gain, wqkv, cosine, sine)


def remote(src, dst, send, recv, device):
    return pltpu.make_async_remote_copy(
        src_ref=src,
        dst_ref=dst,
        send_sem=send,
        recv_sem=recv,
        device_id=device,
        device_id_type=pl.DeviceIdType.MESH,
    )


def greet(c, w, far):
    barrier = pltpu.get_barrier_semaphore()

    def hail(device):
        pl.semaphore_signal(barrier, inc=1, device_id=device, device_id_type=pl.DeviceIdType.MESH)

    for bit in (1, 2, 4):
        hail({"wt": w ^ bit})
    if far:
        hail({"ctx": c ^ 2})

    @pl.when(c < 3)
    def _():
        hail({"ctx": c + 1})

    @pl.when(c > 0)
    def _():
        hail({"ctx": c - 1})

    inner = jnp.logical_and(c > 0, c < 3)

    @pl.when(inner)
    def _():
        pl.semaphore_wait(barrier, 5 + far)

    @pl.when(jnp.logical_not(inner))
    def _():
        pl.semaphore_wait(barrier, 4 + far)


class Gather:
    def __init__(self, pool, sems, c, w):
        self.pool, self.sems, self.c, self.w = pool, sems, c, w
        self.n = pool.shape[2]
        self.n1 = tile_halves(self.n)
        self.x, self.y, self.core = {"wt": w ^ 2}, {"wt": w ^ 4}, {"wt": w ^ 1}

    def copy(self, k, owner, lane, device, part=None):
        ref = self.pool.at[k, owner]
        if part is not None:
            ref = ref.at[pl.ds(part[0], part[1])]
        return remote(ref, ref, self.sems.at[k, lane], self.sems.at[k, lane + 1], device)

    def up(self, k):
        return self.copy(k, self.w, 0, {"ctx": self.c + 1})

    def down(self, k):
        return self.copy(k, self.w, 2, {"ctx": self.c - 1})

    def over_x(self, k, back=0):
        return self.copy(k, self.w ^ back, 4, self.x)

    def over_y(self, k, back=0):
        return self.copy(k, self.w ^ back, 6, self.y)

    def diag_x(self, k, owner):
        return self.copy(k, owner, 8, self.x, (0, self.n1))

    def diag_y(self, k, owner):
        return self.copy(k, owner, 10, self.y, (self.n1, self.n - self.n1))

    def over_core(self, k, quad, back=0):
        return self.copy(k, self.w ^ (2 * quad) ^ back, 12 + 2 * quad, self.core)

    def send_line(self, k, low, high):
        if low:

            @pl.when(self.c < 3)
            def _():
                self.up(k).start()

        if high:

            @pl.when(self.c > 0)
            def _():
                self.down(k).start()

    def send_near(self, k):
        self.over_x(k).start()
        self.over_y(k).start()
        self.over_core(k, 0).start()

    def first(self):
        self.send_line(self.c, True, True)

    def sides(self, s):
        return [(self.c >= s, self.c - s, True), (self.c + s <= 3, self.c + s, False)]

    def line_step(self, s, near=True):
        for valid, k, below in self.sides(s):

            @pl.when(valid)
            def _(k=k, below=below):
                if below:
                    self.up(k).wait_recv()
                else:
                    self.down(k).wait_recv()
                if s < 3:
                    self.send_line(k, below, not below)
                if near:
                    self.send_near(k)

    def each(self, s, act):
        if s == 0:
            act(self.c)
            return
        for valid, k, _ in self.sides(s):

            @pl.when(valid)
            def _(k=k):
                act(k)

    def near_step(self, s):
        def act(k):
            self.over_x(k, 2).wait_recv()
            self.diag_y(k, self.w ^ 2).start()
            self.over_core(k, 1).start()
            self.over_y(k, 4).wait_recv()
            self.diag_x(k, self.w ^ 4).start()
            self.over_core(k, 2).start()

        self.each(s, act)

    def diag_step(self, s):
        def act(k):
            self.diag_x(k, self.w ^ 6).wait_recv()
            self.diag_y(k, self.w ^ 6).wait_recv()
            self.over_core(k, 3).start()

        self.each(s, act)

    def finish(self):
        for k in range(4):
            for quad in range(4):
                self.over_core(k, quad, 1).wait_recv()

    def drain(self):
        for k in range(4):

            @pl.when(jnp.logical_and(k <= self.c, self.c < 3))
            def _(k=k):
                self.up(k).wait_send()

            @pl.when(jnp.logical_and(k >= self.c, self.c > 0))
            def _(k=k):
                self.down(k).wait_send()

            self.over_x(k).wait_send()
            self.over_y(k).wait_send()
            self.diag_x(k, self.w ^ 4).wait_send()
            self.diag_y(k, self.w ^ 2).wait_send()
            for quad in range(4):
                self.over_core(k, quad).wait_send()


def front_kernel(
    table, own_a, own_f, x_ref, gain_ref, cos_ref, sin_ref,
    q_ref, normed_t, rows_ref, kv_ref, late_ref, wqkv, wo, pool_f,
    normed_ref, pool_a, kv_own, sems_a, sems_f, sems_kv, sems,
):
    c, w = lax.axis_index("ctx"), lax.axis_index("wt")
    take_a = pltpu.make_async_copy(own_a, pool_a.at[c, w], sems.at[0])
    take_f = pltpu.make_async_copy(own_f, pool_f.at[c, w], sems.at[1])
    take_a.start()
    take_f.start()
    greet(c, w, 0)
    take_a.wait()
    a = Gather(pool_a, sems_a, c, w)
    f = Gather(pool_f, sems_f, c, w)
    a.first()
    a.send_near(c)

    rows = x_ref.shape[2]
    blk = BLK
    for m in range(2):
        for half in range(rows // blk):
            part = x_ref[m, :, blk * half : blk * half + blk].T
            span = slice(m * rows + blk * half, m * rows + blk * half + blk)
            rows_ref[span, :] = part
            wide = part.astype(f32)
            inverse = lax.rsqrt(jnp.mean(wide * wide, axis=1, keepdims=True) + epsilon)
            normed = (wide * inverse * gain_ref[...]).astype(bf16)
            normed_ref[span, :] = normed
            normed_t[:, span] = normed.T

    a.line_step(1)
    a.near_step(0)
    a.line_step(2)
    take_f.wait()
    f.first()
    a.near_step(1)
    a.diag_step(0)
    a.line_step(3)
    a.near_step(2)
    a.diag_step(1)
    a.near_step(3)
    f.send_near(c)
    a.diag_step(2)
    a.diag_step(3)
    f.line_step(1)
    a.finish()

    flat = pool_a.reshape(pool_a.shape[0] * pool_a.shape[1] * pool_a.shape[2], 32, 128)
    attn_rows(flat, table, wqkv, wo)
    f.line_step(2)
    f.near_step(0)

    lane = lax.broadcasted_iota(jnp.int32, (blk, 128), 1)
    left = lane < 64

    def qkv_block(i, _):
        at = pl.multiple_of(i * blk, blk)
        normed = normed_ref[pl.ds(at, blk), :]
        within = pl.multiple_of((i % (rows // blk)) * blk, blk)
        cosine, sine = cos_ref[pl.ds(within, blk), :], sin_ref[pl.ds(within, blk), :]
        key_cosine = jnp.where(left, cosine, 1.0)
        key_sine = jnp.where(left, sine, 0.0)
        for g in range(KVH):
            spot = QP + 128 * g
            part = jnp.dot(normed, wqkv[:, spot : spot + 128], preferred_element_type=f32)
            part = (part * key_cosine + swap_halves(part) * key_sine).astype(bf16)
            kv_own[i // (rows // blk), g, pl.ds(within, blk), :] = part
        for p in range(8):
            part = jnp.dot(normed, wqkv[:, 128 * p : 128 * p + 128], preferred_element_type=f32)
            part = (part * cosine + swap_halves(part) * sine).astype(bf16).astype(f32) * 0.125
            q_ref[2 * p, pl.ds(at, blk), :] = jnp.where(left, part, 0.0).astype(bf16)
            if 2 * p + 1 < QH:
                other = jnp.where(left, pltpu.roll(part, 64, 1), 0.0).astype(bf16)
                q_ref[2 * p + 1, pl.ds(at, blk), :] = other
        return 0

    def kv_move(src, k, lane, step):
        return remote(src, kv_ref.at[k], sems_kv.at[k, lane], sems_kv.at[k, lane + 1], {"ctx": c + step})

    lax.fori_loop(0, rows // blk, qkv_block, 0)
    keep = pltpu.make_async_copy(kv_own.at[0], kv_ref.at[c], sems.at[2])
    keep.start()

    @pl.when(c < 3)
    def _():
        kv_move(kv_own.at[0], c, 0, 1).start()

    @pl.when(c > 0)
    def _():
        kv_move(kv_own.at[0], c, 2, -1).start()

    lax.fori_loop(rows // blk, 2 * rows // blk, qkv_block, 0)
    late = pltpu.make_async_copy(kv_own.at[1], late_ref, sems.at[3])
    late.start()

    def kv_step(s):
        @pl.when(c >= s)
        def _():
            kv_move(kv_ref.at[c - s], c - s, 0, 1).wait_recv()
            if s < 3:

                @pl.when(c < 3)
                def _():
                    kv_move(kv_ref.at[c - s], c - s, 0, 1).start()

        @pl.when(c + s <= 3)
        def _():
            kv_move(kv_ref.at[c + s], c + s, 2, -1).wait_recv()
            if s < 3:

                @pl.when(c > 0)
                def _():
                    kv_move(kv_ref.at[c + s], c + s, 2, -1).start()

    f.line_step(3)
    f.near_step(1)
    f.diag_step(0)
    kv_step(1)
    f.near_step(2)
    f.diag_step(1)
    f.near_step(3)
    kv_step(2)
    f.diag_step(2)
    f.diag_step(3)
    f.finish()
    kv_step(3)
    keep.wait()
    late.wait()
    for k in range(4):

        @pl.when(jnp.logical_and(k <= c, c < 3))
        def _(k=k):
            kv_move(kv_ref.at[k], k, 0, 1).wait_send()

        @pl.when(jnp.logical_and(k >= c, c > 0))
        def _(k=k):
            kv_move(kv_ref.at[k], k, 2, -1).wait_send()

    a.drain()
    f.drain()


def front(table, own_a, own_f, x_t, gain, cosine, sine):
    micro, _, rows = x_t.shape
    tokens = micro * rows
    n_a, n_f = own_a.shape[0], own_f.shape[0]
    return pl.pallas_call(
        front_kernel,
        out_shape=[
            jax.ShapeDtypeStruct((QH, tokens, 128), bf16),
            jax.ShapeDtypeStruct((D, tokens), bf16),
            jax.ShapeDtypeStruct((tokens, D), bf16),
            jax.ShapeDtypeStruct((4, KVH, rows, 128), bf16),
            jax.ShapeDtypeStruct((KVH, rows, 128), bf16),
            jax.ShapeDtypeStruct((D, CW), bf16),
            jax.ShapeDtypeStruct((QP, D), bf16),
            jax.ShapeDtypeStruct((4, 8, n_f, 32, 128), bf16),
        ],
        in_specs=[SM, ANY, ANY, VM, VM, VM, VM],
        out_specs=[VM, VM, VM, ANY, ANY, VM, VM, ANY],
        scratch_shapes=[
            pltpu.VMEM((tokens, D), bf16),
            pltpu.VMEM((4, 8, n_a, 32, 128), bf16),
            pltpu.VMEM((micro, KVH, rows, 128), bf16),
            pltpu.SemaphoreType.DMA((4, 20)),
            pltpu.SemaphoreType.DMA((4, 20)),
            pltpu.SemaphoreType.DMA((4, 4)),
            pltpu.SemaphoreType.DMA((4,)),
        ],
        compiler_params=params(48, collective_id=0, has_side_effects=True),
        cost_estimate=cost(40e9, 40 << 20),
    )(table, own_a, own_f, x_t, gain, cosine, sine)


class Line:
    def __init__(self, terms, send, recv, sems, c):
        self.terms, self.send, self.recv, self.sems, self.c = terms, send, recv, sems, c
        self.count = recv.shape[2]

    def copy(self, way, k):
        sems = self.sems
        return remote(
            self.send.at[k], self.recv.at[way, k], sems.at[way, k, 0], sems.at[way, k, 1],
            {"ctx": self.c + 1 - 2 * way},
        )

    def loop(self, act):
        def body(j, _):
            act(j)
            return 0

        lax.fori_loop(0, self.count, body, 0)

    def start(self):
        for way in (0, 1):

            @pl.when(self.c == 3 * way)
            def _(way=way):
                for far in (3, 2, 1):
                    k = far if way == 0 else 3 - far

                    def take(j, k=k):
                        self.send[k, j] = self.terms(k, j).astype(bf16)

                    self.loop(take)
                    self.copy(way, k).start()

    def join(self, way, k):
        self.copy(way, k).wait_recv()

        def act(j):
            self.send[k, j] = (self.terms(k, j) + self.recv[way, k, j].astype(f32)).astype(bf16)

        self.loop(act)
        self.copy(way, k).start()

    def step(self, number):
        lists = {1: ((0, 3), (0, 2), (1, 0)), 2: ((1, 0), (1, 1), (0, 3))}
        for inner, order in lists.items():

            @pl.when(self.c == inner)
            def _(order=order):
                self.join(*order[number])

    def finish(self, out):
        c, recv = self.c, self.recv

        @pl.when(c > 0)
        def _():
            self.copy(0, c).wait_recv()

        @pl.when(c < 3)
        def _():
            self.copy(1, c).wait_recv()

        def total(j):
            low = jnp.where(c > 0, recv[0, c, j].astype(f32), 0.0)
            high = jnp.where(c < 3, recv[1, c, j].astype(f32), 0.0)
            out[j] = self.terms(c, j) + low + high

        self.loop(total)

    def drain(self):
        for far in (3, 2, 1):
            for way, k in ((0, far), (1, 3 - far)):

                @pl.when(self.c < k if way == 0 else self.c > k)
                def _(way=way, k=k):
                    self.copy(way, k).wait_send()


class Plane:
    def __init__(self, pool, bufs, sems, c, w):
        self.pool, self.sems, self.c, self.w = pool, sems, c, w
        self.mine, self.theirs, self.diag_send, self.diag_recv, self.near_send, self.near_recv = bufs
        self.n = pool.shape[3]
        n1 = self.n1 = tile_halves(self.n)
        yx, core = w // 2, w % 2
        over_x, over_y, over_core = {"wt": w ^ 2}, {"wt": w ^ 4}, {"wt": w ^ 1}
        self.loads = [
            pltpu.make_async_copy(pool.at[:, yx ^ q, core], self.mine.at[q], sems.at[10 + q, 0]) for q in range(4)
        ]
        self.cores = [
            remote(pool.at[:, yx ^ q, 1 - core], self.theirs.at[q], sems.at[q, 0], sems.at[q, 1], over_core)
            for q in range(4)
        ]
        low, high = slice(0, n1), slice(n1, self.n)
        self.diag_x = self.move(self.diag_send.at[:, low], self.diag_recv.at[:, low], 4, over_x)
        self.diag_y = self.move(self.diag_send.at[:, high], self.diag_recv.at[:, high], 5, over_y)
        self.nears = {}
        for q in (1, 2):
            for part, cut in enumerate((low, high)):
                self.nears[q, part] = self.move(
                    self.near_send.at[q - 1, :, cut],
                    self.near_recv.at[q - 1, :, cut],
                    4 + 2 * q + part,
                    over_x if q == 1 else over_y,
                )

    def move(self, src, dst, lane, device):
        return remote(src, dst, self.sems.at[lane, 0], self.sems.at[lane, 1], device)

    def begin_loads(self):
        for q in (3, 1, 2, 0):
            self.loads[q].start()

    def begin(self):
        for q in (3, 1, 2, 0):
            self.cores[q].start()

    def each(self, act):
        def body(k, _):
            act(k)
            return 0

        lax.fori_loop(0, 4, body, 0)

    def both(self, q, k):
        return self.mine[q, k].astype(f32) + self.theirs[q, k].astype(f32)

    def ready(self, q):
        self.loads[q].wait()
        self.cores[q].wait()

    def diag(self):
        self.ready(3)

        def act(k):
            self.diag_send[k] = self.both(3, k).astype(bf16)

        self.each(act)
        self.diag_x.start()
        self.diag_y.start()

    def near(self, q):
        self.ready(q)

        def act(k):
            self.near_send[q - 1, k] = self.both(q, k).astype(bf16)

        self.each(act)
        self.nears[q, q - 1].start()

    def join(self, q):
        cut = slice(self.n1, self.n) if q == 1 else slice(0, self.n1)
        (self.diag_y if q == 1 else self.diag_x).wait_recv()

        def act(k):
            ours = self.near_send[q - 1, k, cut].astype(f32)
            self.near_send[q - 1, k, cut] = (ours + self.diag_recv[k, cut].astype(f32)).astype(bf16)

        self.each(act)
        self.nears[q, 2 - q].start()

    def arrive(self):
        self.ready(0)
        for part in (0, 1):
            for q in (1, 2):
                self.nears[q, part].wait_recv()

    def own(self, k):
        return self.both(0, k) + self.near_recv[0, k].astype(f32) + self.near_recv[1, k].astype(f32)

    def drain(self):
        self.diag_x.wait_send()
        self.diag_y.wait_send()
        for copy in self.nears.values():
            copy.wait_send()


def plane_scratch(n):
    tile = (32, 128)
    return [
        pltpu.VMEM((4, 4, n) + tile, bf16),
        pltpu.VMEM((4, 4, n) + tile, bf16),
        pltpu.VMEM((4, n) + tile, bf16),
        pltpu.VMEM((4, n) + tile, bf16),
        pltpu.VMEM((2, 4, n) + tile, bf16),
        pltpu.VMEM((2, 4, n) + tile, bf16),
        pltpu.SemaphoreType.DMA((14, 2)),
    ]


def line_scratch(shape):
    return [
        pltpu.VMEM((4,) + shape, bf16),
        pltpu.VMEM((2, 4) + shape, bf16),
        pltpu.SemaphoreType.DMA((2, 4, 2)),
    ]


def return_kernel(pool, kv_ref, sum_ref, kv_out, *scratch):
    c, w = lax.axis_index("ctx"), lax.axis_index("wt")
    plane = Plane(pool, scratch[:6], scratch[6], c, w)
    line = Line(lambda k, j: kv_ref[k, j].astype(f32), *scratch[7:], c)
    plane.begin_loads()
    greet(c, w, 0)
    plane.begin()

    line.start()
    plane.diag()
    plane.near(1)
    plane.near(2)
    line.step(0)
    plane.join(1)
    line.step(1)
    plane.join(2)
    line.step(2)
    plane.arrive()

    def own(k):
        sum_ref[k] = plane.own(k).astype(bf16)

    plane.each(own)
    line.finish(kv_out)
    plane.drain()
    line.drain()


def back_home(pool, kv_terms):
    n = pool.shape[3]
    return pl.pallas_call(
        return_kernel,
        out_shape=[
            jax.ShapeDtypeStruct((4, n, 32, 128), bf16),
            jax.ShapeDtypeStruct(kv_terms.shape[1:], f32),
        ],
        in_specs=[ANY, VM],
        out_specs=[VM, VM],
        scratch_shapes=plane_scratch(n) + line_scratch(kv_terms.shape[1:]),
        compiler_params=params(60, collective_id=2, has_side_effects=True),
        cost_estimate=cost(30e9, 16 << 20),
    )(pool, kv_terms)


def tail_kernel(pool, ffn_ref, gain_ref, sum_ref, ffn_out, gain_out, own, gain_send, gain_recv, sems_gain, *scratch):
    c, w = lax.axis_index("ctx"), lax.axis_index("wt")
    plane = Plane(pool, scratch[:6], scratch[6], c, w)
    line = Line(lambda k, j: own[k, j], *scratch[7:10], c)
    ffn_line = Line(lambda k, j: ffn_ref[k, j].astype(f32), *scratch[10:13], c)
    plane.begin_loads()
    greet(c, w, 1)
    plane.begin()

    stages = [{"wt": w ^ 1}, {"wt": w ^ 2}, {"wt": w ^ 4}, {"ctx": c ^ 1}, {"ctx": c ^ 2}]
    copies = [
        remote(gain_send.at[i], gain_recv.at[i], sems_gain.at[i, 0], sems_gain.at[i, 1], stages[i]) for i in range(5)
    ]
    gain_send[0] = gain_ref[...]
    copies[0].start()

    def gain_step(i):
        copies[i].wait()
        total = gain_send[i] + gain_recv[i]
        if i < 4:
            gain_send[i + 1] = total
            copies[i + 1].start()
        else:
            gain_out[...] = total

    ffn_line.start()
    plane.diag()
    gain_step(0)
    plane.near(1)
    plane.near(2)
    ffn_line.step(0)
    gain_step(1)
    plane.join(1)
    plane.join(2)
    ffn_line.step(1)
    gain_step(2)
    plane.arrive()

    def own_sum(k):
        own[k] = plane.own(k)

    plane.each(own_sum)
    line.start()
    ffn_line.step(2)
    gain_step(3)
    for number in range(3):
        line.step(number)
    ffn_line.finish(ffn_out)
    gain_step(4)
    line.finish(sum_ref)
    plane.drain()
    line.drain()
    ffn_line.drain()


def tail(pool, ffn_terms, gains):
    n, n_f = pool.shape[3], ffn_terms.shape[1]
    tile = (32, 128)
    return pl.pallas_call(
        tail_kernel,
        out_shape=[
            jax.ShapeDtypeStruct((n,) + tile, f32),
            jax.ShapeDtypeStruct((n_f,) + tile, f32),
            jax.ShapeDtypeStruct(gains.shape, f32),
        ],
        in_specs=[ANY, VM, VM],
        out_specs=[VM, VM, VM],
        scratch_shapes=[
            pltpu.VMEM((4, n) + tile, f32),
            pltpu.VMEM((5,) + gains.shape, f32),
            pltpu.VMEM((5,) + gains.shape, f32),
            pltpu.SemaphoreType.DMA((5, 2)),
        ]
        + plane_scratch(n)
        + line_scratch((n,) + tile)
        + line_scratch((n_f,) + tile),
        compiler_params=params(48, collective_id=1, has_side_effects=True),
        cost_estimate=cost(30e9, 16 << 20),
    )(pool, ffn_terms, gains)


META = 4


def load_blocks(meta, part, pool, sems):
    blk = part.shape[2] // 2
    copies = []
    for k in range(2 * part.shape[0]):
        at = pl.multiple_of(meta[META + k] * blk, blk)
        source = part.at[k // 2, :, pl.ds(k % 2 * blk, blk), :]
        copies.append(pltpu.make_async_copy(source, pool.at[:, pl.ds(at, blk), :], sems.at[k]))
    for copy in copies:
        copy.start()
    for copy in copies:
        copy.wait()


def masked(scores, block, q_block, length):
    blk = scores.shape[1]
    key = block + lax.broadcasted_iota(jnp.int32, scores.shape, 0)
    query = q_block * blk + lax.broadcasted_iota(jnp.int32, scores.shape, 1)
    return jnp.where(jnp.logical_and(key <= query, key < length), scores, blocked_score)


def nt_dot(a, b):
    return lax.dot_general(a, b, (((1,), (1,)), ((), ())), preferred_element_type=f32)


def tn_dot(a, b):
    return lax.dot_general(a, b, (((0,), (0,)), ((), ())), preferred_element_type=f32)


def flash_forward_kernel(meta, q_ref, part, out_ref, turned_ref, lse_ref, pool, vt, peak, acc, turned, sems):
    load_blocks(meta, part, pool, sems)
    length = meta[2]
    blk = q_ref.shape[1] // 2
    live_blocks = (length + blk - 1) // blk
    turned[960:, :] = jnp.zeros((64, blk), f32)
    for g in range(KVH):
        vt[g, :64, :] = jnp.ones((64, vt.shape[2]), bf16)
        for k in range(pool.shape[1] // 256):
            vt[g, 64:, 256 * k : 256 * k + 256] = pool[g, 256 * k : 256 * k + 256, :].T[64:]
    for qi in range(2):
        q_block = meta[qi]
        blocks = jnp.minimum(q_block + 1, live_blocks)

        def group(g, _):
            queries = [q_ref[GRP * g + h, blk * qi : blk * qi + blk, :] for h in range(GRP)]
            for h in range(GRP):
                peak[h] = jnp.full((1, blk), blocked_score, f32)
                acc[h] = jnp.zeros((128, blk), f32)

            def step(block, wide, with_mask):
                start = pl.multiple_of(block * blk, blk)
                span = pl.ds(start, wide * blk)
                kv = pool[g, span, :]
                vals = vt[g, :, span]
                scores = [nt_dot(kv, queries[h]) for h in range(GRP)]
                if with_mask:
                    scores = [masked(t, start, q_block, length) for t in scores]
                before = [peak[h] for h in range(GRP)]
                now = [jnp.maximum(before[h], jnp.max(scores[h], axis=0, keepdims=True)) for h in range(GRP)]
                weights = [jnp.exp(scores[h] - now[h]).astype(bf16) for h in range(GRP)]
                for h in range(GRP):
                    peak[h] = now[h]
                    acc[h] = acc[h] * jnp.exp(before[h] - now[h]) + jnp.dot(
                        vals, weights[h], preferred_element_type=f32
                    )

            def plain(pair, _):
                step(2 * pair, 2, False)
                return 0

            lax.fori_loop(0, (blocks - 1) // 2, plain, 0)

            @pl.when(blocks % 2 == 1)
            def _():
                step(blocks - 1, 1, True)

            @pl.when(blocks % 2 == 0)
            def _():
                step(blocks - 2, 2, True)

            for h in range(GRP):
                total = acc[h][0:1, :]
                turned[pl.ds(pl.multiple_of((GRP * g + h) * HD, HD), HD), :] = acc[h][64:, :] / total
                lse_ref[GRP * g + h, :, blk * qi : blk * qi + blk] = peak[h] + jnp.log(total)
            return 0

        lax.fori_loop(0, KVH, group, 0)
        out_ref[blk * qi : blk * qi + blk, :] = turned[...].T.astype(bf16)
        turned_ref[:, blk * qi : blk * qi + blk] = turned[...].astype(bf16)


def flash_forward(m, meta, q, part):
    n_ctx, _, rows, _ = part.shape
    blk = rows // 2
    return pl.pallas_call(
        flash_forward_kernel,
        grid=(1,),
        out_shape=[
            jax.ShapeDtypeStruct((rows, QP), bf16),
            jax.ShapeDtypeStruct((QP, rows), bf16),
            jax.ShapeDtypeStruct((16, 1, rows), f32),
        ],
        in_specs=[SM, pl.BlockSpec((QH, rows, 128), lambda i: (0, m, 0)), ANY],
        out_specs=[
            pl.BlockSpec((rows, QP), lambda i: (0, 0)),
            pl.BlockSpec((QP, rows), lambda i: (0, 0)),
            pl.BlockSpec((16, 1, rows), lambda i: (0, 0, 0)),
        ],
        scratch_shapes=[
            pltpu.VMEM((KVH, n_ctx * rows, 128), bf16),
            pltpu.VMEM((KVH, 128, n_ctx * rows), bf16),
            pltpu.VMEM((GRP, 1, blk), f32),
            pltpu.VMEM((GRP, 128, blk), f32),
            pltpu.VMEM((QP, blk), f32),
            pltpu.SemaphoreType.DMA((2 * n_ctx,)),
        ],
        compiler_params=params(48),
        cost_estimate=cost(40e9, 8 << 20),
    )(meta, q, part)


def flash_backward_kernel(
    meta, q_ref, out_ref, grad_ref, lse_ref, cos_ref, sin_ref, part, gq_ref, gkv_ref,
    pool, kt, wide, delta, total, acc, turned, sides, sems,
):
    load_blocks(meta, part, pool, sems)
    length = meta[2]
    rows = q_ref.shape[1]
    blk = rows // 2
    live_blocks = (length + blk - 1) // blk
    total[...] = jnp.zeros_like(total)
    lane = lax.broadcasted_iota(jnp.int32, (rows, 128), 1)
    pick = lax.broadcasted_iota(jnp.int32, (16, 128), 0) == lax.broadcasted_iota(jnp.int32, (16, 128), 1) // 64
    pick = jnp.where(pick, 1.0, 0.0).astype(bf16)
    for g in range(KVH):
        for k in range(pool.shape[1] // 256):
            kt[g, :, 256 * k : 256 * k + 256] = pool[g, 256 * k : 256 * k + 256, :].T[:64]
    for p in range(8):
        slab = grad_ref[:, 128 * p : 128 * p + 128].astype(f32)
        wide[2 * p] = jnp.where(lane >= 64, pltpu.roll(slab, 64, 1), 0.0).astype(bf16)
        if 2 * p + 1 < QH:
            wide[2 * p + 1] = jnp.where(lane >= 64, slab, 0.0).astype(bf16)
        product = slab * out_ref[:, 128 * p : 128 * p + 128].astype(f32)
        high = product.astype(bf16)
        low = (product - high.astype(f32)).astype(bf16)
        both = nt_dot(pick, high) + nt_dot(pick, low)
        delta[2 * p] = both[0:1, :]
        delta[2 * p + 1] = both[1:2, :]
    turned[960:, :] = jnp.zeros((64, blk), f32)
    for qi in range(2):
        q_block = meta[qi]
        blocks = jnp.where(q_block < live_blocks, q_block + 1, 0)
        span = slice(blk * qi, blk * qi + blk)

        def group(g, _):
            for h in range(GRP):
                acc[h] = jnp.zeros((64, blk), f32)
                sides[2 * blk * h : 2 * blk * h + blk] = q_ref[GRP * g + h, span, :]
                sides[2 * blk * h + blk : 2 * blk * h + 2 * blk] = wide[GRP * g + h, span, :]

            def step(block, count, with_mask):
                start = pl.multiple_of(block * blk, blk)
                keys = pl.ds(start, count * blk)
                kv = pool[g, keys, :]
                keys_t = kt[g, :, keys]
                heads = [GRP * g + h for h in range(GRP)]
                scores = [nt_dot(kv, sides[2 * blk * h : 2 * blk * h + blk]) for h in range(GRP)]
                inner = [nt_dot(kv, sides[2 * blk * h + blk : 2 * blk * h + 2 * blk]) for h in range(GRP)]
                if with_mask:
                    scores = [masked(t, start, q_block, length) for t in scores]
                probs = [jnp.exp(scores[h] - lse_ref[heads[h], :, span]) for h in range(GRP)]
                change = [(probs[h] * (inner[h] - delta[heads[h], :, span])).astype(bf16) for h in range(GRP)]
                terms = []
                for h in range(GRP):
                    terms += [change[h], probs[h].astype(bf16)]
                total[g, keys, :] += jnp.dot(
                    jnp.concatenate(terms, axis=1), sides[...], preferred_element_type=f32
                )
                for h in range(GRP):
                    acc[h] = acc[h] + jnp.dot(keys_t, change[h], preferred_element_type=f32)

            def plain(pair, _):
                step(2 * pair, 2, False)
                return 0

            lax.fori_loop(0, (blocks - 1) // 2, plain, 0)

            @pl.when(jnp.logical_and(blocks > 0, blocks % 2 == 1))
            def _():
                step(blocks - 1, 1, True)

            @pl.when(jnp.logical_and(blocks > 0, blocks % 2 == 0))
            def _():
                step(blocks - 2, 2, True)

            for h in range(GRP):
                turned[pl.ds(pl.multiple_of((GRP * g + h) * HD, HD), HD), :] = acc[h] * 0.125
            return 0

        lax.fori_loop(0, KVH, group, 0)
        grads = turned[...].T
        cosine, sine = cos_ref[span, :], sin_ref[span, :]
        for p in range(8):
            slab = grads[:, 128 * p : 128 * p + 128]
            gq_ref[span, 128 * p : 128 * p + 128] = (slab * cosine - swap_halves(slab) * sine).astype(bf16)
    for k in range(2 * gkv_ref.shape[0]):
        at = pl.multiple_of(meta[META + k] * blk, blk)
        gkv_ref[k // 2, :, k % 2 * blk : k % 2 * blk + blk, :] = total[:, pl.ds(at, blk), :].astype(bf16)


def flash_backward(m, meta, q, out, grad, lse, cosine, sine, part):
    n_ctx, _, rows, _ = part.shape
    blk = rows // 2
    return pl.pallas_call(
        flash_backward_kernel,
        grid=(1,),
        out_shape=[
            jax.ShapeDtypeStruct((rows, QP), bf16),
            jax.ShapeDtypeStruct((n_ctx, KVH, rows, 128), bf16),
        ],
        in_specs=[
            SM,
            pl.BlockSpec((QH, rows, 128), lambda i: (0, m, 0)),
            pl.BlockSpec((rows, QP), lambda i: (0, 0)),
            pl.BlockSpec((rows, QP), lambda i: (m, 0)),
            pl.BlockSpec((16, 1, rows), lambda i: (0, 0, 0)),
            pl.BlockSpec((rows, 128), lambda i: (0, 0)),
            pl.BlockSpec((rows, 128), lambda i: (0, 0)),
            ANY,
        ],
        out_specs=[
            pl.BlockSpec((rows, QP), lambda i: (0, 0)),
            pl.BlockSpec((n_ctx, KVH, rows, 128), lambda i: (0, 0, 0, 0)),
        ],
        scratch_shapes=[
            pltpu.VMEM((KVH, n_ctx * rows, 128), bf16),
            pltpu.VMEM((KVH, 64, n_ctx * rows), bf16),
            pltpu.VMEM((QH, rows, 128), bf16),
            pltpu.VMEM((16, 1, rows), f32),
            pltpu.VMEM((KVH, n_ctx * rows, 128), f32),
            pltpu.VMEM((GRP, 64, blk), f32),
            pltpu.VMEM((QP, blk), f32),
            pltpu.VMEM((2 * GRP * blk, 128), bf16),
            pltpu.SemaphoreType.DMA((2 * n_ctx,)),
        ],
        compiler_params=params(56),
        cost_estimate=cost(50e9, 16 << 20),
    )(meta, q, out, grad, lse, cosine, sine, part)


def assemble_ffn_kernel(table, pool_ref, gu_out, d_out, pool, wgu, wd, sems):
    load = pltpu.make_async_copy(pool_ref, pool, sems.at[0])
    load.start()
    load.wait()
    ffn_rows(pool, table, wgu, wd)
    stores = [pltpu.make_async_copy(wgu, gu_out, sems.at[1]), pltpu.make_async_copy(wd, d_out, sems.at[2])]
    for copy in stores:
        copy.start()
    for copy in stores:
        copy.wait()


def assemble_ffn(table, pool):
    shapes = [(D, 2 * FF), (FF, D)]
    return pl.pallas_call(
        assemble_ffn_kernel,
        out_shape=[jax.ShapeDtypeStruct(s, bf16) for s in shapes],
        in_specs=[SM, ANY],
        out_specs=[ANY, ANY],
        scratch_shapes=[pltpu.VMEM(s, bf16) for s in [pool.shape] + shapes] + [pltpu.SemaphoreType.DMA((3,))],
        compiler_params=params(52),
        cost_estimate=cost(0, 64 << 20),
    )(table, pool)


CHUNK = 512


def middle_kernel(
    scalars, gu_ref, d_ref, out_0, out_1, wo, x_ref, cot_ref, gain_ref,
    mixed_ref, normed_t, hidden_t, ggu_ref, go_ref, branch_ref, residual_ref, attn_ref, gain_out,
    wgu, wd, sems,
):
    i = pl.program_id(0)
    blk = x_ref.shape[0]
    loads = [pltpu.make_async_copy(gu_ref, wgu, sems.at[0]), pltpu.make_async_copy(d_ref, wd, sems.at[1])]

    @pl.when(i == 0)
    def _():
        for load in loads:
            load.start()

    attn = jnp.where(i < 2, out_0[...], out_1[...])
    residual = x_ref[...].astype(f32) + jnp.dot(attn, wo[...], preferred_element_type=f32)
    inverse = lax.rsqrt(jnp.mean(residual * residual, axis=1, keepdims=True) + epsilon)
    gain = gain_ref[...]
    normed = (residual * inverse * gain).astype(bf16)
    normed_t[...] = normed.T
    row = scalars[i % 2] * blk + lax.broadcasted_iota(jnp.int32, (blk, D), 0)
    grad_out = cot_ref[0].T
    grad_out = jnp.where(row < scalars[2 + i // 2], grad_out, jnp.zeros((), bf16))
    go_ref[...] = grad_out

    @pl.when(i == 0)
    def _():
        for load in loads:
            load.wait()

    def first(j):
        at = CHUNK * j
        return (
            jnp.dot(normed, wgu[:, at : at + CHUNK], preferred_element_type=f32),
            jnp.dot(normed, wgu[:, FF + at : FF + at + CHUNK], preferred_element_type=f32),
            nt_dot(grad_out, wd[at : at + CHUNK, :]),
        )

    mixed = residual
    grad_normed = jnp.zeros((blk, D), f32)
    ahead = first(0)
    for j in range(FF // CHUNK):
        at = CHUNK * j
        gate, up, grad_hidden = ahead
        if j + 1 < FF // CHUNK:
            ahead = first(j + 1)
        sigma = jax.nn.sigmoid(gate)
        silu = gate * sigma
        hidden = (silu * up).astype(bf16)
        grad_up = (grad_hidden * silu).astype(bf16)
        grad_gate = (grad_hidden * up * (sigma + silu * (1.0 - sigma))).astype(bf16)
        hidden_t[at : at + CHUNK, :] = hidden.T
        ggu_ref[:, at : at + CHUNK] = grad_gate
        ggu_ref[:, FF + at : FF + at + CHUNK] = grad_up
        mixed = mixed + jnp.dot(hidden, wd[at : at + CHUNK, :], preferred_element_type=f32)
        grad_normed = grad_normed + nt_dot(grad_gate, wgu[:, at : at + CHUNK])
        grad_normed = grad_normed + nt_dot(grad_up, wgu[:, FF + at : FF + at + CHUNK])

    mixed_ref[0] = mixed.astype(bf16).T
    unit = residual * inverse
    scaled = grad_normed * gain
    back = inverse * (scaled - unit * jnp.mean(scaled * unit, axis=1, keepdims=True))
    grad_residual = grad_out.astype(f32) + back
    residual_ref[...] = grad_residual
    branch = grad_residual.astype(bf16)
    branch_ref[...] = branch
    attn_ref[...] = nt_dot(branch, wo[...]).astype(bf16)
    term = jnp.sum(grad_normed * unit, axis=0, keepdims=True)

    @pl.when(i == 0)
    def _():
        gain_out[...] = term

    @pl.when(i > 0)
    def _():
        gain_out[...] += term


def middle(scalars, wgu, wd, outs, wo, x_rows, cot_t, gain):
    micro, _, rows = cot_t.shape
    tokens = micro * rows
    blk = rows // 2

    def rows_of(width, kind):
        return jax.ShapeDtypeStruct((tokens, width), kind), pl.BlockSpec((blk, width), lambda i: (i, 0))

    def columns_of(height):
        return jax.ShapeDtypeStruct((height, tokens), bf16), pl.BlockSpec((height, blk), lambda i: (0, i))

    native = pl.BlockSpec((1, D, blk), lambda i: (i // 2, 0, i % 2))
    whole = pl.BlockSpec((1, D), lambda i: (0, 0))
    results = [
        (jax.ShapeDtypeStruct((micro, D, rows), bf16), native),
        columns_of(D),
        columns_of(FF),
        rows_of(2 * FF, bf16),
        rows_of(D, bf16),
        rows_of(D, bf16),
        rows_of(D, f32),
        rows_of(QP, bf16),
        (jax.ShapeDtypeStruct((1, D), f32), whole),
    ]
    return pl.pallas_call(
        middle_kernel,
        grid=(2 * micro,),
        out_shape=[r[0] for r in results],
        in_specs=[
            SM,
            ANY,
            ANY,
            pl.BlockSpec((blk, QP), lambda i: (jnp.minimum(i, 1), 0)),
            pl.BlockSpec((blk, QP), lambda i: (jnp.maximum(i - 2, 0), 0)),
            pl.BlockSpec((QP, D), lambda i: (0, 0)),
            pl.BlockSpec((blk, D), lambda i: (i, 0)),
            native,
            whole,
        ],
        out_specs=[r[1] for r in results],
        scratch_shapes=[
            pltpu.VMEM((D, 2 * FF), bf16),
            pltpu.VMEM((FF, D), bf16),
            pltpu.SemaphoreType.DMA((2,)),
        ],
        compiler_params=params(62),
        cost_estimate=cost(40e9, 40 << 20),
    )(scalars, wgu, wd, outs[0], outs[1], wo, x_rows, cot_t, gain)


def ffn_grads_kernel(table, normed_t, ggu_ref, hidden_t, go_ref, pool_out, pool, gu_0, d_0, gu_1, d_1, sems):
    j = pl.program_id(0)
    steps = pl.num_programs(0)

    def multiply(part, gu, d):
        columns = slice(512 * part, 512 * part + 512)
        gu[...] = jnp.dot(normed_t[...], ggu_ref[:, columns], preferred_element_type=f32).astype(bf16)
        rows = slice(256 * part, 256 * part + 256)
        d[...] = jnp.dot(hidden_t[rows, :], go_ref[...], preferred_element_type=f32).astype(bf16)

    def put(chunk, gu, d):
        base = 600 * (chunk // 5) + 8 * (chunk % 5)
        for r in range(15):
            for p in range(4):
                at = base + r * 40 + 2 * p
                pick_pair(pool, table, gu, 64 * r, 128 * p, at, at + 1)
        for r in range(4):
            at = 1200 + (4 * chunk + r) * 15
            for p in range(7):
                pick_pair(pool, table, d, 64 * r, 128 * p, at + 2 * p, at + 2 * p + 1)
            pick_single(pool, table, d, 64 * r, 896, at + 14)

    put((2 * j + 2 * steps - 1) % (2 * steps), gu_1, d_1)
    multiply(0, gu_0, d_0)
    put(2 * j, gu_0, d_0)
    multiply(1, gu_1, d_1)

    @pl.when(j == steps - 1)
    def _():
        put(2 * steps - 1, gu_1, d_1)
        flush_pool(pool, [pool_out], sems)


def ffn_grads(table, normed_t, ggu, hidden_t, go, total):
    tokens = go.shape[0]
    return pl.pallas_call(
        ffn_grads_kernel,
        grid=(5,),
        out_shape=jax.ShapeDtypeStruct((total, 32, 128), bf16),
        in_specs=[
            SM,
            pl.BlockSpec((D, tokens), lambda j: (0, 0)),
            pl.BlockSpec((tokens, 1024), lambda j: (0, j)),
            pl.BlockSpec((512, tokens), lambda j: (j, 0)),
            pl.BlockSpec((tokens, D), lambda j: (0, 0)),
        ],
        out_specs=ANY,
        scratch_shapes=[
            pltpu.VMEM((total, 32, 128), bf16),
            pltpu.VMEM((D, 512), bf16),
            pltpu.VMEM((256, D), bf16),
            pltpu.VMEM((D, 512), bf16),
            pltpu.VMEM((256, D), bf16),
            pltpu.SemaphoreType.DMA((1,)),
        ],
        compiler_params=params(52),
        cost_estimate=cost(15e9, 60 << 20),
    )(table, normed_t, ggu, hidden_t, go)


def inward_kernel(
    table, gq_0, gq_1, gkv_0, gkv_1, cos_ref, sin_ref, w_ref, normed_t, out_0, out_1,
    branch_ref, x_ref, residual_ref, gain_ref, grad_ref, gain_out, pool_out,
    cat, dqkv, dwo, pool, sems,
):
    i = pl.program_id(0)
    blk = x_ref.shape[0]
    half = branch_ref.shape[0] // 2
    early = i < 2
    at = pl.ds(pl.multiple_of(i * blk, blk), blk)
    cosine, sine = cos_ref[...], sin_ref[...]
    left = lax.broadcasted_iota(jnp.int32, (blk, 128), 1) < 64
    key_cosine = jnp.where(left, cosine, 1.0)
    key_sine = jnp.where(left, sine, 0.0)
    parts = [jnp.where(early, gq_0[...], gq_1[...])]
    for g in range(KVH):
        slab = jnp.where(early, gkv_0[g].astype(f32), gkv_1[g])
        parts.append((slab * key_cosine - swap_halves(slab) * key_sine).astype(bf16))
    terms = jnp.concatenate(parts, axis=1)
    cat[at, :] = terms
    grad_normed = nt_dot(terms, w_ref[...])
    new_wo = jnp.dot(out_0[...], branch_ref[:half, :], preferred_element_type=f32)
    new_wo = new_wo + jnp.dot(out_1[...], branch_ref[half:, :], preferred_element_type=f32)
    dwo[...] = new_wo.astype(bf16)
    x = x_ref[...].astype(f32)
    inverse = lax.rsqrt(jnp.mean(x * x, axis=1, keepdims=True) + epsilon)
    unit = x * inverse
    scaled = grad_normed * gain_ref[...]
    back = inverse * (scaled - unit * jnp.mean(scaled * unit, axis=1, keepdims=True))
    grad_ref[0] = (residual_ref[...] + back).T
    term = jnp.sum(grad_normed * unit, axis=0, keepdims=True)
    for r in range(4):
        first = 375 + (4 * i + r) * 15
        for p in range(7):
            pick_pair(pool, table, dwo, 64 * r, 128 * p, first + 2 * p, first + 2 * p + 1)
        pick_single(pool, table, dwo, 64 * r, 896, first + 14)

    @pl.when(i == 0)
    def _():
        gain_out[...] = term

    @pl.when(i > 0)
    def _():
        gain_out[...] += term

    @pl.when(i == pl.num_programs(0) - 1)
    def _():
        for low, high in ((0, 512), (512, QP), (QP, CW)):
            dqkv[:, low:high] = jnp.dot(
                normed_t[...], cat[:, low:high], preferred_element_type=f32
            ).astype(bf16)
        for p in range(7):
            for r in range(15):
                pick_pair(pool, table, dqkv, 64 * r, 128 * p, r * 15 + 2 * p, r * 15 + 2 * p + 1)
        for r in range(15):
            pick_single(pool, table, dqkv, 64 * r, 896, r * 15 + 14)
        for g in range(KVH):
            for r in range(15):
                pick_pair(pool, table, dqkv, 64 * r, QP + 128 * g, 225 + r * 5 + g, 300 + r * 5 + g)
        flush_pool(pool.at[pl.ds(0, pool_out.shape[0])], [pool_out], sems)


def inward(table, gq, gkv, cosine, sine, wqkv, normed_t, outs_t, branch, x_rows, residual, gain, total):
    rows = cosine.shape[0]
    tokens = x_rows.shape[0]
    blk = rows // 2
    steps = tokens // blk
    table = jnp.concatenate([table, jnp.full((15,), total, jnp.int32)])

    def early(i):
        return jnp.minimum(i, 1)

    def late(i):
        return jnp.maximum(i - 2, 0)

    def rows_of(width, at=lambda i: i):
        return pl.BlockSpec((blk, width), lambda i: (at(i), 0))

    def slabs(at):
        return pl.BlockSpec((KVH, blk, 128), lambda i: (0, at(i), 0))

    def all_of(*shape):
        return pl.BlockSpec(shape, lambda i: (0, 0))

    features = pl.BlockSpec((QP // steps, rows), lambda i: (i, 0))
    return pl.pallas_call(
        inward_kernel,
        grid=(steps,),
        out_shape=[
            jax.ShapeDtypeStruct((tokens // rows, D, rows), f32),
            jax.ShapeDtypeStruct((1, D), f32),
            jax.ShapeDtypeStruct((total, 32, 128), bf16),
        ],
        in_specs=[
            SM, rows_of(QP, early), rows_of(QP, late), slabs(early), slabs(late),
            rows_of(128, lambda i: i % 2), rows_of(128, lambda i: i % 2),
            all_of(D, CW), all_of(D, tokens), features, features,
            all_of(tokens, D), rows_of(D), rows_of(D), all_of(1, D),
        ],
        out_specs=[pl.BlockSpec((1, D, blk), lambda i: (i // 2, 0, i % 2)), all_of(1, D), ANY],
        scratch_shapes=[
            pltpu.VMEM((tokens, CW), bf16),
            pltpu.VMEM((D, CW), bf16),
            pltpu.VMEM((QP // steps, D), bf16),
            pltpu.VMEM((total + 1, 32, 128), bf16),
            pltpu.SemaphoreType.DMA((1,)),
        ],
        compiler_params=params(60),
        cost_estimate=cost(12e9, 30 << 20),
    )(table, *gq, *gkv, cosine, sine, wqkv, normed_t, *outs_t, branch, x_rows, residual, gain)


TOGETHER = 11


def shampoo_kernel(
    filled, sum_a, sum_f, master, stat_left, stat_right, root_left, root_right,
    grads_out, left_out, right_out, master_out, grads, lefts, rights, gram_left, gram_right, step,
):
    slots = master.shape[1]
    n_a = sum_a.shape[0] // 32
    for source, target in ((root_left, lefts), (root_right, rights)):
        for r in range(32):
            both = jnp.concatenate(
                [source[64 * r : 64 * r + 64, :], source[64 * (r + 32) : 64 * (r + 32) + 64, :]], axis=0
            )
            target[pl.ds(r, slots, stride=32), :] = both.T

    def square(rows):
        return jnp.concatenate([rows[:, :64], rows[:, 64:]], axis=0)

    def folded(rows):
        return jnp.concatenate([rows[:32], rows[32:]], axis=1)

    def keep(source, count, shift):
        def one(s, _):
            grad = source[pl.ds(pl.multiple_of(s * 32, 32), 32), :]
            at = pl.ds(pl.multiple_of((s + shift) * 32, 32), 32)
            grads[at, :] = jnp.where(filled[s + shift] > 0, grad, 0.0)
            return 0

        lax.fori_loop(0, count, one, 0, unroll=8)

    keep(sum_a, n_a, 0)
    keep(sum_f, slots - n_a, n_a)

    def several(i, _):
        spans = [pl.ds(pl.multiple_of((TOGETHER * i + t) * 32, 32), 32) for t in range(TOGETHER)]
        grad = [square(grads[span, :]).astype(bf16) for span in spans]
        left = [square(lefts[span, :]).astype(bf16) for span in spans]
        right = [square(rights[span, :]).astype(bf16) for span in spans]
        half = [jnp.dot(a, g, preferred_element_type=f32) for a, g in zip(left, grad)]
        gram_l = [nt_dot(g, g) for g in grad]
        gram_r = [tn_dot(g, g) for g in grad]
        whole = [jnp.dot(h.astype(bf16), b, preferred_element_type=f32) for h, b in zip(half, right)]
        for t, span in enumerate(spans):
            gram_left[span, :] = folded(gram_l[t])
            gram_right[span, :] = folded(gram_r[t])
            step[span, :] = folded(whole[t])
        return 0

    lax.fori_loop(0, grads.shape[0] // (32 * TOGETHER), several, 0)

    for r in range(32):
        first = slice(64 * r, 64 * r + 64)
        second = slice(64 * (r + 32), 64 * (r + 32) + 64)
        rows = pl.ds(r, slots, stride=32)
        flipped = grads[rows, :].T
        grads_out[first, :] = flipped[:64]
        grads_out[second, :] = flipped[64:]
        for source, stat, out in ((gram_left, stat_left, left_out), (gram_right, stat_right, right_out)):
            flipped = source[rows, :].T
            out[first, :] = decay_rate * stat[first, :] + (1.0 - decay_rate) * flipped[:64]
            out[second, :] = decay_rate * stat[second, :] + (1.0 - decay_rate) * flipped[64:]
        flipped = step[rows, :].T
        master_out[first, :] = master[first, :] - step_rate * flipped[:64]
        master_out[second, :] = master[second, :] - step_rate * flipped[64:]


def shampoo(filled, sum_a, sum_f, *arrays):
    slots = arrays[0].shape[0]
    native = [a.transpose(1, 2, 0).reshape(TL * TL, slots) for a in arrays]
    scratch = pltpu.VMEM((-(-slots // TOGETHER) * TOGETHER * 32, 128), f32)
    results = pl.pallas_call(
        shampoo_kernel,
        out_shape=[jax.ShapeDtypeStruct((TL * TL, slots), f32)] * 4,
        in_specs=[SM] + [VM] * 7,
        out_specs=[VM] * 4,
        scratch_shapes=[scratch] * 6,
        compiler_params=params(48),
        cost_estimate=cost(1e9, 24 << 20),
    )(filled, sum_a.reshape(-1, 128), sum_f.reshape(-1, 128), *native)
    return [r.reshape(TL, TL, slots).transpose(2, 0, 1) for r in results]


def fold(tiles):
    return jnp.concatenate([tiles[:, :32, :], tiles[:, 32:, :]], axis=2)


def shards(
    inputs,
    cotangent,
    lengths,
    order,
    owner_slots,
    master,
    stat_left,
    stat_right,
    root_left,
    root_right,
    gains,
    gain_stats,
):
    micro, rows = inputs.shape[1], inputs.shape[2]
    n_ctx, n_wt = lax.axis_size("ctx"), lax.axis_size("wt")
    devices = n_ctx * n_wt
    line = is_line(n_ctx, n_wt)
    tokens = micro * rows
    cap = master.shape[0]
    cap_a = NTA // devices + NTA // (8 * devices) + 2
    cap_f = cap - cap_a
    c = lax.axis_index("ctx")
    w = lax.axis_index("wt")

    x_t = inputs[0].transpose(0, 2, 1)
    low_master = fold(master.astype(bf16))
    own_a, own_f = low_master[:cap_a], low_master[cap_a:]
    own_a, own_f = low_master[:cap_a], low_master[cap_a:]
    owner, within = owner_slots // cap, owner_slots % cap
    whole_a = owner[:NTA] * cap_a + within[:NTA]
    whole_f = owner[NTA:] * cap_f + within[NTA:] - cap_a

    blocks = order.shape[0]
    ids = jnp.arange(blocks, dtype=jnp.int32)
    my_blocks = jnp.sum(jnp.where(ids[None, :] == 2 * c + jnp.arange(2)[:, None], order[None, :], 0), axis=1)
    position = (my_blocks[:, None] * (rows // 2) + jnp.arange(rows // 2, dtype=jnp.int32)[None, :]).reshape(rows)
    lane = np.arange(128)
    frequency = jnp.asarray(rope_base, f32) ** (-(jnp.asarray(lane % 32, f32)) * 2.0 / HD)
    angle = position.astype(f32)[:, None] * frequency[None, :]
    cosine = jnp.cos(angle)
    sine = jnp.sin(angle) * jnp.where(lane % 64 < 32, -1.0, 1.0).astype(f32)[None, :]
    metas = [
        jnp.concatenate([my_blocks, lengths[0, m][None], c[None], order]).astype(jnp.int32)
        for m in range(micro)
    ]

    if line:
        q, normed_attn_t, x_low, kv_first, kv_late, wqkv, wo, pool_f = front(
            whole_a, own_a, own_f, x_t, gains[0:1], cosine, sine
        )
        pool_f = pool_f.reshape(devices * cap_f, 32, 128)
        chunks = [kv_first, lax.all_gather(kv_late, "ctx", axis=0)]
    else:
        parts_a = [lax.all_gather(own_a, AXES, axis=0, tiled=True)]
        pool_f = lax.all_gather(own_f, AXES, axis=0, tiled=True)
        wqkv, wo = assemble(assemble_attn_kernel, parts_a, whole_a, [(D, CW), (QP, D)])
        x_low = inputs.reshape(tokens, D)
        q, kv, normed_attn = qkv_rows(x_low, gains[0:1], wqkv, cosine, sine, micro)
        normed_attn_t = normed_attn.T
        chunks = [lax.all_gather(kv[m], "ctx", axis=0) for m in range(micro)]
    forward = [flash_forward(0, metas[0], q, chunks[0])]
    wgu, wd = assemble_ffn(after(whole_f, forward[0][0]), pool_f)
    forward.append(flash_forward(1, metas[1], q, after(chunks[1], wgu)))
    scalars = jnp.concatenate([my_blocks, lengths[0]]).astype(jnp.int32)
    cot_t = cotangent[0].transpose(0, 2, 1)
    outs = [f[0] for f in forward]
    (mixed_t, normed_ffn_t, hidden_t, grad_gu, grad_out, grad_branch, grad_residual, grad_attn, gain_ffn) = middle(
        scalars, wgu, wd, outs, wo, x_low, cot_t, gains[1:2]
    )
    def flash_back(m):
        out, _, lse = forward[m]
        return flash_backward(m, metas[m], q, out, grad_attn, lse, cosine, sine, chunks[m])

    gq_0, gkv_0 = flash_back(0)
    gkv_0 = lax.psum_scatter(gkv_0, "ctx", scatter_dimension=0, tiled=False)
    grad_out = after(grad_out, gq_0)
    pool_f = ffn_grads(whole_f, normed_ffn_t, grad_gu, hidden_t, grad_out, devices * cap_f)
    grad_attn = after(grad_attn, pool_f)
    gq_1, gkv_1 = flash_back(1)
    if line:
        near_f, gkv_1 = back_home(pool_f.reshape(4, 4, 2, cap_f, 32, 128), gkv_1)
    else:
        sum_f = lax.psum_scatter(pool_f.astype(f32), AXES, scatter_dimension=0, tiled=True)
        gkv_1 = lax.psum_scatter(gkv_1, "ctx", scatter_dimension=0, tiled=False).astype(f32)
    input_grad_t, gain_attn, pool_a = inward(
        whole_a, (gq_0, gq_1), (gkv_0, gkv_1), cosine, sine, wqkv, normed_attn_t, [f[1] for f in forward], grad_branch, x_low,
        grad_residual, gains[0:1], devices * cap_a,
    )
    gain_terms = jnp.concatenate([gain_attn, gain_ffn])
    if line:
        gain_rows = jnp.pad(gain_terms.reshape(15, 128), ((0, 1), (0, 0)))
        sum_a, sum_f, gain_rows = tail(pool_a.reshape(4, 4, 2, cap_a, 32, 128), near_f, gain_rows)
        gain_grads = gain_rows[:15].reshape(2, D)
    else:
        sum_a = lax.psum_scatter(pool_a.astype(f32), AXES, scatter_dimension=0, tiled=True)
        gain_grads = lax.psum(gain_terms, AXES)

    here = (c * n_wt + w) * cap + jnp.arange(cap, dtype=jnp.int32)
    filled = jnp.max((owner_slots[None, :] == here[:, None]).astype(jnp.int32), axis=1)
    tile_grads, new_left, new_right, new_master = shampoo(
        filled, sum_a, sum_f, master, stat_left, stat_right, root_left, root_right
    )
    new_gain_stats = decay_rate * gain_stats + (1.0 - decay_rate) * gain_grads * gain_grads
    new_gains = gains - gain_rate * gain_grads * lax.rsqrt(new_gain_stats)
    return (
        mixed_t.transpose(0, 2, 1)[None],
        input_grad_t.transpose(0, 2, 1)[None],
        tile_grads,
        new_left,
        new_right,
        new_master,
        gain_grads,
        new_gain_stats,
        new_gains,
    )


def solution(mesh):
    in_specs = (
        P("wt", None, "ctx", None),
        P("wt", None, "ctx", None),
        P("wt", None),
        P(),
        P(),
        P(AXES, None, None),
        P(AXES, None, None),
        P(AXES, None, None),
        P(AXES, None, None),
        P(AXES, None, None),
        P(),
        P(),
    )
    out_specs = (
        P("wt", None, "ctx", None),
        P("wt", None, "ctx", None),
        P(AXES, None, None),
        P(AXES, None, None),
        P(AXES, None, None),
        P(AXES, None, None),
        P(),
        P(),
        P(),
    )
    return jax.shard_map(shards, mesh=mesh, in_specs=in_specs, out_specs=out_specs, check_vma=False)
```

```python
import functools

import jax
import jax.numpy as jnp
import numpy as np
from jax import lax
from jax.experimental import pallas as pl
from jax.experimental.pallas import tpu as pltpu
from jax.sharding import PartitionSpec as P

D = 960
FF = 2560
QH = 15
KVH = 5
HD = 64
TL = 64
QW = 960
KVW = 320
GRP = 3
NTA = 600
NT = 2400
QP = 1024
CW = 1664
BLK = 256
AXES = ("ctx", "wt")

epsilon = 1e-05
decay_rate = 0.95
step_rate = 0.05
gain_rate = 0.05
rope_base = 10000.0
blocked_score = -1e30
bf16 = jnp.bfloat16
f32 = jnp.float32
VM = pl.BlockSpec(memory_space=pltpu.VMEM)
SM = pl.BlockSpec(memory_space=pltpu.SMEM)
ANY = pl.BlockSpec(memory_space=pl.ANY)


def params(megabytes, **kwargs):
    return pltpu.CompilerParams(vmem_limit_bytes=megabytes << 20, **kwargs)


def cost(flops, nbytes, trans=0):
    return pl.CostEstimate(flops=int(flops), bytes_accessed=int(nbytes), transcendentals=int(trans))


def after(x, *others):
    return lax.optimization_barrier((x, others))[0]


def is_line(n_ctx, n_wt):
    return n_ctx == 4 and n_wt == 8


def flip(x, bit):
    return lax.ppermute(x, "wt", [(i, i ^ bit) for i in range(8)])


def tile_halves(n):
    return (n + 1) // 2


def load_parts(parts, pool, sems):
    at = 0
    copies = []
    for i, part in enumerate(parts):
        rows = part.shape[0]
        copies.append(pltpu.make_async_copy(part, pool.at[pl.ds(at, rows)], sems.at[i]))
        at += rows
    for copy in copies:
        copy.start()
    for copy in copies:
        copy.wait()


def place_pair(pool, table, ref, row, lane, a, b):
    first = pool[table[a]]
    second = pool[table[b]]
    ref[pl.ds(row, 32), lane : lane + 128] = jnp.concatenate([first[:, :64], second[:, :64]], axis=1)
    ref[pl.ds(row + 32, 32), lane : lane + 128] = jnp.concatenate([first[:, 64:], second[:, 64:]], axis=1)


def place_single(pool, table, ref, row, lane, a):
    first = pool[table[a]]
    ref[pl.ds(row, 32), lane : lane + 64] = first[:, :64]
    ref[pl.ds(row + 32, 32), lane : lane + 64] = first[:, 64:]


def assemble_attn_kernel(count, table, *refs):
    parts, (wqkv, wo, pool, sems) = refs[:count], refs[count:]
    load_parts(parts, pool, sems)
    attn_rows(pool, table, wqkv, wo)


def attn_rows(pool, table, wqkv, wo):
    def qkv_row(r, _):
        row = pl.multiple_of(r * 64, 64)
        for p in range(7):
            place_pair(pool, table, wqkv, row, 128 * p, r * 15 + 2 * p, r * 15 + 2 * p + 1)
        place_single(pool, table, wqkv, row, 896, r * 15 + 14)
        wqkv[pl.ds(row, 64), 960:1024] = jnp.zeros((64, 64), bf16)
        for g in range(KVH):
            place_pair(pool, table, wqkv, row, QP + 128 * g, 225 + r * 5 + g, 300 + r * 5 + g)
        for p in range(7):
            place_pair(pool, table, wo, row, 128 * p, 375 + r * 15 + 2 * p, 375 + r * 15 + 2 * p + 1)
        place_single(pool, table, wo, row, 896, 375 + r * 15 + 14)
        return 0

    lax.fori_loop(0, 15, qkv_row, 0)
    wo[pl.ds(960, 64), :] = jnp.zeros((64, D), bf16)


def ffn_rows(pool, table, wgu, wd):
    def gu_row(r, _):
        row = pl.multiple_of(r * 64, 64)
        for m in range(2):
            for p in range(20):
                base = 600 * m + r * 40 + 2 * p
                place_pair(pool, table, wgu, row, FF * m + 128 * p, base, base + 1)
        return 0

    lax.fori_loop(0, 15, gu_row, 0)

    def d_row(r, _):
        row = pl.multiple_of(r * 64, 64)
        for p in range(7):
            place_pair(pool, table, wd, row, 128 * p, 1200 + r * 15 + 2 * p, 1200 + r * 15 + 2 * p + 1)
        place_single(pool, table, wd, row, 896, 1200 + r * 15 + 14)
        return 0

    lax.fori_loop(0, 40, d_row, 0)


def assemble(kernel, parts, table, shapes):
    total = sum(p.shape[0] for p in parts)
    out_bytes = sum(2 * a * b for a, b in shapes)
    return pl.pallas_call(
        functools.partial(kernel, len(parts)),
        out_shape=[jax.ShapeDtypeStruct(s, bf16) for s in shapes],
        in_specs=[SM] + [ANY] * len(parts),
        out_specs=[VM] * len(shapes),
        scratch_shapes=[pltpu.VMEM((total, 32, 128), bf16), pltpu.SemaphoreType.DMA((len(parts),))],
        compiler_params=params(52),
        cost_estimate=cost(0, 4 * out_bytes),
    )(table, *parts)


def pick_pair(pool, table, ref, row, lane, a, b):
    block = ref[pl.ds(row, 64), lane : lane + 128]
    pool[table[a]] = jnp.concatenate([block[:32, :64], block[32:, :64]], axis=1)
    pool[table[b]] = jnp.concatenate([block[:32, 64:], block[32:, 64:]], axis=1)


def pick_single(pool, table, ref, row, lane, a):
    block = ref[pl.ds(row, 64), lane : lane + 64]
    pool[table[a]] = jnp.concatenate([block[:32], block[32:]], axis=1)


def flush_pool(pool, outs, sems):
    at = 0
    copies = []
    for i, out in enumerate(outs):
        rows = out.shape[0]
        copies.append(pltpu.make_async_copy(pool.at[pl.ds(at, rows)], out, sems.at[i]))
        at += rows
    for copy in copies:
        copy.start()
    for copy in copies:
        copy.wait()


def swap_halves(x):
    lane = lax.broadcasted_iota(jnp.int32, x.shape, 1)
    return jnp.where(lane % 64 < 32, pltpu.roll(x, 96, 1), pltpu.roll(x, 32, 1))


def qkv_kernel(x_ref, gain_ref, w_ref, cos_ref, sin_ref, q_ref, kv_ref, normed_ref):
    x = x_ref[...].astype(f32)
    inverse = lax.rsqrt(jnp.mean(x * x, axis=1, keepdims=True) + epsilon)
    normed = (x * inverse * gain_ref[...]).astype(bf16)
    normed_ref[...] = normed
    cosine, sine = cos_ref[...], sin_ref[...]
    lane = lax.broadcasted_iota(jnp.int32, cosine.shape, 1)
    left = lane < 64
    for p in range(8):
        rows = jnp.dot(normed, w_ref[:, 128 * p : 128 * p + 128], preferred_element_type=f32)
        rows = (rows * cosine + swap_halves(rows) * sine).astype(bf16).astype(f32) * 0.125
        q_ref[2 * p] = jnp.where(left, rows, 0.0).astype(bf16)
        if 2 * p + 1 < QH:
            q_ref[2 * p + 1] = jnp.where(left, pltpu.roll(rows, 64, 1), 0.0).astype(bf16)
    cosine = jnp.where(left, cosine, 1.0)
    sine = jnp.where(left, sine, 0.0)
    for g in range(KVH):
        at = QP + 128 * g
        rows = jnp.dot(normed, w_ref[:, at : at + 128], preferred_element_type=f32)
        kv_ref[0, g] = (rows * cosine + swap_halves(rows) * sine).astype(bf16)


def qkv_rows(x, gain, wqkv, cosine, sine, micro):
    tokens = x.shape[0]
    rows = tokens // micro
    blk = min(BLK, rows)
    steps = tokens // blk
    per = steps // micro
    return pl.pallas_call(
        qkv_kernel,
        grid=(steps,),
        out_shape=[
            jax.ShapeDtypeStruct((QH, tokens, 128), bf16),
            jax.ShapeDtypeStruct((micro, KVH, rows, 128), bf16),
            jax.ShapeDtypeStruct((tokens, D), bf16),
        ],
        in_specs=[
            pl.BlockSpec((blk, D), lambda i: (i, 0)),
            pl.BlockSpec((1, D), lambda i: (0, 0)),
            pl.BlockSpec((D, CW), lambda i: (0, 0)),
            pl.BlockSpec((blk, 128), lambda i: (i % per, 0)),
            pl.BlockSpec((blk, 128), lambda i: (i % per, 0)),
        ],
        out_specs=[
            pl.BlockSpec((QH, blk, 128), lambda i: (0, i, 0)),
            pl.BlockSpec((1, KVH, blk, 128), lambda i: (i // per, 0, i % per, 0)),
            pl.BlockSpec((blk, D), lambda i: (i, 0)),
        ],
        compiler_params=params(40),
        cost_estimate=cost(2 * tokens * D * CW, 14 << 20),
    )(x, gain, wqkv, cosine, sine)


def remote(src, dst, send, recv, device):
    return pltpu.make_async_remote_copy(
        src_ref=src,
        dst_ref=dst,
        send_sem=send,
        recv_sem=recv,
        device_id=device,
        device_id_type=pl.DeviceIdType.MESH,
    )


def greet(c, w, far):
    barrier = pltpu.get_barrier_semaphore()

    def hail(device):
        pl.semaphore_signal(barrier, inc=1, device_id=device, device_id_type=pl.DeviceIdType.MESH)

    for bit in (1, 2, 4):
        hail({"wt": w ^ bit})
    if far:
        hail({"ctx": c ^ 2})

    @pl.when(c < 3)
    def _():
        hail({"ctx": c + 1})

    @pl.when(c > 0)
    def _():
        hail({"ctx": c - 1})

    inner = jnp.logical_and(c > 0, c < 3)

    @pl.when(inner)
    def _():
        pl.semaphore_wait(barrier, 5 + far)

    @pl.when(jnp.logical_not(inner))
    def _():
        pl.semaphore_wait(barrier, 4 + far)


class Gather:
    def __init__(self, pool, sems, c, w):
        self.pool, self.sems, self.c, self.w = pool, sems, c, w
        self.n = pool.shape[2]
        self.n1 = tile_halves(self.n)
        self.x, self.y, self.core = {"wt": w ^ 2}, {"wt": w ^ 4}, {"wt": w ^ 1}

    def copy(self, k, owner, lane, device, part=None):
        ref = self.pool.at[k, owner]
        if part is not None:
            ref = ref.at[pl.ds(part[0], part[1])]
        return remote(ref, ref, self.sems.at[k, lane], self.sems.at[k, lane + 1], device)

    def up(self, k):
        return self.copy(k, self.w, 0, {"ctx": self.c + 1})

    def down(self, k):
        return self.copy(k, self.w, 2, {"ctx": self.c - 1})

    def over_x(self, k, back=0):
        return self.copy(k, self.w ^ back, 4, self.x)

    def over_y(self, k, back=0):
        return self.copy(k, self.w ^ back, 6, self.y)

    def diag_x(self, k, owner):
        return self.copy(k, owner, 8, self.x, (0, self.n1))

    def diag_y(self, k, owner):
        return self.copy(k, owner, 10, self.y, (self.n1, self.n - self.n1))

    def over_core(self, k, quad, back=0):
        return self.copy(k, self.w ^ (2 * quad) ^ back, 12 + 2 * quad, self.core)

    def send_line(self, k, low, high):
        if low:

            @pl.when(self.c < 3)
            def _():
                self.up(k).start()

        if high:

            @pl.when(self.c > 0)
            def _():
                self.down(k).start()

    def send_near(self, k):
        self.over_x(k).start()
        self.over_y(k).start()
        self.over_core(k, 0).start()

    def first(self):
        self.send_line(self.c, True, True)

    def sides(self, s):
        return [(self.c >= s, self.c - s, True), (self.c + s <= 3, self.c + s, False)]

    def line_step(self, s, near=True):
        for valid, k, below in self.sides(s):

            @pl.when(valid)
            def _(k=k, below=below):
                if below:
                    self.up(k).wait_recv()
                else:
                    self.down(k).wait_recv()
                if s < 3:
                    self.send_line(k, below, not below)
                if near:
                    self.send_near(k)

    def each(self, s, act):
        if s == 0:
            act(self.c)
            return
        for valid, k, _ in self.sides(s):

            @pl.when(valid)
            def _(k=k):
                act(k)

    def near_step(self, s):
        def act(k):
            self.over_x(k, 2).wait_recv()
            self.diag_y(k, self.w ^ 2).start()
            self.over_core(k, 1).start()
            self.over_y(k, 4).wait_recv()
            self.diag_x(k, self.w ^ 4).start()
            self.over_core(k, 2).start()

        self.each(s, act)

    def diag_step(self, s):
        def act(k):
            self.diag_x(k, self.w ^ 6).wait_recv()
            self.diag_y(k, self.w ^ 6).wait_recv()
            self.over_core(k, 3).start()

        self.each(s, act)

    def finish(self):
        for k in range(4):
            for quad in range(4):
                self.over_core(k, quad, 1).wait_recv()

    def drain(self):
        for k in range(4):

            @pl.when(jnp.logical_and(k <= self.c, self.c < 3))
            def _(k=k):
                self.up(k).wait_send()

            @pl.when(jnp.logical_and(k >= self.c, self.c > 0))
            def _(k=k):
                self.down(k).wait_send()

            self.over_x(k).wait_send()
            self.over_y(k).wait_send()
            self.diag_x(k, self.w ^ 4).wait_send()
            self.diag_y(k, self.w ^ 2).wait_send()
            for quad in range(4):
                self.over_core(k, quad).wait_send()


def front_kernel(
    table, own_a, own_f, x_ref, gain_ref, cos_ref, sin_ref,
    q_ref, normed_t, rows_ref, kv_ref, late_ref, wqkv, wo, pool_f,
    normed_ref, pool_a, kv_own, sems_a, sems_f, sems_kv, sems,
):
    c, w = lax.axis_index("ctx"), lax.axis_index("wt")
    take_a = pltpu.make_async_copy(own_a, pool_a.at[c, w], sems.at[0])
    take_f = pltpu.make_async_copy(own_f, pool_f.at[c, w], sems.at[1])
    take_a.start()
    take_f.start()
    greet(c, w, 0)
    take_a.wait()
    a = Gather(pool_a, sems_a, c, w)
    f = Gather(pool_f, sems_f, c, w)
    a.first()
    a.send_near(c)

    rows = x_ref.shape[2]
    blk = BLK
    for m in range(2):
        for half in range(rows // blk):
            part = x_ref[m, :, blk * half : blk * half + blk].T
            span = slice(m * rows + blk * half, m * rows + blk * half + blk)
            rows_ref[span, :] = part
            wide = part.astype(f32)
            inverse = lax.rsqrt(jnp.mean(wide * wide, axis=1, keepdims=True) + epsilon)
            normed = (wide * inverse * gain_ref[...]).astype(bf16)
            normed_ref[span, :] = normed
            normed_t[:, span] = normed.T

    a.line_step(1)
    a.near_step(0)
    a.line_step(2)
    take_f.wait()
    f.first()
    a.near_step(1)
    a.diag_step(0)
    a.line_step(3)
    a.near_step(2)
    a.diag_step(1)
    a.near_step(3)
    f.send_near(c)
    a.diag_step(2)
    a.diag_step(3)
    f.line_step(1)
    a.finish()

    flat = pool_a.reshape(pool_a.shape[0] * pool_a.shape[1] * pool_a.shape[2], 32, 128)
    attn_rows(flat, table, wqkv, wo)
    f.line_step(2)
    f.near_step(0)

    lane = lax.broadcasted_iota(jnp.int32, (blk, 128), 1)
    left = lane < 64

    def qkv_block(i, _):
        at = pl.multiple_of(i * blk, blk)
        normed = normed_ref[pl.ds(at, blk), :]
        within = pl.multiple_of((i % (rows // blk)) * blk, blk)
        cosine, sine = cos_ref[pl.ds(within, blk), :], sin_ref[pl.ds(within, blk), :]
        key_cosine = jnp.where(left, cosine, 1.0)
        key_sine = jnp.where(left, sine, 0.0)
        for g in range(KVH):
            spot = QP + 128 * g
            part = jnp.dot(normed, wqkv[:, spot : spot + 128], preferred_element_type=f32)
            part = (part * key_cosine + swap_halves(part) * key_sine).astype(bf16)
            kv_own[i // (rows // blk), g, pl.ds(within, blk), :] = part
        for p in range(8):
            part = jnp.dot(normed, wqkv[:, 128 * p : 128 * p + 128], preferred_element_type=f32)
            part = (part * cosine + swap_halves(part) * sine).astype(bf16).astype(f32) * 0.125
            q_ref[2 * p, pl.ds(at, blk), :] = jnp.where(left, part, 0.0).astype(bf16)
            if 2 * p + 1 < QH:
                other = jnp.where(left, pltpu.roll(part, 64, 1), 0.0).astype(bf16)
                q_ref[2 * p + 1, pl.ds(at, blk), :] = other
        return 0

    def kv_move(src, k, lane, step):
        return remote(src, kv_ref.at[k], sems_kv.at[k, lane], sems_kv.at[k, lane + 1], {"ctx": c + step})

    lax.fori_loop(0, rows // blk, qkv_block, 0)
    keep = pltpu.make_async_copy(kv_own.at[0], kv_ref.at[c], sems.at[2])
    keep.start()

    @pl.when(c < 3)
    def _():
        kv_move(kv_own.at[0], c, 0, 1).start()

    @pl.when(c > 0)
    def _():
        kv_move(kv_own.at[0], c, 2, -1).start()

    lax.fori_loop(rows // blk, 2 * rows // blk, qkv_block, 0)
    late = pltpu.make_async_copy(kv_own.at[1], late_ref, sems.at[3])
    late.start()

    def kv_step(s):
        @pl.when(c >= s)
        def _():
            kv_move(kv_ref.at[c - s], c - s, 0, 1).wait_recv()
            if s < 3:

                @pl.when(c < 3)
                def _():
                    kv_move(kv_ref.at[c - s], c - s, 0, 1).start()

        @pl.when(c + s <= 3)
        def _():
            kv_move(kv_ref.at[c + s], c + s, 2, -1).wait_recv()
            if s < 3:

                @pl.when(c > 0)
                def _():
                    kv_move(kv_ref.at[c + s], c + s, 2, -1).start()

    f.line_step(3)
    f.near_step(1)
    f.diag_step(0)
    kv_step(1)
    f.near_step(2)
    f.diag_step(1)
    f.near_step(3)
    kv_step(2)
    f.diag_step(2)
    f.diag_step(3)
    f.finish()
    kv_step(3)
    keep.wait()
    late.wait()
    for k in range(4):

        @pl.when(jnp.logical_and(k <= c, c < 3))
        def _(k=k):
            kv_move(kv_ref.at[k], k, 0, 1).wait_send()

        @pl.when(jnp.logical_and(k >= c, c > 0))
        def _(k=k):
            kv_move(kv_ref.at[k], k, 2, -1).wait_send()

    a.drain()
    f.drain()


def front(table, own_a, own_f, x_t, gain, cosine, sine):
    micro, _, rows = x_t.shape
    tokens = micro * rows
    n_a, n_f = own_a.shape[0], own_f.shape[0]
    return pl.pallas_call(
        front_kernel,
        out_shape=[
            jax.ShapeDtypeStruct((QH, tokens, 128), bf16),
            jax.ShapeDtypeStruct((D, tokens), bf16),
            jax.ShapeDtypeStruct((tokens, D), bf16),
            jax.ShapeDtypeStruct((4, KVH, rows, 128), bf16),
            jax.ShapeDtypeStruct((KVH, rows, 128), bf16),
            jax.ShapeDtypeStruct((D, CW), bf16),
            jax.ShapeDtypeStruct((QP, D), bf16),
            jax.ShapeDtypeStruct((4, 8, n_f, 32, 128), bf16),
        ],
        in_specs=[SM, ANY, ANY, VM, VM, VM, VM],
        out_specs=[VM, VM, VM, ANY, ANY, VM, VM, ANY],
        scratch_shapes=[
            pltpu.VMEM((tokens, D), bf16),
            pltpu.VMEM((4, 8, n_a, 32, 128), bf16),
            pltpu.VMEM((micro, KVH, rows, 128), bf16),
            pltpu.SemaphoreType.DMA((4, 20)),
            pltpu.SemaphoreType.DMA((4, 20)),
            pltpu.SemaphoreType.DMA((4, 4)),
            pltpu.SemaphoreType.DMA((4,)),
        ],
        compiler_params=params(48, collective_id=0, has_side_effects=True),
        cost_estimate=cost(40e9, 40 << 20),
    )(table, own_a, own_f, x_t, gain, cosine, sine)


class Line:
    def __init__(self, terms, send, recv, sems, c):
        self.terms, self.send, self.recv, self.sems, self.c = terms, send, recv, sems, c
        self.count = recv.shape[2]

    def copy(self, way, k):
        sems = self.sems
        return remote(
            self.send.at[k], self.recv.at[way, k], sems.at[way, k, 0], sems.at[way, k, 1],
            {"ctx": self.c + 1 - 2 * way},
        )

    def loop(self, act):
        def body(j, _):
            act(j)
            return 0

        lax.fori_loop(0, self.count, body, 0)

    def start(self):
        for way in (0, 1):

            @pl.when(self.c == 3 * way)
            def _(way=way):
                for far in (3, 2, 1):
                    k = far if way == 0 else 3 - far

                    def take(j, k=k):
                        self.send[k, j] = self.terms(k, j).astype(bf16)

                    self.loop(take)
                    self.copy(way, k).start()

    def join(self, way, k):
        self.copy(way, k).wait_recv()

        def act(j):
            self.send[k, j] = (self.terms(k, j) + self.recv[way, k, j].astype(f32)).astype(bf16)

        self.loop(act)
        self.copy(way, k).start()

    def step(self, number):
        lists = {1: ((0, 3), (0, 2), (1, 0)), 2: ((1, 0), (1, 1), (0, 3))}
        for inner, order in lists.items():

            @pl.when(self.c == inner)
            def _(order=order):
                self.join(*order[number])

    def finish(self, out):
        c, recv = self.c, self.recv

        @pl.when(c > 0)
        def _():
            self.copy(0, c).wait_recv()

        @pl.when(c < 3)
        def _():
            self.copy(1, c).wait_recv()

        def total(j):
            low = jnp.where(c > 0, recv[0, c, j].astype(f32), 0.0)
            high = jnp.where(c < 3, recv[1, c, j].astype(f32), 0.0)
            out[j] = self.terms(c, j) + low + high

        self.loop(total)

    def drain(self):
        for far in (3, 2, 1):
            for way, k in ((0, far), (1, 3 - far)):

                @pl.when(self.c < k if way == 0 else self.c > k)
                def _(way=way, k=k):
                    self.copy(way, k).wait_send()


class Plane:
    def __init__(self, pool, bufs, sems, c, w):
        self.pool, self.sems, self.c, self.w = pool, sems, c, w
        self.mine, self.theirs, self.diag_send, self.diag_recv, self.near_send, self.near_recv = bufs
        self.n = pool.shape[3]
        n1 = self.n1 = tile_halves(self.n)
        yx, core = w // 2, w % 2
        over_x, over_y, over_core = {"wt": w ^ 2}, {"wt": w ^ 4}, {"wt": w ^ 1}
        self.loads = [
            pltpu.make_async_copy(pool.at[:, yx ^ q, core], self.mine.at[q], sems.at[10 + q, 0]) for q in range(4)
        ]
        self.cores = [
            remote(pool.at[:, yx ^ q, 1 - core], self.theirs.at[q], sems.at[q, 0], sems.at[q, 1], over_core)
            for q in range(4)
        ]
        low, high = slice(0, n1), slice(n1, self.n)
        self.diag_x = self.move(self.diag_send.at[:, low], self.diag_recv.at[:, low], 4, over_x)
        self.diag_y = self.move(self.diag_send.at[:, high], self.diag_recv.at[:, high], 5, over_y)
        self.nears = {}
        for q in (1, 2):
            for part, cut in enumerate((low, high)):
                self.nears[q, part] = self.move(
                    self.near_send.at[q - 1, :, cut],
                    self.near_recv.at[q - 1, :, cut],
                    4 + 2 * q + part,
                    over_x if q == 1 else over_y,
                )

    def move(self, src, dst, lane, device):
        return remote(src, dst, self.sems.at[lane, 0], self.sems.at[lane, 1], device)

    def begin_loads(self):
        for q in (3, 1, 2, 0):
            self.loads[q].start()

    def begin(self):
        for q in (3, 1, 2, 0):
            self.cores[q].start()

    def each(self, act):
        def body(k, _):
            act(k)
            return 0

        lax.fori_loop(0, 4, body, 0)

    def both(self, q, k):
        return self.mine[q, k].astype(f32) + self.theirs[q, k].astype(f32)

    def ready(self, q):
        self.loads[q].wait()
        self.cores[q].wait()

    def diag(self):
        self.ready(3)

        def act(k):
            self.diag_send[k] = self.both(3, k).astype(bf16)

        self.each(act)
        self.diag_x.start()
        self.diag_y.start()

    def near(self, q):
        self.ready(q)

        def act(k):
            self.near_send[q - 1, k] = self.both(q, k).astype(bf16)

        self.each(act)
        self.nears[q, q - 1].start()

    def join(self, q):
        cut = slice(self.n1, self.n) if q == 1 else slice(0, self.n1)
        (self.diag_y if q == 1 else self.diag_x).wait_recv()

        def act(k):
            ours = self.near_send[q - 1, k, cut].astype(f32)
            self.near_send[q - 1, k, cut] = (ours + self.diag_recv[k, cut].astype(f32)).astype(bf16)

        self.each(act)
        self.nears[q, 2 - q].start()

    def join_out(self, q, out):
        cut = slice(self.n1, self.n) if q == 1 else slice(0, self.n1)
        (self.diag_y if q == 1 else self.diag_x).wait_recv()

        def act(k):
            ours = self.near_send[q - 1, k, cut].astype(f32)
            out[k] = (ours + self.diag_recv[k, cut].astype(f32)).astype(bf16)

        self.each(act)

    def arrive_half(self):
        self.ready(0)
        self.nears[1, 0].wait_recv()
        self.nears[2, 1].wait_recv()

    def own_half(self, k):
        n1 = self.n1
        near = jnp.concatenate([self.near_recv[0, k, :n1], self.near_recv[1, k, n1:]], axis=0)
        return self.both(0, k) + near.astype(f32)

    def drain_half(self):
        self.diag_x.wait_send()
        self.diag_y.wait_send()
        self.nears[1, 0].wait_send()
        self.nears[2, 1].wait_send()

    def arrive(self):
        self.ready(0)
        for part in (0, 1):
            for q in (1, 2):
                self.nears[q, part].wait_recv()

    def own(self, k):
        return self.both(0, k) + self.near_recv[0, k].astype(f32) + self.near_recv[1, k].astype(f32)

    def drain(self):
        self.diag_x.wait_send()
        self.diag_y.wait_send()
        for copy in self.nears.values():
            copy.wait_send()


def plane_scratch(n):
    tile = (32, 128)
    return [
        pltpu.VMEM((4, 4, n) + tile, bf16),
        pltpu.VMEM((4, 4, n) + tile, bf16),
        pltpu.VMEM((4, n) + tile, bf16),
        pltpu.VMEM((4, n) + tile, bf16),
        pltpu.VMEM((2, 4, n) + tile, bf16),
        pltpu.VMEM((2, 4, n) + tile, bf16),
        pltpu.SemaphoreType.DMA((14, 2)),
    ]


def line_scratch(shape):
    return [
        pltpu.VMEM((4,) + shape, bf16),
        pltpu.VMEM((2, 4) + shape, bf16),
        pltpu.SemaphoreType.DMA((2, 4, 2)),
    ]


def return_kernel(pool, kv_ref, sum_ref, x_out, y_out, kv_out, *scratch):
    c, w = lax.axis_index("ctx"), lax.axis_index("wt")
    plane = Plane(pool, scratch[:6], scratch[6], c, w)
    line = Line(lambda k, j: kv_ref[k, j].astype(f32), *scratch[7:], c)
    plane.begin_loads()
    greet(c, w, 0)
    plane.begin()

    line.start()
    plane.diag()
    plane.near(1)
    plane.near(2)
    line.step(0)
    plane.join_out(1, x_out)
    line.step(1)
    plane.join_out(2, y_out)
    line.step(2)
    plane.arrive_half()

    def own(k):
        sum_ref[k] = plane.own_half(k).astype(bf16)

    plane.each(own)
    line.finish(kv_out)
    plane.drain_half()
    line.drain()


def back_home(pool, kv_terms):
    n = pool.shape[3]
    n1 = tile_halves(n)
    return pl.pallas_call(
        return_kernel,
        out_shape=[
            jax.ShapeDtypeStruct((4, n, 32, 128), bf16),
            jax.ShapeDtypeStruct((4, n - n1, 32, 128), bf16),
            jax.ShapeDtypeStruct((4, n1, 32, 128), bf16),
            jax.ShapeDtypeStruct(kv_terms.shape[1:], f32),
        ],
        in_specs=[ANY, VM],
        out_specs=[VM] * 4,
        scratch_shapes=plane_scratch(n) + line_scratch(kv_terms.shape[1:]),
        compiler_params=params(60, collective_id=2, has_side_effects=True),
        cost_estimate=cost(30e9, 16 << 20),
    )(pool, kv_terms)


def tail_kernel(pool, gain_ref, sum_ref, gain_out, own, gain_send, gain_recv, sems_gain, *scratch):
    c, w = lax.axis_index("ctx"), lax.axis_index("wt")
    plane = Plane(pool, scratch[:6], scratch[6], c, w)
    line = Line(lambda k, j: own[k, j], *scratch[7:10], c)
    plane.begin_loads()
    greet(c, w, 1)
    plane.begin()

    stages = [{"wt": w ^ 1}, {"wt": w ^ 2}, {"wt": w ^ 4}, {"ctx": c ^ 1}, {"ctx": c ^ 2}]
    copies = [
        remote(gain_send.at[i], gain_recv.at[i], sems_gain.at[i, 0], sems_gain.at[i, 1], stages[i]) for i in range(5)
    ]
    gain_send[0] = gain_ref[...]
    copies[0].start()

    def gain_step(i):
        copies[i].wait()
        total = gain_send[i] + gain_recv[i]
        if i < 4:
            gain_send[i + 1] = total
            copies[i + 1].start()
        else:
            gain_out[...] = total

    plane.diag()
    gain_step(0)
    plane.near(1)
    plane.near(2)
    gain_step(1)
    plane.join(1)
    plane.join(2)
    gain_step(2)
    plane.arrive()

    def own_sum(k):
        own[k] = plane.own(k)

    plane.each(own_sum)
    line.start()
    gain_step(3)
    for number in range(3):
        line.step(number)
    gain_step(4)
    line.finish(sum_ref)
    plane.drain()
    line.drain()


def tail(pool, gains):
    n = pool.shape[3]
    tile = (32, 128)
    return pl.pallas_call(
        tail_kernel,
        out_shape=[
            jax.ShapeDtypeStruct((n,) + tile, f32),
            jax.ShapeDtypeStruct(gains.shape, f32),
        ],
        in_specs=[ANY, VM],
        out_specs=[VM, VM],
        scratch_shapes=[
            pltpu.VMEM((4, n) + tile, f32),
            pltpu.VMEM((5,) + gains.shape, f32),
            pltpu.VMEM((5,) + gains.shape, f32),
            pltpu.SemaphoreType.DMA((5, 2)),
        ]
        + plane_scratch(n)
        + line_scratch((n,) + tile),
        compiler_params=params(48, collective_id=1, has_side_effects=True),
        cost_estimate=cost(30e9, 16 << 20),
    )(pool, gains)


META = 4


def load_blocks(meta, part, pool, sems):
    blk = part.shape[2] // 2
    copies = []
    for k in range(2 * part.shape[0]):
        at = pl.multiple_of(meta[META + k] * blk, blk)
        source = part.at[k // 2, :, pl.ds(k % 2 * blk, blk), :]
        copies.append(pltpu.make_async_copy(source, pool.at[:, pl.ds(at, blk), :], sems.at[k]))
    for copy in copies:
        copy.start()
    for copy in copies:
        copy.wait()


def masked(scores, block, q_block, length):
    blk = scores.shape[1]
    key = block + lax.broadcasted_iota(jnp.int32, scores.shape, 0)
    query = q_block * blk + lax.broadcasted_iota(jnp.int32, scores.shape, 1)
    return jnp.where(jnp.logical_and(key <= query, key < length), scores, blocked_score)


def nt_dot(a, b):
    return lax.dot_general(a, b, (((1,), (1,)), ((), ())), preferred_element_type=f32)


def tn_dot(a, b):
    return lax.dot_general(a, b, (((0,), (0,)), ((), ())), preferred_element_type=f32)


def flash_forward_kernel(meta, q_ref, part, out_ref, turned_ref, lse_ref, pool, vt, peak, acc, turned, sems):
    load_blocks(meta, part, pool, sems)
    length = meta[2]
    blk = q_ref.shape[1] // 2
    live_blocks = (length + blk - 1) // blk
    turned[960:, :] = jnp.zeros((64, blk), f32)
    for g in range(KVH):
        vt[g, :64, :] = jnp.ones((64, vt.shape[2]), bf16)
        for k in range(pool.shape[1] // 256):
            vt[g, 64:, 256 * k : 256 * k + 256] = pool[g, 256 * k : 256 * k + 256, :].T[64:]
    for qi in range(2):
        q_block = meta[qi]
        blocks = jnp.minimum(q_block + 1, live_blocks)

        def group(g, _):
            queries = [q_ref[GRP * g + h, blk * qi : blk * qi + blk, :] for h in range(GRP)]
            for h in range(GRP):
                peak[h] = jnp.full((1, blk), blocked_score, f32)
                acc[h] = jnp.zeros((128, blk), f32)

            def step(block, wide, with_mask):
                start = pl.multiple_of(block * blk, blk)
                span = pl.ds(start, wide * blk)
                kv = pool[g, span, :]
                vals = vt[g, :, span]
                scores = [nt_dot(kv, queries[h]) for h in range(GRP)]
                if with_mask:
                    scores = [masked(t, start, q_block, length) for t in scores]
                before = [peak[h] for h in range(GRP)]
                now = [jnp.maximum(before[h], jnp.max(scores[h], axis=0, keepdims=True)) for h in range(GRP)]
                weights = [jnp.exp(scores[h] - now[h]).astype(bf16) for h in range(GRP)]
                for h in range(GRP):
                    peak[h] = now[h]
                    acc[h] = acc[h] * jnp.exp(before[h] - now[h]) + jnp.dot(
                        vals, weights[h], preferred_element_type=f32
                    )

            def plain(pair, _):
                step(2 * pair, 2, False)
                return 0

            pairs = (blocks - 1) // 2

            def plain4(quad, _):
                step(4 * quad, 4, False)
                return 0

            lax.fori_loop(0, pairs // 2, plain4, 0)

            @pl.when(pairs % 2 == 1)
            def _():
                plain(pairs - 1, 0)

            @pl.when(blocks % 2 == 1)
            def _():
                step(blocks - 1, 1, True)

            @pl.when(blocks % 2 == 0)
            def _():
                step(blocks - 2, 2, True)

            for h in range(GRP):
                total = acc[h][0:1, :]
                turned[pl.ds(pl.multiple_of((GRP * g + h) * HD, HD), HD), :] = acc[h][64:, :] / total
                lse_ref[GRP * g + h, :, blk * qi : blk * qi + blk] = peak[h] + jnp.log(total)
            return 0

        lax.fori_loop(0, KVH, group, 0)
        out_ref[blk * qi : blk * qi + blk, :] = turned[...].T.astype(bf16)
        turned_ref[:, blk * qi : blk * qi + blk] = turned[...].astype(bf16)


def flash_forward(m, meta, q, part):
    n_ctx, _, rows, _ = part.shape
    blk = rows // 2
    return pl.pallas_call(
        flash_forward_kernel,
        grid=(1,),
        out_shape=[
            jax.ShapeDtypeStruct((rows, QP), bf16),
            jax.ShapeDtypeStruct((QP, rows), bf16),
            jax.ShapeDtypeStruct((16, 1, rows), f32),
        ],
        in_specs=[SM, pl.BlockSpec((QH, rows, 128), lambda i: (0, m, 0)), ANY],
        out_specs=[
            pl.BlockSpec((rows, QP), lambda i: (0, 0)),
            pl.BlockSpec((QP, rows), lambda i: (0, 0)),
            pl.BlockSpec((16, 1, rows), lambda i: (0, 0, 0)),
        ],
        scratch_shapes=[
            pltpu.VMEM((KVH, n_ctx * rows, 128), bf16),
            pltpu.VMEM((KVH, 128, n_ctx * rows), bf16),
            pltpu.VMEM((GRP, 1, blk), f32),
            pltpu.VMEM((GRP, 128, blk), f32),
            pltpu.VMEM((QP, blk), f32),
            pltpu.SemaphoreType.DMA((2 * n_ctx,)),
        ],
        compiler_params=params(48),
        cost_estimate=cost(40e9, 8 << 20),
    )(meta, q, part)


def flash_backward_kernel(
    meta, q_ref, out_ref, grad_ref, lse_ref, cos_ref, sin_ref, part, gq_ref, gkv_ref,
    pool, kt, wide, delta, total, acc, turned, sides, sems,
):
    load_blocks(meta, part, pool, sems)
    length = meta[2]
    rows = q_ref.shape[1]
    blk = rows // 2
    live_blocks = (length + blk - 1) // blk
    total[...] = jnp.zeros_like(total)
    lane = lax.broadcasted_iota(jnp.int32, (rows, 128), 1)
    pick = lax.broadcasted_iota(jnp.int32, (16, 128), 0) == lax.broadcasted_iota(jnp.int32, (16, 128), 1) // 64
    pick = jnp.where(pick, 1.0, 0.0).astype(bf16)
    for g in range(KVH):
        for k in range(pool.shape[1] // 256):
            kt[g, :, 256 * k : 256 * k + 256] = pool[g, 256 * k : 256 * k + 256, :].T[:64]
    for p in range(8):
        slab = grad_ref[:, 128 * p : 128 * p + 128].astype(f32)
        wide[2 * p] = jnp.where(lane >= 64, pltpu.roll(slab, 64, 1), 0.0).astype(bf16)
        if 2 * p + 1 < QH:
            wide[2 * p + 1] = jnp.where(lane >= 64, slab, 0.0).astype(bf16)
        product = slab * out_ref[:, 128 * p : 128 * p + 128].astype(f32)
        high = product.astype(bf16)
        low = (product - high.astype(f32)).astype(bf16)
        both = nt_dot(pick, high) + nt_dot(pick, low)
        delta[2 * p] = both[0:1, :]
        delta[2 * p + 1] = both[1:2, :]
    turned[960:, :] = jnp.zeros((64, blk), f32)
    for qi in range(2):
        q_block = meta[qi]
        blocks = jnp.where(q_block < live_blocks, q_block + 1, 0)
        span = slice(blk * qi, blk * qi + blk)

        def group(g, _):
            for h in range(GRP):
                acc[h] = jnp.zeros((64, blk), f32)
                sides[2 * blk * h : 2 * blk * h + blk] = q_ref[GRP * g + h, span, :]
                sides[2 * blk * h + blk : 2 * blk * h + 2 * blk] = wide[GRP * g + h, span, :]

            def step(block, count, with_mask):
                start = pl.multiple_of(block * blk, blk)
                keys = pl.ds(start, count * blk)
                kv = pool[g, keys, :]
                keys_t = kt[g, :, keys]
                heads = [GRP * g + h for h in range(GRP)]
                scores = [nt_dot(kv, sides[2 * blk * h : 2 * blk * h + blk]) for h in range(GRP)]
                inner = [nt_dot(kv, sides[2 * blk * h + blk : 2 * blk * h + 2 * blk]) for h in range(GRP)]
                if with_mask:
                    scores = [masked(t, start, q_block, length) for t in scores]
                probs = [jnp.exp(scores[h] - lse_ref[heads[h], :, span]) for h in range(GRP)]
                change = [(probs[h] * (inner[h] - delta[heads[h], :, span])).astype(bf16) for h in range(GRP)]
                terms = []
                for h in range(GRP):
                    terms += [change[h], probs[h].astype(bf16)]
                total[g, keys, :] += jnp.dot(
                    jnp.concatenate(terms, axis=1), sides[...], preferred_element_type=f32
                )
                for h in range(GRP):
                    acc[h] = acc[h] + jnp.dot(keys_t, change[h], preferred_element_type=f32)

            def plain(pair, _):
                step(2 * pair, 2, False)
                return 0

            lax.fori_loop(0, (blocks - 1) // 2, plain, 0)

            @pl.when(jnp.logical_and(blocks > 0, blocks % 2 == 1))
            def _():
                step(blocks - 1, 1, True)

            @pl.when(jnp.logical_and(blocks > 0, blocks % 2 == 0))
            def _():
                step(blocks - 2, 2, True)

            for h in range(GRP):
                turned[pl.ds(pl.multiple_of((GRP * g + h) * HD, HD), HD), :] = acc[h] * 0.125
            return 0

        lax.fori_loop(0, KVH, group, 0)
        grads = turned[...].T
        cosine, sine = cos_ref[span, :], sin_ref[span, :]
        for p in range(8):
            slab = grads[:, 128 * p : 128 * p + 128]
            gq_ref[span, 128 * p : 128 * p + 128] = (slab * cosine - swap_halves(slab) * sine).astype(bf16)
    for k in range(2 * gkv_ref.shape[0]):
        at = pl.multiple_of(meta[META + k] * blk, blk)
        gkv_ref[k // 2, :, k % 2 * blk : k % 2 * blk + blk, :] = total[:, pl.ds(at, blk), :].astype(bf16)


def flash_backward(m, meta, q, out, grad, lse, cosine, sine, part):
    n_ctx, _, rows, _ = part.shape
    blk = rows // 2
    return pl.pallas_call(
        flash_backward_kernel,
        grid=(1,),
        out_shape=[
            jax.ShapeDtypeStruct((rows, QP), bf16),
            jax.ShapeDtypeStruct((n_ctx, KVH, rows, 128), bf16),
        ],
        in_specs=[
            SM,
            pl.BlockSpec((QH, rows, 128), lambda i: (0, m, 0)),
            pl.BlockSpec((rows, QP), lambda i: (0, 0)),
            pl.BlockSpec((rows, QP), lambda i: (m, 0)),
            pl.BlockSpec((16, 1, rows), lambda i: (0, 0, 0)),
            pl.BlockSpec((rows, 128), lambda i: (0, 0)),
            pl.BlockSpec((rows, 128), lambda i: (0, 0)),
            ANY,
        ],
        out_specs=[
            pl.BlockSpec((rows, QP), lambda i: (0, 0)),
            pl.BlockSpec((n_ctx, KVH, rows, 128), lambda i: (0, 0, 0, 0)),
        ],
        scratch_shapes=[
            pltpu.VMEM((KVH, n_ctx * rows, 128), bf16),
            pltpu.VMEM((KVH, 64, n_ctx * rows), bf16),
            pltpu.VMEM((QH, rows, 128), bf16),
            pltpu.VMEM((16, 1, rows), f32),
            pltpu.VMEM((KVH, n_ctx * rows, 128), f32),
            pltpu.VMEM((GRP, 64, blk), f32),
            pltpu.VMEM((QP, blk), f32),
            pltpu.VMEM((2 * GRP * blk, 128), bf16),
            pltpu.SemaphoreType.DMA((2 * n_ctx,)),
        ],
        compiler_params=params(56),
        cost_estimate=cost(50e9, 16 << 20),
    )(meta, q, out, grad, lse, cosine, sine, part)


def assemble_ffn_kernel(table, pool_ref, gu_out, d_out, pool, wgu, wd, sems):
    load = pltpu.make_async_copy(pool_ref, pool, sems.at[0])
    load.start()
    load.wait()
    ffn_rows(pool, table, wgu, wd)
    stores = [pltpu.make_async_copy(wgu, gu_out, sems.at[1]), pltpu.make_async_copy(wd, d_out, sems.at[2])]
    for copy in stores:
        copy.start()
    for copy in stores:
        copy.wait()


def assemble_ffn(table, pool):
    shapes = [(D, 2 * FF), (FF, D)]
    return pl.pallas_call(
        assemble_ffn_kernel,
        out_shape=[jax.ShapeDtypeStruct(s, bf16) for s in shapes],
        in_specs=[SM, ANY],
        out_specs=[ANY, ANY],
        scratch_shapes=[pltpu.VMEM(s, bf16) for s in [pool.shape] + shapes] + [pltpu.SemaphoreType.DMA((3,))],
        compiler_params=params(52),
        cost_estimate=cost(0, 64 << 20),
    )(table, pool)


CHUNK = 512


def middle_kernel(
    scalars, gu_ref, d_ref, out_0, out_1, wo, x_ref, cot_ref, gain_ref,
    mixed_ref, normed_t, hidden_t, ggu_ref, go_ref, branch_ref, residual_ref, attn_ref, gain_out,
    wgu, wd, sems,
):
    i = pl.program_id(0)
    blk = x_ref.shape[0]
    loads = [pltpu.make_async_copy(gu_ref, wgu, sems.at[0]), pltpu.make_async_copy(d_ref, wd, sems.at[1])]

    @pl.when(i == 0)
    def _():
        for load in loads:
            load.start()

    attn = jnp.where(i < 2, out_0[...], out_1[...])
    residual = x_ref[...].astype(f32) + jnp.dot(attn, wo[...], preferred_element_type=f32)
    inverse = lax.rsqrt(jnp.mean(residual * residual, axis=1, keepdims=True) + epsilon)
    gain = gain_ref[...]
    normed = (residual * inverse * gain).astype(bf16)
    normed_t[...] = normed.T
    row = scalars[i % 2] * blk + lax.broadcasted_iota(jnp.int32, (blk, D), 0)
    grad_out = cot_ref[0].T
    grad_out = jnp.where(row < scalars[2 + i // 2], grad_out, jnp.zeros((), bf16))
    go_ref[...] = grad_out

    @pl.when(i == 0)
    def _():
        for load in loads:
            load.wait()

    def first(j):
        at = CHUNK * j
        return (
            jnp.dot(normed, wgu[:, at : at + CHUNK], preferred_element_type=f32),
            jnp.dot(normed, wgu[:, FF + at : FF + at + CHUNK], preferred_element_type=f32),
            nt_dot(grad_out, wd[at : at + CHUNK, :]),
        )

    mixed = residual
    grad_normed = jnp.zeros((blk, D), f32)
    ahead = first(0)
    for j in range(FF // CHUNK):
        at = CHUNK * j
        gate, up, grad_hidden = ahead
        if j + 1 < FF // CHUNK:
            ahead = first(j + 1)
        sigma = jax.nn.sigmoid(gate)
        silu = gate * sigma
        hidden = (silu * up).astype(bf16)
        grad_up = (grad_hidden * silu).astype(bf16)
        grad_gate = (grad_hidden * up * (sigma + silu * (1.0 - sigma))).astype(bf16)
        hidden_t[at : at + CHUNK, :] = hidden.T
        ggu_ref[:, at : at + CHUNK] = grad_gate
        ggu_ref[:, FF + at : FF + at + CHUNK] = grad_up
        mixed = mixed + jnp.dot(hidden, wd[at : at + CHUNK, :], preferred_element_type=f32)
        grad_normed = grad_normed + nt_dot(grad_gate, wgu[:, at : at + CHUNK])
        grad_normed = grad_normed + nt_dot(grad_up, wgu[:, FF + at : FF + at + CHUNK])

    mixed_ref[0] = mixed.astype(bf16).T
    unit = residual * inverse
    scaled = grad_normed * gain
    back = inverse * (scaled - unit * jnp.mean(scaled * unit, axis=1, keepdims=True))
    grad_residual = grad_out.astype(f32) + back
    residual_ref[...] = grad_residual
    branch = grad_residual.astype(bf16)
    branch_ref[...] = branch
    attn_ref[...] = nt_dot(branch, wo[...]).astype(bf16)
    term = jnp.sum(grad_normed * unit, axis=0, keepdims=True)

    @pl.when(i == 0)
    def _():
        gain_out[...] = term

    @pl.when(i > 0)
    def _():
        gain_out[...] += term


def middle(scalars, wgu, wd, outs, wo, x_rows, cot_t, gain):
    micro, _, rows = cot_t.shape
    tokens = micro * rows
    blk = rows // 2

    def rows_of(width, kind):
        return jax.ShapeDtypeStruct((tokens, width), kind), pl.BlockSpec((blk, width), lambda i: (i, 0))

    def columns_of(height):
        return jax.ShapeDtypeStruct((height, tokens), bf16), pl.BlockSpec((height, blk), lambda i: (0, i))

    native = pl.BlockSpec((1, D, blk), lambda i: (i // 2, 0, i % 2))
    whole = pl.BlockSpec((1, D), lambda i: (0, 0))
    results = [
        (jax.ShapeDtypeStruct((micro, D, rows), bf16), native),
        columns_of(D),
        columns_of(FF),
        rows_of(2 * FF, bf16),
        rows_of(D, bf16),
        rows_of(D, bf16),
        rows_of(D, f32),
        rows_of(QP, bf16),
        (jax.ShapeDtypeStruct((1, D), f32), whole),
    ]
    return pl.pallas_call(
        middle_kernel,
        grid=(2 * micro,),
        out_shape=[r[0] for r in results],
        in_specs=[
            SM,
            ANY,
            ANY,
            pl.BlockSpec((blk, QP), lambda i: (jnp.minimum(i, 1), 0)),
            pl.BlockSpec((blk, QP), lambda i: (jnp.maximum(i - 2, 0), 0)),
            pl.BlockSpec((QP, D), lambda i: (0, 0)),
            pl.BlockSpec((blk, D), lambda i: (i, 0)),
            native,
            whole,
        ],
        out_specs=[r[1] for r in results],
        scratch_shapes=[
            pltpu.VMEM((D, 2 * FF), bf16),
            pltpu.VMEM((FF, D), bf16),
            pltpu.SemaphoreType.DMA((2,)),
        ],
        compiler_params=params(62),
        cost_estimate=cost(40e9, 40 << 20),
    )(scalars, wgu, wd, outs[0], outs[1], wo, x_rows, cot_t, gain)


def ffn_grads_kernel(table, normed_t, ggu_ref, hidden_t, go_ref, pool_out, pool, gu_0, d_0, gu_1, d_1, sems):
    j = pl.program_id(0)
    steps = pl.num_programs(0)

    def multiply(part, gu, d):
        columns = slice(512 * part, 512 * part + 512)
        gu[...] = jnp.dot(normed_t[...], ggu_ref[:, columns], preferred_element_type=f32).astype(bf16)
        rows = slice(256 * part, 256 * part + 256)
        d[...] = jnp.dot(hidden_t[rows, :], go_ref[...], preferred_element_type=f32).astype(bf16)

    def put(chunk, gu, d):
        base = 600 * (chunk // 5) + 8 * (chunk % 5)
        for r in range(15):
            for p in range(4):
                at = base + r * 40 + 2 * p
                pick_pair(pool, table, gu, 64 * r, 128 * p, at, at + 1)
        for r in range(4):
            at = 1200 + (4 * chunk + r) * 15
            for p in range(7):
                pick_pair(pool, table, d, 64 * r, 128 * p, at + 2 * p, at + 2 * p + 1)
            pick_single(pool, table, d, 64 * r, 896, at + 14)

    put((2 * j + 2 * steps - 1) % (2 * steps), gu_1, d_1)
    multiply(0, gu_0, d_0)
    put(2 * j, gu_0, d_0)
    multiply(1, gu_1, d_1)

    @pl.when(j == steps - 1)
    def _():
        put(2 * steps - 1, gu_1, d_1)
        flush_pool(pool, [pool_out], sems)


def ffn_grads(table, normed_t, ggu, hidden_t, go, total):
    tokens = go.shape[0]
    return pl.pallas_call(
        ffn_grads_kernel,
        grid=(5,),
        out_shape=jax.ShapeDtypeStruct((total, 32, 128), bf16),
        in_specs=[
            SM,
            pl.BlockSpec((D, tokens), lambda j: (0, 0)),
            pl.BlockSpec((tokens, 1024), lambda j: (0, j)),
            pl.BlockSpec((512, tokens), lambda j: (j, 0)),
            pl.BlockSpec((tokens, D), lambda j: (0, 0)),
        ],
        out_specs=ANY,
        scratch_shapes=[
            pltpu.VMEM((total, 32, 128), bf16),
            pltpu.VMEM((D, 512), bf16),
            pltpu.VMEM((256, D), bf16),
            pltpu.VMEM((D, 512), bf16),
            pltpu.VMEM((256, D), bf16),
            pltpu.SemaphoreType.DMA((1,)),
        ],
        compiler_params=params(52),
        cost_estimate=cost(15e9, 60 << 20),
    )(table, normed_t, ggu, hidden_t, go)


def inward_kernel(
    table, gq_0, gq_1, gkv_0, gkv_1, cos_ref, sin_ref, w_ref, normed_t, out_0, out_1,
    branch_ref, x_ref, residual_ref, gain_ref, grad_ref, gain_out, pool_out,
    cat, dqkv, dwo, pool, sems,
):
    i = pl.program_id(0)
    blk = x_ref.shape[0]
    half = branch_ref.shape[0] // 2
    early = i < 2
    at = pl.ds(pl.multiple_of(i * blk, blk), blk)
    cosine, sine = cos_ref[...], sin_ref[...]
    left = lax.broadcasted_iota(jnp.int32, (blk, 128), 1) < 64
    key_cosine = jnp.where(left, cosine, 1.0)
    key_sine = jnp.where(left, sine, 0.0)
    parts = [jnp.where(early, gq_0[...], gq_1[...])]
    for g in range(KVH):
        slab = jnp.where(early, gkv_0[g].astype(f32), gkv_1[g])
        parts.append((slab * key_cosine - swap_halves(slab) * key_sine).astype(bf16))
    terms = jnp.concatenate(parts, axis=1)
    cat[at, :] = terms
    grad_normed = nt_dot(terms, w_ref[...])
    new_wo = jnp.dot(out_0[...], branch_ref[:half, :], preferred_element_type=f32)
    new_wo = new_wo + jnp.dot(out_1[...], branch_ref[half:, :], preferred_element_type=f32)
    dwo[...] = new_wo.astype(bf16)
    x = x_ref[...].astype(f32)
    inverse = lax.rsqrt(jnp.mean(x * x, axis=1, keepdims=True) + epsilon)
    unit = x * inverse
    scaled = grad_normed * gain_ref[...]
    back = inverse * (scaled - unit * jnp.mean(scaled * unit, axis=1, keepdims=True))
    grad_ref[0] = (residual_ref[...] + back).T
    term = jnp.sum(grad_normed * unit, axis=0, keepdims=True)
    for r in range(4):
        first = 375 + (4 * i + r) * 15
        for p in range(7):
            pick_pair(pool, table, dwo, 64 * r, 128 * p, first + 2 * p, first + 2 * p + 1)
        pick_single(pool, table, dwo, 64 * r, 896, first + 14)

    @pl.when(i == 0)
    def _():
        gain_out[...] = term

    @pl.when(i > 0)
    def _():
        gain_out[...] += term

    @pl.when(i == pl.num_programs(0) - 1)
    def _():
        for low, high in ((0, 512), (512, QP), (QP, CW)):
            dqkv[:, low:high] = jnp.dot(
                normed_t[...], cat[:, low:high], preferred_element_type=f32
            ).astype(bf16)
        for p in range(7):
            for r in range(15):
                pick_pair(pool, table, dqkv, 64 * r, 128 * p, r * 15 + 2 * p, r * 15 + 2 * p + 1)
        for r in range(15):
            pick_single(pool, table, dqkv, 64 * r, 896, r * 15 + 14)
        for g in range(KVH):
            for r in range(15):
                pick_pair(pool, table, dqkv, 64 * r, QP + 128 * g, 225 + r * 5 + g, 300 + r * 5 + g)
        flush_pool(pool.at[pl.ds(0, pool_out.shape[0])], [pool_out], sems)


def inward(table, gq, gkv, cosine, sine, wqkv, normed_t, outs_t, branch, x_rows, residual, gain, total):
    rows = cosine.shape[0]
    tokens = x_rows.shape[0]
    blk = rows // 2
    steps = tokens // blk
    table = jnp.concatenate([table, jnp.full((15,), total, jnp.int32)])

    def early(i):
        return jnp.minimum(i, 1)

    def late(i):
        return jnp.maximum(i - 2, 0)

    def rows_of(width, at=lambda i: i):
        return pl.BlockSpec((blk, width), lambda i: (at(i), 0))

    def slabs(at):
        return pl.BlockSpec((KVH, blk, 128), lambda i: (0, at(i), 0))

    def all_of(*shape):
        return pl.BlockSpec(shape, lambda i: (0, 0))

    features = pl.BlockSpec((QP // steps, rows), lambda i: (i, 0))
    return pl.pallas_call(
        inward_kernel,
        grid=(steps,),
        out_shape=[
            jax.ShapeDtypeStruct((tokens // rows, D, rows), f32),
            jax.ShapeDtypeStruct((1, D), f32),
            jax.ShapeDtypeStruct((total, 32, 128), bf16),
        ],
        in_specs=[
            SM, rows_of(QP, early), rows_of(QP, late), slabs(early), slabs(late),
            rows_of(128, lambda i: i % 2), rows_of(128, lambda i: i % 2),
            all_of(D, CW), all_of(D, tokens), features, features,
            all_of(tokens, D), rows_of(D), rows_of(D), all_of(1, D),
        ],
        out_specs=[pl.BlockSpec((1, D, blk), lambda i: (i // 2, 0, i % 2)), all_of(1, D), ANY],
        scratch_shapes=[
            pltpu.VMEM((tokens, CW), bf16),
            pltpu.VMEM((D, CW), bf16),
            pltpu.VMEM((QP // steps, D), bf16),
            pltpu.VMEM((total + 1, 32, 128), bf16),
            pltpu.SemaphoreType.DMA((1,)),
        ],
        compiler_params=params(60),
        cost_estimate=cost(12e9, 30 << 20),
    )(table, *gq, *gkv, cosine, sine, wqkv, normed_t, *outs_t, branch, x_rows, residual, gain)


TOGETHER = 11


def shampoo_kernel(
    filled, sum_a, sum_f, master, stat_left, stat_right, root_left, root_right,
    grads_out, left_out, right_out, master_out, grads, lefts, rights, gram_left, gram_right, step,
):
    slots = master.shape[1]
    n_a = sum_a.shape[0] // 32
    for source, target in ((root_left, lefts), (root_right, rights)):
        for r in range(32):
            both = jnp.concatenate(
                [source[64 * r : 64 * r + 64, :], source[64 * (r + 32) : 64 * (r + 32) + 64, :]], axis=0
            )
            target[pl.ds(r, slots, stride=32), :] = both.T

    def square(rows):
        return jnp.concatenate([rows[:, :64], rows[:, 64:]], axis=0)

    def folded(rows):
        return jnp.concatenate([rows[:32], rows[32:]], axis=1)

    def keep(source, count, shift):
        def one(s, _):
            grad = source[pl.ds(pl.multiple_of(s * 32, 32), 32), :]
            at = pl.ds(pl.multiple_of((s + shift) * 32, 32), 32)
            grads[at, :] = jnp.where(filled[s + shift] > 0, grad.astype(f32), 0.0)
            return 0

        lax.fori_loop(0, count, one, 0, unroll=8)

    keep(sum_a, n_a, 0)
    keep(sum_f, slots - n_a, n_a)

    def several(i, _):
        spans = [pl.ds(pl.multiple_of((TOGETHER * i + t) * 32, 32), 32) for t in range(TOGETHER)]
        grad = [square(grads[span, :]).astype(bf16) for span in spans]
        left = [square(lefts[span, :]).astype(bf16) for span in spans]
        right = [square(rights[span, :]).astype(bf16) for span in spans]
        half = [jnp.dot(a, g, preferred_element_type=f32) for a, g in zip(left, grad)]
        gram_l = [nt_dot(g, g) for g in grad]
        gram_r = [tn_dot(g, g) for g in grad]
        whole = [jnp.dot(h.astype(bf16), b, preferred_element_type=f32) for h, b in zip(half, right)]
        for t, span in enumerate(spans):
            gram_left[span, :] = folded(gram_l[t])
            gram_right[span, :] = folded(gram_r[t])
            step[span, :] = folded(whole[t])
        return 0

    lax.fori_loop(0, grads.shape[0] // (32 * TOGETHER), several, 0)

    for r in range(32):
        first = slice(64 * r, 64 * r + 64)
        second = slice(64 * (r + 32), 64 * (r + 32) + 64)
        rows = pl.ds(r, slots, stride=32)
        flipped = grads[rows, :].T
        grads_out[first, :] = flipped[:64]
        grads_out[second, :] = flipped[64:]
        for source, stat, out in ((gram_left, stat_left, left_out), (gram_right, stat_right, right_out)):
            flipped = source[rows, :].T
            out[first, :] = decay_rate * stat[first, :] + (1.0 - decay_rate) * flipped[:64]
            out[second, :] = decay_rate * stat[second, :] + (1.0 - decay_rate) * flipped[64:]
        flipped = step[rows, :].T
        master_out[first, :] = master[first, :] - step_rate * flipped[:64]
        master_out[second, :] = master[second, :] - step_rate * flipped[64:]


def shampoo(filled, sum_a, sum_f, *arrays):
    slots = arrays[0].shape[0]
    native = [a.transpose(1, 2, 0).reshape(TL * TL, slots) for a in arrays]
    scratch = pltpu.VMEM((-(-slots // TOGETHER) * TOGETHER * 32, 128), f32)
    results = pl.pallas_call(
        shampoo_kernel,
        out_shape=[jax.ShapeDtypeStruct((TL * TL, slots), f32)] * 4,
        in_specs=[SM] + [VM] * 7,
        out_specs=[VM] * 4,
        scratch_shapes=[scratch] * 6,
        compiler_params=params(48),
        cost_estimate=cost(1e9, 24 << 20),
    )(filled, sum_a.reshape(-1, 128), sum_f.reshape(-1, 128), *native)
    return [r.reshape(TL, TL, slots).transpose(2, 0, 1) for r in results]


def fold(tiles):
    return jnp.concatenate([tiles[:, :32, :], tiles[:, 32:, :]], axis=2)


def shards(
    inputs,
    cotangent,
    lengths,
    order,
    owner_slots,
    master,
    stat_left,
    stat_right,
    root_left,
    root_right,
    gains,
    gain_stats,
):
    micro, rows = inputs.shape[1], inputs.shape[2]
    n_ctx, n_wt = lax.axis_size("ctx"), lax.axis_size("wt")
    devices = n_ctx * n_wt
    line = is_line(n_ctx, n_wt)
    tokens = micro * rows
    cap = master.shape[0]
    cap_a = NTA // devices + NTA // (8 * devices) + 2
    cap_f = cap - cap_a
    c = lax.axis_index("ctx")
    w = lax.axis_index("wt")

    x_t = inputs[0].transpose(0, 2, 1)
    low_master = fold(master.astype(bf16))
    own_a, own_f = low_master[:cap_a], low_master[cap_a:]
    own_a, own_f = low_master[:cap_a], low_master[cap_a:]
    owner, within = owner_slots // cap, owner_slots % cap
    whole_a = owner[:NTA] * cap_a + within[:NTA]
    whole_f = owner[NTA:] * cap_f + within[NTA:] - cap_a

    blocks = order.shape[0]
    ids = jnp.arange(blocks, dtype=jnp.int32)
    my_blocks = jnp.sum(jnp.where(ids[None, :] == 2 * c + jnp.arange(2)[:, None], order[None, :], 0), axis=1)
    position = (my_blocks[:, None] * (rows // 2) + jnp.arange(rows // 2, dtype=jnp.int32)[None, :]).reshape(rows)
    lane = np.arange(128)
    frequency = jnp.asarray(rope_base, f32) ** (-(jnp.asarray(lane % 32, f32)) * 2.0 / HD)
    angle = position.astype(f32)[:, None] * frequency[None, :]
    cosine = jnp.cos(angle)
    sine = jnp.sin(angle) * jnp.where(lane % 64 < 32, -1.0, 1.0).astype(f32)[None, :]
    metas = [
        jnp.concatenate([my_blocks, lengths[0, m][None], c[None], order]).astype(jnp.int32)
        for m in range(micro)
    ]

    if line:
        q, normed_attn_t, x_low, kv_first, kv_late, wqkv, wo, pool_f = front(
            whole_a, own_a, own_f, x_t, gains[0:1], cosine, sine
        )
        pool_f = pool_f.reshape(devices * cap_f, 32, 128)
        chunks = [kv_first, lax.all_gather(kv_late, "ctx", axis=0)]
    else:
        parts_a = [lax.all_gather(own_a, AXES, axis=0, tiled=True)]
        pool_f = lax.all_gather(own_f, AXES, axis=0, tiled=True)
        wqkv, wo = assemble(assemble_attn_kernel, parts_a, whole_a, [(D, CW), (QP, D)])
        x_low = inputs.reshape(tokens, D)
        q, kv, normed_attn = qkv_rows(x_low, gains[0:1], wqkv, cosine, sine, micro)
        normed_attn_t = normed_attn.T
        chunks = [lax.all_gather(kv[m], "ctx", axis=0) for m in range(micro)]
    forward = [flash_forward(0, metas[0], q, chunks[0])]
    wgu, wd = assemble_ffn(after(whole_f, forward[0][0]), pool_f)
    forward.append(flash_forward(1, metas[1], q, after(chunks[1], wgu)))
    scalars = jnp.concatenate([my_blocks, lengths[0]]).astype(jnp.int32)
    cot_t = cotangent[0].transpose(0, 2, 1)
    outs = [f[0] for f in forward]
    (mixed_t, normed_ffn_t, hidden_t, grad_gu, grad_out, grad_branch, grad_residual, grad_attn, gain_ffn) = middle(
        scalars, wgu, wd, outs, wo, x_low, cot_t, gains[1:2]
    )
    def flash_back(m):
        out, _, lse = forward[m]
        return flash_backward(m, metas[m], q, out, grad_attn, lse, cosine, sine, chunks[m])

    gq_0, gkv_0 = flash_back(0)
    gkv_0 = lax.psum_scatter(gkv_0, "ctx", scatter_dimension=0, tiled=False)
    grad_out = after(grad_out, gq_0)
    pool_f = ffn_grads(whole_f, normed_ffn_t, grad_gu, hidden_t, grad_out, devices * cap_f)
    grad_attn = after(grad_attn, pool_f)
    gq_1, gkv_1 = flash_back(1)
    if line:
        near_f, half_x, half_y, gkv_1 = back_home(pool_f.reshape(4, 4, 2, cap_f, 32, 128), gkv_1)
        other_x, other_y = flip(half_x, 2), flip(half_y, 4)
    else:
        sum_f = lax.psum_scatter(pool_f.astype(f32), AXES, scatter_dimension=0, tiled=True)
        gkv_1 = lax.psum_scatter(gkv_1, "ctx", scatter_dimension=0, tiled=False).astype(f32)
    input_grad_t, gain_attn, pool_a = inward(
        whole_a, (gq_0, gq_1), (gkv_0, gkv_1), cosine, sine, wqkv, normed_attn_t, [f[1] for f in forward], grad_branch, x_low,
        grad_residual, gains[0:1], devices * cap_a,
    )
    gain_terms = jnp.concatenate([gain_attn, gain_ffn])
    if line:
        others = jnp.concatenate(after([other_y, other_x], pool_a), axis=1)
        near_f = (near_f.astype(f32) + others.astype(f32)).astype(bf16)
        sum_f = lax.psum_scatter(near_f, "ctx", scatter_dimension=0, tiled=False)
        gain_rows = jnp.pad(gain_terms.reshape(15, 128), ((0, 1), (0, 0)))
        sum_a, gain_rows = tail(pool_a.reshape(4, 4, 2, cap_a, 32, 128), gain_rows)
        gain_grads = gain_rows[:15].reshape(2, D)
    else:
        sum_a = lax.psum_scatter(pool_a.astype(f32), AXES, scatter_dimension=0, tiled=True)
        gain_grads = lax.psum(gain_terms, AXES)

    here = (c * n_wt + w) * cap + jnp.arange(cap, dtype=jnp.int32)
    filled = jnp.max((owner_slots[None, :] == here[:, None]).astype(jnp.int32), axis=1)
    tile_grads, new_left, new_right, new_master = shampoo(
        filled, sum_a, sum_f, master, stat_left, stat_right, root_left, root_right
    )
    new_gain_stats = decay_rate * gain_stats + (1.0 - decay_rate) * gain_grads * gain_grads
    new_gains = gains - gain_rate * gain_grads * lax.rsqrt(new_gain_stats)
    return (
        mixed_t.transpose(0, 2, 1)[None],
        input_grad_t.transpose(0, 2, 1)[None],
        tile_grads,
        new_left,
        new_right,
        new_master,
        gain_grads,
        new_gain_stats,
        new_gains,
    )


def solution(mesh):
    in_specs = (
        P("wt", None, "ctx", None),
        P("wt", None, "ctx", None),
        P("wt", None),
        P(),
        P(),
        P(AXES, None, None),
        P(AXES, None, None),
        P(AXES, None, None),
        P(AXES, None, None),
        P(AXES, None, None),
        P(),
        P(),
    )
    out_specs = (
        P("wt", None, "ctx", None),
        P("wt", None, "ctx", None),
        P(AXES, None, None),
        P(AXES, None, None),
        P(AXES, None, None),
        P(AXES, None, None),
        P(),
        P(),
        P(),
    )
    return jax.shard_map(shards, mesh=mesh, in_specs=in_specs, out_specs=out_specs, check_vma=False)
```

```python
import functools

import jax
import jax.numpy as jnp
import numpy as np
from jax import lax
from jax.experimental import pallas as pl
from jax.experimental.pallas import tpu as pltpu
from jax.sharding import PartitionSpec as P

D = 960
FF = 2560
QH = 15
KVH = 5
HD = 64
TL = 64
QW = 960
KVW = 320
GRP = 3
NTA = 600
NT = 2400
QP = 1024
CW = 1664
BLK = 256
AXES = ("ctx", "wt")

epsilon = 1e-05
decay_rate = 0.95
step_rate = 0.05
gain_rate = 0.05
rope_base = 10000.0
blocked_score = -1e30
bf16 = jnp.bfloat16
f32 = jnp.float32
VM = pl.BlockSpec(memory_space=pltpu.VMEM)
SM = pl.BlockSpec(memory_space=pltpu.SMEM)
ANY = pl.BlockSpec(memory_space=pl.ANY)


def params(megabytes, **kwargs):
    return pltpu.CompilerParams(vmem_limit_bytes=megabytes << 20, **kwargs)


def cost(flops, nbytes, trans=0):
    return pl.CostEstimate(flops=int(flops), bytes_accessed=int(nbytes), transcendentals=int(trans))


def after(x, *others):
    return lax.optimization_barrier((x, others))[0]


def is_line(n_ctx, n_wt):
    return n_ctx == 4 and n_wt == 8


def flip(x, bit):
    return lax.ppermute(x, "wt", [(i, i ^ bit) for i in range(8)])


def tile_halves(n):
    return (n + 1) // 2


def load_parts(parts, pool, sems):
    at = 0
    copies = []
    for i, part in enumerate(parts):
        rows = part.shape[0]
        copies.append(pltpu.make_async_copy(part, pool.at[pl.ds(at, rows)], sems.at[i]))
        at += rows
    for copy in copies:
        copy.start()
    for copy in copies:
        copy.wait()


def place_pair(pool, table, ref, row, lane, a, b):
    first = pool[table[a]]
    second = pool[table[b]]
    ref[pl.ds(row, 32), lane : lane + 128] = jnp.concatenate([first[:, :64], second[:, :64]], axis=1)
    ref[pl.ds(row + 32, 32), lane : lane + 128] = jnp.concatenate([first[:, 64:], second[:, 64:]], axis=1)


def place_single(pool, table, ref, row, lane, a):
    first = pool[table[a]]
    ref[pl.ds(row, 32), lane : lane + 64] = first[:, :64]
    ref[pl.ds(row + 32, 32), lane : lane + 64] = first[:, 64:]


def assemble_attn_kernel(count, table, *refs):
    parts, (wqkv, wo, pool, sems) = refs[:count], refs[count:]
    load_parts(parts, pool, sems)
    attn_rows(pool, table, wqkv, wo)


def attn_rows(pool, table, wqkv, wo):
    def qkv_row(r, _):
        row = pl.multiple_of(r * 64, 64)
        for p in range(7):
            place_pair(pool, table, wqkv, row, 128 * p, r * 15 + 2 * p, r * 15 + 2 * p + 1)
        place_single(pool, table, wqkv, row, 896, r * 15 + 14)
        wqkv[pl.ds(row, 64), 960:1024] = jnp.zeros((64, 64), bf16)
        for g in range(KVH):
            place_pair(pool, table, wqkv, row, QP + 128 * g, 225 + r * 5 + g, 300 + r * 5 + g)
        for p in range(7):
            place_pair(pool, table, wo, row, 128 * p, 375 + r * 15 + 2 * p, 375 + r * 15 + 2 * p + 1)
        place_single(pool, table, wo, row, 896, 375 + r * 15 + 14)
        return 0

    lax.fori_loop(0, 15, qkv_row, 0)
    wo[pl.ds(960, 64), :] = jnp.zeros((64, D), bf16)


def gu_rows(pool, table, wgu, first, last):
    def gu_row(r, _):
        row = pl.multiple_of(r * 64, 64)
        for m in range(2):
            for p in range(20):
                base = 600 * m + r * 40 + 2 * p
                place_pair(pool, table, wgu, row, FF * m + 128 * p, base, base + 1)
        return 0

    lax.fori_loop(first, last, gu_row, 0)


def d_rows(pool, table, wd, first, last):
    def d_row(r, _):
        row = pl.multiple_of(r * 64, 64)
        for p in range(7):
            place_pair(pool, table, wd, row, 128 * p, 1200 + r * 15 + 2 * p, 1200 + r * 15 + 2 * p + 1)
        place_single(pool, table, wd, row, 896, 1200 + r * 15 + 14)
        return 0

    lax.fori_loop(first, last, d_row, 0)


def assemble(kernel, parts, table, shapes):
    total = sum(p.shape[0] for p in parts)
    out_bytes = sum(2 * a * b for a, b in shapes)
    return pl.pallas_call(
        functools.partial(kernel, len(parts)),
        out_shape=[jax.ShapeDtypeStruct(s, bf16) for s in shapes],
        in_specs=[SM] + [ANY] * len(parts),
        out_specs=[VM] * len(shapes),
        scratch_shapes=[pltpu.VMEM((total, 32, 128), bf16), pltpu.SemaphoreType.DMA((len(parts),))],
        compiler_params=params(52),
        cost_estimate=cost(0, 4 * out_bytes),
    )(table, *parts)


def pick_pair(pool, table, ref, row, lane, a, b):
    block = ref[pl.ds(row, 64), lane : lane + 128]
    pool[table[a]] = jnp.concatenate([block[:32, :64], block[32:, :64]], axis=1)
    pool[table[b]] = jnp.concatenate([block[:32, 64:], block[32:, 64:]], axis=1)


def pick_single(pool, table, ref, row, lane, a):
    block = ref[pl.ds(row, 64), lane : lane + 64]
    pool[table[a]] = jnp.concatenate([block[:32], block[32:]], axis=1)


def flush_pool(pool, outs, sems):
    at = 0
    copies = []
    for i, out in enumerate(outs):
        rows = out.shape[0]
        copies.append(pltpu.make_async_copy(pool.at[pl.ds(at, rows)], out, sems.at[i]))
        at += rows
    for copy in copies:
        copy.start()
    for copy in copies:
        copy.wait()


def swap_halves(x):
    lane = lax.broadcasted_iota(jnp.int32, x.shape, 1)
    return jnp.where(lane % 64 < 32, pltpu.roll(x, 96, 1), pltpu.roll(x, 32, 1))


def qkv_kernel(x_ref, gain_ref, w_ref, cos_ref, sin_ref, q_ref, kv_ref, normed_ref):
    x = x_ref[...].astype(f32)
    inverse = lax.rsqrt(jnp.mean(x * x, axis=1, keepdims=True) + epsilon)
    normed = (x * inverse * gain_ref[...]).astype(bf16)
    normed_ref[...] = normed
    cosine, sine = cos_ref[...], sin_ref[...]
    lane = lax.broadcasted_iota(jnp.int32, cosine.shape, 1)
    left = lane < 64
    for p in range(8):
        rows = jnp.dot(normed, w_ref[:, 128 * p : 128 * p + 128], preferred_element_type=f32)
        rows = (rows * cosine + swap_halves(rows) * sine).astype(bf16).astype(f32) * 0.125
        q_ref[2 * p] = jnp.where(left, rows, 0.0).astype(bf16)
        if 2 * p + 1 < QH:
            q_ref[2 * p + 1] = jnp.where(left, pltpu.roll(rows, 64, 1), 0.0).astype(bf16)
    cosine = jnp.where(left, cosine, 1.0)
    sine = jnp.where(left, sine, 0.0)
    for g in range(KVH):
        at = QP + 128 * g
        rows = jnp.dot(normed, w_ref[:, at : at + 128], preferred_element_type=f32)
        kv_ref[0, g] = (rows * cosine + swap_halves(rows) * sine).astype(bf16)


def qkv_rows(x, gain, wqkv, cosine, sine, micro):
    tokens = x.shape[0]
    rows = tokens // micro
    blk = min(BLK, rows)
    steps = tokens // blk
    per = steps // micro
    return pl.pallas_call(
        qkv_kernel,
        grid=(steps,),
        out_shape=[
            jax.ShapeDtypeStruct((QH, tokens, 128), bf16),
            jax.ShapeDtypeStruct((micro, KVH, rows, 128), bf16),
            jax.ShapeDtypeStruct((tokens, D), bf16),
        ],
        in_specs=[
            pl.BlockSpec((blk, D), lambda i: (i, 0)),
            pl.BlockSpec((1, D), lambda i: (0, 0)),
            pl.BlockSpec((D, CW), lambda i: (0, 0)),
            pl.BlockSpec((blk, 128), lambda i: (i % per, 0)),
            pl.BlockSpec((blk, 128), lambda i: (i % per, 0)),
        ],
        out_specs=[
            pl.BlockSpec((QH, blk, 128), lambda i: (0, i, 0)),
            pl.BlockSpec((1, KVH, blk, 128), lambda i: (i // per, 0, i % per, 0)),
            pl.BlockSpec((blk, D), lambda i: (i, 0)),
        ],
        compiler_params=params(40),
        cost_estimate=cost(2 * tokens * D * CW, 14 << 20),
    )(x, gain, wqkv, cosine, sine)


def remote(src, dst, send, recv, device):
    return pltpu.make_async_remote_copy(
        src_ref=src,
        dst_ref=dst,
        send_sem=send,
        recv_sem=recv,
        device_id=device,
        device_id_type=pl.DeviceIdType.MESH,
    )


def greet(c, w, far):
    barrier = pltpu.get_barrier_semaphore()

    def hail(device):
        pl.semaphore_signal(barrier, inc=1, device_id=device, device_id_type=pl.DeviceIdType.MESH)

    for bit in (1, 2, 4):
        hail({"wt": w ^ bit})
    if far:
        hail({"ctx": c ^ 2})

    @pl.when(c < 3)
    def _():
        hail({"ctx": c + 1})

    @pl.when(c > 0)
    def _():
        hail({"ctx": c - 1})

    inner = jnp.logical_and(c > 0, c < 3)

    @pl.when(inner)
    def _():
        pl.semaphore_wait(barrier, 5 + far)

    @pl.when(jnp.logical_not(inner))
    def _():
        pl.semaphore_wait(barrier, 4 + far)


class Gather:
    def __init__(self, pool, sems, c, w):
        self.pool, self.sems, self.c, self.w = pool, sems, c, w
        self.n = pool.shape[2]
        self.n1 = tile_halves(self.n)
        self.x, self.y, self.core = {"wt": w ^ 2}, {"wt": w ^ 4}, {"wt": w ^ 1}

    def copy(self, k, owner, lane, device, part=None):
        ref = self.pool.at[k, owner]
        if part is not None:
            ref = ref.at[pl.ds(part[0], part[1])]
        return remote(ref, ref, self.sems.at[k, lane], self.sems.at[k, lane + 1], device)

    def up(self, k):
        return self.copy(k, self.w, 0, {"ctx": self.c + 1})

    def down(self, k):
        return self.copy(k, self.w, 2, {"ctx": self.c - 1})

    def over_x(self, k, back=0):
        return self.copy(k, self.w ^ back, 4, self.x)

    def over_y(self, k, back=0):
        return self.copy(k, self.w ^ back, 6, self.y)

    def diag_x(self, k, owner):
        return self.copy(k, owner, 8, self.x, (0, self.n1))

    def diag_y(self, k, owner):
        return self.copy(k, owner, 10, self.y, (self.n1, self.n - self.n1))

    def over_core(self, k, quad, back=0):
        return self.copy(k, self.w ^ (2 * quad) ^ back, 12 + 2 * quad, self.core)

    def send_line(self, k, low, high):
        if low:

            @pl.when(self.c < 3)
            def _():
                self.up(k).start()

        if high:

            @pl.when(self.c > 0)
            def _():
                self.down(k).start()

    def send_near(self, k):
        self.over_x(k).start()
        self.over_y(k).start()
        self.over_core(k, 0).start()

    def first(self):
        self.send_line(self.c, True, True)

    def sides(self, s):
        return [(self.c >= s, self.c - s, True), (self.c + s <= 3, self.c + s, False)]

    def line_step(self, s, near=True):
        for valid, k, below in self.sides(s):

            @pl.when(valid)
            def _(k=k, below=below):
                if below:
                    self.up(k).wait_recv()
                else:
                    self.down(k).wait_recv()
                if s < 3:
                    self.send_line(k, below, not below)
                if near:
                    self.send_near(k)

    def each(self, s, act):
        if s == 0:
            act(self.c)
            return
        for valid, k, _ in self.sides(s):

            @pl.when(valid)
            def _(k=k):
                act(k)

    def near_step(self, s):
        def act(k):
            self.over_x(k, 2).wait_recv()
            self.diag_y(k, self.w ^ 2).start()
            self.over_core(k, 1).start()
            self.over_y(k, 4).wait_recv()
            self.diag_x(k, self.w ^ 4).start()
            self.over_core(k, 2).start()

        self.each(s, act)

    def diag_step(self, s):
        def act(k):
            self.diag_x(k, self.w ^ 6).wait_recv()
            self.diag_y(k, self.w ^ 6).wait_recv()
            self.over_core(k, 3).start()

        self.each(s, act)

    def finish(self):
        for k in range(4):
            for quad in range(4):
                self.over_core(k, quad, 1).wait_recv()

    def drain(self):
        for k in range(4):

            @pl.when(jnp.logical_and(k <= self.c, self.c < 3))
            def _(k=k):
                self.up(k).wait_send()

            @pl.when(jnp.logical_and(k >= self.c, self.c > 0))
            def _(k=k):
                self.down(k).wait_send()

            self.over_x(k).wait_send()
            self.over_y(k).wait_send()
            self.diag_x(k, self.w ^ 4).wait_send()
            self.diag_y(k, self.w ^ 2).wait_send()
            for quad in range(4):
                self.over_core(k, quad).wait_send()


def front_kernel(
    table, own_a, own_f, x_ref, gain_ref, cos_ref, sin_ref,
    q_ref, normed_t, rows_ref, kv_ref, late_ref, wqkv, wo, pool_f,
    normed_ref, pool_a, kv_own, sems_a, sems_f, sems_kv, sems,
):
    c, w = lax.axis_index("ctx"), lax.axis_index("wt")
    take_a = pltpu.make_async_copy(own_a, pool_a.at[c, w], sems.at[0])
    take_f = pltpu.make_async_copy(own_f, pool_f.at[c, w], sems.at[1])
    take_a.start()
    take_f.start()
    greet(c, w, 0)
    take_a.wait()
    a = Gather(pool_a, sems_a, c, w)
    f = Gather(pool_f, sems_f, c, w)
    a.first()
    a.send_near(c)

    rows = x_ref.shape[2]
    blk = BLK
    for m in range(2):
        for half in range(rows // blk):
            part = x_ref[m, :, blk * half : blk * half + blk].T
            span = slice(m * rows + blk * half, m * rows + blk * half + blk)
            rows_ref[span, :] = part
            wide = part.astype(f32)
            inverse = lax.rsqrt(jnp.mean(wide * wide, axis=1, keepdims=True) + epsilon)
            normed = (wide * inverse * gain_ref[...]).astype(bf16)
            normed_ref[span, :] = normed
            normed_t[:, span] = normed.T

    a.line_step(1)
    a.near_step(0)
    a.line_step(2)
    take_f.wait()
    f.first()
    a.near_step(1)
    a.diag_step(0)
    a.line_step(3)
    a.near_step(2)
    a.diag_step(1)
    a.near_step(3)
    f.send_near(c)
    a.diag_step(2)
    a.diag_step(3)
    f.line_step(1)
    a.finish()

    flat = pool_a.reshape(pool_a.shape[0] * pool_a.shape[1] * pool_a.shape[2], 32, 128)
    attn_rows(flat, table, wqkv, wo)
    f.line_step(2)
    f.near_step(0)

    lane = lax.broadcasted_iota(jnp.int32, (blk, 128), 1)
    left = lane < 64

    def qkv_block(i, _):
        at = pl.multiple_of(i * blk, blk)
        normed = normed_ref[pl.ds(at, blk), :]
        within = pl.multiple_of((i % (rows // blk)) * blk, blk)
        cosine, sine = cos_ref[pl.ds(within, blk), :], sin_ref[pl.ds(within, blk), :]
        key_cosine = jnp.where(left, cosine, 1.0)
        key_sine = jnp.where(left, sine, 0.0)
        for g in range(KVH):
            spot = QP + 128 * g
            part = jnp.dot(normed, wqkv[:, spot : spot + 128], preferred_element_type=f32)
            part = (part * key_cosine + swap_halves(part) * key_sine).astype(bf16)
            kv_own[i // (rows // blk), g, pl.ds(within, blk), :] = part
        for p in range(8):
            part = jnp.dot(normed, wqkv[:, 128 * p : 128 * p + 128], preferred_element_type=f32)
            part = (part * cosine + swap_halves(part) * sine).astype(bf16).astype(f32) * 0.125
            q_ref[2 * p, pl.ds(at, blk), :] = jnp.where(left, part, 0.0).astype(bf16)
            if 2 * p + 1 < QH:
                other = jnp.where(left, pltpu.roll(part, 64, 1), 0.0).astype(bf16)
                q_ref[2 * p + 1, pl.ds(at, blk), :] = other
        return 0

    def kv_move(src, k, lane, step):
        return remote(src, kv_ref.at[k], sems_kv.at[k, lane], sems_kv.at[k, lane + 1], {"ctx": c + step})

    lax.fori_loop(0, rows // blk, qkv_block, 0)
    keep = pltpu.make_async_copy(kv_own.at[0], kv_ref.at[c], sems.at[2])
    keep.start()

    @pl.when(c < 3)
    def _():
        kv_move(kv_own.at[0], c, 0, 1).start()

    @pl.when(c > 0)
    def _():
        kv_move(kv_own.at[0], c, 2, -1).start()

    lax.fori_loop(rows // blk, 2 * rows // blk, qkv_block, 0)
    late = pltpu.make_async_copy(kv_own.at[1], late_ref, sems.at[3])
    late.start()

    def kv_step(s):
        @pl.when(c >= s)
        def _():
            kv_move(kv_ref.at[c - s], c - s, 0, 1).wait_recv()
            if s < 3:

                @pl.when(c < 3)
                def _():
                    kv_move(kv_ref.at[c - s], c - s, 0, 1).start()

        @pl.when(c + s <= 3)
        def _():
            kv_move(kv_ref.at[c + s], c + s, 2, -1).wait_recv()
            if s < 3:

                @pl.when(c > 0)
                def _():
                    kv_move(kv_ref.at[c + s], c + s, 2, -1).start()

    f.line_step(3)
    f.near_step(1)
    f.diag_step(0)
    kv_step(1)
    f.near_step(2)
    f.diag_step(1)
    f.near_step(3)
    kv_step(2)
    f.diag_step(2)
    f.diag_step(3)
    f.finish()
    kv_step(3)
    keep.wait()
    late.wait()
    for k in range(4):

        @pl.when(jnp.logical_and(k <= c, c < 3))
        def _(k=k):
            kv_move(kv_ref.at[k], k, 0, 1).wait_send()

        @pl.when(jnp.logical_and(k >= c, c > 0))
        def _(k=k):
            kv_move(kv_ref.at[k], k, 2, -1).wait_send()

    a.drain()
    f.drain()


def front(table, own_a, own_f, x_t, gain, cosine, sine):
    micro, _, rows = x_t.shape
    tokens = micro * rows
    n_a, n_f = own_a.shape[0], own_f.shape[0]
    return pl.pallas_call(
        front_kernel,
        out_shape=[
            jax.ShapeDtypeStruct((QH, tokens, 128), bf16),
            jax.ShapeDtypeStruct((D, tokens), bf16),
            jax.ShapeDtypeStruct((tokens, D), bf16),
            jax.ShapeDtypeStruct((4, KVH, rows, 128), bf16),
            jax.ShapeDtypeStruct((KVH, rows, 128), bf16),
            jax.ShapeDtypeStruct((D, CW), bf16),
            jax.ShapeDtypeStruct((QP, D), bf16),
            jax.ShapeDtypeStruct((4, 8, n_f, 32, 128), bf16),
        ],
        in_specs=[SM, ANY, ANY, VM, VM, VM, VM],
        out_specs=[VM, VM, VM, ANY, ANY, VM, VM, ANY],
        scratch_shapes=[
            pltpu.VMEM((tokens, D), bf16),
            pltpu.VMEM((4, 8, n_a, 32, 128), bf16),
            pltpu.VMEM((micro, KVH, rows, 128), bf16),
            pltpu.SemaphoreType.DMA((4, 20)),
            pltpu.SemaphoreType.DMA((4, 20)),
            pltpu.SemaphoreType.DMA((4, 4)),
            pltpu.SemaphoreType.DMA((4,)),
        ],
        compiler_params=params(48, collective_id=0, has_side_effects=True),
        cost_estimate=cost(40e9, 40 << 20),
    )(table, own_a, own_f, x_t, gain, cosine, sine)


class Line:
    def __init__(self, terms, send, recv, sems, c):
        self.terms, self.send, self.recv, self.sems, self.c = terms, send, recv, sems, c
        self.count = recv.shape[2]

    def copy(self, way, k):
        sems = self.sems
        return remote(
            self.send.at[k], self.recv.at[way, k], sems.at[way, k, 0], sems.at[way, k, 1],
            {"ctx": self.c + 1 - 2 * way},
        )

    def loop(self, act):
        def body(j, _):
            act(j)
            return 0

        lax.fori_loop(0, self.count, body, 0)

    def start(self):
        for way in (0, 1):

            @pl.when(self.c == 3 * way)
            def _(way=way):
                for far in (3, 2, 1):
                    k = far if way == 0 else 3 - far

                    def take(j, k=k):
                        self.send[k, j] = self.terms(k, j).astype(bf16)

                    self.loop(take)
                    self.copy(way, k).start()

    def join(self, way, k):
        self.copy(way, k).wait_recv()

        def act(j):
            self.send[k, j] = (self.terms(k, j) + self.recv[way, k, j].astype(f32)).astype(bf16)

        self.loop(act)
        self.copy(way, k).start()

    def step(self, number):
        lists = {1: ((0, 3), (0, 2), (1, 0)), 2: ((1, 0), (1, 1), (0, 3))}
        for inner, order in lists.items():

            @pl.when(self.c == inner)
            def _(order=order):
                self.join(*order[number])

    def finish(self, out):
        c, recv = self.c, self.recv

        @pl.when(c > 0)
        def _():
            self.copy(0, c).wait_recv()

        @pl.when(c < 3)
        def _():
            self.copy(1, c).wait_recv()

        def total(j):
            low = jnp.where(c > 0, recv[0, c, j].astype(f32), 0.0)
            high = jnp.where(c < 3, recv[1, c, j].astype(f32), 0.0)
            out[j] = self.terms(c, j) + low + high

        self.loop(total)

    def drain(self):
        for far in (3, 2, 1):
            for way, k in ((0, far), (1, 3 - far)):

                @pl.when(self.c < k if way == 0 else self.c > k)
                def _(way=way, k=k):
                    self.copy(way, k).wait_send()


class Plane:
    def __init__(self, pool, bufs, sems, c, w):
        self.pool, self.sems, self.c, self.w = pool, sems, c, w
        self.mine, self.theirs, self.diag_send, self.diag_recv, self.near_send, self.near_recv = bufs
        self.n = pool.shape[3]
        n1 = self.n1 = tile_halves(self.n)
        yx, core = w // 2, w % 2
        over_x, over_y, over_core = {"wt": w ^ 2}, {"wt": w ^ 4}, {"wt": w ^ 1}
        self.loads = [
            pltpu.make_async_copy(pool.at[:, yx ^ q, core], self.mine.at[q], sems.at[10 + q, 0]) for q in range(4)
        ]
        self.cores = [
            remote(pool.at[:, yx ^ q, 1 - core], self.theirs.at[q], sems.at[q, 0], sems.at[q, 1], over_core)
            for q in range(4)
        ]
        low, high = slice(0, n1), slice(n1, self.n)
        self.diag_x = self.move(self.diag_send.at[:, low], self.diag_recv.at[:, low], 4, over_x)
        self.diag_y = self.move(self.diag_send.at[:, high], self.diag_recv.at[:, high], 5, over_y)
        self.nears = {}
        for q in (1, 2):
            for part, cut in enumerate((low, high)):
                self.nears[q, part] = self.move(
                    self.near_send.at[q - 1, :, cut],
                    self.near_recv.at[q - 1, :, cut],
                    4 + 2 * q + part,
                    over_x if q == 1 else over_y,
                )

    def move(self, src, dst, lane, device):
        return remote(src, dst, self.sems.at[lane, 0], self.sems.at[lane, 1], device)

    def begin_loads(self):
        for q in (3, 1, 2, 0):
            self.loads[q].start()

    def begin(self):
        for q in (3, 1, 2, 0):
            self.cores[q].start()

    def each(self, act):
        def body(k, _):
            act(k)
            return 0

        lax.fori_loop(0, 4, body, 0)

    def both(self, q, k):
        return self.mine[q, k].astype(f32) + self.theirs[q, k].astype(f32)

    def ready(self, q):
        self.loads[q].wait()
        self.cores[q].wait()

    def diag(self):
        self.ready(3)

        def act(k):
            self.diag_send[k] = self.both(3, k).astype(bf16)

        self.each(act)
        self.diag_x.start()
        self.diag_y.start()

    def near(self, q):
        self.ready(q)

        def act(k):
            self.near_send[q - 1, k] = self.both(q, k).astype(bf16)

        self.each(act)
        self.nears[q, q - 1].start()

    def join(self, q):
        cut = slice(self.n1, self.n) if q == 1 else slice(0, self.n1)
        (self.diag_y if q == 1 else self.diag_x).wait_recv()

        def act(k):
            ours = self.near_send[q - 1, k, cut].astype(f32)
            self.near_send[q - 1, k, cut] = (ours + self.diag_recv[k, cut].astype(f32)).astype(bf16)

        self.each(act)
        self.nears[q, 2 - q].start()

    def join_out(self, q, out):
        cut = slice(self.n1, self.n) if q == 1 else slice(0, self.n1)
        (self.diag_y if q == 1 else self.diag_x).wait_recv()

        def act(k):
            ours = self.near_send[q - 1, k, cut].astype(f32)
            out[k] = (ours + self.diag_recv[k, cut].astype(f32)).astype(bf16)

        self.each(act)

    def arrive_half(self):
        self.ready(0)
        self.nears[1, 0].wait_recv()
        self.nears[2, 1].wait_recv()

    def own_half(self, k):
        n1 = self.n1
        near = jnp.concatenate([self.near_recv[0, k, :n1], self.near_recv[1, k, n1:]], axis=0)
        return self.both(0, k) + near.astype(f32)

    def drain_half(self):
        self.diag_x.wait_send()
        self.diag_y.wait_send()
        self.nears[1, 0].wait_send()
        self.nears[2, 1].wait_send()

    def arrive(self):
        self.ready(0)
        for part in (0, 1):
            for q in (1, 2):
                self.nears[q, part].wait_recv()

    def own(self, k):
        return self.both(0, k) + self.near_recv[0, k].astype(f32) + self.near_recv[1, k].astype(f32)

    def drain(self):
        self.diag_x.wait_send()
        self.diag_y.wait_send()
        for copy in self.nears.values():
            copy.wait_send()


def plane_scratch(n):
    tile = (32, 128)
    return [
        pltpu.VMEM((4, 4, n) + tile, bf16),
        pltpu.VMEM((4, 4, n) + tile, bf16),
        pltpu.VMEM((4, n) + tile, bf16),
        pltpu.VMEM((4, n) + tile, bf16),
        pltpu.VMEM((2, 4, n) + tile, bf16),
        pltpu.VMEM((2, 4, n) + tile, bf16),
        pltpu.SemaphoreType.DMA((14, 2)),
    ]


def line_scratch(shape):
    return [
        pltpu.VMEM((4,) + shape, bf16),
        pltpu.VMEM((2, 4) + shape, bf16),
        pltpu.SemaphoreType.DMA((2, 4, 2)),
    ]


def return_kernel(pool, kv_ref, sum_ref, x_out, y_out, kv_out, *scratch):
    c, w = lax.axis_index("ctx"), lax.axis_index("wt")
    plane = Plane(pool, scratch[:6], scratch[6], c, w)
    line = Line(lambda k, j: kv_ref[k, j].astype(f32), *scratch[7:], c)
    plane.begin_loads()
    greet(c, w, 0)
    plane.begin()

    line.start()
    plane.diag()
    plane.near(1)
    plane.near(2)
    line.step(0)
    plane.join_out(1, x_out)
    line.step(1)
    plane.join_out(2, y_out)
    line.step(2)
    plane.arrive_half()

    def own(k):
        sum_ref[k] = plane.own_half(k).astype(bf16)

    plane.each(own)
    line.finish(kv_out)
    plane.drain_half()
    line.drain()


def back_home(pool, kv_terms):
    n = pool.shape[3]
    n1 = tile_halves(n)
    return pl.pallas_call(
        return_kernel,
        out_shape=[
            jax.ShapeDtypeStruct((4, n, 32, 128), bf16),
            jax.ShapeDtypeStruct((4, n - n1, 32, 128), bf16),
            jax.ShapeDtypeStruct((4, n1, 32, 128), bf16),
            jax.ShapeDtypeStruct(kv_terms.shape[1:], f32),
        ],
        in_specs=[ANY, VM],
        out_specs=[VM] * 4,
        scratch_shapes=plane_scratch(n) + line_scratch(kv_terms.shape[1:]),
        compiler_params=params(60, collective_id=2, has_side_effects=True),
        cost_estimate=cost(30e9, 16 << 20),
    )(pool, kv_terms)


def tail_kernel(
    pool, ffn_ref, over_x, over_y, gain_ref, sum_ref, ffn_out, gain_out, own, gain_send, gain_recv, sems_gain, *scratch
):
    c, w = lax.axis_index("ctx"), lax.axis_index("wt")
    plane = Plane(pool, scratch[:6], scratch[6], c, w)
    line = Line(lambda k, j: own[k, j], *scratch[7:10], c)
    n1 = over_y.shape[1]

    def ffn_term(k, j):
        joined = jnp.where(j < n1, over_y[k, jnp.minimum(j, n1 - 1)], over_x[k, jnp.maximum(j - n1, 0)])
        return ffn_ref[k, j].astype(f32) + joined.astype(f32)

    ffn_line = Line(ffn_term, *scratch[10:13], c)
    plane.begin_loads()
    greet(c, w, 1)
    plane.begin()

    stages = [{"wt": w ^ 1}, {"wt": w ^ 2}, {"wt": w ^ 4}, {"ctx": c ^ 1}, {"ctx": c ^ 2}]
    copies = [
        remote(gain_send.at[i], gain_recv.at[i], sems_gain.at[i, 0], sems_gain.at[i, 1], stages[i]) for i in range(5)
    ]
    gain_send[0] = gain_ref[...]
    copies[0].start()

    def gain_step(i):
        copies[i].wait()
        total = gain_send[i] + gain_recv[i]
        if i < 4:
            gain_send[i + 1] = total
            copies[i + 1].start()
        else:
            gain_out[...] = total

    ffn_line.start()
    plane.diag()
    gain_step(0)
    plane.near(1)
    plane.near(2)
    ffn_line.step(0)
    gain_step(1)
    plane.join(1)
    plane.join(2)
    ffn_line.step(1)
    gain_step(2)
    plane.arrive()

    def own_sum(k):
        own[k] = plane.own(k)

    plane.each(own_sum)
    line.start()
    ffn_line.step(2)
    gain_step(3)
    for number in range(3):
        line.step(number)
    ffn_line.finish(ffn_out)
    gain_step(4)
    line.finish(sum_ref)
    plane.drain()
    line.drain()
    ffn_line.drain()


def tail(pool, ffn_terms, over_x, over_y, gains):
    n, n_f = pool.shape[3], ffn_terms.shape[1]
    tile = (32, 128)
    return pl.pallas_call(
        tail_kernel,
        out_shape=[
            jax.ShapeDtypeStruct((n,) + tile, f32),
            jax.ShapeDtypeStruct((n_f,) + tile, f32),
            jax.ShapeDtypeStruct(gains.shape, f32),
        ],
        in_specs=[ANY, VM, VM, VM, VM],
        out_specs=[VM, VM, VM],
        scratch_shapes=[
            pltpu.VMEM((4, n) + tile, f32),
            pltpu.VMEM((5,) + gains.shape, f32),
            pltpu.VMEM((5,) + gains.shape, f32),
            pltpu.SemaphoreType.DMA((5, 2)),
        ]
        + plane_scratch(n)
        + line_scratch((n,) + tile)
        + line_scratch((n_f,) + tile),
        compiler_params=params(48, collective_id=1, has_side_effects=True),
        cost_estimate=cost(30e9, 16 << 20),
    )(pool, ffn_terms, over_x, over_y, gains)


META = 4


def load_blocks(meta, part, pool, sems):
    blk = part.shape[2] // 2
    copies = []
    for k in range(2 * part.shape[0]):
        at = pl.multiple_of(meta[META + k] * blk, blk)
        source = part.at[k // 2, :, pl.ds(k % 2 * blk, blk), :]
        copies.append(pltpu.make_async_copy(source, pool.at[:, pl.ds(at, blk), :], sems.at[k]))
    for copy in copies:
        copy.start()
    for copy in copies:
        copy.wait()


def masked(scores, block, q_block, length):
    blk = scores.shape[1]
    key = block + lax.broadcasted_iota(jnp.int32, scores.shape, 0)
    query = q_block * blk + lax.broadcasted_iota(jnp.int32, scores.shape, 1)
    return jnp.where(jnp.logical_and(key <= query, key < length), scores, blocked_score)


def nt_dot(a, b):
    return lax.dot_general(a, b, (((1,), (1,)), ((), ())), preferred_element_type=f32)


def tn_dot(a, b):
    return lax.dot_general(a, b, (((0,), (0,)), ((), ())), preferred_element_type=f32)


def flash_forward_kernel(meta, q_ref, part, out_ref, turned_ref, lse_ref, pool, vt, peak, acc, turned, sems):
    load_blocks(meta, part, pool, sems)
    length = meta[2]
    blk = q_ref.shape[1] // 2
    live_blocks = (length + blk - 1) // blk
    turned[960:, :] = jnp.zeros((64, blk), f32)
    for g in range(KVH):
        vt[g, :64, :] = jnp.ones((64, vt.shape[2]), bf16)
        for k in range(pool.shape[1] // 256):
            vt[g, 64:, 256 * k : 256 * k + 256] = pool[g, 256 * k : 256 * k + 256, :].T[64:]
    for qi in range(2):
        q_block = meta[qi]
        blocks = jnp.minimum(q_block + 1, live_blocks)

        def group(g, _):
            queries = [q_ref[GRP * g + h, blk * qi : blk * qi + blk, :] for h in range(GRP)]
            for h in range(GRP):
                peak[h] = jnp.full((1, blk), blocked_score, f32)
                acc[h] = jnp.zeros((128, blk), f32)

            def step(block, wide, with_mask):
                start = pl.multiple_of(block * blk, blk)
                span = pl.ds(start, wide * blk)
                kv = pool[g, span, :]
                vals = vt[g, :, span]
                scores = [nt_dot(kv, queries[h]) for h in range(GRP)]
                if with_mask:
                    scores = [masked(t, start, q_block, length) for t in scores]
                before = [peak[h] for h in range(GRP)]
                now = [jnp.maximum(before[h], jnp.max(scores[h], axis=0, keepdims=True)) for h in range(GRP)]
                weights = [jnp.exp(scores[h] - now[h]).astype(bf16) for h in range(GRP)]
                for h in range(GRP):
                    peak[h] = now[h]
                    acc[h] = acc[h] * jnp.exp(before[h] - now[h]) + jnp.dot(
                        vals, weights[h], preferred_element_type=f32
                    )

            def plain(pair, _):
                step(2 * pair, 2, False)
                return 0

            pairs = (blocks - 1) // 2

            def plain4(quad, _):
                step(4 * quad, 4, False)
                return 0

            lax.fori_loop(0, pairs // 2, plain4, 0)

            @pl.when(pairs % 2 == 1)
            def _():
                plain(pairs - 1, 0)

            @pl.when(blocks % 2 == 1)
            def _():
                step(blocks - 1, 1, True)

            @pl.when(blocks % 2 == 0)
            def _():
                step(blocks - 2, 2, True)

            for h in range(GRP):
                total = acc[h][0:1, :]
                turned[pl.ds(pl.multiple_of((GRP * g + h) * HD, HD), HD), :] = acc[h][64:, :] / total
                lse_ref[GRP * g + h, :, blk * qi : blk * qi + blk] = peak[h] + jnp.log(total)
            return 0

        lax.fori_loop(0, KVH, group, 0)
        out_ref[blk * qi : blk * qi + blk, :] = turned[...].T.astype(bf16)
        turned_ref[:, blk * qi : blk * qi + blk] = turned[...].astype(bf16)


def flash_forward(m, meta, q, part):
    n_ctx, _, rows, _ = part.shape
    blk = rows // 2
    return pl.pallas_call(
        flash_forward_kernel,
        grid=(1,),
        out_shape=[
            jax.ShapeDtypeStruct((rows, QP), bf16),
            jax.ShapeDtypeStruct((QP, rows), bf16),
            jax.ShapeDtypeStruct((16, 1, rows), f32),
        ],
        in_specs=[SM, pl.BlockSpec((QH, rows, 128), lambda i: (0, m, 0)), ANY],
        out_specs=[
            pl.BlockSpec((rows, QP), lambda i: (0, 0)),
            pl.BlockSpec((QP, rows), lambda i: (0, 0)),
            pl.BlockSpec((16, 1, rows), lambda i: (0, 0, 0)),
        ],
        scratch_shapes=[
            pltpu.VMEM((KVH, n_ctx * rows, 128), bf16),
            pltpu.VMEM((KVH, 128, n_ctx * rows), bf16),
            pltpu.VMEM((GRP, 1, blk), f32),
            pltpu.VMEM((GRP, 128, blk), f32),
            pltpu.VMEM((QP, blk), f32),
            pltpu.SemaphoreType.DMA((2 * n_ctx,)),
        ],
        compiler_params=params(48),
        cost_estimate=cost(40e9, 8 << 20),
    )(meta, q, part)


def flash_backward_kernel(
    meta, q_ref, out_ref, grad_ref, lse_ref, cos_ref, sin_ref, part, gq_ref, gkv_ref,
    pool, kt, wide, delta, total, acc, turned, sides, sems,
):
    load_blocks(meta, part, pool, sems)
    length = meta[2]
    rows = q_ref.shape[1]
    blk = rows // 2
    live_blocks = (length + blk - 1) // blk
    total[...] = jnp.zeros_like(total)
    lane = lax.broadcasted_iota(jnp.int32, (rows, 128), 1)
    pick = lax.broadcasted_iota(jnp.int32, (16, 128), 0) == lax.broadcasted_iota(jnp.int32, (16, 128), 1) // 64
    pick = jnp.where(pick, 1.0, 0.0).astype(bf16)
    for g in range(KVH):
        for k in range(pool.shape[1] // 256):
            kt[g, :, 256 * k : 256 * k + 256] = pool[g, 256 * k : 256 * k + 256, :].T[:64]
    for p in range(8):
        slab = grad_ref[:, 128 * p : 128 * p + 128].astype(f32)
        wide[2 * p] = jnp.where(lane >= 64, pltpu.roll(slab, 64, 1), 0.0).astype(bf16)
        if 2 * p + 1 < QH:
            wide[2 * p + 1] = jnp.where(lane >= 64, slab, 0.0).astype(bf16)
        product = slab * out_ref[:, 128 * p : 128 * p + 128].astype(f32)
        high = product.astype(bf16)
        low = (product - high.astype(f32)).astype(bf16)
        both = nt_dot(pick, high) + nt_dot(pick, low)
        delta[2 * p] = both[0:1, :]
        delta[2 * p + 1] = both[1:2, :]
    turned[960:, :] = jnp.zeros((64, blk), f32)
    for qi in range(2):
        q_block = meta[qi]
        blocks = jnp.where(q_block < live_blocks, q_block + 1, 0)
        span = slice(blk * qi, blk * qi + blk)

        def group(g, _):
            for h in range(GRP):
                acc[h] = jnp.zeros((64, blk), f32)
                sides[2 * blk * h : 2 * blk * h + blk] = q_ref[GRP * g + h, span, :]
                sides[2 * blk * h + blk : 2 * blk * h + 2 * blk] = wide[GRP * g + h, span, :]

            def step(block, count, with_mask):
                start = pl.multiple_of(block * blk, blk)
                keys = pl.ds(start, count * blk)
                kv = pool[g, keys, :]
                keys_t = kt[g, :, keys]
                heads = [GRP * g + h for h in range(GRP)]
                scores = [nt_dot(kv, sides[2 * blk * h : 2 * blk * h + blk]) for h in range(GRP)]
                inner = [nt_dot(kv, sides[2 * blk * h + blk : 2 * blk * h + 2 * blk]) for h in range(GRP)]
                if with_mask:
                    scores = [masked(t, start, q_block, length) for t in scores]
                probs = [jnp.exp(scores[h] - lse_ref[heads[h], :, span]) for h in range(GRP)]
                change = [(probs[h] * (inner[h] - delta[heads[h], :, span])).astype(bf16) for h in range(GRP)]
                terms = []
                for h in range(GRP):
                    terms += [change[h], probs[h].astype(bf16)]
                total[g, keys, :] += jnp.dot(
                    jnp.concatenate(terms, axis=1), sides[...], preferred_element_type=f32
                )
                for h in range(GRP):
                    acc[h] = acc[h] + jnp.dot(keys_t, change[h], preferred_element_type=f32)

            def plain(pair, _):
                step(2 * pair, 2, False)
                return 0

            pairs = (blocks - 1) // 2

            def plain4(quad, _):
                step(4 * quad, 4, False)
                return 0

            lax.fori_loop(0, pairs // 2, plain4, 0)

            @pl.when(jnp.logical_and(pairs > 0, pairs % 2 == 1))
            def _():
                plain(pairs - 1, 0)

            @pl.when(jnp.logical_and(blocks > 0, blocks % 2 == 1))
            def _():
                step(blocks - 1, 1, True)

            @pl.when(jnp.logical_and(blocks > 0, blocks % 2 == 0))
            def _():
                step(blocks - 2, 2, True)

            for h in range(GRP):
                turned[pl.ds(pl.multiple_of((GRP * g + h) * HD, HD), HD), :] = acc[h] * 0.125
            return 0

        lax.fori_loop(0, KVH, group, 0)
        grads = turned[...].T
        cosine, sine = cos_ref[span, :], sin_ref[span, :]
        for p in range(8):
            slab = grads[:, 128 * p : 128 * p + 128]
            gq_ref[span, 128 * p : 128 * p + 128] = (slab * cosine - swap_halves(slab) * sine).astype(bf16)
    for k in range(2 * gkv_ref.shape[0]):
        at = pl.multiple_of(meta[META + k] * blk, blk)
        gkv_ref[k // 2, :, k % 2 * blk : k % 2 * blk + blk, :] = total[:, pl.ds(at, blk), :].astype(bf16)


def flash_backward(m, meta, q, out, grad, lse, cosine, sine, part):
    n_ctx, _, rows, _ = part.shape
    blk = rows // 2
    return pl.pallas_call(
        flash_backward_kernel,
        grid=(1,),
        out_shape=[
            jax.ShapeDtypeStruct((rows, QP), bf16),
            jax.ShapeDtypeStruct((n_ctx, KVH, rows, 128), bf16),
        ],
        in_specs=[
            SM,
            pl.BlockSpec((QH, rows, 128), lambda i: (0, m, 0)),
            pl.BlockSpec((rows, QP), lambda i: (0, 0)),
            pl.BlockSpec((rows, QP), lambda i: (m, 0)),
            pl.BlockSpec((16, 1, rows), lambda i: (0, 0, 0)),
            pl.BlockSpec((rows, 128), lambda i: (0, 0)),
            pl.BlockSpec((rows, 128), lambda i: (0, 0)),
            ANY,
        ],
        out_specs=[
            pl.BlockSpec((rows, QP), lambda i: (0, 0)),
            pl.BlockSpec((n_ctx, KVH, rows, 128), lambda i: (0, 0, 0, 0)),
        ],
        scratch_shapes=[
            pltpu.VMEM((KVH, n_ctx * rows, 128), bf16),
            pltpu.VMEM((KVH, 64, n_ctx * rows), bf16),
            pltpu.VMEM((QH, rows, 128), bf16),
            pltpu.VMEM((16, 1, rows), f32),
            pltpu.VMEM((KVH, n_ctx * rows, 128), f32),
            pltpu.VMEM((GRP, 64, blk), f32),
            pltpu.VMEM((QP, blk), f32),
            pltpu.VMEM((2 * GRP * blk, 128), bf16),
            pltpu.SemaphoreType.DMA((2 * n_ctx,)),
        ],
        compiler_params=params(56),
        cost_estimate=cost(50e9, 16 << 20),
    )(meta, q, out, grad, lse, cosine, sine, part)


def assemble_ffn_kernel(table, pool_ref, gu_out, d_out, pool, wgu, wd, sems):
    load = pltpu.make_async_copy(pool_ref, pool, sems.at[0])
    load.start()
    load.wait()
    stores = []
    for part in range(5):
        gu_rows(pool, table, wgu, 3 * part, 3 * part + 3)
        span = pl.ds(192 * part, 192)
        stores.append(pltpu.make_async_copy(wgu.at[span], gu_out.at[span], sems.at[1 + part]))
        stores[-1].start()
    for part in range(4):
        d_rows(pool, table, wd, 10 * part, 10 * part + 10)
        span = pl.ds(640 * part, 640)
        stores.append(pltpu.make_async_copy(wd.at[span], d_out.at[span], sems.at[6 + part]))
        stores[-1].start()
    for copy in stores:
        copy.wait()


def assemble_ffn(table, pool):
    shapes = [(D, 2 * FF), (FF, D)]
    return pl.pallas_call(
        assemble_ffn_kernel,
        out_shape=[jax.ShapeDtypeStruct(s, bf16) for s in shapes],
        in_specs=[SM, ANY],
        out_specs=[ANY, ANY],
        scratch_shapes=[pltpu.VMEM(s, bf16) for s in [pool.shape] + shapes] + [pltpu.SemaphoreType.DMA((10,))],
        compiler_params=params(52),
        cost_estimate=cost(0, 64 << 20),
    )(table, pool)


CHUNK = 512


def middle_kernel(
    scalars, gu_ref, d_ref, out_0, out_1, wo, x_ref, cot_ref, gain_ref,
    mixed_ref, normed_t, hidden_t, ggu_ref, go_ref, branch_ref, residual_ref, attn_ref, gain_out,
    wgu, wd, sems,
):
    i = pl.program_id(0)
    blk = x_ref.shape[0]
    loads = [pltpu.make_async_copy(gu_ref, wgu, sems.at[0]), pltpu.make_async_copy(d_ref, wd, sems.at[1])]

    @pl.when(i == 0)
    def _():
        for load in loads:
            load.start()

    attn = jnp.where(i < 2, out_0[...], out_1[...])
    residual = x_ref[...].astype(f32) + jnp.dot(attn, wo[...], preferred_element_type=f32)
    inverse = lax.rsqrt(jnp.mean(residual * residual, axis=1, keepdims=True) + epsilon)
    gain = gain_ref[...]
    normed = (residual * inverse * gain).astype(bf16)
    normed_t[...] = normed.T
    row = scalars[i % 2] * blk + lax.broadcasted_iota(jnp.int32, (blk, D), 0)
    grad_out = cot_ref[0].T
    grad_out = jnp.where(row < scalars[2 + i // 2], grad_out, jnp.zeros((), bf16))
    go_ref[...] = grad_out

    @pl.when(i == 0)
    def _():
        for load in loads:
            load.wait()

    def first(j):
        at = CHUNK * j
        return (
            jnp.dot(normed, wgu[:, at : at + CHUNK], preferred_element_type=f32),
            jnp.dot(normed, wgu[:, FF + at : FF + at + CHUNK], preferred_element_type=f32),
            nt_dot(grad_out, wd[at : at + CHUNK, :]),
        )

    mixed = residual
    grad_normed = jnp.zeros((blk, D), f32)
    ahead = first(0)
    for j in range(FF // CHUNK):
        at = CHUNK * j
        gate, up, grad_hidden = ahead
        if j + 1 < FF // CHUNK:
            ahead = first(j + 1)
        sigma = jax.nn.sigmoid(gate)
        silu = gate * sigma
        hidden = (silu * up).astype(bf16)
        grad_up = (grad_hidden * silu).astype(bf16)
        grad_gate = (grad_hidden * up * (sigma + silu * (1.0 - sigma))).astype(bf16)
        hidden_t[at : at + CHUNK, :] = hidden.T
        ggu_ref[:, at : at + CHUNK] = grad_gate
        ggu_ref[:, FF + at : FF + at + CHUNK] = grad_up
        mixed = mixed + jnp.dot(hidden, wd[at : at + CHUNK, :], preferred_element_type=f32)
        grad_normed = grad_normed + nt_dot(grad_gate, wgu[:, at : at + CHUNK])
        grad_normed = grad_normed + nt_dot(grad_up, wgu[:, FF + at : FF + at + CHUNK])

    mixed_ref[0] = mixed.astype(bf16).T
    unit = residual * inverse
    scaled = grad_normed * gain
    back = inverse * (scaled - unit * jnp.mean(scaled * unit, axis=1, keepdims=True))
    grad_residual = grad_out.astype(f32) + back
    residual_ref[...] = grad_residual
    branch = grad_residual.astype(bf16)
    branch_ref[...] = branch
    attn_ref[...] = nt_dot(branch, wo[...]).astype(bf16)
    term = jnp.sum(grad_normed * unit, axis=0, keepdims=True)

    @pl.when(i == 0)
    def _():
        gain_out[...] = term

    @pl.when(i > 0)
    def _():
        gain_out[...] += term


def middle(scalars, wgu, wd, outs, wo, x_rows, cot_t, gain):
    micro, _, rows = cot_t.shape
    tokens = micro * rows
    blk = rows // 2

    def rows_of(width, kind):
        return jax.ShapeDtypeStruct((tokens, width), kind), pl.BlockSpec((blk, width), lambda i: (i, 0))

    def columns_of(height):
        return jax.ShapeDtypeStruct((height, tokens), bf16), pl.BlockSpec((height, blk), lambda i: (0, i))

    native = pl.BlockSpec((1, D, blk), lambda i: (i // 2, 0, i % 2))
    whole = pl.BlockSpec((1, D), lambda i: (0, 0))
    results = [
        (jax.ShapeDtypeStruct((micro, D, rows), bf16), native),
        columns_of(D),
        columns_of(FF),
        rows_of(2 * FF, bf16),
        rows_of(D, bf16),
        rows_of(D, bf16),
        rows_of(D, f32),
        rows_of(QP, bf16),
        (jax.ShapeDtypeStruct((1, D), f32), whole),
    ]
    return pl.pallas_call(
        middle_kernel,
        grid=(2 * micro,),
        out_shape=[r[0] for r in results],
        in_specs=[
            SM,
            ANY,
            ANY,
            pl.BlockSpec((blk, QP), lambda i: (jnp.minimum(i, 1), 0)),
            pl.BlockSpec((blk, QP), lambda i: (jnp.maximum(i - 2, 0), 0)),
            pl.BlockSpec((QP, D), lambda i: (0, 0)),
            pl.BlockSpec((blk, D), lambda i: (i, 0)),
            native,
            whole,
        ],
        out_specs=[r[1] for r in results],
        scratch_shapes=[
            pltpu.VMEM((D, 2 * FF), bf16),
            pltpu.VMEM((FF, D), bf16),
            pltpu.SemaphoreType.DMA((2,)),
        ],
        compiler_params=params(62),
        cost_estimate=cost(40e9, 40 << 20),
    )(scalars, wgu, wd, outs[0], outs[1], wo, x_rows, cot_t, gain)


def ffn_grads_kernel(table, normed_t, ggu_ref, hidden_t, go_ref, pool_out, pool, gu_0, d_0, gu_1, d_1, sems):
    j = pl.program_id(0)
    steps = pl.num_programs(0)

    def multiply(part, gu, d):
        columns = slice(512 * part, 512 * part + 512)
        gu[...] = jnp.dot(normed_t[...], ggu_ref[:, columns], preferred_element_type=f32).astype(bf16)
        rows = slice(256 * part, 256 * part + 256)
        d[...] = jnp.dot(hidden_t[rows, :], go_ref[...], preferred_element_type=f32).astype(bf16)

    def put(chunk, gu, d):
        base = 600 * (chunk // 5) + 8 * (chunk % 5)
        for r in range(15):
            for p in range(4):
                at = base + r * 40 + 2 * p
                pick_pair(pool, table, gu, 64 * r, 128 * p, at, at + 1)
        for r in range(4):
            at = 1200 + (4 * chunk + r) * 15
            for p in range(7):
                pick_pair(pool, table, d, 64 * r, 128 * p, at + 2 * p, at + 2 * p + 1)
            pick_single(pool, table, d, 64 * r, 896, at + 14)

    put((2 * j + 2 * steps - 1) % (2 * steps), gu_1, d_1)
    multiply(0, gu_0, d_0)
    put(2 * j, gu_0, d_0)
    multiply(1, gu_1, d_1)

    @pl.when(j == steps - 1)
    def _():
        put(2 * steps - 1, gu_1, d_1)
        flush_pool(pool, [pool_out], sems)


def ffn_grads(table, normed_t, ggu, hidden_t, go, total):
    tokens = go.shape[0]
    return pl.pallas_call(
        ffn_grads_kernel,
        grid=(5,),
        out_shape=jax.ShapeDtypeStruct((total, 32, 128), bf16),
        in_specs=[
            SM,
            pl.BlockSpec((D, tokens), lambda j: (0, 0)),
            pl.BlockSpec((tokens, 1024), lambda j: (0, j)),
            pl.BlockSpec((512, tokens), lambda j: (j, 0)),
            pl.BlockSpec((tokens, D), lambda j: (0, 0)),
        ],
        out_specs=ANY,
        scratch_shapes=[
            pltpu.VMEM((total, 32, 128), bf16),
            pltpu.VMEM((D, 512), bf16),
            pltpu.VMEM((256, D), bf16),
            pltpu.VMEM((D, 512), bf16),
            pltpu.VMEM((256, D), bf16),
            pltpu.SemaphoreType.DMA((1,)),
        ],
        compiler_params=params(52),
        cost_estimate=cost(15e9, 60 << 20),
    )(table, normed_t, ggu, hidden_t, go)


def inward_kernel(
    table, gq_0, gq_1, gkv_0, gkv_1, cos_ref, sin_ref, w_ref, normed_t, out_0, out_1,
    branch_ref, x_ref, residual_ref, gain_ref, grad_ref, gain_out, pool_out,
    cat, dqkv, dwo, pool, sems,
):
    i = pl.program_id(0)
    blk = x_ref.shape[0]
    half = branch_ref.shape[0] // 2
    early = i < 2
    at = pl.ds(pl.multiple_of(i * blk, blk), blk)
    cosine, sine = cos_ref[...], sin_ref[...]
    left = lax.broadcasted_iota(jnp.int32, (blk, 128), 1) < 64
    key_cosine = jnp.where(left, cosine, 1.0)
    key_sine = jnp.where(left, sine, 0.0)
    parts = [jnp.where(early, gq_0[...], gq_1[...])]
    for g in range(KVH):
        slab = jnp.where(early, gkv_0[g].astype(f32), gkv_1[g])
        parts.append((slab * key_cosine - swap_halves(slab) * key_sine).astype(bf16))
    terms = jnp.concatenate(parts, axis=1)
    cat[at, :] = terms
    grad_normed = nt_dot(terms, w_ref[...])
    new_wo = jnp.dot(out_0[...], branch_ref[:half, :], preferred_element_type=f32)
    new_wo = new_wo + jnp.dot(out_1[...], branch_ref[half:, :], preferred_element_type=f32)
    dwo[...] = new_wo.astype(bf16)
    x = x_ref[...].astype(f32)
    inverse = lax.rsqrt(jnp.mean(x * x, axis=1, keepdims=True) + epsilon)
    unit = x * inverse
    scaled = grad_normed * gain_ref[...]
    back = inverse * (scaled - unit * jnp.mean(scaled * unit, axis=1, keepdims=True))
    grad_ref[0] = (residual_ref[...] + back).T
    term = jnp.sum(grad_normed * unit, axis=0, keepdims=True)
    for r in range(4):
        first = 375 + (4 * i + r) * 15
        for p in range(7):
            pick_pair(pool, table, dwo, 64 * r, 128 * p, first + 2 * p, first + 2 * p + 1)
        pick_single(pool, table, dwo, 64 * r, 896, first + 14)

    @pl.when(i == 0)
    def _():
        gain_out[...] = term

    @pl.when(i > 0)
    def _():
        gain_out[...] += term

    @pl.when(i == pl.num_programs(0) - 1)
    def _():
        for low, high in ((0, 512), (512, QP), (QP, CW)):
            dqkv[:, low:high] = jnp.dot(
                normed_t[...], cat[:, low:high], preferred_element_type=f32
            ).astype(bf16)
        for p in range(7):
            for r in range(15):
                pick_pair(pool, table, dqkv, 64 * r, 128 * p, r * 15 + 2 * p, r * 15 + 2 * p + 1)
        for r in range(15):
            pick_single(pool, table, dqkv, 64 * r, 896, r * 15 + 14)
        for g in range(KVH):
            for r in range(15):
                pick_pair(pool, table, dqkv, 64 * r, QP + 128 * g, 225 + r * 5 + g, 300 + r * 5 + g)
        flush_pool(pool.at[pl.ds(0, pool_out.shape[0])], [pool_out], sems)


def inward(table, gq, gkv, cosine, sine, wqkv, normed_t, outs_t, branch, x_rows, residual, gain, total):
    rows = cosine.shape[0]
    tokens = x_rows.shape[0]
    blk = rows // 2
    steps = tokens // blk
    table = jnp.concatenate([table, jnp.full((15,), total, jnp.int32)])

    def early(i):
        return jnp.minimum(i, 1)

    def late(i):
        return jnp.maximum(i - 2, 0)

    def rows_of(width, at=lambda i: i):
        return pl.BlockSpec((blk, width), lambda i: (at(i), 0))

    def slabs(at):
        return pl.BlockSpec((KVH, blk, 128), lambda i: (0, at(i), 0))

    def all_of(*shape):
        return pl.BlockSpec(shape, lambda i: (0, 0))

    features = pl.BlockSpec((QP // steps, rows), lambda i: (i, 0))
    return pl.pallas_call(
        inward_kernel,
        grid=(steps,),
        out_shape=[
            jax.ShapeDtypeStruct((tokens // rows, D, rows), f32),
            jax.ShapeDtypeStruct((1, D), f32),
            jax.ShapeDtypeStruct((total, 32, 128), bf16),
        ],
        in_specs=[
            SM, rows_of(QP, early), rows_of(QP, late), slabs(early), slabs(late),
            rows_of(128, lambda i: i % 2), rows_of(128, lambda i: i % 2),
            all_of(D, CW), all_of(D, tokens), features, features,
            all_of(tokens, D), rows_of(D), rows_of(D), all_of(1, D),
        ],
        out_specs=[pl.BlockSpec((1, D, blk), lambda i: (i // 2, 0, i % 2)), all_of(1, D), ANY],
        scratch_shapes=[
            pltpu.VMEM((tokens, CW), bf16),
            pltpu.VMEM((D, CW), bf16),
            pltpu.VMEM((QP // steps, D), bf16),
            pltpu.VMEM((total + 1, 32, 128), bf16),
            pltpu.SemaphoreType.DMA((1,)),
        ],
        compiler_params=params(60),
        cost_estimate=cost(12e9, 30 << 20),
    )(table, *gq, *gkv, cosine, sine, wqkv, normed_t, *outs_t, branch, x_rows, residual, gain)


TOGETHER = 11


def shampoo_kernel(
    filled, sum_a, sum_f, master, stat_left, stat_right, root_left, root_right,
    grads_out, left_out, right_out, master_out, grads, lefts, rights, gram_left, gram_right, step,
):
    slots = master.shape[1]
    n_a = sum_a.shape[0] // 32
    for source, target in ((root_left, lefts), (root_right, rights)):
        for r in range(32):
            both = jnp.concatenate(
                [source[64 * r : 64 * r + 64, :], source[64 * (r + 32) : 64 * (r + 32) + 64, :]], axis=0
            )
            target[pl.ds(r, slots, stride=32), :] = both.T

    def square(rows):
        return jnp.concatenate([rows[:, :64], rows[:, 64:]], axis=0)

    def folded(rows):
        return jnp.concatenate([rows[:32], rows[32:]], axis=1)

    def keep(source, count, shift):
        def one(s, _):
            grad = source[pl.ds(pl.multiple_of(s * 32, 32), 32), :]
            at = pl.ds(pl.multiple_of((s + shift) * 32, 32), 32)
            grads[at, :] = jnp.where(filled[s + shift] > 0, grad.astype(f32), 0.0)
            return 0

        lax.fori_loop(0, count, one, 0, unroll=8)

    keep(sum_a, n_a, 0)
    keep(sum_f, slots - n_a, n_a)

    def several(i, _):
        spans = [pl.ds(pl.multiple_of((TOGETHER * i + t) * 32, 32), 32) for t in range(TOGETHER)]
        grad = [square(grads[span, :]).astype(bf16) for span in spans]
        left = [square(lefts[span, :]).astype(bf16) for span in spans]
        right = [square(rights[span, :]).astype(bf16) for span in spans]
        half = [jnp.dot(a, g, preferred_element_type=f32) for a, g in zip(left, grad)]
        gram_l = [nt_dot(g, g) for g in grad]
        gram_r = [tn_dot(g, g) for g in grad]
        whole = [jnp.dot(h.astype(bf16), b, preferred_element_type=f32) for h, b in zip(half, right)]
        for t, span in enumerate(spans):
            gram_left[span, :] = folded(gram_l[t])
            gram_right[span, :] = folded(gram_r[t])
            step[span, :] = folded(whole[t])
        return 0

    lax.fori_loop(0, grads.shape[0] // (32 * TOGETHER), several, 0)

    for r in range(32):
        first = slice(64 * r, 64 * r + 64)
        second = slice(64 * (r + 32), 64 * (r + 32) + 64)
        rows = pl.ds(r, slots, stride=32)
        flipped = grads[rows, :].T
        grads_out[first, :] = flipped[:64]
        grads_out[second, :] = flipped[64:]
        for source, stat, out in ((gram_left, stat_left, left_out), (gram_right, stat_right, right_out)):
            flipped = source[rows, :].T
            out[first, :] = decay_rate * stat[first, :] + (1.0 - decay_rate) * flipped[:64]
            out[second, :] = decay_rate * stat[second, :] + (1.0 - decay_rate) * flipped[64:]
        flipped = step[rows, :].T
        master_out[first, :] = master[first, :] - step_rate * flipped[:64]
        master_out[second, :] = master[second, :] - step_rate * flipped[64:]


def shampoo(filled, sum_a, sum_f, *arrays):
    slots = arrays[0].shape[0]
    native = [a.transpose(1, 2, 0).reshape(TL * TL, slots) for a in arrays]
    scratch = pltpu.VMEM((-(-slots // TOGETHER) * TOGETHER * 32, 128), f32)
    results = pl.pallas_call(
        shampoo_kernel,
        out_shape=[jax.ShapeDtypeStruct((TL * TL, slots), f32)] * 4,
        in_specs=[SM] + [VM] * 7,
        out_specs=[VM] * 4,
        scratch_shapes=[scratch] * 6,
        compiler_params=params(48),
        cost_estimate=cost(1e9, 24 << 20),
    )(filled, sum_a.reshape(-1, 128), sum_f.reshape(-1, 128), *native)
    return [r.reshape(TL, TL, slots).transpose(2, 0, 1) for r in results]


def fold(tiles):
    return jnp.concatenate([tiles[:, :32, :], tiles[:, 32:, :]], axis=2)


def shards(
    inputs,
    cotangent,
    lengths,
    order,
    owner_slots,
    master,
    stat_left,
    stat_right,
    root_left,
    root_right,
    gains,
    gain_stats,
):
    micro, rows = inputs.shape[1], inputs.shape[2]
    n_ctx, n_wt = lax.axis_size("ctx"), lax.axis_size("wt")
    devices = n_ctx * n_wt
    line = is_line(n_ctx, n_wt)
    tokens = micro * rows
    cap = master.shape[0]
    cap_a = NTA // devices + NTA // (8 * devices) + 2
    cap_f = cap - cap_a
    c = lax.axis_index("ctx")
    w = lax.axis_index("wt")

    x_t = inputs[0].transpose(0, 2, 1)
    low_master = fold(master.astype(bf16))
    own_a, own_f = low_master[:cap_a], low_master[cap_a:]
    own_a, own_f = low_master[:cap_a], low_master[cap_a:]
    owner, within = owner_slots // cap, owner_slots % cap
    whole_a = owner[:NTA] * cap_a + within[:NTA]
    whole_f = owner[NTA:] * cap_f + within[NTA:] - cap_a

    blocks = order.shape[0]
    ids = jnp.arange(blocks, dtype=jnp.int32)
    my_blocks = jnp.sum(jnp.where(ids[None, :] == 2 * c + jnp.arange(2)[:, None], order[None, :], 0), axis=1)
    position = (my_blocks[:, None] * (rows // 2) + jnp.arange(rows // 2, dtype=jnp.int32)[None, :]).reshape(rows)
    lane = np.arange(128)
    frequency = jnp.asarray(rope_base, f32) ** (-(jnp.asarray(lane % 32, f32)) * 2.0 / HD)
    angle = position.astype(f32)[:, None] * frequency[None, :]
    cosine = jnp.cos(angle)
    sine = jnp.sin(angle) * jnp.where(lane % 64 < 32, -1.0, 1.0).astype(f32)[None, :]
    metas = [
        jnp.concatenate([my_blocks, lengths[0, m][None], c[None], order]).astype(jnp.int32)
        for m in range(micro)
    ]

    if line:
        q, normed_attn_t, x_low, kv_first, kv_late, wqkv, wo, pool_f = front(
            whole_a, own_a, own_f, x_t, gains[0:1], cosine, sine
        )
        pool_f = pool_f.reshape(devices * cap_f, 32, 128)
        chunks = [kv_first, lax.all_gather(kv_late, "ctx", axis=0)]
    else:
        parts_a = [lax.all_gather(own_a, AXES, axis=0, tiled=True)]
        pool_f = lax.all_gather(own_f, AXES, axis=0, tiled=True)
        wqkv, wo = assemble(assemble_attn_kernel, parts_a, whole_a, [(D, CW), (QP, D)])
        x_low = inputs.reshape(tokens, D)
        q, kv, normed_attn = qkv_rows(x_low, gains[0:1], wqkv, cosine, sine, micro)
        normed_attn_t = normed_attn.T
        chunks = [lax.all_gather(kv[m], "ctx", axis=0) for m in range(micro)]
    forward = [flash_forward(0, metas[0], q, chunks[0])]
    wgu, wd = assemble_ffn(after(whole_f, forward[0][0]), pool_f)
    forward.append(flash_forward(1, metas[1], q, after(chunks[1], wgu)))
    scalars = jnp.concatenate([my_blocks, lengths[0]]).astype(jnp.int32)
    cot_t = cotangent[0].transpose(0, 2, 1)
    outs = [f[0] for f in forward]
    (mixed_t, normed_ffn_t, hidden_t, grad_gu, grad_out, grad_branch, grad_residual, grad_attn, gain_ffn) = middle(
        scalars, wgu, wd, outs, wo, x_low, cot_t, gains[1:2]
    )
    def flash_back(m):
        out, _, lse = forward[m]
        return flash_backward(m, metas[m], q, out, grad_attn, lse, cosine, sine, chunks[m])

    gq_0, gkv_0 = flash_back(0)
    gkv_0 = lax.psum_scatter(gkv_0, "ctx", scatter_dimension=0, tiled=False)
    grad_out = after(grad_out, gq_0)
    pool_f = ffn_grads(whole_f, normed_ffn_t, grad_gu, hidden_t, grad_out, devices * cap_f)
    grad_attn = after(grad_attn, pool_f)
    gq_1, gkv_1 = flash_back(1)
    if line:
        near_f, half_x, half_y, gkv_1 = back_home(pool_f.reshape(4, 4, 2, cap_f, 32, 128), gkv_1)
        other_x, other_y = flip(half_x, 2), flip(half_y, 4)
    else:
        sum_f = lax.psum_scatter(pool_f.astype(f32), AXES, scatter_dimension=0, tiled=True)
        gkv_1 = lax.psum_scatter(gkv_1, "ctx", scatter_dimension=0, tiled=False).astype(f32)
    input_grad_t, gain_attn, pool_a = inward(
        whole_a, (gq_0, gq_1), (gkv_0, gkv_1), cosine, sine, wqkv, normed_attn_t, [f[1] for f in forward], grad_branch, x_low,
        grad_residual, gains[0:1], devices * cap_a,
    )
    gain_terms = jnp.concatenate([gain_attn, gain_ffn])
    if line:
        other_y, other_x = after([other_y, other_x], pool_a)
        gain_rows = jnp.pad(gain_terms.reshape(15, 128), ((0, 1), (0, 0)))
        pool_a = pool_a.reshape(4, 4, 2, cap_a, 32, 128)
        sum_a, sum_f, gain_rows = tail(pool_a, near_f, other_x, other_y, gain_rows)
        gain_grads = gain_rows[:15].reshape(2, D)
    else:
        sum_a = lax.psum_scatter(pool_a.astype(f32), AXES, scatter_dimension=0, tiled=True)
        gain_grads = lax.psum(gain_terms, AXES)

    here = (c * n_wt + w) * cap + jnp.arange(cap, dtype=jnp.int32)
    filled = jnp.max((owner_slots[None, :] == here[:, None]).astype(jnp.int32), axis=1)
    tile_grads, new_left, new_right, new_master = shampoo(
        filled, sum_a, sum_f, master, stat_left, stat_right, root_left, root_right
    )
    new_gain_stats = decay_rate * gain_stats + (1.0 - decay_rate) * gain_grads * gain_grads
    new_gains = gains - gain_rate * gain_grads * lax.rsqrt(new_gain_stats)
    return (
        mixed_t.transpose(0, 2, 1)[None],
        input_grad_t.transpose(0, 2, 1)[None],
        tile_grads,
        new_left,
        new_right,
        new_master,
        gain_grads,
        new_gain_stats,
        new_gains,
    )


def solution(mesh):
    in_specs = (
        P("wt", None, "ctx", None),
        P("wt", None, "ctx", None),
        P("wt", None),
        P(),
        P(),
        P(AXES, None, None),
        P(AXES, None, None),
        P(AXES, None, None),
        P(AXES, None, None),
        P(AXES, None, None),
        P(),
        P(),
    )
    out_specs = (
        P("wt", None, "ctx", None),
        P("wt", None, "ctx", None),
        P(AXES, None, None),
        P(AXES, None, None),
        P(AXES, None, None),
        P(AXES, None, None),
        P(),
        P(),
        P(),
    )
    return jax.shard_map(shards, mesh=mesh, in_specs=in_specs, out_specs=out_specs, check_vma=False)
```

```python
import functools

import jax
import jax.numpy as jnp
import numpy as np
from jax import lax
from jax.experimental import pallas as pl
from jax.experimental.pallas import tpu as pltpu
from jax.sharding import PartitionSpec as P

D = 960
FF = 2560
QH = 15
KVH = 5
HD = 64
TL = 64
QW = 960
KVW = 320
GRP = 3
NTA = 600
NT = 2400
QP = 1024
CW = 1664
BLK = 256
AXES = ("ctx", "wt")

epsilon = 1e-05
decay_rate = 0.95
step_rate = 0.05
gain_rate = 0.05
rope_base = 10000.0
blocked_score = -1e30
bf16 = jnp.bfloat16
f32 = jnp.float32
VM = pl.BlockSpec(memory_space=pltpu.VMEM)
SM = pl.BlockSpec(memory_space=pltpu.SMEM)
ANY = pl.BlockSpec(memory_space=pl.ANY)


def params(megabytes, **kwargs):
    return pltpu.CompilerParams(vmem_limit_bytes=megabytes << 20, **kwargs)


def cost(flops, nbytes, trans=0):
    return pl.CostEstimate(flops=int(flops), bytes_accessed=int(nbytes), transcendentals=int(trans))


def after(x, *others):
    return lax.optimization_barrier((x, others))[0]


def is_line(n_ctx, n_wt):
    return n_ctx == 4 and n_wt == 8


def flip(x, bit):
    return lax.ppermute(x, "wt", [(i, i ^ bit) for i in range(8)])


def tile_halves(n):
    return (n + 1) // 2


def load_parts(parts, pool, sems):
    at = 0
    copies = []
    for i, part in enumerate(parts):
        rows = part.shape[0]
        copies.append(pltpu.make_async_copy(part, pool.at[pl.ds(at, rows)], sems.at[i]))
        at += rows
    for copy in copies:
        copy.start()
    for copy in copies:
        copy.wait()


def place_pair(pool, table, ref, row, lane, a, b):
    first = pool[table[a]]
    second = pool[table[b]]
    ref[pl.ds(row, 32), lane : lane + 128] = jnp.concatenate([first[:, :64], second[:, :64]], axis=1)
    ref[pl.ds(row + 32, 32), lane : lane + 128] = jnp.concatenate([first[:, 64:], second[:, 64:]], axis=1)


def place_single(pool, table, ref, row, lane, a):
    first = pool[table[a]]
    ref[pl.ds(row, 32), lane : lane + 64] = first[:, :64]
    ref[pl.ds(row + 32, 32), lane : lane + 64] = first[:, 64:]


def assemble_attn_kernel(count, table, *refs):
    parts, (wqkv, wo, pool, sems) = refs[:count], refs[count:]
    load_parts(parts, pool, sems)
    attn_rows(pool, table, wqkv, wo)


def attn_rows(pool, table, wqkv, wo):
    def qkv_row(r, _):
        row = pl.multiple_of(r * 64, 64)
        for p in range(7):
            place_pair(pool, table, wqkv, row, 128 * p, r * 15 + 2 * p, r * 15 + 2 * p + 1)
        place_single(pool, table, wqkv, row, 896, r * 15 + 14)
        wqkv[pl.ds(row, 64), 960:1024] = jnp.zeros((64, 64), bf16)
        for g in range(KVH):
            place_pair(pool, table, wqkv, row, QP + 128 * g, 225 + r * 5 + g, 300 + r * 5 + g)
        for p in range(7):
            place_pair(pool, table, wo, row, 128 * p, 375 + r * 15 + 2 * p, 375 + r * 15 + 2 * p + 1)
        place_single(pool, table, wo, row, 896, 375 + r * 15 + 14)
        return 0

    lax.fori_loop(0, 15, qkv_row, 0)
    wo[pl.ds(960, 64), :] = jnp.zeros((64, D), bf16)


def gu_rows(pool, table, wgu, first, last):
    def gu_row(r, _):
        row = pl.multiple_of(r * 64, 64)
        for m in range(2):
            for p in range(20):
                base = 600 * m + r * 40 + 2 * p
                place_pair(pool, table, wgu, row, FF * m + 128 * p, base, base + 1)
        return 0

    lax.fori_loop(first, last, gu_row, 0)


def d_rows(pool, table, wd, first, last):
    def d_row(r, _):
        row = pl.multiple_of(r * 64, 64)
        for p in range(7):
            place_pair(pool, table, wd, row, 128 * p, 1200 + r * 15 + 2 * p, 1200 + r * 15 + 2 * p + 1)
        place_single(pool, table, wd, row, 896, 1200 + r * 15 + 14)
        return 0

    lax.fori_loop(first, last, d_row, 0)


def assemble(kernel, parts, table, shapes):
    total = sum(p.shape[0] for p in parts)
    out_bytes = sum(2 * a * b for a, b in shapes)
    return pl.pallas_call(
        functools.partial(kernel, len(parts)),
        out_shape=[jax.ShapeDtypeStruct(s, bf16) for s in shapes],
        in_specs=[SM] + [ANY] * len(parts),
        out_specs=[VM] * len(shapes),
        scratch_shapes=[pltpu.VMEM((total, 32, 128), bf16), pltpu.SemaphoreType.DMA((len(parts),))],
        compiler_params=params(52),
        cost_estimate=cost(0, 4 * out_bytes),
    )(table, *parts)


def pick_pair(pool, table, ref, row, lane, a, b):
    block = ref[pl.ds(row, 64), lane : lane + 128]
    pool[table[a]] = jnp.concatenate([block[:32, :64], block[32:, :64]], axis=1)
    pool[table[b]] = jnp.concatenate([block[:32, 64:], block[32:, 64:]], axis=1)


def pick_single(pool, table, ref, row, lane, a):
    block = ref[pl.ds(row, 64), lane : lane + 64]
    pool[table[a]] = jnp.concatenate([block[:32], block[32:]], axis=1)


def flush_pool(pool, outs, sems):
    at = 0
    copies = []
    for i, out in enumerate(outs):
        rows = out.shape[0]
        copies.append(pltpu.make_async_copy(pool.at[pl.ds(at, rows)], out, sems.at[i]))
        at += rows
    for copy in copies:
        copy.start()
    for copy in copies:
        copy.wait()


def swap_halves(x):
    lane = lax.broadcasted_iota(jnp.int32, x.shape, 1)
    return jnp.where(lane % 64 < 32, pltpu.roll(x, 96, 1), pltpu.roll(x, 32, 1))


def qkv_kernel(x_ref, gain_ref, w_ref, cos_ref, sin_ref, q_ref, kv_ref, normed_ref):
    x = x_ref[...].astype(f32)
    inverse = lax.rsqrt(jnp.mean(x * x, axis=1, keepdims=True) + epsilon)
    normed = (x * inverse * gain_ref[...]).astype(bf16)
    normed_ref[...] = normed
    cosine, sine = cos_ref[...], sin_ref[...]
    lane = lax.broadcasted_iota(jnp.int32, cosine.shape, 1)
    left = lane < 64
    for p in range(8):
        rows = jnp.dot(normed, w_ref[:, 128 * p : 128 * p + 128], preferred_element_type=f32)
        rows = (rows * cosine + swap_halves(rows) * sine).astype(bf16).astype(f32) * 0.125
        q_ref[2 * p] = jnp.where(left, rows, 0.0).astype(bf16)
        if 2 * p + 1 < QH:
            q_ref[2 * p + 1] = jnp.where(left, pltpu.roll(rows, 64, 1), 0.0).astype(bf16)
    cosine = jnp.where(left, cosine, 1.0)
    sine = jnp.where(left, sine, 0.0)
    for g in range(KVH):
        at = QP + 128 * g
        rows = jnp.dot(normed, w_ref[:, at : at + 128], preferred_element_type=f32)
        kv_ref[0, g] = (rows * cosine + swap_halves(rows) * sine).astype(bf16)


def qkv_rows(x, gain, wqkv, cosine, sine, micro):
    tokens = x.shape[0]
    rows = tokens // micro
    blk = min(BLK, rows)
    steps = tokens // blk
    per = steps // micro
    return pl.pallas_call(
        qkv_kernel,
        grid=(steps,),
        out_shape=[
            jax.ShapeDtypeStruct((QH, tokens, 128), bf16),
            jax.ShapeDtypeStruct((micro, KVH, rows, 128), bf16),
            jax.ShapeDtypeStruct((tokens, D), bf16),
        ],
        in_specs=[
            pl.BlockSpec((blk, D), lambda i: (i, 0)),
            pl.BlockSpec((1, D), lambda i: (0, 0)),
            pl.BlockSpec((D, CW), lambda i: (0, 0)),
            pl.BlockSpec((blk, 128), lambda i: (i % per, 0)),
            pl.BlockSpec((blk, 128), lambda i: (i % per, 0)),
        ],
        out_specs=[
            pl.BlockSpec((QH, blk, 128), lambda i: (0, i, 0)),
            pl.BlockSpec((1, KVH, blk, 128), lambda i: (i // per, 0, i % per, 0)),
            pl.BlockSpec((blk, D), lambda i: (i, 0)),
        ],
        compiler_params=params(40),
        cost_estimate=cost(2 * tokens * D * CW, 14 << 20),
    )(x, gain, wqkv, cosine, sine)


def remote(src, dst, send, recv, device):
    return pltpu.make_async_remote_copy(
        src_ref=src,
        dst_ref=dst,
        send_sem=send,
        recv_sem=recv,
        device_id=device,
        device_id_type=pl.DeviceIdType.MESH,
    )


def greet(c, w, far):
    barrier = pltpu.get_barrier_semaphore()

    def hail(device):
        pl.semaphore_signal(barrier, inc=1, device_id=device, device_id_type=pl.DeviceIdType.MESH)

    for bit in (1, 2, 4):
        hail({"wt": w ^ bit})
    if far:
        hail({"ctx": c ^ 2})

    @pl.when(c < 3)
    def _():
        hail({"ctx": c + 1})

    @pl.when(c > 0)
    def _():
        hail({"ctx": c - 1})

    inner = jnp.logical_and(c > 0, c < 3)

    @pl.when(inner)
    def _():
        pl.semaphore_wait(barrier, 5 + far)

    @pl.when(jnp.logical_not(inner))
    def _():
        pl.semaphore_wait(barrier, 4 + far)


class Gather:
    def __init__(self, pool, sems, c, w):
        self.pool, self.sems, self.c, self.w = pool, sems, c, w
        self.n = pool.shape[2]
        self.n1 = tile_halves(self.n)
        self.x, self.y, self.core = {"wt": w ^ 2}, {"wt": w ^ 4}, {"wt": w ^ 1}

    def copy(self, k, owner, lane, device, part=None):
        ref = self.pool.at[k, owner]
        if part is not None:
            ref = ref.at[pl.ds(part[0], part[1])]
        return remote(ref, ref, self.sems.at[k, lane], self.sems.at[k, lane + 1], device)

    def up(self, k):
        return self.copy(k, self.w, 0, {"ctx": self.c + 1})

    def down(self, k):
        return self.copy(k, self.w, 2, {"ctx": self.c - 1})

    def over_x(self, k, back=0):
        return self.copy(k, self.w ^ back, 4, self.x)

    def over_y(self, k, back=0):
        return self.copy(k, self.w ^ back, 6, self.y)

    def diag_x(self, k, owner):
        return self.copy(k, owner, 8, self.x, (0, self.n1))

    def diag_y(self, k, owner):
        return self.copy(k, owner, 10, self.y, (self.n1, self.n - self.n1))

    def over_core(self, k, quad, back=0):
        return self.copy(k, self.w ^ (2 * quad) ^ back, 12 + 2 * quad, self.core)

    def send_line(self, k, low, high):
        if low:

            @pl.when(self.c < 3)
            def _():
                self.up(k).start()

        if high:

            @pl.when(self.c > 0)
            def _():
                self.down(k).start()

    def send_near(self, k):
        self.over_x(k).start()
        self.over_y(k).start()
        self.over_core(k, 0).start()

    def first(self):
        self.send_line(self.c, True, True)

    def sides(self, s):
        return [(self.c >= s, self.c - s, True), (self.c + s <= 3, self.c + s, False)]

    def line_step(self, s, near=True):
        for valid, k, below in self.sides(s):

            @pl.when(valid)
            def _(k=k, below=below):
                if below:
                    self.up(k).wait_recv()
                else:
                    self.down(k).wait_recv()
                if s < 3:
                    self.send_line(k, below, not below)
                if near:
                    self.send_near(k)

    def each(self, s, act):
        if s == 0:
            act(self.c)
            return
        for valid, k, _ in self.sides(s):

            @pl.when(valid)
            def _(k=k):
                act(k)

    def near_step(self, s):
        def act(k):
            self.over_x(k, 2).wait_recv()
            self.diag_y(k, self.w ^ 2).start()
            self.over_core(k, 1).start()
            self.over_y(k, 4).wait_recv()
            self.diag_x(k, self.w ^ 4).start()
            self.over_core(k, 2).start()

        self.each(s, act)

    def diag_step(self, s):
        def act(k):
            self.diag_x(k, self.w ^ 6).wait_recv()
            self.diag_y(k, self.w ^ 6).wait_recv()
            self.over_core(k, 3).start()

        self.each(s, act)

    def finish(self):
        for k in range(4):
            for quad in range(4):
                self.over_core(k, quad, 1).wait_recv()

    def drain(self):
        for k in range(4):

            @pl.when(jnp.logical_and(k <= self.c, self.c < 3))
            def _(k=k):
                self.up(k).wait_send()

            @pl.when(jnp.logical_and(k >= self.c, self.c > 0))
            def _(k=k):
                self.down(k).wait_send()

            self.over_x(k).wait_send()
            self.over_y(k).wait_send()
            self.diag_x(k, self.w ^ 4).wait_send()
            self.diag_y(k, self.w ^ 2).wait_send()
            for quad in range(4):
                self.over_core(k, quad).wait_send()


def front_kernel(
    table, own_a, own_f, x_ref, gain_ref, cos_ref, sin_ref,
    q_ref, normed_t, rows_ref, kv_ref, late_ref, wqkv, wo, pool_f,
    normed_ref, pool_a, kv_own, sems_a, sems_f, sems_kv, sems,
):
    c, w = lax.axis_index("ctx"), lax.axis_index("wt")
    take_a = pltpu.make_async_copy(own_a, pool_a.at[c, w], sems.at[0])
    take_f = pltpu.make_async_copy(own_f, pool_f.at[c, w], sems.at[1])
    take_a.start()
    take_f.start()
    greet(c, w, 0)
    take_a.wait()
    a = Gather(pool_a, sems_a, c, w)
    f = Gather(pool_f, sems_f, c, w)
    a.first()
    a.send_near(c)

    rows = x_ref.shape[2]
    blk = BLK
    for m in range(2):
        for half in range(rows // blk):
            part = x_ref[m, :, blk * half : blk * half + blk].T
            span = slice(m * rows + blk * half, m * rows + blk * half + blk)
            rows_ref[span, :] = part
            wide = part.astype(f32)
            inverse = lax.rsqrt(jnp.mean(wide * wide, axis=1, keepdims=True) + epsilon)
            normed = (wide * inverse * gain_ref[...]).astype(bf16)
            normed_ref[span, :] = normed
            normed_t[:, span] = normed.T

    a.line_step(1)
    a.near_step(0)
    a.line_step(2)
    take_f.wait()
    f.first()
    a.near_step(1)
    a.diag_step(0)
    a.line_step(3)
    a.near_step(2)
    a.diag_step(1)
    a.near_step(3)
    f.send_near(c)
    a.diag_step(2)
    a.diag_step(3)
    f.line_step(1)
    a.finish()

    flat = pool_a.reshape(pool_a.shape[0] * pool_a.shape[1] * pool_a.shape[2], 32, 128)
    attn_rows(flat, table, wqkv, wo)
    f.line_step(2)
    f.near_step(0)

    lane = lax.broadcasted_iota(jnp.int32, (blk, 128), 1)
    left = lane < 64

    def qkv_block(i, _):
        at = pl.multiple_of(i * blk, blk)
        normed = normed_ref[pl.ds(at, blk), :]
        within = pl.multiple_of((i % (rows // blk)) * blk, blk)
        cosine, sine = cos_ref[pl.ds(within, blk), :], sin_ref[pl.ds(within, blk), :]
        key_cosine = jnp.where(left, cosine, 1.0)
        key_sine = jnp.where(left, sine, 0.0)
        for g in range(KVH):
            spot = QP + 128 * g
            part = jnp.dot(normed, wqkv[:, spot : spot + 128], preferred_element_type=f32)
            part = (part * key_cosine + swap_halves(part) * key_sine).astype(bf16)
            kv_own[i // (rows // blk), g, pl.ds(within, blk), :] = part
        for p in range(8):
            part = jnp.dot(normed, wqkv[:, 128 * p : 128 * p + 128], preferred_element_type=f32)
            part = (part * cosine + swap_halves(part) * sine).astype(bf16).astype(f32) * 0.125
            q_ref[2 * p, pl.ds(at, blk), :] = jnp.where(left, part, 0.0).astype(bf16)
            if 2 * p + 1 < QH:
                other = jnp.where(left, pltpu.roll(part, 64, 1), 0.0).astype(bf16)
                q_ref[2 * p + 1, pl.ds(at, blk), :] = other
        return 0

    def kv_move(src, k, lane, step):
        return remote(src, kv_ref.at[k], sems_kv.at[k, lane], sems_kv.at[k, lane + 1], {"ctx": c + step})

    lax.fori_loop(0, rows // blk, qkv_block, 0)
    keep = pltpu.make_async_copy(kv_own.at[0], kv_ref.at[c], sems.at[2])
    keep.start()

    @pl.when(c < 3)
    def _():
        kv_move(kv_own.at[0], c, 0, 1).start()

    @pl.when(c > 0)
    def _():
        kv_move(kv_own.at[0], c, 2, -1).start()

    lax.fori_loop(rows // blk, 2 * rows // blk, qkv_block, 0)
    late = pltpu.make_async_copy(kv_own.at[1], late_ref, sems.at[3])
    late.start()

    def kv_step(s):
        @pl.when(c >= s)
        def _():
            kv_move(kv_ref.at[c - s], c - s, 0, 1).wait_recv()
            if s < 3:

                @pl.when(c < 3)
                def _():
                    kv_move(kv_ref.at[c - s], c - s, 0, 1).start()

        @pl.when(c + s <= 3)
        def _():
            kv_move(kv_ref.at[c + s], c + s, 2, -1).wait_recv()
            if s < 3:

                @pl.when(c > 0)
                def _():
                    kv_move(kv_ref.at[c + s], c + s, 2, -1).start()

    f.line_step(3)
    f.near_step(1)
    f.diag_step(0)
    kv_step(1)
    f.near_step(2)
    f.diag_step(1)
    f.near_step(3)
    kv_step(2)
    f.diag_step(2)
    f.diag_step(3)
    f.finish()
    kv_step(3)
    keep.wait()
    late.wait()
    for k in range(4):

        @pl.when(jnp.logical_and(k <= c, c < 3))
        def _(k=k):
            kv_move(kv_ref.at[k], k, 0, 1).wait_send()

        @pl.when(jnp.logical_and(k >= c, c > 0))
        def _(k=k):
            kv_move(kv_ref.at[k], k, 2, -1).wait_send()

    a.drain()
    f.drain()


def front(table, own_a, own_f, x_t, gain, cosine, sine):
    micro, _, rows = x_t.shape
    tokens = micro * rows
    n_a, n_f = own_a.shape[0], own_f.shape[0]
    return pl.pallas_call(
        front_kernel,
        out_shape=[
            jax.ShapeDtypeStruct((QH, tokens, 128), bf16),
            jax.ShapeDtypeStruct((D, tokens), bf16),
            jax.ShapeDtypeStruct((tokens, D), bf16),
            jax.ShapeDtypeStruct((4, KVH, rows, 128), bf16),
            jax.ShapeDtypeStruct((KVH, rows, 128), bf16),
            jax.ShapeDtypeStruct((D, CW), bf16),
            jax.ShapeDtypeStruct((QP, D), bf16),
            jax.ShapeDtypeStruct((4, 8, n_f, 32, 128), bf16),
        ],
        in_specs=[SM, ANY, ANY, VM, VM, VM, VM],
        out_specs=[VM, VM, VM, ANY, ANY, VM, VM, ANY],
        scratch_shapes=[
            pltpu.VMEM((tokens, D), bf16),
            pltpu.VMEM((4, 8, n_a, 32, 128), bf16),
            pltpu.VMEM((micro, KVH, rows, 128), bf16),
            pltpu.SemaphoreType.DMA((4, 20)),
            pltpu.SemaphoreType.DMA((4, 20)),
            pltpu.SemaphoreType.DMA((4, 4)),
            pltpu.SemaphoreType.DMA((4,)),
        ],
        compiler_params=params(48, collective_id=0, has_side_effects=True),
        cost_estimate=cost(40e9, 40 << 20),
    )(table, own_a, own_f, x_t, gain, cosine, sine)


class Line:
    def __init__(self, terms, send, recv, sems, c):
        self.terms, self.send, self.recv, self.sems, self.c = terms, send, recv, sems, c
        self.count = recv.shape[2]

    def copy(self, way, k):
        sems = self.sems
        return remote(
            self.send.at[k], self.recv.at[way, k], sems.at[way, k, 0], sems.at[way, k, 1],
            {"ctx": self.c + 1 - 2 * way},
        )

    def loop(self, act):
        def body(j, _):
            act(j)
            return 0

        lax.fori_loop(0, self.count, body, 0)

    def start(self):
        for way in (0, 1):

            @pl.when(self.c == 3 * way)
            def _(way=way):
                for far in (3, 2, 1):
                    k = far if way == 0 else 3 - far

                    def take(j, k=k):
                        self.send[k, j] = self.terms(k, j).astype(bf16)

                    self.loop(take)
                    self.copy(way, k).start()

    def join(self, way, k):
        self.copy(way, k).wait_recv()

        def act(j):
            self.send[k, j] = (self.terms(k, j) + self.recv[way, k, j].astype(f32)).astype(bf16)

        self.loop(act)
        self.copy(way, k).start()

    def step(self, number):
        lists = {1: ((0, 3), (0, 2), (1, 0)), 2: ((1, 0), (1, 1), (0, 3))}
        for inner, order in lists.items():

            @pl.when(self.c == inner)
            def _(order=order):
                self.join(*order[number])

    def finish(self, out):
        c, recv = self.c, self.recv

        @pl.when(c > 0)
        def _():
            self.copy(0, c).wait_recv()

        @pl.when(c < 3)
        def _():
            self.copy(1, c).wait_recv()

        def total(j):
            low = jnp.where(c > 0, recv[0, c, j].astype(f32), 0.0)
            high = jnp.where(c < 3, recv[1, c, j].astype(f32), 0.0)
            out[j] = self.terms(c, j) + low + high

        self.loop(total)

    def drain(self):
        for far in (3, 2, 1):
            for way, k in ((0, far), (1, 3 - far)):

                @pl.when(self.c < k if way == 0 else self.c > k)
                def _(way=way, k=k):
                    self.copy(way, k).wait_send()


class Plane:
    def __init__(self, pool, bufs, sems, c, w):
        self.pool, self.sems, self.c, self.w = pool, sems, c, w
        self.mine, self.theirs, self.diag_send, self.diag_recv, self.near_send, self.near_recv = bufs
        self.n = pool.shape[3]
        n1 = self.n1 = tile_halves(self.n)
        yx, core = w // 2, w % 2
        over_x, over_y, over_core = {"wt": w ^ 2}, {"wt": w ^ 4}, {"wt": w ^ 1}
        self.loads = [
            pltpu.make_async_copy(pool.at[:, yx ^ q, core], self.mine.at[q], sems.at[10 + q, 0]) for q in range(4)
        ]
        self.cores = [
            remote(pool.at[:, yx ^ q, 1 - core], self.theirs.at[q], sems.at[q, 0], sems.at[q, 1], over_core)
            for q in range(4)
        ]
        low, high = slice(0, n1), slice(n1, self.n)
        self.diag_x = self.move(self.diag_send.at[:, low], self.diag_recv.at[:, low], 4, over_x)
        self.diag_y = self.move(self.diag_send.at[:, high], self.diag_recv.at[:, high], 5, over_y)
        self.nears = {}
        for q in (1, 2):
            for part, cut in enumerate((low, high)):
                self.nears[q, part] = self.move(
                    self.near_send.at[q - 1, :, cut],
                    self.near_recv.at[q - 1, :, cut],
                    4 + 2 * q + part,
                    over_x if q == 1 else over_y,
                )

    def move(self, src, dst, lane, device):
        return remote(src, dst, self.sems.at[lane, 0], self.sems.at[lane, 1], device)

    def begin_loads(self):
        for q in (3, 1, 2, 0):
            self.loads[q].start()

    def begin(self):
        for q in (3, 1, 2, 0):
            self.cores[q].start()

    def each(self, act):
        def body(k, _):
            act(k)
            return 0

        lax.fori_loop(0, 4, body, 0)

    def both(self, q, k):
        return self.mine[q, k].astype(f32) + self.theirs[q, k].astype(f32)

    def ready(self, q):
        self.loads[q].wait()
        self.cores[q].wait()

    def diag(self):
        self.ready(3)

        def act(k):
            self.diag_send[k] = self.both(3, k).astype(bf16)

        self.each(act)
        self.diag_x.start()
        self.diag_y.start()

    def near(self, q):
        self.ready(q)

        def act(k):
            self.near_send[q - 1, k] = self.both(q, k).astype(bf16)

        self.each(act)
        self.nears[q, q - 1].start()

    def join(self, q):
        cut = slice(self.n1, self.n) if q == 1 else slice(0, self.n1)
        (self.diag_y if q == 1 else self.diag_x).wait_recv()

        def act(k):
            ours = self.near_send[q - 1, k, cut].astype(f32)
            self.near_send[q - 1, k, cut] = (ours + self.diag_recv[k, cut].astype(f32)).astype(bf16)

        self.each(act)
        self.nears[q, 2 - q].start()

    def join_out(self, q, out):
        cut = slice(self.n1, self.n) if q == 1 else slice(0, self.n1)
        (self.diag_y if q == 1 else self.diag_x).wait_recv()

        def act(k):
            ours = self.near_send[q - 1, k, cut].astype(f32)
            out[k] = (ours + self.diag_recv[k, cut].astype(f32)).astype(bf16)

        self.each(act)

    def arrive_half(self):
        self.ready(0)
        self.nears[1, 0].wait_recv()
        self.nears[2, 1].wait_recv()

    def own_half(self, k):
        n1 = self.n1
        near = jnp.concatenate([self.near_recv[0, k, :n1], self.near_recv[1, k, n1:]], axis=0)
        return self.both(0, k) + near.astype(f32)

    def drain_half(self):
        self.diag_x.wait_send()
        self.diag_y.wait_send()
        self.nears[1, 0].wait_send()
        self.nears[2, 1].wait_send()

    def arrive(self):
        self.ready(0)
        for part in (0, 1):
            for q in (1, 2):
                self.nears[q, part].wait_recv()

    def own(self, k):
        return self.both(0, k) + self.near_recv[0, k].astype(f32) + self.near_recv[1, k].astype(f32)

    def drain(self):
        self.diag_x.wait_send()
        self.diag_y.wait_send()
        for copy in self.nears.values():
            copy.wait_send()


def plane_scratch(n):
    tile = (32, 128)
    return [
        pltpu.VMEM((4, 4, n) + tile, bf16),
        pltpu.VMEM((4, 4, n) + tile, bf16),
        pltpu.VMEM((4, n) + tile, bf16),
        pltpu.VMEM((4, n) + tile, bf16),
        pltpu.VMEM((2, 4, n) + tile, bf16),
        pltpu.VMEM((2, 4, n) + tile, bf16),
        pltpu.SemaphoreType.DMA((14, 2)),
    ]


def line_scratch(shape):
    return [
        pltpu.VMEM((4,) + shape, bf16),
        pltpu.VMEM((2, 4) + shape, bf16),
        pltpu.SemaphoreType.DMA((2, 4, 2)),
    ]


def return_kernel(pool, kv_ref, sum_ref, x_out, y_out, kv_out, *scratch):
    c, w = lax.axis_index("ctx"), lax.axis_index("wt")
    plane = Plane(pool, scratch[:6], scratch[6], c, w)
    line = Line(lambda k, j: kv_ref[k, j].astype(f32), *scratch[7:], c)
    plane.begin_loads()
    greet(c, w, 0)
    plane.begin()

    line.start()
    plane.diag()
    plane.near(1)
    plane.near(2)
    line.step(0)
    plane.join_out(1, x_out)
    line.step(1)
    plane.join_out(2, y_out)
    line.step(2)
    plane.arrive_half()

    def own(k):
        sum_ref[k] = plane.own_half(k).astype(bf16)

    plane.each(own)
    line.finish(kv_out)
    plane.drain_half()
    line.drain()


def back_home(pool, kv_terms):
    n = pool.shape[3]
    n1 = tile_halves(n)
    return pl.pallas_call(
        return_kernel,
        out_shape=[
            jax.ShapeDtypeStruct((4, n, 32, 128), bf16),
            jax.ShapeDtypeStruct((4, n - n1, 32, 128), bf16),
            jax.ShapeDtypeStruct((4, n1, 32, 128), bf16),
            jax.ShapeDtypeStruct(kv_terms.shape[1:], f32),
        ],
        in_specs=[ANY, VM],
        out_specs=[VM] * 4,
        scratch_shapes=plane_scratch(n) + line_scratch(kv_terms.shape[1:]),
        compiler_params=params(60, collective_id=2, has_side_effects=True),
        cost_estimate=cost(30e9, 16 << 20),
    )(pool, kv_terms)


def tail_kernel(
    pool, ffn_ref, over_x, over_y, gain_ref, sum_ref, ffn_out, gain_out, own, gain_send, gain_recv, sems_gain, *scratch
):
    c, w = lax.axis_index("ctx"), lax.axis_index("wt")
    plane = Plane(pool, scratch[:6], scratch[6], c, w)
    line = Line(lambda k, j: own[k, j], *scratch[7:10], c)
    n1 = over_y.shape[1]

    def ffn_term(k, j):
        joined = jnp.where(j < n1, over_y[k, jnp.minimum(j, n1 - 1)], over_x[k, jnp.maximum(j - n1, 0)])
        return ffn_ref[k, j].astype(f32) + joined.astype(f32)

    ffn_line = Line(ffn_term, *scratch[10:13], c)
    plane.begin_loads()
    greet(c, w, 1)
    plane.begin()

    stages = [{"wt": w ^ 1}, {"wt": w ^ 2}, {"wt": w ^ 4}, {"ctx": c ^ 1}, {"ctx": c ^ 2}]
    copies = [
        remote(gain_send.at[i], gain_recv.at[i], sems_gain.at[i, 0], sems_gain.at[i, 1], stages[i]) for i in range(5)
    ]
    gain_send[0] = gain_ref[...]
    copies[0].start()

    def gain_step(i):
        copies[i].wait()
        total = gain_send[i] + gain_recv[i]
        if i < 4:
            gain_send[i + 1] = total
            copies[i + 1].start()
        else:
            gain_out[...] = total

    ffn_line.start()
    plane.diag()
    gain_step(0)
    plane.near(1)
    plane.near(2)
    ffn_line.step(0)
    gain_step(1)
    plane.join(1)
    plane.join(2)
    ffn_line.step(1)
    gain_step(2)
    plane.arrive()

    def own_sum(k):
        own[k] = plane.own(k)

    plane.each(own_sum)
    line.start()
    ffn_line.step(2)
    gain_step(3)
    for number in range(3):
        line.step(number)
    ffn_line.finish(ffn_out)
    gain_step(4)
    line.finish(sum_ref)
    plane.drain()
    line.drain()
    ffn_line.drain()


def tail(pool, ffn_terms, over_x, over_y, gains):
    n, n_f = pool.shape[3], ffn_terms.shape[1]
    tile = (32, 128)
    return pl.pallas_call(
        tail_kernel,
        out_shape=[
            jax.ShapeDtypeStruct((n,) + tile, f32),
            jax.ShapeDtypeStruct((n_f,) + tile, f32),
            jax.ShapeDtypeStruct(gains.shape, f32),
        ],
        in_specs=[ANY, VM, VM, VM, VM],
        out_specs=[VM, VM, VM],
        scratch_shapes=[
            pltpu.VMEM((4, n) + tile, f32),
            pltpu.VMEM((5,) + gains.shape, f32),
            pltpu.VMEM((5,) + gains.shape, f32),
            pltpu.SemaphoreType.DMA((5, 2)),
        ]
        + plane_scratch(n)
        + line_scratch((n,) + tile)
        + line_scratch((n_f,) + tile),
        compiler_params=params(48, collective_id=1, has_side_effects=True),
        cost_estimate=cost(30e9, 16 << 20),
    )(pool, ffn_terms, over_x, over_y, gains)


META = 4


def load_blocks(meta, part, pool, sems):
    blk = part.shape[2] // 2
    copies = []
    for k in range(2 * part.shape[0]):
        at = pl.multiple_of(meta[META + k] * blk, blk)
        source = part.at[k // 2, :, pl.ds(k % 2 * blk, blk), :]
        copies.append(pltpu.make_async_copy(source, pool.at[:, pl.ds(at, blk), :], sems.at[k]))
    for copy in copies:
        copy.start()
    for copy in copies:
        copy.wait()


def masked(scores, block, q_block, length):
    blk = scores.shape[1]
    key = block + lax.broadcasted_iota(jnp.int32, scores.shape, 0)
    query = q_block * blk + lax.broadcasted_iota(jnp.int32, scores.shape, 1)
    return jnp.where(jnp.logical_and(key <= query, key < length), scores, blocked_score)


def nt_dot(a, b):
    return lax.dot_general(a, b, (((1,), (1,)), ((), ())), preferred_element_type=f32)


def tn_dot(a, b):
    return lax.dot_general(a, b, (((0,), (0,)), ((), ())), preferred_element_type=f32)


def flash_forward_kernel(meta, q_ref, part, out_ref, turned_ref, lse_ref, pool, vt, peak, acc, turned, sems):
    load_blocks(meta, part, pool, sems)
    length = meta[2]
    blk = q_ref.shape[1] // 2
    live_blocks = (length + blk - 1) // blk
    turned[960:, :] = jnp.zeros((64, blk), f32)
    for g in range(KVH):
        vt[g, :64, :] = jnp.ones((64, vt.shape[2]), bf16)
        for k in range(pool.shape[1] // 256):
            vt[g, 64:, 256 * k : 256 * k + 256] = pool[g, 256 * k : 256 * k + 256, :].T[64:]
    for qi in range(2):
        q_block = meta[qi]
        blocks = jnp.minimum(q_block + 1, live_blocks)

        def group(g, _):
            queries = [q_ref[GRP * g + h, blk * qi : blk * qi + blk, :] for h in range(GRP)]
            for h in range(GRP):
                peak[h] = jnp.full((1, blk), blocked_score, f32)
                acc[h] = jnp.zeros((128, blk), f32)

            def step(block, wide, with_mask):
                start = pl.multiple_of(block * blk, blk)
                span = pl.ds(start, wide * blk)
                kv = pool[g, span, :]
                vals = vt[g, :, span]
                scores = [nt_dot(kv, queries[h]) for h in range(GRP)]
                if with_mask:
                    scores = [masked(t, start, q_block, length) for t in scores]
                before = [peak[h] for h in range(GRP)]
                now = [jnp.maximum(before[h], jnp.max(scores[h], axis=0, keepdims=True)) for h in range(GRP)]
                weights = [jnp.exp(scores[h] - now[h]).astype(bf16) for h in range(GRP)]
                for h in range(GRP):
                    peak[h] = now[h]
                    acc[h] = acc[h] * jnp.exp(before[h] - now[h]) + jnp.dot(
                        vals, weights[h], preferred_element_type=f32
                    )

            def plain(pair, _):
                step(2 * pair, 2, False)
                return 0

            pairs = (blocks - 1) // 2

            def plain4(quad, _):
                step(4 * quad, 4, False)
                return 0

            lax.fori_loop(0, pairs // 2, plain4, 0)

            @pl.when(pairs % 2 == 1)
            def _():
                plain(pairs - 1, 0)

            @pl.when(blocks % 2 == 1)
            def _():
                step(blocks - 1, 1, True)

            @pl.when(blocks % 2 == 0)
            def _():
                step(blocks - 2, 2, True)

            for h in range(GRP):
                total = acc[h][0:1, :]
                turned[pl.ds(pl.multiple_of((GRP * g + h) * HD, HD), HD), :] = acc[h][64:, :] / total
                lse_ref[GRP * g + h, :, blk * qi : blk * qi + blk] = peak[h] + jnp.log(total)
            return 0

        lax.fori_loop(0, KVH, group, 0)
        out_ref[blk * qi : blk * qi + blk, :] = turned[...].T.astype(bf16)
        turned_ref[:, blk * qi : blk * qi + blk] = turned[...].astype(bf16)


def flash_forward(m, meta, q, part):
    n_ctx, _, rows, _ = part.shape
    blk = rows // 2
    return pl.pallas_call(
        flash_forward_kernel,
        grid=(1,),
        out_shape=[
            jax.ShapeDtypeStruct((rows, QP), bf16),
            jax.ShapeDtypeStruct((QP, rows), bf16),
            jax.ShapeDtypeStruct((16, 1, rows), f32),
        ],
        in_specs=[SM, pl.BlockSpec((QH, rows, 128), lambda i: (0, m, 0)), ANY],
        out_specs=[
            pl.BlockSpec((rows, QP), lambda i: (0, 0)),
            pl.BlockSpec((QP, rows), lambda i: (0, 0)),
            pl.BlockSpec((16, 1, rows), lambda i: (0, 0, 0)),
        ],
        scratch_shapes=[
            pltpu.VMEM((KVH, n_ctx * rows, 128), bf16),
            pltpu.VMEM((KVH, 128, n_ctx * rows), bf16),
            pltpu.VMEM((GRP, 1, blk), f32),
            pltpu.VMEM((GRP, 128, blk), f32),
            pltpu.VMEM((QP, blk), f32),
            pltpu.SemaphoreType.DMA((2 * n_ctx,)),
        ],
        compiler_params=params(48),
        cost_estimate=cost(40e9, 8 << 20),
    )(meta, q, part)


def flash_backward_kernel(
    meta, q_ref, out_ref, grad_ref, lse_ref, cos_ref, sin_ref, part, gq_ref, gkv_ref,
    pool, kt, wide, delta, total, acc, turned, sides, sems,
):
    load_blocks(meta, part, pool, sems)
    length = meta[2]
    rows = q_ref.shape[1]
    blk = rows // 2
    live_blocks = (length + blk - 1) // blk
    total[...] = jnp.zeros_like(total)
    lane = lax.broadcasted_iota(jnp.int32, (rows, 128), 1)
    pick = lax.broadcasted_iota(jnp.int32, (16, 128), 0) == lax.broadcasted_iota(jnp.int32, (16, 128), 1) // 64
    pick = jnp.where(pick, 1.0, 0.0).astype(bf16)
    for g in range(KVH):
        for k in range(pool.shape[1] // 256):
            kt[g, :, 256 * k : 256 * k + 256] = pool[g, 256 * k : 256 * k + 256, :].T[:64]
    for p in range(8):
        slab = grad_ref[:, 128 * p : 128 * p + 128].astype(f32)
        wide[2 * p] = jnp.where(lane >= 64, pltpu.roll(slab, 64, 1), 0.0).astype(bf16)
        if 2 * p + 1 < QH:
            wide[2 * p + 1] = jnp.where(lane >= 64, slab, 0.0).astype(bf16)
        product = slab * out_ref[:, 128 * p : 128 * p + 128].astype(f32)
        high = product.astype(bf16)
        low = (product - high.astype(f32)).astype(bf16)
        both = nt_dot(pick, high) + nt_dot(pick, low)
        delta[2 * p] = both[0:1, :]
        delta[2 * p + 1] = both[1:2, :]
    turned[960:, :] = jnp.zeros((64, blk), f32)
    for qi in range(2):
        q_block = meta[qi]
        blocks = jnp.where(q_block < live_blocks, q_block + 1, 0)
        span = slice(blk * qi, blk * qi + blk)

        def group(g, _):
            for h in range(GRP):
                acc[h] = jnp.zeros((64, blk), f32)
                sides[2 * blk * h : 2 * blk * h + blk] = q_ref[GRP * g + h, span, :]
                sides[2 * blk * h + blk : 2 * blk * h + 2 * blk] = wide[GRP * g + h, span, :]

            def step(block, count, with_mask):
                start = pl.multiple_of(block * blk, blk)
                keys = pl.ds(start, count * blk)
                kv = pool[g, keys, :]
                keys_t = kt[g, :, keys]
                heads = [GRP * g + h for h in range(GRP)]
                scores = [nt_dot(kv, sides[2 * blk * h : 2 * blk * h + blk]) for h in range(GRP)]
                inner = [nt_dot(kv, sides[2 * blk * h + blk : 2 * blk * h + 2 * blk]) for h in range(GRP)]
                if with_mask:
                    scores = [masked(t, start, q_block, length) for t in scores]
                probs = [jnp.exp(scores[h] - lse_ref[heads[h], :, span]) for h in range(GRP)]
                change = [(probs[h] * (inner[h] - delta[heads[h], :, span])).astype(bf16) for h in range(GRP)]
                terms = []
                for h in range(GRP):
                    terms += [change[h], probs[h].astype(bf16)]
                total[g, keys, :] += jnp.dot(
                    jnp.concatenate(terms, axis=1), sides[...], preferred_element_type=f32
                )
                for h in range(GRP):
                    acc[h] = acc[h] + jnp.dot(keys_t, change[h], preferred_element_type=f32)

            def plain(pair, _):
                step(2 * pair, 2, False)
                return 0

            pairs = (blocks - 1) // 2

            def plain4(quad, _):
                step(4 * quad, 4, False)
                return 0

            lax.fori_loop(0, pairs // 2, plain4, 0)

            @pl.when(jnp.logical_and(pairs > 0, pairs % 2 == 1))
            def _():
                plain(pairs - 1, 0)

            @pl.when(jnp.logical_and(blocks > 0, blocks % 2 == 1))
            def _():
                step(blocks - 1, 1, True)

            @pl.when(jnp.logical_and(blocks > 0, blocks % 2 == 0))
            def _():
                step(blocks - 2, 2, True)

            for h in range(GRP):
                turned[pl.ds(pl.multiple_of((GRP * g + h) * HD, HD), HD), :] = acc[h] * 0.125
            return 0

        lax.fori_loop(0, KVH, group, 0)
        grads = turned[...].T
        cosine, sine = cos_ref[span, :], sin_ref[span, :]
        for p in range(8):
            slab = grads[:, 128 * p : 128 * p + 128]
            gq_ref[span, 128 * p : 128 * p + 128] = (slab * cosine - swap_halves(slab) * sine).astype(bf16)
    for k in range(2 * gkv_ref.shape[0]):
        at = pl.multiple_of(meta[META + k] * blk, blk)
        gkv_ref[k // 2, :, k % 2 * blk : k % 2 * blk + blk, :] = total[:, pl.ds(at, blk), :].astype(bf16)


def flash_backward(m, meta, q, out, grad, lse, cosine, sine, part):
    n_ctx, _, rows, _ = part.shape
    blk = rows // 2
    return pl.pallas_call(
        flash_backward_kernel,
        grid=(1,),
        out_shape=[
            jax.ShapeDtypeStruct((rows, QP), bf16),
            jax.ShapeDtypeStruct((n_ctx, KVH, rows, 128), bf16),
        ],
        in_specs=[
            SM,
            pl.BlockSpec((QH, rows, 128), lambda i: (0, m, 0)),
            pl.BlockSpec((rows, QP), lambda i: (0, 0)),
            pl.BlockSpec((rows, QP), lambda i: (m, 0)),
            pl.BlockSpec((16, 1, rows), lambda i: (0, 0, 0)),
            pl.BlockSpec((rows, 128), lambda i: (0, 0)),
            pl.BlockSpec((rows, 128), lambda i: (0, 0)),
            ANY,
        ],
        out_specs=[
            pl.BlockSpec((rows, QP), lambda i: (0, 0)),
            pl.BlockSpec((n_ctx, KVH, rows, 128), lambda i: (0, 0, 0, 0)),
        ],
        scratch_shapes=[
            pltpu.VMEM((KVH, n_ctx * rows, 128), bf16),
            pltpu.VMEM((KVH, 64, n_ctx * rows), bf16),
            pltpu.VMEM((QH, rows, 128), bf16),
            pltpu.VMEM((16, 1, rows), f32),
            pltpu.VMEM((KVH, n_ctx * rows, 128), f32),
            pltpu.VMEM((GRP, 64, blk), f32),
            pltpu.VMEM((QP, blk), f32),
            pltpu.VMEM((2 * GRP * blk, 128), bf16),
            pltpu.SemaphoreType.DMA((2 * n_ctx,)),
        ],
        compiler_params=params(56),
        cost_estimate=cost(50e9, 16 << 20),
    )(meta, q, out, grad, lse, cosine, sine, part)


def assemble_ffn_kernel(table, pool_ref, gu_out, d_out, pool, wgu, wd, sems):
    load = pltpu.make_async_copy(pool_ref, pool, sems.at[0])
    load.start()
    load.wait()
    stores = []
    for part in range(5):
        gu_rows(pool, table, wgu, 3 * part, 3 * part + 3)
        span = pl.ds(192 * part, 192)
        stores.append(pltpu.make_async_copy(wgu.at[span], gu_out.at[span], sems.at[1 + part]))
        stores[-1].start()
    for part in range(4):
        d_rows(pool, table, wd, 10 * part, 10 * part + 10)
        span = pl.ds(640 * part, 640)
        stores.append(pltpu.make_async_copy(wd.at[span], d_out.at[span], sems.at[6 + part]))
        stores[-1].start()
    for copy in stores:
        copy.wait()


def assemble_ffn(table, pool):
    shapes = [(D, 2 * FF), (FF, D)]
    return pl.pallas_call(
        assemble_ffn_kernel,
        out_shape=[jax.ShapeDtypeStruct(s, bf16) for s in shapes],
        in_specs=[SM, ANY],
        out_specs=[ANY, ANY],
        scratch_shapes=[pltpu.VMEM(s, bf16) for s in [pool.shape] + shapes] + [pltpu.SemaphoreType.DMA((10,))],
        compiler_params=params(52),
        cost_estimate=cost(0, 64 << 20),
    )(table, pool)


CHUNK = 512


def middle_kernel(
    table_0, table_1, gu_ref, d_ref, out_0, out_1, wo, x_ref, cot_ref, gain_ref,
    mixed_ref, normed_t, hidden_t, ggu_ref, go_ref, branch_ref, residual_ref, attn_ref, gain_out,
    wgu, wd, sems,
):
    i = pl.program_id(0)
    blk = x_ref.shape[0]
    loads = [pltpu.make_async_copy(gu_ref, wgu, sems.at[0]), pltpu.make_async_copy(d_ref, wd, sems.at[1])]

    @pl.when(i == 0)
    def _():
        for load in loads:
            load.start()

    attn = jnp.where(i < 2, out_0[...], out_1[...])
    residual = x_ref[...].astype(f32) + jnp.dot(attn, wo[...], preferred_element_type=f32)
    inverse = lax.rsqrt(jnp.mean(residual * residual, axis=1, keepdims=True) + epsilon)
    gain = gain_ref[...]
    normed = (residual * inverse * gain).astype(bf16)
    normed_t[...] = normed.T
    row = table_0[i % 2] * blk + lax.broadcasted_iota(jnp.int32, (blk, D), 0)
    grad_out = cot_ref[0].T
    grad_out = jnp.where(row < jnp.where(i < 2, table_0[2], table_1[2]), grad_out, jnp.zeros((), bf16))
    go_ref[...] = grad_out

    @pl.when(i == 0)
    def _():
        for load in loads:
            load.wait()

    def first(j):
        at = CHUNK * j
        return (
            jnp.dot(normed, wgu[:, at : at + CHUNK], preferred_element_type=f32),
            jnp.dot(normed, wgu[:, FF + at : FF + at + CHUNK], preferred_element_type=f32),
            nt_dot(grad_out, wd[at : at + CHUNK, :]),
        )

    mixed = residual
    grad_normed = jnp.zeros((blk, D), f32)
    ahead = first(0)
    for j in range(FF // CHUNK):
        at = CHUNK * j
        gate, up, grad_hidden = ahead
        if j + 1 < FF // CHUNK:
            ahead = first(j + 1)
        sigma = jax.nn.sigmoid(gate)
        silu = gate * sigma
        hidden = (silu * up).astype(bf16)
        grad_up = (grad_hidden * silu).astype(bf16)
        grad_gate = (grad_hidden * up * (sigma + silu * (1.0 - sigma))).astype(bf16)
        hidden_t[at : at + CHUNK, :] = hidden.T
        ggu_ref[:, at : at + CHUNK] = grad_gate
        ggu_ref[:, FF + at : FF + at + CHUNK] = grad_up
        mixed = mixed + jnp.dot(hidden, wd[at : at + CHUNK, :], preferred_element_type=f32)
        grad_normed = grad_normed + nt_dot(grad_gate, wgu[:, at : at + CHUNK])
        grad_normed = grad_normed + nt_dot(grad_up, wgu[:, FF + at : FF + at + CHUNK])

    mixed_ref[0] = mixed.astype(bf16).T
    unit = residual * inverse
    scaled = grad_normed * gain
    back = inverse * (scaled - unit * jnp.mean(scaled * unit, axis=1, keepdims=True))
    grad_residual = grad_out.astype(f32) + back
    residual_ref[...] = grad_residual
    branch = grad_residual.astype(bf16)
    branch_ref[...] = branch
    attn_ref[...] = nt_dot(branch, wo[...]).astype(bf16)
    term = jnp.sum(grad_normed * unit, axis=0, keepdims=True)

    @pl.when(i == 0)
    def _():
        gain_out[...] = term

    @pl.when(i > 0)
    def _():
        gain_out[...] += term


def middle(tables, wgu, wd, outs, wo, x_rows, cot_t, gain):
    micro, _, rows = cot_t.shape
    tokens = micro * rows
    blk = rows // 2

    def rows_of(width, kind):
        return jax.ShapeDtypeStruct((tokens, width), kind), pl.BlockSpec((blk, width), lambda i: (i, 0))

    def columns_of(height):
        return jax.ShapeDtypeStruct((height, tokens), bf16), pl.BlockSpec((height, blk), lambda i: (0, i))

    native = pl.BlockSpec((1, D, blk), lambda i: (i // 2, 0, i % 2))
    whole = pl.BlockSpec((1, D), lambda i: (0, 0))
    results = [
        (jax.ShapeDtypeStruct((micro, D, rows), bf16), native),
        columns_of(D),
        columns_of(FF),
        rows_of(2 * FF, bf16),
        rows_of(D, bf16),
        rows_of(D, bf16),
        rows_of(D, f32),
        rows_of(QP, bf16),
        (jax.ShapeDtypeStruct((1, D), f32), whole),
    ]
    return pl.pallas_call(
        middle_kernel,
        grid=(2 * micro,),
        out_shape=[r[0] for r in results],
        in_specs=[
            SM,
            SM,
            ANY,
            ANY,
            pl.BlockSpec((blk, QP), lambda i: (jnp.minimum(i, 1), 0)),
            pl.BlockSpec((blk, QP), lambda i: (jnp.maximum(i - 2, 0), 0)),
            pl.BlockSpec((QP, D), lambda i: (0, 0)),
            pl.BlockSpec((blk, D), lambda i: (i, 0)),
            native,
            whole,
        ],
        out_specs=[r[1] for r in results],
        scratch_shapes=[
            pltpu.VMEM((D, 2 * FF), bf16),
            pltpu.VMEM((FF, D), bf16),
            pltpu.SemaphoreType.DMA((2,)),
        ],
        compiler_params=params(62),
        cost_estimate=cost(40e9, 40 << 20),
    )(*tables, wgu, wd, outs[0], outs[1], wo, x_rows, cot_t, gain)


def ffn_grads_kernel(table, normed_t, ggu_ref, hidden_t, go_ref, pool_out, pool, gu_0, d_0, gu_1, d_1, sems):
    j = pl.program_id(0)
    steps = pl.num_programs(0)

    def multiply(part, gu, d):
        columns = slice(512 * part, 512 * part + 512)
        gu[...] = jnp.dot(normed_t[...], ggu_ref[:, columns], preferred_element_type=f32).astype(bf16)
        rows = slice(256 * part, 256 * part + 256)
        d[...] = jnp.dot(hidden_t[rows, :], go_ref[...], preferred_element_type=f32).astype(bf16)

    def put(chunk, gu, d):
        base = 600 * (chunk // 5) + 8 * (chunk % 5)
        for r in range(15):
            for p in range(4):
                at = base + r * 40 + 2 * p
                pick_pair(pool, table, gu, 64 * r, 128 * p, at, at + 1)
        for r in range(4):
            at = 1200 + (4 * chunk + r) * 15
            for p in range(7):
                pick_pair(pool, table, d, 64 * r, 128 * p, at + 2 * p, at + 2 * p + 1)
            pick_single(pool, table, d, 64 * r, 896, at + 14)

    put((2 * j + 2 * steps - 1) % (2 * steps), gu_1, d_1)
    multiply(0, gu_0, d_0)
    put(2 * j, gu_0, d_0)
    multiply(1, gu_1, d_1)

    @pl.when(j == steps - 1)
    def _():
        put(2 * steps - 1, gu_1, d_1)
        flush_pool(pool, [pool_out], sems)


def ffn_grads(table, normed_t, ggu, hidden_t, go, total):
    tokens = go.shape[0]
    return pl.pallas_call(
        ffn_grads_kernel,
        grid=(5,),
        out_shape=jax.ShapeDtypeStruct((total, 32, 128), bf16),
        in_specs=[
            SM,
            pl.BlockSpec((D, tokens), lambda j: (0, 0)),
            pl.BlockSpec((tokens, 1024), lambda j: (0, j)),
            pl.BlockSpec((512, tokens), lambda j: (j, 0)),
            pl.BlockSpec((tokens, D), lambda j: (0, 0)),
        ],
        out_specs=ANY,
        scratch_shapes=[
            pltpu.VMEM((total, 32, 128), bf16),
            pltpu.VMEM((D, 512), bf16),
            pltpu.VMEM((256, D), bf16),
            pltpu.VMEM((D, 512), bf16),
            pltpu.VMEM((256, D), bf16),
            pltpu.SemaphoreType.DMA((1,)),
        ],
        compiler_params=params(52),
        cost_estimate=cost(15e9, 60 << 20),
    )(table, normed_t, ggu, hidden_t, go)


def inward_kernel(
    table, gq_0, gq_1, gkv_0, gkv_1, cos_ref, sin_ref, w_ref, normed_t, out_0, out_1,
    branch_ref, x_ref, residual_ref, gain_ref, ffn_term, grad_ref, gain_out, pool_out,
    cat, dqkv, dwo, pool, sems,
):
    i = pl.program_id(0)
    blk = x_ref.shape[0]
    half = branch_ref.shape[0] // 2
    early = i < 2
    at = pl.ds(pl.multiple_of(i * blk, blk), blk)
    cosine, sine = cos_ref[...], sin_ref[...]
    left = lax.broadcasted_iota(jnp.int32, (blk, 128), 1) < 64
    key_cosine = jnp.where(left, cosine, 1.0)
    key_sine = jnp.where(left, sine, 0.0)
    parts = [jnp.where(early, gq_0[...], gq_1[...])]
    for g in range(KVH):
        slab = jnp.where(early, gkv_0[g].astype(f32), gkv_1[g])
        parts.append((slab * key_cosine - swap_halves(slab) * key_sine).astype(bf16))
    terms = jnp.concatenate(parts, axis=1)
    cat[at, :] = terms
    grad_normed = nt_dot(terms, w_ref[...])
    new_wo = jnp.dot(out_0[...], branch_ref[:half, :], preferred_element_type=f32)
    new_wo = new_wo + jnp.dot(out_1[...], branch_ref[half:, :], preferred_element_type=f32)
    dwo[...] = new_wo.astype(bf16)
    x = x_ref[...].astype(f32)
    inverse = lax.rsqrt(jnp.mean(x * x, axis=1, keepdims=True) + epsilon)
    unit = x * inverse
    scaled = grad_normed * gain_ref[...]
    back = inverse * (scaled - unit * jnp.mean(scaled * unit, axis=1, keepdims=True))
    grad_ref[0] = (residual_ref[...] + back).T
    term = jnp.sum(grad_normed * unit, axis=0, keepdims=True)
    for r in range(4):
        first = 375 + (4 * i + r) * 15
        for p in range(7):
            pick_pair(pool, table, dwo, 64 * r, 128 * p, first + 2 * p, first + 2 * p + 1)
        pick_single(pool, table, dwo, 64 * r, 896, first + 14)

    @pl.when(i == 0)
    def _():
        gain_out[0:1, :] = term
        gain_out[1:2, :] = ffn_term[...]

    @pl.when(i > 0)
    def _():
        gain_out[0:1, :] += term

    @pl.when(i == pl.num_programs(0) - 1)
    def _():
        for low, high in ((0, 512), (512, QP), (QP, CW)):
            dqkv[:, low:high] = jnp.dot(
                normed_t[...], cat[:, low:high], preferred_element_type=f32
            ).astype(bf16)
        for p in range(7):
            for r in range(15):
                pick_pair(pool, table, dqkv, 64 * r, 128 * p, r * 15 + 2 * p, r * 15 + 2 * p + 1)
        for r in range(15):
            pick_single(pool, table, dqkv, 64 * r, 896, r * 15 + 14)
        for g in range(KVH):
            for r in range(15):
                pick_pair(pool, table, dqkv, 64 * r, QP + 128 * g, 225 + r * 5 + g, 300 + r * 5 + g)
        flush_pool(pool.at[pl.ds(0, pool_out.shape[0])], [pool_out], sems)


def inward(table, gq, gkv, cosine, sine, wqkv, normed_t, outs_t, branch, x_rows, residual, gain, ffn_term, total):
    rows = cosine.shape[0]
    tokens = x_rows.shape[0]
    blk = rows // 2
    steps = tokens // blk
    table = jnp.concatenate([table, jnp.full((15,), total, jnp.int32)])

    def early(i):
        return jnp.minimum(i, 1)

    def late(i):
        return jnp.maximum(i - 2, 0)

    def rows_of(width, at=lambda i: i):
        return pl.BlockSpec((blk, width), lambda i: (at(i), 0))

    def slabs(at):
        return pl.BlockSpec((KVH, blk, 128), lambda i: (0, at(i), 0))

    def all_of(*shape):
        return pl.BlockSpec(shape, lambda i: (0, 0))

    features = pl.BlockSpec((QP // steps, rows), lambda i: (i, 0))
    return pl.pallas_call(
        inward_kernel,
        grid=(steps,),
        out_shape=[
            jax.ShapeDtypeStruct((tokens // rows, D, rows), f32),
            jax.ShapeDtypeStruct((2, D), f32),
            jax.ShapeDtypeStruct((total, 32, 128), bf16),
        ],
        in_specs=[
            SM, rows_of(QP, early), rows_of(QP, late), slabs(early), slabs(late),
            rows_of(128, lambda i: i % 2), rows_of(128, lambda i: i % 2),
            all_of(D, CW), all_of(D, tokens), features, features,
            all_of(tokens, D), rows_of(D), rows_of(D), all_of(1, D), all_of(1, D),
        ],
        out_specs=[pl.BlockSpec((1, D, blk), lambda i: (i // 2, 0, i % 2)), all_of(2, D), ANY],
        scratch_shapes=[
            pltpu.VMEM((tokens, CW), bf16),
            pltpu.VMEM((D, CW), bf16),
            pltpu.VMEM((QP // steps, D), bf16),
            pltpu.VMEM((total + 1, 32, 128), bf16),
            pltpu.SemaphoreType.DMA((1,)),
        ],
        compiler_params=params(60),
        cost_estimate=cost(12e9, 30 << 20),
    )(table, *gq, *gkv, cosine, sine, wqkv, normed_t, *outs_t, branch, x_rows, residual, gain, ffn_term)


TOGETHER = 11


def shampoo_kernel(
    filled, sum_a, sum_f, master, stat_left, stat_right, root_left, root_right,
    grads_out, left_out, right_out, master_out, grads, lefts, rights, gram_left, gram_right, step,
):
    slots = master.shape[1]
    n_a = sum_a.shape[0] // 32
    for source, target in ((root_left, lefts), (root_right, rights)):
        for r in range(32):
            both = jnp.concatenate(
                [source[64 * r : 64 * r + 64, :], source[64 * (r + 32) : 64 * (r + 32) + 64, :]], axis=0
            )
            target[pl.ds(r, slots, stride=32), :] = both.T

    def square(rows):
        return jnp.concatenate([rows[:, :64], rows[:, 64:]], axis=0)

    def folded(rows):
        return jnp.concatenate([rows[:32], rows[32:]], axis=1)

    def keep(source, count, shift):
        def one(s, _):
            grad = source[pl.ds(pl.multiple_of(s * 32, 32), 32), :]
            at = pl.ds(pl.multiple_of((s + shift) * 32, 32), 32)
            grads[at, :] = jnp.where(filled[s + shift] > 0, grad.astype(f32), 0.0)
            return 0

        lax.fori_loop(0, count, one, 0, unroll=8)

    keep(sum_a, n_a, 0)
    keep(sum_f, slots - n_a, n_a)

    def several(i, _):
        spans = [pl.ds(pl.multiple_of((TOGETHER * i + t) * 32, 32), 32) for t in range(TOGETHER)]
        grad = [square(grads[span, :]).astype(bf16) for span in spans]
        left = [square(lefts[span, :]).astype(bf16) for span in spans]
        right = [square(rights[span, :]).astype(bf16) for span in spans]
        half = [jnp.dot(a, g, preferred_element_type=f32) for a, g in zip(left, grad)]
        gram_l = [nt_dot(g, g) for g in grad]
        gram_r = [tn_dot(g, g) for g in grad]
        whole = [jnp.dot(h.astype(bf16), b, preferred_element_type=f32) for h, b in zip(half, right)]
        for t, span in enumerate(spans):
            gram_left[span, :] = folded(gram_l[t])
            gram_right[span, :] = folded(gram_r[t])
            step[span, :] = folded(whole[t])
        return 0

    lax.fori_loop(0, grads.shape[0] // (32 * TOGETHER), several, 0)

    for r in range(32):
        first = slice(64 * r, 64 * r + 64)
        second = slice(64 * (r + 32), 64 * (r + 32) + 64)
        rows = pl.ds(r, slots, stride=32)
        flipped = grads[rows, :].T
        grads_out[first, :] = flipped[:64]
        grads_out[second, :] = flipped[64:]
        for source, stat, out in ((gram_left, stat_left, left_out), (gram_right, stat_right, right_out)):
            flipped = source[rows, :].T
            out[first, :] = decay_rate * stat[first, :] + (1.0 - decay_rate) * flipped[:64]
            out[second, :] = decay_rate * stat[second, :] + (1.0 - decay_rate) * flipped[64:]
        flipped = step[rows, :].T
        master_out[first, :] = master[first, :] - step_rate * flipped[:64]
        master_out[second, :] = master[second, :] - step_rate * flipped[64:]


def shampoo(filled, sum_a, sum_f, *arrays):
    slots = arrays[0].shape[0]
    native = [a.transpose(1, 2, 0).reshape(TL * TL, slots) for a in arrays]
    scratch = pltpu.VMEM((-(-slots // TOGETHER) * TOGETHER * 32, 128), f32)
    results = pl.pallas_call(
        shampoo_kernel,
        out_shape=[jax.ShapeDtypeStruct((TL * TL, slots), f32)] * 4,
        in_specs=[SM] + [VM] * 7,
        out_specs=[VM] * 4,
        scratch_shapes=[scratch] * 6,
        compiler_params=params(48),
        cost_estimate=cost(1e9, 24 << 20),
    )(filled, sum_a.reshape(-1, 128), sum_f.reshape(-1, 128), *native)
    return [r.reshape(TL, TL, slots).transpose(2, 0, 1) for r in results]


def fold(tiles):
    return jnp.concatenate([tiles[:, :32, :], tiles[:, 32:, :]], axis=2)


def shards(
    inputs,
    cotangent,
    lengths,
    order,
    owner_slots,
    master,
    stat_left,
    stat_right,
    root_left,
    root_right,
    gains,
    gain_stats,
):
    micro, rows = inputs.shape[1], inputs.shape[2]
    n_ctx, n_wt = lax.axis_size("ctx"), lax.axis_size("wt")
    devices = n_ctx * n_wt
    line = is_line(n_ctx, n_wt)
    tokens = micro * rows
    cap = master.shape[0]
    cap_a = NTA // devices + NTA // (8 * devices) + 2
    cap_f = cap - cap_a
    c = lax.axis_index("ctx")
    w = lax.axis_index("wt")

    x_t = inputs[0].transpose(0, 2, 1)
    low_master = fold(master.astype(bf16))
    own_a, own_f = low_master[:cap_a], low_master[cap_a:]
    own_a, own_f = low_master[:cap_a], low_master[cap_a:]
    owner, within = owner_slots // cap, owner_slots % cap
    whole_a = owner[:NTA] * cap_a + within[:NTA]
    whole_f = owner[NTA:] * cap_f + within[NTA:] - cap_a

    blocks = order.shape[0]
    ids = jnp.arange(blocks, dtype=jnp.int32)
    my_blocks = jnp.sum(jnp.where(ids[None, :] == 2 * c + jnp.arange(2)[:, None], order[None, :], 0), axis=1)
    position = (my_blocks[:, None] * (rows // 2) + jnp.arange(rows // 2, dtype=jnp.int32)[None, :]).reshape(rows)
    lane = np.arange(128)
    frequency = jnp.asarray(rope_base, f32) ** (-(jnp.asarray(lane % 32, f32)) * 2.0 / HD)
    angle = position.astype(f32)[:, None] * frequency[None, :]
    cosine = jnp.cos(angle)
    sine = jnp.sin(angle) * jnp.where(lane % 64 < 32, -1.0, 1.0).astype(f32)[None, :]
    metas = [
        jnp.concatenate([my_blocks, lengths[0, m][None], c[None], order]).astype(jnp.int32)
        for m in range(micro)
    ]

    if line:
        q, normed_attn_t, x_low, kv_first, kv_late, wqkv, wo, pool_f = front(
            whole_a, own_a, own_f, x_t, gains[0:1], cosine, sine
        )
        pool_f = pool_f.reshape(devices * cap_f, 32, 128)
        chunks = [kv_first, lax.all_gather(kv_late, "ctx", axis=0)]
    else:
        parts_a = [lax.all_gather(own_a, AXES, axis=0, tiled=True)]
        pool_f = lax.all_gather(own_f, AXES, axis=0, tiled=True)
        wqkv, wo = assemble(assemble_attn_kernel, parts_a, whole_a, [(D, CW), (QP, D)])
        x_low = inputs.reshape(tokens, D)
        q, kv, normed_attn = qkv_rows(x_low, gains[0:1], wqkv, cosine, sine, micro)
        normed_attn_t = normed_attn.T
        chunks = [lax.all_gather(kv[m], "ctx", axis=0) for m in range(micro)]
    forward = [flash_forward(0, metas[0], q, chunks[0])]
    wgu, wd = assemble_ffn(after(whole_f, forward[0][0]), pool_f)
    forward.append(flash_forward(1, metas[1], q, after(chunks[1], wgu)))
    cot_t = cotangent[0].transpose(0, 2, 1)
    outs = [f[0] for f in forward]
    (mixed_t, normed_ffn_t, hidden_t, grad_gu, grad_out, grad_branch, grad_residual, grad_attn, gain_ffn) = middle(
        metas, wgu, wd, outs, wo, x_low, cot_t, gains[1:2]
    )
    def flash_back(m):
        out, _, lse = forward[m]
        return flash_backward(m, metas[m], q, out, grad_attn, lse, cosine, sine, chunks[m])

    gq_0, gkv_0 = flash_back(0)
    gkv_0 = lax.psum_scatter(gkv_0, "ctx", scatter_dimension=0, tiled=False)
    grad_out = after(grad_out, gq_0)
    pool_f = ffn_grads(whole_f, normed_ffn_t, grad_gu, hidden_t, grad_out, devices * cap_f)
    grad_attn = after(grad_attn, pool_f)
    gq_1, gkv_1 = flash_back(1)
    if line:
        near_f, half_x, half_y, gkv_1 = back_home(pool_f.reshape(4, 4, 2, cap_f, 32, 128), gkv_1)
        other_x, other_y = flip(half_x, 2), flip(half_y, 4)
    else:
        sum_f = lax.psum_scatter(pool_f.astype(f32), AXES, scatter_dimension=0, tiled=True)
        gkv_1 = lax.psum_scatter(gkv_1, "ctx", scatter_dimension=0, tiled=False).astype(f32)
    input_grad_t, gain_terms, pool_a = inward(
        whole_a, (gq_0, gq_1), (gkv_0, gkv_1), cosine, sine, wqkv, normed_attn_t, [f[1] for f in forward], grad_branch, x_low,
        grad_residual, gains[0:1], gain_ffn, devices * cap_a,
    )
    if line:
        other_y, other_x = after([other_y, other_x], pool_a)
        pool_a = pool_a.reshape(4, 4, 2, cap_a, 32, 128)
        sum_a, sum_f, gain_grads = tail(pool_a, near_f, other_x, other_y, gain_terms)
    else:
        sum_a = lax.psum_scatter(pool_a.astype(f32), AXES, scatter_dimension=0, tiled=True)
        gain_grads = lax.psum(gain_terms, AXES)

    here = (c * n_wt + w) * cap + jnp.arange(cap, dtype=jnp.int32)
    filled = jnp.max((owner_slots[None, :] == here[:, None]).astype(jnp.int32), axis=1)
    tile_grads, new_left, new_right, new_master = shampoo(
        filled, sum_a, sum_f, master, stat_left, stat_right, root_left, root_right
    )
    new_gain_stats = decay_rate * gain_stats + (1.0 - decay_rate) * gain_grads * gain_grads
    new_gains = gains - gain_rate * gain_grads * lax.rsqrt(new_gain_stats)
    return (
        mixed_t.transpose(0, 2, 1)[None],
        input_grad_t.transpose(0, 2, 1)[None],
        tile_grads,
        new_left,
        new_right,
        new_master,
        gain_grads,
        new_gain_stats,
        new_gains,
    )


def solution(mesh):
    in_specs = (
        P("wt", None, "ctx", None),
        P("wt", None, "ctx", None),
        P("wt", None),
        P(),
        P(),
        P(AXES, None, None),
        P(AXES, None, None),
        P(AXES, None, None),
        P(AXES, None, None),
        P(AXES, None, None),
        P(),
        P(),
    )
    out_specs = (
        P("wt", None, "ctx", None),
        P("wt", None, "ctx", None),
        P(AXES, None, None),
        P(AXES, None, None),
        P(AXES, None, None),
        P(AXES, None, None),
        P(),
        P(),
        P(),
    )
    return jax.shard_map(shards, mesh=mesh, in_specs=in_specs, out_specs=out_specs, check_vma=False)
```
